32 devices in a mesh: vel: 2 (over x), cx: 4 (over y, core), cy: 4 (over z).
Axes of the slice: x: 2, y: 2, z: 4, core: 2. Of those that a mesh axis runs over, the one named last changes fastest.
Arguments:
- distribution: float32 [64, 16, 4, 13824], P('cx', 'cy', None, 'vel'), may hold values from 0.1 to 2
- refine_level: int32 [64, 16, 4], P('cx', 'cy'), may hold values from 0 to 2, as said below
- gain_one: float32 [24, 24, 24], replicated, may hold values from 0 to 2
- gain_two: float32 [24, 24, 24], replicated, may hold values from 0 to 2
- loss_kernel: float32 [24, 24, 24], replicated, may hold values from 0 to 2
Outputs:
- evolved: float32 [64, 16, 4, 13824], P('cx', 'cy', None, 'vel')
The draws below stay inside these ranges and needn't reach their ends.
Inputs may be any that keep to these rules, and one draw needn't show every extreme that they name: `refine_level`: in each block of 256 cells (the 16 x 4 x 4 cells of one index of cx and cy) at most 128 cells have a level above 0, and some block has exactly 128.
All inputs are finite; a program needn't handle non-finite values.
Results may differ from the reference program's by a relative error of at most 0.0022.
Values may be sent and summed in bfloat16 or wider, within the bound.
No kernel may reach another device: no remote copies, remote signals or barrier semaphores. Data moves between devices by JAX's collectives and lax.ppermute only.
A program may use at most 128 MiB of HBM per device.

```python
import math
import jax
import jax.numpy as jnp
from jax import lax

NV = 24
CX = 16
CY = 4
CZ = 4
VEL = 13824
NX = 64
NY = 16
NZ = 4
BLOCK = 256
BLOCKS = 16
ACT_MAX = 128


def draw_refine_level(key, part):
    key_count, key_full, key_rank, key_level = jax.random.split(key, 4)
    halving = jax.random.randint(key_count, (BLOCKS,), 0, 4)
    counts = jnp.right_shift(jnp.full((BLOCKS,), ACT_MAX, jnp.int32), halving)
    full_block = jax.random.randint(key_full, (), 0, BLOCKS)
    counts = jnp.where(jnp.arange(BLOCKS) == full_block, ACT_MAX, counts)
    rank_order = jax.vmap(lambda rank_key: jax.random.permutation(rank_key, BLOCK))(jax.random.split(key_rank, BLOCKS))
    active = rank_order < counts[:, None]
    levels = jax.random.randint(key_level, (BLOCKS, BLOCK), 1, 3) * active.astype(jnp.int32)
    level_grid = levels.reshape(NX // CX, NY // CY, CX, CY, CZ).transpose(0, 2, 1, 3, 4)
    return level_grid.reshape(NX, NY, NZ)


def block_scale(own_key, extent, pieces, smallest, largest):
    def one(axis_at, blocks):
        steps = jax.random.uniform(jax.random.fold_in(jax.random.fold_in(own_key, 6), axis_at), (blocks,), jnp.float32, smallest / len(pieces), largest / len(pieces))
        return jnp.repeat(jnp.exp(steps), extent[axis_at] // blocks).reshape((-1,) + (1,) * (len(extent) - axis_at - 1))

    level = one(*pieces[0])
    for cut in pieces[1:]:
        level = level * one(*cut)
    return level


def setup_inputs(seed: int = 0) -> dict:
    arg_keys = jax.random.split(jax.random.key(seed), 6)
    distribution = jnp.clip(jnp.exp(math.log(2.0) - 2.9957323 * jax.random.uniform(arg_keys[0], (NX, NY, NZ, VEL), jnp.float32) ** block_scale(arg_keys[0], (NX, NY, NZ, VEL), ((0, 4), (1, 4), (3, 2)), -0.2, 0.2)), 0.1, 2.0)
    refine_level = draw_refine_level(jax.random.fold_in(arg_keys[5], 71), 0)
    gain_one = jnp.clip(jax.random.uniform(arg_keys[2], (NV, NV, NV), jnp.float32, 0.0, 2.0), 0.0, 2.0)
    gain_two = jnp.clip(jax.random.uniform(arg_keys[3], (NV, NV, NV), jnp.float32, 0.0, 2.0), 0.0, 2.0)
    loss_kernel = jnp.clip(jax.random.uniform(arg_keys[4], (NV, NV, NV), jnp.float32, 0.0, 2.0), 0.0, 2.0)
    return {"distribution": distribution, "refine_level": refine_level, "gain_one": gain_one, "gain_two": gain_two, "loss_kernel": loss_kernel}


def dft_tables(points):
    indices = jnp.arange(points, dtype=jnp.int32)
    products = (indices[:, None] * indices[None, :]) % points
    angles = products.astype(jnp.float32) * (2.0 * math.pi / points)
    cosine = jnp.cos(angles)
    sine_table = jnp.sin(angles)
    forward = jnp.stack([jnp.stack([cosine, sine_table]), jnp.stack([-sine_table, cosine])])
    inverse = jnp.stack([jnp.stack([cosine, -sine_table]), jnp.stack([sine_table, cosine])])
    return forward.astype(jnp.bfloat16), inverse.astype(jnp.bfloat16)


def contract(pattern, left_side, right_side):
    return jnp.einsum(pattern, left_side.astype(jnp.float32), right_side.astype(jnp.float32))


def collide(cells, forward, inverse, gain_one, gain_two, loss_kernel):
    points = forward.shape[-1]
    cell_count = cells.shape[0]
    field = cells.reshape(cell_count, points, points, points)
    section_z = contract("nabz,qzw->qnabw", field, forward[:, 0]).astype(jnp.bfloat16)
    section_y = contract("pnayc,qpyw->qnawc", section_z, forward).astype(jnp.bfloat16)
    spectrum = contract("pnxbc,qpxw->qnwbc", section_y, forward)
    scale_factor = 1.0 / float(points ** 3)

    def filtered(kernel):
        weighted = (spectrum * (kernel * scale_factor)[None, None]).astype(jnp.bfloat16)
        back_x = contract("pnxbc,qpxw->qnwbc", weighted, inverse).astype(jnp.bfloat16)
        back_y = contract("pnayc,qpyw->qnawc", back_x, inverse).astype(jnp.bfloat16)
        return contract("pnabz,pzw->nabw", back_y, inverse[0])

    gain_term = filtered(gain_one) * filtered(gain_two)
    result = gain_term - field.astype(jnp.float32) * filtered(loss_kernel)
    return result.reshape(cell_count, points ** 3)


def courants(points, first_vel, local_count):
    vel_index = first_vel + jnp.arange(local_count, dtype=jnp.int32)
    index_x = vel_index // (points * points)
    index_y = (vel_index // points) % points
    index_z = vel_index % points

    def speed(index_part):
        return 0.3 * (2.0 * index_part.astype(jnp.float32) - (points - 1)) / (points - 1)

    return speed(index_x), speed(index_y), speed(index_z)


def upwind_flux(courant, center, lower_side, upper_side):
    return jnp.maximum(courant, 0.0) * (center - lower_side) + jnp.minimum(courant, 0.0) * (upper_side - center)


def reference(distribution, refine_level, gain_one, gain_two, loss_kernel):
    points = gain_one.shape[0]
    courant_x, courant_y, courant_z = courants(points, 0, points ** 3)
    fluxes = upwind_flux(courant_x, distribution, jnp.roll(distribution, 1, 0), jnp.roll(distribution, -1, 0))
    fluxes = fluxes + upwind_flux(courant_y, distribution, jnp.roll(distribution, 1, 1), jnp.roll(distribution, -1, 1))
    fluxes = fluxes + upwind_flux(courant_z, distribution, jnp.roll(distribution, 1, 2), jnp.roll(distribution, -1, 2))
    read = distribution - fluxes
    forward, inverse = dft_tables(points)
    cell_blocks = read.reshape(-1, BLOCK, points ** 3).astype(jnp.bfloat16)
    collision = lax.map(lambda cell_block: collide(cell_block, forward, inverse, gain_one, gain_two, loss_kernel), cell_blocks)
    collision = collision.reshape(read.shape)
    weight = 0.25 * refine_level.astype(jnp.float32)
    return read + weight[..., None] * collision
```

```python
import functools
import math

import jax
import jax.numpy as jnp
import ml_dtypes
import numpy as np
from jax import lax
from jax.experimental import pallas as pl
from jax.experimental.pallas import tpu as pltpu
from jax.sharding import PartitionSpec as P


def extended(array, sides, width):
    for axis, dim in sides:
        count, length = (lax.axis_size(axis), array.shape[dim])
        up = [(i, (i + 1) % count) for i in range(count)]
        down = [(j, i) for i, j in up]
        last = lax.slice_in_dim(array, length - width, length, axis=dim)
        leading = lax.slice_in_dim(array, 0, width, axis=dim)
        before = lax.ppermute(last, axis, up)
        after = lax.ppermute(leading, axis, down)
        array = jnp.concatenate([before, array, after], axis=dim)
    return array


def dft_tables(points):
    indices = jnp.arange(points, dtype=jnp.int32)
    products = indices[:, None] * indices[None, :] % points
    angles = products.astype(jnp.float32) * (2.0 * math.pi / points)
    cosine = jnp.cos(angles)
    sine_table = jnp.sin(angles)
    forward = jnp.stack([jnp.stack([cosine, sine_table]), jnp.stack([-sine_table, cosine])])
    inverse = jnp.stack([jnp.stack([cosine, -sine_table]), jnp.stack([sine_table, cosine])])
    return (forward.astype(jnp.bfloat16), inverse.astype(jnp.bfloat16))


def contract(pattern, left_side, right_side):
    return jnp.einsum(pattern, left_side, right_side, preferred_element_type=jnp.float32)


def collide(cells, forward, inverse, gain_one, gain_two, loss_kernel):
    points = forward.shape[-1]
    cell_count = cells.shape[0]
    field = cells.reshape(cell_count, points, points, points)
    section_z = contract("nabz,qzw->qnabw", field, forward[:, 0]).astype(jnp.bfloat16)
    section_y = contract("pnayc,qpyw->qnawc", section_z, forward).astype(jnp.bfloat16)
    spectrum = contract("pnxbc,qpxw->qnwbc", section_y, forward)
    scale_factor = 1.0 / float(points**3)

    def filtered(kernel):
        weighted = (spectrum * (kernel * scale_factor)[None, None]).astype(jnp.bfloat16)
        back_x = contract("pnxbc,qpxw->qnwbc", weighted, inverse).astype(jnp.bfloat16)
        back_y = contract("pnayc,qpyw->qnawc", back_x, inverse).astype(jnp.bfloat16)
        return contract("pnabz,pzw->nabw", back_y, inverse[0])

    gain_term = filtered(gain_one) * filtered(gain_two)
    result = gain_term - field.astype(jnp.float32) * filtered(loss_kernel)
    return result.reshape(cell_count, points**3)


def courants(points, first_vel, local_count):
    vel_index = first_vel + jnp.arange(local_count, dtype=jnp.int32)
    index_x = vel_index // (points * points)
    index_y = vel_index // points % points
    index_z = vel_index % points

    def speed(index_part):
        return 0.3 * (2.0 * index_part.astype(jnp.float32) - (points - 1)) / (points - 1)

    return (speed(index_x), speed(index_y), speed(index_z))


def upwind_flux(courant, center, lower_side, upper_side):
    return jnp.maximum(courant, 0.0) * (center - lower_side) + jnp.minimum(courant, 0.0) * (
        upper_side - center
    )


def plain_device(distribution, refine_level, gain_one, gain_two, loss_kernel):
    points = gain_one.shape[0]
    width_x, width_y, width_z, local_vel = distribution.shape
    first_vel = lax.axis_index("vel") * local_vel
    courant_x, courant_y, courant_z = courants(points, first_vel, local_vel)
    padded = extended(distribution, (("cx", 0), ("cy", 1)), 1)
    fluxes = upwind_flux(courant_x, distribution, padded[:-2, 1:-1], padded[2:, 1:-1])
    fluxes = fluxes + upwind_flux(courant_y, distribution, padded[1:-1, :-2], padded[1:-1, 2:])
    fluxes = fluxes + upwind_flux(
        courant_z, distribution, jnp.roll(distribution, 1, 2), jnp.roll(distribution, -1, 2)
    )
    read = distribution - fluxes
    block_cells = width_x * width_y * width_z
    groups = lax.axis_size("vel")
    flattened = read.reshape(block_cells, local_vel).astype(jnp.bfloat16)
    forward, inverse = dft_tables(points)
    active = refine_level.reshape(block_cells) > 0
    slot_index = jnp.cumsum(active.astype(jnp.int32)) - 1
    capacity = block_cells // 2
    picker = (
        (slot_index[None, :] == jnp.arange(capacity, dtype=jnp.int32)[:, None]) & active[None, :]
    ).astype(jnp.bfloat16)
    chosen = jnp.dot(picker, flattened, preferred_element_type=jnp.float32).astype(jnp.bfloat16)
    terms = collide(
        lax.all_to_all(
            chosen.reshape(groups, capacity // groups, local_vel),
            "vel",
            split_axis=0,
            concat_axis=2,
            tiled=True,
        )[0],
        forward,
        inverse,
        gain_one,
        gain_two,
        loss_kernel,
    )[None]
    packed = lax.all_to_all(
        terms.astype(jnp.bfloat16), "vel", split_axis=2, concat_axis=0, tiled=True
    ).astype(terms.dtype)
    packed_rows = packed.reshape(capacity, local_vel)
    safe_slot = jnp.clip(slot_index, 0, capacity - 1)
    rates = jnp.where(active[:, None], packed_rows[safe_slot], 0.0)
    weight = 0.25 * refine_level.astype(jnp.float32)
    return read + weight[..., None] * rates.reshape(width_x, width_y, width_z, local_vel)

LANES = 128
PLANES = 4


def half_set(points):
    middle = points // 2
    pairs = [(b, c) for c in range(1, middle) for b in range(points)]
    pairs += [(b, c) for c in (0, middle) for b in range(middle + 1)]
    weights = [1.0 if b % middle == 0 and c % middle == 0 else 2.0 for b, c in pairs]
    return np.array(pairs), np.array(weights)


def plane_table(points, padded, margin):
    pairs, _ = half_set(points)
    first, second = np.divmod(np.arange(points * points), points)
    products = (first[:, None] * pairs[None, :, 0] + second[:, None] * pairs[None, :, 1]) % points
    angles = 2.0 * np.pi * products / points
    table = np.zeros((points * points + 2 * margin, 2 * padded), np.float32)
    rows = slice(margin, margin + points * points)
    table[rows, : len(pairs)] = np.cos(angles)
    table[rows, padded : padded + len(pairs)] = -np.sin(angles)
    return table.astype(ml_dtypes.bfloat16)


def frequency_weights(kernels, padded):
    points = kernels[0].shape[0]
    pairs, weights = half_set(points)
    plus = np.zeros((points * points, padded), np.float32)
    minus = np.zeros((points * points, padded), np.float32)
    column = np.arange(len(pairs))
    plus[pairs[:, 0] * points + pairs[:, 1], column] = 1.0
    minus[(-pairs[:, 0]) % points * points + (-pairs[:, 1]) % points, column] = 1.0
    scale = np.zeros((padded,), np.float32)
    scale[: len(pairs)] = 0.5 * weights / points**3
    stacked = jnp.stack(kernels).reshape(3, points, points * points)
    mirrored = jnp.concatenate([stacked[:, :1], jnp.flip(stacked[:, 1:], 1)], axis=1)
    both = jnp.concatenate([stacked, mirrored], axis=2).reshape(3 * points, -1)
    select = jnp.asarray(np.concatenate([plus, minus]))
    picked = jnp.dot(both, select, precision=lax.Precision.HIGHEST)
    return (picked * scale).reshape(3, points, padded)


def transform_3(x, sign, wanted=(0, 1, 2)):
    (ar, ai), (br, bi), (cr, ci) = x
    sr, si = br + cr, bi + ci
    out = {}
    if 0 in wanted:
        out[0] = (ar + sr, ai + si)
    if 1 in wanted or 2 in wanted:
        height = sign * math.sqrt(0.75)
        mr, mi = ar - 0.5 * sr, ai - 0.5 * si
        er, ei = height * (br - cr), height * (bi - ci)
        if 1 in wanted:
            out[1] = (mr - ei, mi + er)
        if 2 in wanted:
            out[2] = (mr + ei, mi - er)
    return out


def transform_4(x, sign):
    (ar, ai), (br, bi), (cr, ci), (dr, di) = x
    pr, pi, qr, qi = ar + cr, ai + ci, ar - cr, ai - ci
    sr, si, tr, ti = br + dr, bi + di, br - dr, bi - di
    if sign < 0:
        tr, ti = -tr, -ti
    return [(pr + sr, pi + si), (qr - ti, qi + tr), (pr - sr, pi - si), (qr + ti, qi - tr)]


def transform_8(x, sign):
    even = transform_4(x[0::2], sign)
    odd = transform_4(x[1::2], sign)
    root = math.sqrt(0.5)
    (r0, i0), (r1, i1), (r2, i2), (r3, i3) = odd
    if sign > 0:
        turned = [(r0, i0), (root * (r1 - i1), root * (i1 + r1)), (-i2, r2)]
        turned.append((-root * (r3 + i3), root * (r3 - i3)))
    else:
        turned = [(r0, i0), (root * (r1 + i1), root * (i1 - r1)), (i2, -r2)]
        turned.append((root * (i3 - r3), -root * (i3 + r3)))
    low = [(e[0] + t[0], e[1] + t[1]) for e, t in zip(even, turned)]
    high = [(e[0] - t[0], e[1] - t[1]) for e, t in zip(even, turned)]
    return low + high


def spectrum_of(load):
    stage = {}
    for n2 in range(8):
        part = transform_3([load((8 * n1 + 3 * n2) % 24) for n1 in range(3)], -1)
        for k1 in range(3):
            stage[k1, n2] = part[k1]
    result = {}
    for k1 in range(3):
        part = transform_8([stage[k1, n2] for n2 in range(8)], -1)
        for k2 in range(8):
            result[(16 * k1 + 9 * k2) % 24] = part[k2]
    return result


def first_half_of(spectrum):
    stage = {}
    for k1 in range(3):
        part = transform_8([spectrum[(16 * k1 + 9 * k2) % 24] for k2 in range(8)], 1)
        for n2 in range(8):
            stage[k1, n2] = part[n2]
    result = {}
    for n2 in range(8):
        wanted = {n1: (8 * n1 + 3 * n2) % 24 for n1 in range(3) if (8 * n1 + 3 * n2) % 24 < 12}
        part = transform_3([stage[k1, n2] for k1 in range(3)], 1, tuple(wanted))
        for n1, index in wanted.items():
            result[index] = part[n1]
    return result


def tile_pair(ref, step, rows):
    parts = []
    for parity in range(2):
        at = (2 * step + parity) * LANES
        part = ref[:, :, :, at : at + LANES]
        parts.append(part.reshape(rows, part.shape[2], LANES))
    return jnp.concatenate(parts, axis=1)


def edges_kernel(edge_ref, speed_ref, low_ref, high_ref, plane_ref, down_ref, up_ref, across_ref):
    steps = speed_ref.shape[1] // 8
    width = low_ref.shape[0]
    below = [speed_ref[1, 8 * s : 8 * s + 8, :][None] < 0.0 for s in range(steps)]

    def put(ref, at, value):
        ref[at] = value.reshape(-1, LANES).astype(jnp.bfloat16)

    first = [tile_pair(low_ref, s, width) for s in range(steps)]
    put(down_ref, 0, first[0])
    for m in range(1, steps // 2 + 1):
        put(down_ref, m, jnp.where(below[2 * m - 1], first[2 * m - 1], first[2 * m]))
    last = [tile_pair(high_ref, s, width) for s in range(steps)]
    for m in range(steps // 2):
        put(up_ref, m, jnp.where(below[2 * m], last[2 * m + 1], last[2 * m]))
    put(up_ref, steps // 2, last[steps - 1])
    for s in range(steps):
        put(across_ref, s, tile_pair(plane_ref, s, plane_ref.shape[1]))


def upwind_kernel(
    side_ref, speed_ref, picker_ref, block_ref, down_ref, up_ref, across_ref, read_ref, *chosen_refs
):
    width_x, width_y, width_z, lanes = block_ref.shape
    rows = width_x * width_y
    steps = lanes // (2 * LANES)
    ahead = side_ref[0] == 0
    place = lax.broadcasted_iota(jnp.int32, (1, 8, LANES), 1) % width_z
    cells = []
    for u in range(steps):
        step = pl.program_id(0) * steps + u
        speed = [speed_ref[d, 8 * u : 8 * u + 8, :] for d in range(3)]
        flat = tile_pair(block_ref, u, rows)
        field = flat.reshape(width_x, width_y, 8, LANES)
        falls = speed[1] < 0.0
        above = down_ref[(step + 1) // 2].astype(jnp.float32).reshape(width_x, 1, 8, LANES)
        under = up_ref[step // 2].astype(jnp.float32).reshape(width_x, 1, 8, LANES)
        border = jnp.where(falls[None, None], above, under)
        beside_y = jnp.where(
            falls[None, None],
            jnp.concatenate([field[:, 1:], border], axis=1),
            jnp.concatenate([border, field[:, :-1]], axis=1),
        )
        outer = across_ref[step].astype(jnp.float32).reshape(1, width_y, 8, LANES)
        beside_x = jnp.where(
            ahead,
            jnp.concatenate([field[1:], outer], axis=0),
            jnp.concatenate([outer, field[:-1]], axis=0),
        )
        upper = jnp.where(place == width_z - 1, pltpu.roll(flat, 3, 1), pltpu.roll(flat, 7, 1))
        lower = jnp.where(place == 0, pltpu.roll(flat, 5, 1), pltpu.roll(flat, 1, 1))
        beside_z = jnp.where((speed[2] < 0.0)[None], upper, lower)
        fluxes = jnp.abs(speed[0])[None, None] * (field - beside_x)
        fluxes = fluxes + jnp.abs(speed[1])[None, None] * (field - beside_y)
        fluxes = fluxes.reshape(rows, 8, LANES) + jnp.abs(speed[2])[None] * (flat - beside_z)
        read = flat - fluxes
        read_ref[:, 8 * u : 8 * u + 8, :] = read
        cells.append(read.reshape(rows * 8, LANES).astype(jnp.bfloat16))
    picked = jnp.dot(
        picker_ref[...], jnp.concatenate(cells, axis=1), preferred_element_type=jnp.float32
    ).astype(jnp.bfloat16)
    slots = chosen_refs[0].shape[0]
    for parity in range(2):
        for which, ref in enumerate(chosen_refs):
            first = (parity * len(chosen_refs) + which) * slots
            for u in range(steps):
                at = (2 * u + parity) * LANES
                ref[:, at : at + LANES] = picked[first : first + slots, u * LANES : (u + 1) * LANES]


def collide_kernel(parts, weight_ref, table_ref, *refs):
    own_refs, other_refs = refs[:parts], refs[parts : 2 * parts]
    terms_ref, section, back = refs[2 * parts :]
    slots = own_refs[0].shape[0]
    padded = weight_ref.shape[2]
    height = table_ref.shape[0]
    window = height - 64
    pair_lanes = 2 * (height - 128)
    pairs = own_refs[0].shape[1] // pair_lanes
    half = 2 * pairs * parts
    for parity in range(2):
        rows = []
        for ref in own_refs + other_refs:
            for p in range(pairs):
                at = p * pair_lanes + parity * (pair_lanes - window)
                rows.append(ref[:, at : at + window])
        start = 64 * (1 - parity)
        out = jnp.dot(
            jnp.concatenate(rows, axis=0),
            table_ref[start : start + window, :],
            preferred_element_type=jnp.float32,
        )
        for at in range(half):
            section[2 * at + parity] = out[at * slots : (at + 1) * slots]

    lane_tiles = padded // LANES

    def transform(index, carry):
        row = pl.multiple_of(index // lane_tiles * 16, 16)
        lane = pl.multiple_of(index % lane_tiles * LANES, LANES)
        results = []
        for octet in range(2):
            here = pl.ds(row + 8 * octet, 8)

            def load(i):
                real = section[i, here, pl.ds(lane, LANES)]
                return real, section[i, here, pl.ds(padded + lane, LANES)]

            spectrum = spectrum_of(load)
            per_kernel = []
            for which in range(3):
                weighted = {}
                for a, (real, imag) in spectrum.items():
                    weight = weight_ref[which, pl.ds(a, 1), pl.ds(lane, LANES)]
                    weighted[a] = (real * weight, imag * weight)
                per_kernel.append(first_half_of(weighted))
            results.append(per_kernel)
        for which in range(3):
            for i in range(half):
                for q in range(2):
                    value = jnp.concatenate([results[o][which][i][q] for o in range(2)], axis=0)
                    back[i % 2, which, i // 2, pl.ds(row, 16), pl.ds(q * padded + lane, LANES)] = (
                        value.astype(jnp.bfloat16)
                    )
        return carry

    lax.fori_loop(0, slots // 16 * lane_tiles, transform, 0)

    outs = []
    for parity in range(2):
        start = 64 * (1 - parity)
        outs.append(
            lax.dot_general(
                back[parity].reshape(3 * (half // 2) * slots, 2 * padded),
                table_ref[start : start + window, :],
                (((1,), (1,)), ((), ())),
                preferred_element_type=jnp.float32,
            ).reshape(3, half // 2, slots, window)
        )
    tiles = pair_lanes // LANES
    near = lax.broadcasted_iota(jnp.int32, (slots, LANES), 1) < 64
    for at in range(half // 2):
        own = own_refs[at // pairs]
        for tile in range(tiles):
            lane = tile * LANES
            odd_lane = lane - (pair_lanes - window)
            values = []
            for which in range(3):
                if tile < tiles // 2:
                    value = outs[0][which, at, :, lane : lane + LANES]
                elif tile > tiles // 2:
                    value = outs[1][which, at, :, odd_lane : odd_lane + LANES]
                else:
                    value = jnp.where(
                        near,
                        outs[0][which, at, :, lane : lane + LANES],
                        outs[1][which, at, :, odd_lane : odd_lane + LANES],
                    )
                values.append(value)
            from_lane = at % pairs * pair_lanes + lane
            cells = own[:, from_lane : from_lane + LANES].astype(jnp.float32)
            term = values[0] * values[1] - cells * values[2]
            to_lane = at * pair_lanes + lane
            terms_ref[:, to_lane : to_lane + LANES] = term.astype(jnp.bfloat16)


def evolve_kernel(parts, spread_ref, *refs):
    read_refs, term_refs, out_ref = refs[:parts], refs[parts:-1], refs[-1]
    width_x, width_y, width_z, lanes = out_ref.shape
    steps = lanes // (2 * LANES)
    rows = width_x * width_y
    per_part = pl.num_programs(0) // parts
    columns = []
    for u in range(steps):
        stacked = []
        for parity in range(2):
            at = (2 * u + parity) * LANES
            stacked += [ref[:, at : at + LANES] for ref in term_refs]
        columns.append(jnp.concatenate(stacked, axis=0))
    added = jnp.dot(
        spread_ref[...], jnp.concatenate(columns, axis=1), preferred_element_type=jnp.float32
    )
    for part in range(parts):

        @pl.when(pl.program_id(0) // per_part == part)
        def _():
            for u in range(steps):
                here = added[:, u * LANES : (u + 1) * LANES].reshape(rows, 8, LANES)
                value = read_refs[part][:, 8 * u : 8 * u + 8, :] + here
                for parity in range(2):
                    at = (2 * u + parity) * LANES
                    piece = value[:, parity * width_z : (parity + 1) * width_z, :]
                    out_ref[:, :, :, at : at + LANES] = piece.reshape(
                        width_x, width_y, width_z, LANES
                    )


def params(mib):
    return pltpu.CompilerParams(vmem_limit_bytes=mib * 2**20)


def fast_fits(distribution, points):
    width_x, width_y, width_z, local_vel = distribution.shape
    group = PLANES * points * points
    return (
        points == 24
        and lax.axis_size("vel") == 2
        and width_z == 4
        and local_vel * 2 == points**3
        and local_vel % group == 0
        and width_x * width_y * width_z % 128 == 0
    )


def fast_device(distribution, refine_level, gain_one, gain_two, loss_kernel):
    points = gain_one.shape[0]
    width_x, width_y, width_z, local_vel = distribution.shape
    block_rows = width_x * width_y
    block_cells = block_rows * width_z
    group = PLANES * points * points
    parts = local_vel // group
    group_rows = group // LANES * width_z
    steps = group_rows // 8
    capacity = block_cells // 2
    batches = 2
    slots = capacity // batches
    vel_at = lax.axis_index("vel")
    count_x, count_y = lax.axis_size("cx"), lax.axis_size("cy")

    speeds = jnp.stack(courants(points, vel_at * local_vel, local_vel))
    speeds = jnp.broadcast_to(
        speeds.reshape(3, local_vel // LANES, 1, LANES), (3, local_vel // LANES, width_z, LANES)
    ).reshape(3, local_vel // LANES * width_z, LANES)
    side = vel_at.reshape(1).astype(jnp.int32)
    edge = jnp.where(vel_at == 0, 0, width_x - 1).reshape(1).astype(jnp.int32)

    level = refine_level.reshape(block_cells)
    active = level > 0
    cell_at = jnp.arange(block_cells, dtype=jnp.int32)
    before = (cell_at[:, None] < cell_at[None, :]) & active[:, None]
    slot_index = jnp.where(active, jnp.sum(before.astype(jnp.int32), axis=0), -1)
    spot = slot_index.reshape(block_rows, 1, width_z)
    parity = jnp.arange(2, dtype=jnp.int32)[None, :, None]
    shape = (block_rows, 2, width_z)
    wanted = jnp.where(spot >= 0, spot + capacity * parity, -1)
    wanted = jnp.broadcast_to(wanted, shape).reshape(-1)
    numbers = jnp.arange(2 * capacity, dtype=jnp.int32)
    picker = (numbers[:, None] == wanted[None, :]).astype(jnp.bfloat16)
    strength = jnp.broadcast_to(
        (0.25 * level.astype(jnp.float32)).reshape(block_rows, 1, width_z), shape
    ).reshape(-1)
    spread = jnp.where(wanted[:, None] == numbers[None, :], strength[:, None], 0.0)
    spread = spread.astype(jnp.bfloat16)

    padded = -(-len(half_set(points)[1]) // LANES) * LANES
    weights = frequency_weights((gain_one, gain_two, loss_kernel), padded)
    table = jnp.asarray(plane_table(points, padded, 64))

    towards_lower = [(j, (j - 1) % count_y) for j in range(count_y)]
    towards_upper = [(j, (j + 1) % count_y) for j in range(count_y)]
    across_pairs = [(i, (i - 1) % count_x) for i in range(count_x)]
    across_pairs += [(count_x + i, count_x + (i + 1) % count_x) for i in range(count_x)]
    swap = [(0, 1), (1, 0)]
    bf16 = jnp.bfloat16

    halos = []
    for g in range(parts):
        half_steps = steps // 2 + 1
        down, up, across = pl.pallas_call(
            edges_kernel,
            grid_spec=pltpu.PrefetchScalarGridSpec(
                num_scalar_prefetch=1,
                grid=(1,),
                in_specs=[
                    pl.BlockSpec((3, group_rows, LANES), lambda i, e, g=g: (0, g, 0)),
                    pl.BlockSpec((width_x, 1, width_z, group), lambda i, e, g=g: (0, 0, 0, g)),
                    pl.BlockSpec(
                        (width_x, 1, width_z, group), lambda i, e, g=g: (0, width_y - 1, 0, g)
                    ),
                    pl.BlockSpec((1, width_y, width_z, group), lambda i, e, g=g: (e[0], 0, 0, g)),
                ],
                out_specs=[
                    pl.BlockSpec((half_steps, width_x * 8, LANES), lambda i, e: (0, 0, 0)),
                    pl.BlockSpec((half_steps, width_x * 8, LANES), lambda i, e: (0, 0, 0)),
                    pl.BlockSpec((steps, width_y * 8, LANES), lambda i, e: (0, 0, 0)),
                ],
            ),
            out_shape=[
                jax.ShapeDtypeStruct((half_steps, width_x * 8, LANES), bf16),
                jax.ShapeDtypeStruct((half_steps, width_x * 8, LANES), bf16),
                jax.ShapeDtypeStruct((steps, width_y * 8, LANES), bf16),
            ],
            compiler_params=params(56),
            name="edges",
        )(edge, speeds, distribution, distribution, distribution)
        halos.append(
            (
                lax.ppermute(down, "cy", towards_lower),
                lax.ppermute(up, "cy", towards_upper),
                lax.ppermute(across, ("vel", "cx"), across_pairs),
            )
        )

    reads, own, other = [], [], []
    wide = 3
    for g in range(parts):
        whole = [pl.BlockSpec(h.shape, lambda i: (0, 0, 0)) for h in halos[g]]
        at = steps // wide * g
        read, *chosen = pl.pallas_call(
            upwind_kernel,
            grid=(steps // wide,),
            in_specs=[
                pl.BlockSpec(memory_space=pltpu.SMEM),
                pl.BlockSpec((3, 8 * wide, LANES), lambda i, at=at: (0, at + i, 0)),
                pl.BlockSpec(picker.shape, lambda i: (0, 0)),
                pl.BlockSpec(
                    (width_x, width_y, width_z, 2 * wide * LANES),
                    lambda i, at=at: (0, 0, 0, at + i),
                ),
                *whole,
            ],
            out_specs=[pl.BlockSpec((block_rows, 8 * wide, LANES), lambda i: (0, i, 0))]
            + [pl.BlockSpec((slots, 2 * wide * LANES), lambda i: (0, i))] * batches,
            out_shape=[jax.ShapeDtypeStruct((block_rows, group_rows, LANES), jnp.float32)]
            + [jax.ShapeDtypeStruct((slots, group), bf16)] * batches,
            compiler_params=params(56),
            name="upwind",
        )(side, speeds, picker, distribution, *halos[g])
        reads.append(read)
        own.append(chosen)
        other.append([lax.ppermute(c, "vel", swap) for c in chosen])

    terms = []
    half = points // 2
    for batch in range(batches):
        terms.append(
            pl.pallas_call(
                functools.partial(collide_kernel, parts),
                out_shape=jax.ShapeDtypeStruct((slots, local_vel), bf16),
                scratch_shapes=[
                    pltpu.VMEM((points, slots, 2 * padded), jnp.float32),
                    pltpu.VMEM((2, 3, half // 2, slots, 2 * padded), bf16),
                ],
                compiler_params=params(56),
                name="collide",
            )(
                weights,
                table,
                *[own[g][batch] for g in range(parts)],
                *[other[g][batch] for g in range(parts)],
            )
        )

    per_part = steps // wide

    def read_spec(g):
        return pl.BlockSpec(
            (block_rows, 8 * wide, LANES),
            lambda i: (0, jnp.clip(i - g * per_part, 0, per_part - 1), 0),
        )

    return pl.pallas_call(
        functools.partial(evolve_kernel, parts),
        grid=(parts * per_part,),
        in_specs=[pl.BlockSpec(spread.shape, lambda i: (0, 0))]
        + [read_spec(g) for g in range(parts)]
        + [pl.BlockSpec((slots, 2 * wide * LANES), lambda i: (0, i))] * batches,
        out_specs=pl.BlockSpec(
            (width_x, width_y, width_z, 2 * wide * LANES), lambda i: (0, 0, 0, i)
        ),
        out_shape=jax.ShapeDtypeStruct(distribution.shape, jnp.float32),
        compiler_params=params(56),
        name="evolve",
    )(spread, *reads, *terms)


def per_device(distribution, refine_level, gain_one, gain_two, loss_kernel):
    if fast_fits(distribution, gain_one.shape[0]):
        return fast_device(distribution, refine_level, gain_one, gain_two, loss_kernel)
    return plain_device(distribution, refine_level, gain_one, gain_two, loss_kernel)


def solution(mesh):
    placed = (P("cx", "cy", None, "vel"), P("cx", "cy", None), P(), P(), P())
    return jax.shard_map(
        per_device,
        mesh=mesh,
        in_specs=placed,
        out_specs=P("cx", "cy", None, "vel"),
        check_vma=False,
    )
```

```python
import functools
import math

import jax
import jax.numpy as jnp
import ml_dtypes
import numpy as np
from jax import lax
from jax.experimental import pallas as pl
from jax.experimental.pallas import tpu as pltpu
from jax.sharding import PartitionSpec as P


def extended(array, sides, width):
    for axis, dim in sides:
        count, length = (lax.axis_size(axis), array.shape[dim])
        up = [(i, (i + 1) % count) for i in range(count)]
        down = [(j, i) for i, j in up]
        last = lax.slice_in_dim(array, length - width, length, axis=dim)
        leading = lax.slice_in_dim(array, 0, width, axis=dim)
        before = lax.ppermute(last, axis, up)
        after = lax.ppermute(leading, axis, down)
        array = jnp.concatenate([before, array, after], axis=dim)
    return array


def dft_tables(points):
    indices = jnp.arange(points, dtype=jnp.int32)
    products = indices[:, None] * indices[None, :] % points
    angles = products.astype(jnp.float32) * (2.0 * math.pi / points)
    cosine = jnp.cos(angles)
    sine_table = jnp.sin(angles)
    forward = jnp.stack([jnp.stack([cosine, sine_table]), jnp.stack([-sine_table, cosine])])
    inverse = jnp.stack([jnp.stack([cosine, -sine_table]), jnp.stack([sine_table, cosine])])
    return (forward.astype(jnp.bfloat16), inverse.astype(jnp.bfloat16))


def contract(pattern, left_side, right_side):
    return jnp.einsum(pattern, left_side, right_side, preferred_element_type=jnp.float32)


def collide(cells, forward, inverse, gain_one, gain_two, loss_kernel):
    points = forward.shape[-1]
    cell_count = cells.shape[0]
    field = cells.reshape(cell_count, points, points, points)
    section_z = contract("nabz,qzw->qnabw", field, forward[:, 0]).astype(jnp.bfloat16)
    section_y = contract("pnayc,qpyw->qnawc", section_z, forward).astype(jnp.bfloat16)
    spectrum = contract("pnxbc,qpxw->qnwbc", section_y, forward)
    scale_factor = 1.0 / float(points**3)

    def filtered(kernel):
        weighted = (spectrum * (kernel * scale_factor)[None, None]).astype(jnp.bfloat16)
        back_x = contract("pnxbc,qpxw->qnwbc", weighted, inverse).astype(jnp.bfloat16)
        back_y = contract("pnayc,qpyw->qnawc", back_x, inverse).astype(jnp.bfloat16)
        return contract("pnabz,pzw->nabw", back_y, inverse[0])

    gain_term = filtered(gain_one) * filtered(gain_two)
    result = gain_term - field.astype(jnp.float32) * filtered(loss_kernel)
    return result.reshape(cell_count, points**3)


def courants(points, first_vel, local_count):
    vel_index = first_vel + jnp.arange(local_count, dtype=jnp.int32)
    index_x = vel_index // (points * points)
    index_y = vel_index // points % points
    index_z = vel_index % points

    def speed(index_part):
        return 0.3 * (2.0 * index_part.astype(jnp.float32) - (points - 1)) / (points - 1)

    return (speed(index_x), speed(index_y), speed(index_z))


def upwind_flux(courant, center, lower_side, upper_side):
    return jnp.maximum(courant, 0.0) * (center - lower_side) + jnp.minimum(courant, 0.0) * (
        upper_side - center
    )


def plain_device(distribution, refine_level, gain_one, gain_two, loss_kernel):
    points = gain_one.shape[0]
    width_x, width_y, width_z, local_vel = distribution.shape
    first_vel = lax.axis_index("vel") * local_vel
    courant_x, courant_y, courant_z = courants(points, first_vel, local_vel)
    padded = extended(distribution, (("cx", 0), ("cy", 1)), 1)
    fluxes = upwind_flux(courant_x, distribution, padded[:-2, 1:-1], padded[2:, 1:-1])
    fluxes = fluxes + upwind_flux(courant_y, distribution, padded[1:-1, :-2], padded[1:-1, 2:])
    fluxes = fluxes + upwind_flux(
        courant_z, distribution, jnp.roll(distribution, 1, 2), jnp.roll(distribution, -1, 2)
    )
    read = distribution - fluxes
    block_cells = width_x * width_y * width_z
    groups = lax.axis_size("vel")
    flattened = read.reshape(block_cells, local_vel).astype(jnp.bfloat16)
    forward, inverse = dft_tables(points)
    active = refine_level.reshape(block_cells) > 0
    slot_index = jnp.cumsum(active.astype(jnp.int32)) - 1
    capacity = block_cells // 2
    picker = (
        (slot_index[None, :] == jnp.arange(capacity, dtype=jnp.int32)[:, None]) & active[None, :]
    ).astype(jnp.bfloat16)
    chosen = jnp.dot(picker, flattened, preferred_element_type=jnp.float32).astype(jnp.bfloat16)
    terms = collide(
        lax.all_to_all(
            chosen.reshape(groups, capacity // groups, local_vel),
            "vel",
            split_axis=0,
            concat_axis=2,
            tiled=True,
        )[0],
        forward,
        inverse,
        gain_one,
        gain_two,
        loss_kernel,
    )[None]
    packed = lax.all_to_all(
        terms.astype(jnp.bfloat16), "vel", split_axis=2, concat_axis=0, tiled=True
    ).astype(terms.dtype)
    packed_rows = packed.reshape(capacity, local_vel)
    safe_slot = jnp.clip(slot_index, 0, capacity - 1)
    rates = jnp.where(active[:, None], packed_rows[safe_slot], 0.0)
    weight = 0.25 * refine_level.astype(jnp.float32)
    return read + weight[..., None] * rates.reshape(width_x, width_y, width_z, local_vel)

LANES = 128
PLANES = 4


def half_set(points):
    middle = points // 2
    pairs = [(b, c) for c in range(1, middle) for b in range(points)]
    pairs += [(b, c) for c in (0, middle) for b in range(middle + 1)]
    weights = [1.0 if b % middle == 0 and c % middle == 0 else 2.0 for b, c in pairs]
    return np.array(pairs), np.array(weights)


def plane_table(points, padded, margin):
    pairs, _ = half_set(points)
    first, second = np.divmod(np.arange(points * points), points)
    products = (first[:, None] * pairs[None, :, 0] + second[:, None] * pairs[None, :, 1]) % points
    angles = 2.0 * np.pi * products / points
    table = np.zeros((points * points + 2 * margin, 2 * padded), np.float32)
    rows = slice(margin, margin + points * points)
    table[rows, : len(pairs)] = np.cos(angles)
    table[rows, padded : padded + len(pairs)] = -np.sin(angles)
    return table.astype(ml_dtypes.bfloat16)


def frequency_weights(kernels, padded):
    points = kernels[0].shape[0]
    pairs, weights = half_set(points)
    plus = np.zeros((points * points, padded), np.float32)
    minus = np.zeros((points * points, padded), np.float32)
    column = np.arange(len(pairs))
    plus[pairs[:, 0] * points + pairs[:, 1], column] = 1.0
    minus[(-pairs[:, 0]) % points * points + (-pairs[:, 1]) % points, column] = 1.0
    scale = np.zeros((padded,), np.float32)
    scale[: len(pairs)] = 0.5 * weights / points**3
    stacked = jnp.stack(kernels).reshape(3, points, points * points)
    mirrored = jnp.concatenate([stacked[:, :1], jnp.flip(stacked[:, 1:], 1)], axis=1)
    both = jnp.concatenate([stacked, mirrored], axis=2).reshape(3 * points, -1)
    select = jnp.asarray(np.concatenate([plus, minus]))
    picked = jnp.dot(both, select, precision=lax.Precision.HIGHEST)
    return (picked * scale).reshape(3, points, padded)


def transform_3(x, sign, wanted=(0, 1, 2)):
    (ar, ai), (br, bi), (cr, ci) = x
    sr, si = br + cr, bi + ci
    out = {}
    if 0 in wanted:
        out[0] = (ar + sr, ai + si)
    if 1 in wanted or 2 in wanted:
        height = sign * math.sqrt(0.75)
        mr, mi = ar - 0.5 * sr, ai - 0.5 * si
        er, ei = height * (br - cr), height * (bi - ci)
        if 1 in wanted:
            out[1] = (mr - ei, mi + er)
        if 2 in wanted:
            out[2] = (mr + ei, mi - er)
    return out


def transform_4(x, sign):
    (ar, ai), (br, bi), (cr, ci), (dr, di) = x
    pr, pi, qr, qi = ar + cr, ai + ci, ar - cr, ai - ci
    sr, si, tr, ti = br + dr, bi + di, br - dr, bi - di
    if sign < 0:
        tr, ti = -tr, -ti
    return [(pr + sr, pi + si), (qr - ti, qi + tr), (pr - sr, pi - si), (qr + ti, qi - tr)]


def transform_8(x, sign):
    even = transform_4(x[0::2], sign)
    odd = transform_4(x[1::2], sign)
    root = math.sqrt(0.5)
    (r0, i0), (r1, i1), (r2, i2), (r3, i3) = odd
    if sign > 0:
        turned = [(r0, i0), (root * (r1 - i1), root * (i1 + r1)), (-i2, r2)]
        turned.append((-root * (r3 + i3), root * (r3 - i3)))
    else:
        turned = [(r0, i0), (root * (r1 + i1), root * (i1 - r1)), (i2, -r2)]
        turned.append((root * (i3 - r3), -root * (i3 + r3)))
    low = [(e[0] + t[0], e[1] + t[1]) for e, t in zip(even, turned)]
    high = [(e[0] - t[0], e[1] - t[1]) for e, t in zip(even, turned)]
    return low + high


def spectrum_of(load):
    stage = {}
    for n2 in range(8):
        part = transform_3([load((8 * n1 + 3 * n2) % 24) for n1 in range(3)], -1)
        for k1 in range(3):
            stage[k1, n2] = part[k1]
    result = {}
    for k1 in range(3):
        part = transform_8([stage[k1, n2] for n2 in range(8)], -1)
        for k2 in range(8):
            result[(16 * k1 + 9 * k2) % 24] = part[k2]
    return result


def first_half_of(spectrum):
    stage = {}
    for k1 in range(3):
        part = transform_8([spectrum[(16 * k1 + 9 * k2) % 24] for k2 in range(8)], 1)
        for n2 in range(8):
            stage[k1, n2] = part[n2]
    result = {}
    for n2 in range(8):
        wanted = {n1: (8 * n1 + 3 * n2) % 24 for n1 in range(3) if (8 * n1 + 3 * n2) % 24 < 12}
        part = transform_3([stage[k1, n2] for k1 in range(3)], 1, tuple(wanted))
        for n1, index in wanted.items():
            result[index] = part[n1]
    return result


def tile_pair(ref, step, rows):
    parts = []
    for parity in range(2):
        at = (2 * step + parity) * LANES
        part = ref[:, :, :, at : at + LANES]
        parts.append(part.reshape(rows, part.shape[2], LANES))
    return jnp.concatenate(parts, axis=1)


def edges_kernel(edge_ref, speed_ref, low_ref, high_ref, plane_ref, down_ref, up_ref, across_ref):
    steps = speed_ref.shape[1] // 8
    width = low_ref.shape[0]
    below = [speed_ref[1, 8 * s : 8 * s + 8, :][None] < 0.0 for s in range(steps)]

    def put(ref, at, value):
        ref[at] = value.reshape(-1, LANES).astype(jnp.bfloat16)

    first = [tile_pair(low_ref, s, width) for s in range(steps)]
    put(down_ref, 0, first[0])
    for m in range(1, steps // 2 + 1):
        put(down_ref, m, jnp.where(below[2 * m - 1], first[2 * m - 1], first[2 * m]))
    last = [tile_pair(high_ref, s, width) for s in range(steps)]
    for m in range(steps // 2):
        put(up_ref, m, jnp.where(below[2 * m], last[2 * m + 1], last[2 * m]))
    put(up_ref, steps // 2, last[steps - 1])
    for s in range(steps):
        put(across_ref, s, tile_pair(plane_ref, s, plane_ref.shape[1]))


def upwind_kernel(
    side_ref,
    speed_ref,
    picker_ref,
    block_ref,
    down_ref,
    up_ref,
    across_ref,
    read_ref,
    *refs,
):
    *chosen_refs, wide, border, cells = refs
    width_x, width_y, width_z, lanes = block_ref.shape
    steps = lanes // (2 * LANES)
    beside = jnp.where(side_ref[0] == 0, 2, 0)
    place = lax.broadcasted_iota(jnp.int32, (1, 8, LANES), 1) % width_z
    for u in range(steps):
        step = pl.program_id(0) * steps + u
        speed = [speed_ref[d, 8 * u : 8 * u + 8, :][None] for d in range(3)]
        size = [jnp.abs(c) for c in speed]
        falls = speed[1] < 0.0
        sinks = speed[2] < 0.0
        outer = across_ref[step].astype(jnp.float32).reshape(width_y, 8, LANES)
        wide[0] = outer
        wide[width_x + 1] = outer
        above = down_ref[(step + 1) // 2].astype(jnp.float32).reshape(width_x, 8, LANES)
        under = up_ref[step // 2].astype(jnp.float32).reshape(width_x, 8, LANES)
        border[...] = jnp.where(falls, above, under)

        def spread_out(x, carry):
            at = 2 * u * LANES
            parts = [block_ref[x, :, :, at + p * LANES : at + (p + 1) * LANES] for p in range(2)]
            wide[x + 1] = jnp.concatenate(parts, axis=1)
            return carry

        lax.fori_loop(0, width_x, spread_out, 0, unroll=2)

        def advance(x, carry):
            field = wide[x + 1]
            edge = border[pl.ds(x, 1)]
            fluxes = size[0] * (field - wide[x + beside])
            beside_y = jnp.where(
                falls,
                jnp.concatenate([field[1:], edge], axis=0),
                jnp.concatenate([edge, field[:-1]], axis=0),
            )
            fluxes = fluxes + size[1] * (field - beside_y)
            upper = jnp.where(
                place == width_z - 1, pltpu.roll(field, 3, 1), pltpu.roll(field, 7, 1)
            )
            lower = jnp.where(place == 0, pltpu.roll(field, 5, 1), pltpu.roll(field, 1, 1))
            fluxes = fluxes + size[2] * (field - jnp.where(sinks, upper, lower))
            read = field - fluxes
            read_ref[pl.ds(x * width_y, width_y), 8 * u : 8 * u + 8, :] = read
            rows = width_y * 8
            at = pl.multiple_of(x * rows, rows)
            cells[pl.ds(at, rows), u * LANES : (u + 1) * LANES] = read.reshape(
                rows, LANES
            ).astype(jnp.bfloat16)
            return carry

        lax.fori_loop(0, width_x, advance, 0, unroll=2)
    picked = jnp.dot(
        picker_ref[...], cells[...], preferred_element_type=jnp.float32
    ).astype(jnp.bfloat16)
    capacity = picked.shape[0] // 2
    for parity in range(2):
        first = parity * capacity
        for ref in chosen_refs:
            slots = ref.shape[0]
            for u in range(steps):
                at = (2 * u + parity) * LANES
                ref[:, at : at + LANES] = picked[first : first + slots, u * LANES : (u + 1) * LANES]
            first += slots


def filter_parts(parts, weight_ref, table_ref, own_refs, other_refs, section, back):
    slots = own_refs[0].shape[0]
    padded = weight_ref.shape[2]
    height = table_ref.shape[0]
    window = height - 64
    pair_lanes = 2 * (height - 128)
    pairs = own_refs[0].shape[1] // pair_lanes
    half = 2 * pairs * parts
    for parity in range(2):
        rows = []
        for ref in own_refs + other_refs:
            for p in range(pairs):
                at = p * pair_lanes + parity * (pair_lanes - window)
                rows.append(ref[:, at : at + window])
        start = 64 * (1 - parity)
        out = jnp.dot(
            jnp.concatenate(rows, axis=0),
            table_ref[start : start + window, :],
            preferred_element_type=jnp.float32,
        )
        for at in range(half):
            section[2 * at + parity] = out[at * slots : (at + 1) * slots]

    lane_tiles = padded // LANES

    def transform(index, carry):
        row = pl.multiple_of(index // lane_tiles * 16, 16)
        lane = pl.multiple_of(index % lane_tiles * LANES, LANES)
        results = []
        for octet in range(2):
            here = pl.ds(row + 8 * octet, 8)

            def load(i):
                real = section[i, here, pl.ds(lane, LANES)]
                return real, section[i, here, pl.ds(padded + lane, LANES)]

            spectrum = spectrum_of(load)
            per_kernel = []
            for which in range(3):
                weighted = {}
                for a, (real, imag) in spectrum.items():
                    weight = weight_ref[which, pl.ds(a, 1), pl.ds(lane, LANES)]
                    weighted[a] = (real * weight, imag * weight)
                per_kernel.append(first_half_of(weighted))
            results.append(per_kernel)
        for which in range(3):
            for i in range(half):
                for q in range(2):
                    value = jnp.concatenate([results[o][which][i][q] for o in range(2)], axis=0)
                    back[i % 2, which, i // 2, pl.ds(row, 16), pl.ds(q * padded + lane, LANES)] = (
                        value.astype(jnp.bfloat16)
                    )
        return carry

    lax.fori_loop(0, slots // 16 * lane_tiles, transform, 0)


def terms_of(part, table_ref, own_ref, back, put):
    slots, lanes = own_ref.shape
    height = table_ref.shape[0]
    window = height - 64
    pair_lanes = 2 * (height - 128)
    pairs = lanes // pair_lanes
    outs = []
    for parity in range(2):
        start = 64 * (1 - parity)
        outs.append(
            lax.dot_general(
                back[parity, :, part * pairs : (part + 1) * pairs].reshape(
                    3 * pairs * slots, back.shape[-1]
                ),
                table_ref[start : start + window, :],
                (((1,), (1,)), ((), ())),
                preferred_element_type=jnp.float32,
            ).reshape(3, pairs, slots, window)
        )
    tiles = pair_lanes // LANES
    near = lax.broadcasted_iota(jnp.int32, (slots, LANES), 1) < 64
    for at in range(pairs):
        for tile in range(tiles):
            lane = tile * LANES
            odd_lane = lane - (pair_lanes - window)
            values = []
            for which in range(3):
                if tile < tiles // 2:
                    value = outs[0][which, at, :, lane : lane + LANES]
                elif tile > tiles // 2:
                    value = outs[1][which, at, :, odd_lane : odd_lane + LANES]
                else:
                    value = jnp.where(
                        near,
                        outs[0][which, at, :, lane : lane + LANES],
                        outs[1][which, at, :, odd_lane : odd_lane + LANES],
                    )
                values.append(value)
            lane = at * pair_lanes + lane
            cells = own_ref[:, lane : lane + LANES].astype(jnp.float32)
            put(at * tiles + tile, (values[0] * values[1] - cells * values[2]).astype(jnp.bfloat16))


def collide_kernel(parts, weight_ref, table_ref, *refs):
    own_refs, other_refs = refs[:parts], refs[parts : 2 * parts]
    terms_ref, section, back = refs[2 * parts :]
    filter_parts(parts, weight_ref, table_ref, own_refs, other_refs, section, back)
    for part in range(parts):
        first = part * own_refs[0].shape[1]

        def put(tile, value):
            terms_ref[:, first + tile * LANES : first + (tile + 1) * LANES] = value

        terms_of(part, table_ref, own_refs[part], back, put)


def finish_kernel(parts, weight_ref, table_ref, spread_ref, early_ref, *refs):
    own_refs, other_refs = refs[:parts], refs[parts : 2 * parts]
    read_refs = refs[2 * parts : 3 * parts]
    out_ref, section, back, reads, spots, added, staged, read_sems, out_sems = refs[3 * parts :]
    width_x, width_y, width_z, lanes = staged.shape[1:]
    tiles = lanes // LANES
    loads = [
        pltpu.make_async_copy(read_refs[part], reads.at[part], read_sems.at[part])
        for part in range(parts)
    ]
    for load in loads:
        load.start()
    filter_parts(parts, weight_ref, table_ref, own_refs, other_refs, section, back)
    early = early_ref.shape[0]
    capacity = early + own_refs[0].shape[0]
    stores = []
    for part in range(parts):

        def put(tile, value):
            first = tile % 2 * capacity
            columns = slice(tile // 2 * LANES, (tile // 2 + 1) * LANES)
            lane = part * lanes + tile * LANES
            spots[first : first + early, columns] = early_ref[:, lane : lane + LANES]
            spots[first + early : first + capacity, columns] = value

        terms_of(part, table_ref, own_refs[part], back, put)
        added[...] = jnp.dot(spread_ref[...], spots[...], preferred_element_type=jnp.float32)
        loads[part].wait()
        slot = part % 2
        if part >= 2:
            stores[part - 2].wait()

        def add(x, carry):
            for y in range(width_y):
                row = x * width_y + y
                at = pl.multiple_of(row * 8, 8)
                for u in range(tiles // 2):
                    value = (
                        reads[part, row, 8 * u : 8 * u + 8, :]
                        + added[pl.ds(at, 8), u * LANES : (u + 1) * LANES]
                    )
                    for parity in range(2):
                        lane = (2 * u + parity) * LANES
                        piece = value[parity * width_z : (parity + 1) * width_z]
                        staged[slot, x, y, :, lane : lane + LANES] = piece
            return carry

        lax.fori_loop(0, width_x, add, 0)
        store = pltpu.make_async_copy(
            staged.at[slot],
            out_ref.at[:, :, :, part * lanes : (part + 1) * lanes],
            out_sems.at[part],
        )
        store.start()
        stores.append(store)
    for store in stores[-2:]:
        store.wait()


def params(mib):
    return pltpu.CompilerParams(vmem_limit_bytes=mib * 2**20)


def fast_fits(distribution, points):
    width_x, width_y, width_z, local_vel = distribution.shape
    group = PLANES * points * points
    return (
        points == 24
        and lax.axis_size("vel") == 2
        and width_z == 4
        and local_vel * 2 == points**3
        and local_vel % group == 0
        and width_x * width_y * width_z % 128 == 0
    )


def fast_device(distribution, refine_level, gain_one, gain_two, loss_kernel):
    points = gain_one.shape[0]
    width_x, width_y, width_z, local_vel = distribution.shape
    block_rows = width_x * width_y
    block_cells = block_rows * width_z
    group = PLANES * points * points
    parts = local_vel // group
    group_rows = group // LANES * width_z
    steps = group_rows // 8
    capacity = block_cells // 2
    late = capacity * 3 // 8 // 16 * 16
    counts = (capacity - late, late)
    vel_at = lax.axis_index("vel")
    count_x, count_y = lax.axis_size("cx"), lax.axis_size("cy")

    speeds = jnp.stack(courants(points, vel_at * local_vel, local_vel))
    speeds = jnp.broadcast_to(
        speeds.reshape(3, local_vel // LANES, 1, LANES), (3, local_vel // LANES, width_z, LANES)
    ).reshape(3, local_vel // LANES * width_z, LANES)
    side = vel_at.reshape(1).astype(jnp.int32)
    edge = jnp.where(vel_at == 0, 0, width_x - 1).reshape(1).astype(jnp.int32)

    level = refine_level.reshape(block_cells)
    active = level > 0
    cell_at = jnp.arange(block_cells, dtype=jnp.int32)
    before = (cell_at[:, None] < cell_at[None, :]) & active[:, None]
    slot_index = jnp.where(active, jnp.sum(before.astype(jnp.int32), axis=0), -1)
    spot = slot_index.reshape(block_rows, 1, width_z)
    parity = jnp.arange(2, dtype=jnp.int32)[None, :, None]
    shape = (block_rows, 2, width_z)
    wanted = jnp.where(spot >= 0, spot + capacity * parity, -1)
    wanted = jnp.broadcast_to(wanted, shape).reshape(-1)
    numbers = jnp.arange(2 * capacity, dtype=jnp.int32)
    picker = (numbers[:, None] == wanted[None, :]).astype(jnp.bfloat16)
    strength = jnp.broadcast_to(
        (0.25 * level.astype(jnp.float32)).reshape(block_rows, 1, width_z), shape
    ).reshape(-1)
    spread = jnp.where(wanted[:, None] == numbers[None, :], strength[:, None], 0.0)
    spread = spread.astype(jnp.bfloat16)

    padded = -(-len(half_set(points)[1]) // LANES) * LANES
    weights = frequency_weights((gain_one, gain_two, loss_kernel), padded)
    table = jnp.asarray(plane_table(points, padded, 64))

    towards_lower = [(j, (j - 1) % count_y) for j in range(count_y)]
    towards_upper = [(j, (j + 1) % count_y) for j in range(count_y)]
    across_pairs = [(i, (i - 1) % count_x) for i in range(count_x)]
    across_pairs += [(count_x + i, count_x + (i + 1) % count_x) for i in range(count_x)]
    swap = [(0, 1), (1, 0)]
    bf16 = jnp.bfloat16

    half_steps = steps // 2 + 1
    edges = []
    for g in range(parts):
        edges.append(
            pl.pallas_call(
                edges_kernel,
                grid_spec=pltpu.PrefetchScalarGridSpec(
                    num_scalar_prefetch=1,
                    grid=(1,),
                    in_specs=[
                        pl.BlockSpec((3, group_rows, LANES), lambda i, e, g=g: (0, g, 0)),
                        pl.BlockSpec((width_x, 1, width_z, group), lambda i, e, g=g: (0, 0, 0, g)),
                        pl.BlockSpec(
                            (width_x, 1, width_z, group), lambda i, e, g=g: (0, width_y - 1, 0, g)
                        ),
                        pl.BlockSpec(
                            (1, width_y, width_z, group), lambda i, e, g=g: (e[0], 0, 0, g)
                        ),
                    ],
                    out_specs=[
                        pl.BlockSpec((half_steps, width_x * 8, LANES), lambda i, e: (0, 0, 0)),
                        pl.BlockSpec((half_steps, width_x * 8, LANES), lambda i, e: (0, 0, 0)),
                        pl.BlockSpec((steps, width_y * 8, LANES), lambda i, e: (0, 0, 0)),
                    ],
                ),
                out_shape=[
                    jax.ShapeDtypeStruct((half_steps, width_x * 8, LANES), bf16),
                    jax.ShapeDtypeStruct((half_steps, width_x * 8, LANES), bf16),
                    jax.ShapeDtypeStruct((steps, width_y * 8, LANES), bf16),
                ],
                compiler_params=params(60 if g == 0 else 16),
                name="edges",
            )(edge, speeds, distribution, distribution, distribution)
        )

    wide = 3

    def upwind(g, halo):
        at = steps // wide * g
        return pl.pallas_call(
            upwind_kernel,
            grid=(steps // wide,),
            in_specs=[
                pl.BlockSpec(memory_space=pltpu.SMEM),
                pl.BlockSpec((3, 8 * wide, LANES), lambda i: (0, at + i, 0)),
                pl.BlockSpec(picker.shape, lambda i: (0, 0)),
                pl.BlockSpec(
                    (width_x, width_y, width_z, 2 * wide * LANES), lambda i: (0, 0, 0, at + i)
                ),
                *[pl.BlockSpec(h.shape, lambda i: (0, 0, 0)) for h in halo],
            ],
            out_specs=[pl.BlockSpec((block_rows, 8 * wide, LANES), lambda i: (0, i, 0))]
            + [pl.BlockSpec((count, 2 * wide * LANES), lambda i: (0, i)) for count in counts],
            out_shape=[jax.ShapeDtypeStruct((block_rows, group_rows, LANES), jnp.float32)]
            + [jax.ShapeDtypeStruct((count, group), bf16) for count in counts],
            scratch_shapes=[
                pltpu.VMEM((width_x + 2, width_y, 8, LANES), jnp.float32),
                pltpu.VMEM((width_x, 8, LANES), jnp.float32),
                pltpu.VMEM((block_rows * 8, wide * LANES), bf16),
            ],
            compiler_params=params(20),
            name="upwind",
        )(side, speeds, picker, distribution, *halo)

    reads, own, other = [], [], []
    for g in range(parts):
        down, up, across = edges[g]
        if own:
            down, up, across, own[-1] = lax.optimization_barrier((down, up, across, own[-1]))
        halo = (
            lax.ppermute(down, "cy", towards_lower),
            lax.ppermute(up, "cy", towards_upper),
            lax.ppermute(across, ("vel", "cx"), across_pairs),
        )
        read, *chosen = upwind(g, halo)
        reads.append(read)
        own.append(chosen)
    early = [lax.ppermute(own[g][0], "vel", swap) for g in range(parts)]
    first_late = lax.ppermute(own[0][1], "vel", swap)
    *later, _ = lax.optimization_barrier((*[own[g][1] for g in range(1, parts)], early[-1]))
    lates = [first_late] + [lax.ppermute(x, "vel", swap) for x in later]

    def scratch(count):
        return [
            pltpu.VMEM((points, count, 2 * padded), jnp.float32),
            pltpu.VMEM((2, 3, points // 4, count, 2 * padded), bf16),
        ]

    terms = pl.pallas_call(
        functools.partial(collide_kernel, parts),
        out_shape=jax.ShapeDtypeStruct((counts[0], local_vel), bf16),
        scratch_shapes=scratch(counts[0]),
        compiler_params=params(36),
        name="collide",
    )(weights, table, *[chosen[0] for chosen in own], *early)

    local = pl.BlockSpec(memory_space=pltpu.VMEM)
    anywhere = pl.BlockSpec(memory_space=pl.ANY)
    return pl.pallas_call(
        functools.partial(finish_kernel, parts),
        in_specs=[local] * (4 + 2 * parts) + [anywhere] * parts,
        out_specs=anywhere,
        out_shape=jax.ShapeDtypeStruct(distribution.shape, jnp.float32),
        scratch_shapes=scratch(counts[1])
        + [
            pltpu.VMEM((parts, block_rows, group_rows, LANES), jnp.float32),
            pltpu.VMEM((2 * capacity, group // 2), bf16),
            pltpu.VMEM((block_rows * 8, group // 2), jnp.float32),
            pltpu.VMEM((2, width_x, width_y, width_z, group), jnp.float32),
            pltpu.SemaphoreType.DMA((parts,)),
            pltpu.SemaphoreType.DMA((parts,)),
        ],
        compiler_params=params(44),
        name="finish",
    )(weights, table, spread, terms, *[chosen[1] for chosen in own], *lates, *reads)


def per_device(distribution, refine_level, gain_one, gain_two, loss_kernel):
    if fast_fits(distribution, gain_one.shape[0]):
        return fast_device(distribution, refine_level, gain_one, gain_two, loss_kernel)
    return plain_device(distribution, refine_level, gain_one, gain_two, loss_kernel)


def solution(mesh):
    placed = (P("cx", "cy", None, "vel"), P("cx", "cy", None), P(), P(), P())
    return jax.shard_map(
        per_device,
        mesh=mesh,
        in_specs=placed,
        out_specs=P("cx", "cy", None, "vel"),
        check_vma=False,
    )
```

```python
import functools
import math

import jax
import jax.numpy as jnp
import ml_dtypes
import numpy as np
from jax import lax
from jax.experimental import pallas as pl
from jax.experimental.pallas import tpu as pltpu
from jax.sharding import PartitionSpec as P


def extended(array, sides, width):
    for axis, dim in sides:
        count, length = (lax.axis_size(axis), array.shape[dim])
        up = [(i, (i + 1) % count) for i in range(count)]
        down = [(j, i) for i, j in up]
        last = lax.slice_in_dim(array, length - width, length, axis=dim)
        leading = lax.slice_in_dim(array, 0, width, axis=dim)
        before = lax.ppermute(last, axis, up)
        after = lax.ppermute(leading, axis, down)
        array = jnp.concatenate([before, array, after], axis=dim)
    return array


def dft_tables(points):
    indices = jnp.arange(points, dtype=jnp.int32)
    products = indices[:, None] * indices[None, :] % points
    angles = products.astype(jnp.float32) * (2.0 * math.pi / points)
    cosine = jnp.cos(angles)
    sine_table = jnp.sin(angles)
    forward = jnp.stack([jnp.stack([cosine, sine_table]), jnp.stack([-sine_table, cosine])])
    inverse = jnp.stack([jnp.stack([cosine, -sine_table]), jnp.stack([sine_table, cosine])])
    return (forward.astype(jnp.bfloat16), inverse.astype(jnp.bfloat16))


def contract(pattern, left_side, right_side):
    return jnp.einsum(pattern, left_side, right_side, preferred_element_type=jnp.float32)


def collide(cells, forward, inverse, gain_one, gain_two, loss_kernel):
    points = forward.shape[-1]
    cell_count = cells.shape[0]
    field = cells.reshape(cell_count, points, points, points)
    section_z = contract("nabz,qzw->qnabw", field, forward[:, 0]).astype(jnp.bfloat16)
    section_y = contract("pnayc,qpyw->qnawc", section_z, forward).astype(jnp.bfloat16)
    spectrum = contract("pnxbc,qpxw->qnwbc", section_y, forward)
    scale_factor = 1.0 / float(points**3)

    def filtered(kernel):
        weighted = (spectrum * (kernel * scale_factor)[None, None]).astype(jnp.bfloat16)
        back_x = contract("pnxbc,qpxw->qnwbc", weighted, inverse).astype(jnp.bfloat16)
        back_y = contract("pnayc,qpyw->qnawc", back_x, inverse).astype(jnp.bfloat16)
        return contract("pnabz,pzw->nabw", back_y, inverse[0])

    gain_term = filtered(gain_one) * filtered(gain_two)
    result = gain_term - field.astype(jnp.float32) * filtered(loss_kernel)
    return result.reshape(cell_count, points**3)


def courants(points, first_vel, local_count):
    vel_index = first_vel + jnp.arange(local_count, dtype=jnp.int32)
    index_x = vel_index // (points * points)
    index_y = vel_index // points % points
    index_z = vel_index % points

    def speed(index_part):
        return 0.3 * (2.0 * index_part.astype(jnp.float32) - (points - 1)) / (points - 1)

    return (speed(index_x), speed(index_y), speed(index_z))


def upwind_flux(courant, center, lower_side, upper_side):
    return jnp.maximum(courant, 0.0) * (center - lower_side) + jnp.minimum(courant, 0.0) * (
        upper_side - center
    )


def plain_device(distribution, refine_level, gain_one, gain_two, loss_kernel):
    points = gain_one.shape[0]
    width_x, width_y, width_z, local_vel = distribution.shape
    first_vel = lax.axis_index("vel") * local_vel
    courant_x, courant_y, courant_z = courants(points, first_vel, local_vel)
    padded = extended(distribution, (("cx", 0), ("cy", 1)), 1)
    fluxes = upwind_flux(courant_x, distribution, padded[:-2, 1:-1], padded[2:, 1:-1])
    fluxes = fluxes + upwind_flux(courant_y, distribution, padded[1:-1, :-2], padded[1:-1, 2:])
    fluxes = fluxes + upwind_flux(
        courant_z, distribution, jnp.roll(distribution, 1, 2), jnp.roll(distribution, -1, 2)
    )
    read = distribution - fluxes
    block_cells = width_x * width_y * width_z
    groups = lax.axis_size("vel")
    flattened = read.reshape(block_cells, local_vel).astype(jnp.bfloat16)
    forward, inverse = dft_tables(points)
    active = refine_level.reshape(block_cells) > 0
    slot_index = jnp.cumsum(active.astype(jnp.int32)) - 1
    capacity = block_cells // 2
    picker = (
        (slot_index[None, :] == jnp.arange(capacity, dtype=jnp.int32)[:, None]) & active[None, :]
    ).astype(jnp.bfloat16)
    chosen = jnp.dot(picker, flattened, preferred_element_type=jnp.float32).astype(jnp.bfloat16)
    terms = collide(
        lax.all_to_all(
            chosen.reshape(groups, capacity // groups, local_vel),
            "vel",
            split_axis=0,
            concat_axis=2,
            tiled=True,
        )[0],
        forward,
        inverse,
        gain_one,
        gain_two,
        loss_kernel,
    )[None]
    packed = lax.all_to_all(
        terms.astype(jnp.bfloat16), "vel", split_axis=2, concat_axis=0, tiled=True
    ).astype(terms.dtype)
    packed_rows = packed.reshape(capacity, local_vel)
    safe_slot = jnp.clip(slot_index, 0, capacity - 1)
    rates = jnp.where(active[:, None], packed_rows[safe_slot], 0.0)
    weight = 0.25 * refine_level.astype(jnp.float32)
    return read + weight[..., None] * rates.reshape(width_x, width_y, width_z, local_vel)

LANES = 128
PLANES = 4


def half_set(points):
    middle = points // 2
    pairs = [(b, c) for c in range(1, middle) for b in range(points)]
    pairs += [(b, c) for c in (0, middle) for b in range(middle + 1)]
    weights = [1.0 if b % middle == 0 and c % middle == 0 else 2.0 for b, c in pairs]
    return np.array(pairs), np.array(weights)


def plane_table(points, padded, margin):
    pairs, _ = half_set(points)
    first, second = np.divmod(np.arange(points * points), points)
    products = (first[:, None] * pairs[None, :, 0] + second[:, None] * pairs[None, :, 1]) % points
    angles = 2.0 * np.pi * products / points
    table = np.zeros((points * points + 2 * margin, 2 * padded), np.float32)
    rows = slice(margin, margin + points * points)
    table[rows, : len(pairs)] = np.cos(angles)
    table[rows, padded : padded + len(pairs)] = -np.sin(angles)
    return table.astype(ml_dtypes.bfloat16)


def frequency_select(points, padded):
    pairs, weights = half_set(points)
    select = np.zeros((points * points, 2 * padded), np.float32)
    column = np.arange(len(pairs))
    select[pairs[:, 0] * points + pairs[:, 1], column] = 1.0
    mirror = (-pairs[:, 0]) % points * points + (-pairs[:, 1]) % points
    select[mirror, padded + column] = 1.0
    scale = np.zeros((1, padded), np.float32)
    scale[0, : len(pairs)] = 0.5 * weights / points**3
    return select.astype(ml_dtypes.bfloat16), scale


def weights_kernel(stacked_ref, select_ref, scale_ref, out_ref):
    kernels, points, padded = out_ref.shape
    rest = stacked_ref[...]
    picked = None
    for _ in range(3):
        piece = rest.astype(jnp.bfloat16)
        rest = rest - piece.astype(jnp.float32)
        part = jnp.dot(piece, select_ref[...], preferred_element_type=jnp.float32)
        picked = part if picked is None else picked + part
    for which in range(kernels):
        for a in range(points):
            row, mirror = which * points + a, which * points + (-a) % points
            both = picked[row : row + 1, :padded] + picked[mirror : mirror + 1, padded:]
            out_ref[which, a : a + 1, :] = both * scale_ref[...]


def transform_3(x, sign, wanted=(0, 1, 2)):
    (ar, ai), (br, bi), (cr, ci) = x
    sr, si = br + cr, bi + ci
    out = {}
    if 0 in wanted:
        out[0] = (ar + sr, ai + si)
    if 1 in wanted or 2 in wanted:
        height = sign * math.sqrt(0.75)
        mr, mi = ar - 0.5 * sr, ai - 0.5 * si
        er, ei = height * (br - cr), height * (bi - ci)
        if 1 in wanted:
            out[1] = (mr - ei, mi + er)
        if 2 in wanted:
            out[2] = (mr + ei, mi - er)
    return out


def transform_4(x, sign):
    (ar, ai), (br, bi), (cr, ci), (dr, di) = x
    pr, pi, qr, qi = ar + cr, ai + ci, ar - cr, ai - ci
    sr, si, tr, ti = br + dr, bi + di, br - dr, bi - di
    if sign < 0:
        tr, ti = -tr, -ti
    return [(pr + sr, pi + si), (qr - ti, qi + tr), (pr - sr, pi - si), (qr + ti, qi - tr)]


def transform_8(x, sign):
    even = transform_4(x[0::2], sign)
    odd = transform_4(x[1::2], sign)
    root = math.sqrt(0.5)
    (r0, i0), (r1, i1), (r2, i2), (r3, i3) = odd
    if sign > 0:
        turned = [(r0, i0), (root * (r1 - i1), root * (i1 + r1)), (-i2, r2)]
        turned.append((-root * (r3 + i3), root * (r3 - i3)))
    else:
        turned = [(r0, i0), (root * (r1 + i1), root * (i1 - r1)), (i2, -r2)]
        turned.append((root * (i3 - r3), -root * (i3 + r3)))
    low = [(e[0] + t[0], e[1] + t[1]) for e, t in zip(even, turned)]
    high = [(e[0] - t[0], e[1] - t[1]) for e, t in zip(even, turned)]
    return low + high


def spectrum_of(load):
    stage = {}
    for n2 in range(8):
        part = transform_3([load((8 * n1 + 3 * n2) % 24) for n1 in range(3)], -1)
        for k1 in range(3):
            stage[k1, n2] = part[k1]
    result = {}
    for k1 in range(3):
        part = transform_8([stage[k1, n2] for n2 in range(8)], -1)
        for k2 in range(8):
            result[(16 * k1 + 9 * k2) % 24] = part[k2]
    return result


def first_half_of(spectrum):
    stage = {}
    for k1 in range(3):
        part = transform_8([spectrum[(16 * k1 + 9 * k2) % 24] for k2 in range(8)], 1)
        for n2 in range(8):
            stage[k1, n2] = part[n2]
    result = {}
    for n2 in range(8):
        wanted = {n1: (8 * n1 + 3 * n2) % 24 for n1 in range(3) if (8 * n1 + 3 * n2) % 24 < 12}
        part = transform_3([stage[k1, n2] for k1 in range(3)], 1, tuple(wanted))
        for n1, index in wanted.items():
            result[index] = part[n1]
    return result


def tile_pair(ref, step, rows):
    parts = []
    for parity in range(2):
        at = (2 * step + parity) * LANES
        part = ref[:, :, :, at : at + LANES]
        parts.append(part.reshape(rows, part.shape[2], LANES))
    return jnp.concatenate(parts, axis=1)


def edges_kernel(
    first, edge_ref, falls_ref, field_ref, down_ref, up_ref, across_ref, low_ref, high_ref, plane_ref, sems
):
    steps = falls_ref.shape[0] // 8
    here = pl.ds(first, low_ref.shape[3])
    last_y = field_ref.shape[1] - 1
    sources = [
        field_ref.at[:, pl.ds(0, 1), :, here],
        field_ref.at[:, pl.ds(last_y, 1), :, here],
        field_ref.at[pl.ds(edge_ref[0], 1), :, :, here],
    ]
    loads = [
        pltpu.make_async_copy(source, ref, sems.at[at])
        for at, (source, ref) in enumerate(zip(sources, (low_ref, high_ref, plane_ref)))
    ]
    for load in loads:
        load.start()
    width = low_ref.shape[0]
    below = [falls_ref[8 * s : 8 * s + 8, :][None] > 0.0 for s in range(steps)]

    def put(ref, at, value):
        ref[at] = value.reshape(-1, LANES).astype(jnp.bfloat16)

    loads[0].wait()
    lowest = [tile_pair(low_ref, s, width) for s in range(steps)]
    put(down_ref, 0, lowest[0])
    for m in range(1, steps // 2 + 1):
        put(down_ref, m, jnp.where(below[2 * m - 1], lowest[2 * m - 1], lowest[2 * m]))
    loads[1].wait()
    last = [tile_pair(high_ref, s, width) for s in range(steps)]
    for m in range(steps // 2):
        put(up_ref, m, jnp.where(below[2 * m], last[2 * m + 1], last[2 * m]))
    put(up_ref, steps // 2, last[steps - 1])
    loads[2].wait()
    for s in range(steps):
        put(across_ref, s, tile_pair(plane_ref, s, plane_ref.shape[1]))


def upwind_kernel(
    base,
    side_ref,
    speed_ref,
    picker_ref,
    field_ref,
    down_ref,
    up_ref,
    across_ref,
    *refs,
):
    carried_refs, (read_ref, early_ref, late_ref), scratch = refs[:-8], refs[-8:-5], refs[-5:]
    blocks, wide, border, cells, sems = scratch
    chunks, width_x, width_y, width_z, lanes = blocks.shape
    steps = lanes // (2 * LANES)
    loads = []
    for t in range(chunks):
        source = field_ref.at[:, :, :, pl.ds(base + t * lanes, lanes)]
        loads.append(pltpu.make_async_copy(source, blocks.at[t], sems.at[t]))
        loads[-1].start()
    beside = jnp.where(side_ref[0] == 0, 2, 0)
    place = lax.broadcasted_iota(jnp.int32, (1, 8, LANES), 1) % width_z
    capacity = picker_ref.shape[0] // 2
    late = late_ref.shape[0]
    early = capacity - late
    for ref in carried_refs:
        early_ref[early:, :] = ref[...]
    for t in range(chunks):
        sizes, falls, sinks = [], [], []
        for u in range(steps):
            step = t * steps + u
            speed = [speed_ref[d, 8 * step : 8 * step + 8, :][None] for d in range(3)]
            sizes.append([jnp.abs(c) for c in speed])
            falls.append(speed[1] < 0.0)
            sinks.append(speed[2] < 0.0)
            outer = across_ref[step].astype(jnp.float32).reshape(width_y, 8, LANES)
            wide[u, 0] = outer
            wide[u, width_x + 1] = outer
            above = down_ref[(step + 1) // 2].astype(jnp.float32).reshape(width_x, 8, LANES)
            under = up_ref[step // 2].astype(jnp.float32).reshape(width_x, 8, LANES)
            border[u] = jnp.where(falls[u], above, under)
        loads[t].wait()

        def spread_out(x, carry):
            for u in range(steps):
                at = 2 * u * LANES
                parts = [
                    blocks[t, x, :, :, at + p * LANES : at + (p + 1) * LANES] for p in range(2)
                ]
                wide[u, x + 1] = jnp.concatenate(parts, axis=1)
            return carry

        lax.fori_loop(0, width_x, spread_out, 0, unroll=4)

        def advance(x, carry):
            for u in range(steps):
                field = wide[u, x + 1]
                edge = border[u, pl.ds(x, 1)]
                fluxes = sizes[u][0] * (field - wide[u, x + beside])
                beside_y = jnp.where(
                    falls[u],
                    jnp.concatenate([field[1:], edge], axis=0),
                    jnp.concatenate([edge, field[:-1]], axis=0),
                )
                fluxes = fluxes + sizes[u][1] * (field - beside_y)
                upper = jnp.where(
                    place == width_z - 1, pltpu.roll(field, 3, 1), pltpu.roll(field, 7, 1)
                )
                lower = jnp.where(place == 0, pltpu.roll(field, 5, 1), pltpu.roll(field, 1, 1))
                fluxes = fluxes + sizes[u][2] * (field - jnp.where(sinks[u], upper, lower))
                read = field - fluxes
                row = 8 * (t * steps + u)
                read_ref[pl.ds(x * width_y, width_y), row : row + 8, :] = read
                rows = width_y * 8
                at = pl.multiple_of(x * rows, rows)
                cells[pl.ds(at, rows), u * LANES : (u + 1) * LANES] = read.reshape(
                    rows, LANES
                ).astype(jnp.bfloat16)
            return carry

        lax.fori_loop(0, width_x, advance, 0, unroll=2)
        picked = jnp.dot(
            picker_ref[...], cells[...], preferred_element_type=jnp.float32
        ).astype(jnp.bfloat16)
        for parity in range(2):
            first = parity * capacity
            for u in range(steps):
                tile = 2 * (t * steps + u) + parity
                here = slice(tile * LANES, (tile + 1) * LANES)
                values = picked[first : first + capacity, u * LANES : (u + 1) * LANES]
                early_ref[:early, here] = values[:early]
                late_ref[:, here] = values[early:]


def filter_parts(parts, weight_ref, table_ref, own_refs, other_refs, section, back):
    slots = section.shape[1]
    padded = weight_ref.shape[2]
    height = table_ref.shape[0]
    window = height - 64
    pair_lanes = 2 * (height - 128)
    pairs = own_refs[0][0].shape[1] // pair_lanes
    half = 2 * pairs * parts
    for parity in range(2):
        rows = []
        for ref, first in own_refs + other_refs:
            for p in range(pairs):
                at = p * pair_lanes + parity * (pair_lanes - window)
                rows.append(ref[first : first + slots, at : at + window])
        start = 64 * (1 - parity)
        out = jnp.dot(
            jnp.concatenate(rows, axis=0),
            table_ref[start : start + window, :],
            preferred_element_type=jnp.float32,
        )
        for at in range(half):
            section[2 * at + parity] = out[at * slots : (at + 1) * slots]

    lane_tiles = padded // LANES

    def transform(index, carry):
        row = pl.multiple_of(index // lane_tiles * 16, 16)
        lane = pl.multiple_of(index % lane_tiles * LANES, LANES)
        results = []
        for octet in range(2):
            here = pl.ds(row + 8 * octet, 8)

            def load(i):
                real = section[i, here, pl.ds(lane, LANES)]
                return real, section[i, here, pl.ds(padded + lane, LANES)]

            spectrum = spectrum_of(load)
            per_kernel = []
            for which in range(3):
                weighted = {}
                for a, (real, imag) in spectrum.items():
                    weight = weight_ref[which, pl.ds(a, 1), pl.ds(lane, LANES)]
                    weighted[a] = (real * weight, imag * weight)
                per_kernel.append(first_half_of(weighted))
            results.append(per_kernel)
        for which in range(3):
            for i in range(half):
                for q in range(2):
                    value = jnp.concatenate([results[o][which][i][q] for o in range(2)], axis=0)
                    back[i % 2, which, i // 2, pl.ds(row, 16), pl.ds(q * padded + lane, LANES)] = (
                        value.astype(jnp.bfloat16)
                    )
        return carry

    lax.fori_loop(0, slots // 16 * lane_tiles, transform, 0)


def terms_of(part, table_ref, own, back, put):
    own_ref, first = own
    slots, lanes = back.shape[3], own_ref.shape[1]
    height = table_ref.shape[0]
    window = height - 64
    pair_lanes = 2 * (height - 128)
    pairs = lanes // pair_lanes
    outs = []
    for parity in range(2):
        start = 64 * (1 - parity)
        outs.append(
            lax.dot_general(
                back[parity, :, part * pairs : (part + 1) * pairs].reshape(
                    3 * pairs * slots, back.shape[-1]
                ),
                table_ref[start : start + window, :],
                (((1,), (1,)), ((), ())),
                preferred_element_type=jnp.float32,
            ).reshape(3, pairs, slots, window)
        )
    tiles = pair_lanes // LANES
    near = lax.broadcasted_iota(jnp.int32, (slots, LANES), 1) < 64
    for at in range(pairs):
        for tile in range(tiles):
            lane = tile * LANES
            odd_lane = lane - (pair_lanes - window)
            values = []
            for which in range(3):
                if tile < tiles // 2:
                    value = outs[0][which, at, :, lane : lane + LANES]
                elif tile > tiles // 2:
                    value = outs[1][which, at, :, odd_lane : odd_lane + LANES]
                else:
                    value = jnp.where(
                        near,
                        outs[0][which, at, :, lane : lane + LANES],
                        outs[1][which, at, :, odd_lane : odd_lane + LANES],
                    )
                values.append(value)
            lane = at * pair_lanes + lane
            cells = own_ref[first : first + slots, lane : lane + LANES].astype(jnp.float32)
            put(at * tiles + tile, (values[0] * values[1] - cells * values[2]).astype(jnp.bfloat16))


def collide_kernel(firsts, weight_ref, table_ref, *refs):
    parts = len(firsts) // 2
    windows = list(zip(refs, firsts))
    own_refs, other_refs = windows[:parts], windows[parts:]
    terms_ref, section, back = refs[2 * parts :]
    filter_parts(parts, weight_ref, table_ref, own_refs, other_refs, section, back)
    for part in range(parts):
        first = part * own_refs[0][0].shape[1]

        def put(tile, value):
            terms_ref[:, first + tile * LANES : first + (tile + 1) * LANES] = value

        terms_of(part, table_ref, own_refs[part], back, put)


def finish_kernel(firsts, weight_ref, table_ref, spread_ref, early_ref, *refs):
    parts = len(firsts) // 2
    windows = list(zip(refs, firsts))
    own_refs, other_refs = windows[:parts], windows[parts:]
    read_refs = refs[2 * parts : 3 * parts]
    out_ref, section, back, reads, spots, added, staged, read_sems, out_sems = refs[3 * parts :]
    width_x, width_y, width_z, lanes = staged.shape[1:]
    tiles = lanes // LANES
    loads = [
        pltpu.make_async_copy(read_refs[part], reads.at[part], read_sems.at[part])
        for part in range(parts)
    ]
    for load in loads:
        load.start()
    filter_parts(parts, weight_ref, table_ref, own_refs, other_refs, section, back)
    early = early_ref.shape[0]
    capacity = early + section.shape[1]
    stores = []
    for part in range(parts):

        def put(tile, value):
            first = tile % 2 * capacity
            columns = slice(tile // 2 * LANES, (tile // 2 + 1) * LANES)
            lane = part * lanes + tile * LANES
            spots[first : first + early, columns] = early_ref[:, lane : lane + LANES]
            spots[first + early : first + capacity, columns] = value

        terms_of(part, table_ref, own_refs[part], back, put)
        added[...] = jnp.dot(spread_ref[...], spots[...], preferred_element_type=jnp.float32)
        loads[part].wait()
        slot = part % 2
        if part >= 2:
            stores[part - 2].wait()

        def add(x, carry):
            for y in range(width_y):
                row = x * width_y + y
                at = pl.multiple_of(row * 8, 8)
                for u in range(tiles // 2):
                    value = (
                        reads[part, row, 8 * u : 8 * u + 8, :]
                        + added[pl.ds(at, 8), u * LANES : (u + 1) * LANES]
                    )
                    for parity in range(2):
                        lane = (2 * u + parity) * LANES
                        piece = value[parity * width_z : (parity + 1) * width_z]
                        staged[slot, x, y, :, lane : lane + LANES] = piece
            return carry

        lax.fori_loop(0, width_x, add, 0)
        store = pltpu.make_async_copy(
            staged.at[slot],
            out_ref.at[:, :, :, part * lanes : (part + 1) * lanes],
            out_sems.at[part],
        )
        store.start()
        stores.append(store)
    for store in stores[-2:]:
        store.wait()


def params(mib):
    return pltpu.CompilerParams(vmem_limit_bytes=mib * 2**20)


def cost(flops, size):
    return pl.CostEstimate(flops=flops, bytes_accessed=size, transcendentals=0)


def fast_fits(distribution, points):
    width_x, width_y, width_z, local_vel = distribution.shape
    group = PLANES * points * points
    return (
        points == 24
        and lax.axis_size("vel") == 2
        and width_z == 4
        and local_vel * 2 == points**3
        and local_vel % group == 0
        and width_x * width_y * width_z % 128 == 0
    )


def fast_device(distribution, refine_level, gain_one, gain_two, loss_kernel):
    points = gain_one.shape[0]
    width_x, width_y, width_z, local_vel = distribution.shape
    block_rows = width_x * width_y
    block_cells = block_rows * width_z
    group = PLANES * points * points
    parts = local_vel // group
    group_rows = group // LANES * width_z
    steps = group_rows // 8
    capacity = block_cells // 2
    late = capacity * 3 // 8 // 16 * 16
    counts = (capacity - late, late)
    vel_at = lax.axis_index("vel")
    count_x, count_y = lax.axis_size("cx"), lax.axis_size("cy")

    tiles = local_vel // LANES
    speeds = jnp.stack(courants(points, vel_at * local_vel, local_vel))
    speeds = jnp.broadcast_to(
        speeds.reshape(3, tiles, 1, LANES), (3, tiles, width_z, LANES)
    ).reshape(3, parts, tiles * width_z // parts, LANES)
    speeds = [speeds[:, g] for g in range(parts)]
    falls = np.arange(group) // points % points < points // 2
    falls = np.repeat(falls.reshape(-1, 1, LANES), width_z, axis=1).reshape(-1, LANES)
    falls = jnp.asarray(falls.astype(np.float32))
    side = vel_at.reshape(1).astype(jnp.int32)
    edge = jnp.where(vel_at == 0, 0, width_x - 1).reshape(1).astype(jnp.int32)

    level = refine_level.reshape(block_cells)
    active = level > 0
    cell_at = jnp.arange(block_cells, dtype=jnp.int32)
    before = (cell_at[:, None] < cell_at[None, :]) & active[:, None]
    slot_index = jnp.where(active, jnp.sum(before.astype(jnp.int32), axis=0), -1)
    spot = slot_index.reshape(block_rows, 1, width_z)
    parity = jnp.arange(2, dtype=jnp.int32)[None, :, None]
    shape = (block_rows, 2, width_z)
    wanted = jnp.where(spot >= 0, spot + capacity * parity, -1)
    wanted = jnp.broadcast_to(wanted, shape).reshape(-1)
    numbers = jnp.arange(2 * capacity, dtype=jnp.int32)
    picker = (numbers[:, None] == wanted[None, :]).astype(jnp.bfloat16)
    strength = jnp.broadcast_to(
        (0.25 * level.astype(jnp.float32)).reshape(block_rows, 1, width_z), shape
    ).reshape(-1)
    spread = jnp.where(wanted[:, None] == numbers[None, :], strength[:, None], 0.0)
    spread = spread.astype(jnp.bfloat16)

    padded = -(-len(half_set(points)[1]) // LANES) * LANES
    select, scale = frequency_select(points, padded)
    table = jnp.asarray(plane_table(points, padded, 64))

    towards_lower = [(j, (j - 1) % count_y) for j in range(count_y)]
    towards_upper = [(j, (j + 1) % count_y) for j in range(count_y)]
    across_pairs = [(i, (i - 1) % count_x) for i in range(count_x)]
    across_pairs += [(count_x + i, count_x + (i + 1) % count_x) for i in range(count_x)]
    swap = [(0, 1), (1, 0)]
    bf16 = jnp.bfloat16

    half_steps = steps // 2 + 1
    local = pl.BlockSpec(memory_space=pltpu.VMEM)
    scalar = pl.BlockSpec(memory_space=pltpu.SMEM)
    remote = pl.BlockSpec(memory_space=pltpu.HBM)

    def edges_of(g):
        return pl.pallas_call(
            functools.partial(edges_kernel, g * group),
            in_specs=[scalar, local, remote],
            out_specs=[local] * 3,
            out_shape=[
                jax.ShapeDtypeStruct((half_steps, width_x * 8, LANES), bf16),
                jax.ShapeDtypeStruct((half_steps, width_x * 8, LANES), bf16),
                jax.ShapeDtypeStruct((steps, width_y * 8, LANES), bf16),
            ],
            scratch_shapes=[
                pltpu.VMEM((width_x, 1, width_z, group), jnp.float32),
                pltpu.VMEM((width_x, 1, width_z, group), jnp.float32),
                pltpu.VMEM((1, width_y, width_z, group), jnp.float32),
                pltpu.SemaphoreType.DMA((3,)),
            ],
            compiler_params=params(58 if g == 0 else 16),
            cost_estimate=cost(1, 1),
            name="edges",
        )(edge, falls, distribution)

    edges = [edges_of(g) for g in range(parts)]
    wide = 3
    chunks = steps // wide

    def upwind(g, halo, carried):
        heights = (capacity if carried else counts[0], counts[1])
        return pl.pallas_call(
            functools.partial(upwind_kernel, g * group),
            in_specs=[scalar, local, local, remote] + [local] * (len(halo) + len(carried)),
            out_specs=[local] * 3,
            out_shape=[jax.ShapeDtypeStruct((block_rows, group_rows, LANES), jnp.float32)]
            + [jax.ShapeDtypeStruct((height, group), bf16) for height in heights],
            scratch_shapes=[
                pltpu.VMEM((chunks, width_x, width_y, width_z, group // chunks), jnp.float32),
                pltpu.VMEM((wide, width_x + 2, width_y, 8, LANES), jnp.float32),
                pltpu.VMEM((wide, width_x, 8, LANES), jnp.float32),
                pltpu.VMEM((block_rows * 8, wide * LANES), bf16),
                pltpu.SemaphoreType.DMA((chunks,)),
            ],
            compiler_params=params(20),
            cost_estimate=cost(1, 1),
            name="upwind",
        )(side, speeds[g], picker, distribution, *halo, *carried)

    def turn(value, *earlier):
        return lax.optimization_barrier((value, *earlier))[0]

    def swapped(value):
        return lax.ppermute(value, "vel", swap)

    reads, firsts, lasts, halos, early = [], [], [], [], []
    for g in range(parts):
        operands = edges[g] if g == 0 else turn(edges[g], halos[-1])
        down, up, across = operands
        halos.append(
            (
                lax.ppermute(down, "cy", towards_lower),
                lax.ppermute(up, "cy", towards_upper),
                lax.ppermute(across, ("vel", "cx"), across_pairs),
            )
        )
    for g in range(parts):
        halo = halos[g] if g == 0 else turn(halos[g], firsts[-1])
        if g > 1:
            halo = turn(halo, early[g - 2])
        read, first, last = upwind(g, halo, lasts[:1] if g == 1 else [])
        reads.append(read)
        firsts.append(first)
        lasts.append(last)
        early.append(swapped(first))
    later = turn(jnp.concatenate(lasts[1:], axis=0), *early[1:])
    late = swapped(later)

    kernels = turn((gain_one, gain_two, loss_kernel), firsts[-1])
    weights = pl.pallas_call(
        weights_kernel,
        out_shape=jax.ShapeDtypeStruct((3, points, padded), jnp.float32),
        compiler_params=params(12),
        cost_estimate=cost(1, 1),
        name="weights",
    )(
        jnp.concatenate([k.reshape(points, points * points) for k in kernels], axis=0),
        jnp.asarray(select),
        jnp.asarray(scale),
    )

    def scratch(count):
        return [
            pltpu.VMEM((points, count, 2 * padded), jnp.float32),
            pltpu.VMEM((2, 3, points // 4, count, 2 * padded), bf16),
        ]

    terms = pl.pallas_call(
        functools.partial(collide_kernel, (0,) * (2 * parts)),
        out_shape=jax.ShapeDtypeStruct((counts[0], local_vel), bf16),
        scratch_shapes=scratch(counts[0]),
        compiler_params=params(32),
        cost_estimate=cost(1, 1),
            name="collide",
    )(weights, table, *firsts, *early)

    lates = [early[1]] + [late] * (parts - 1)
    late_firsts = (0,) * parts + (counts[0],) + tuple(counts[1] * g for g in range(parts - 1))
    anywhere = pl.BlockSpec(memory_space=pl.ANY)
    return pl.pallas_call(
        functools.partial(finish_kernel, late_firsts),
        in_specs=[local] * (4 + 2 * parts) + [anywhere] * parts,
        out_specs=anywhere,
        out_shape=jax.ShapeDtypeStruct(distribution.shape, jnp.float32),
        scratch_shapes=scratch(counts[1])
        + [
            pltpu.VMEM((parts, block_rows, group_rows, LANES), jnp.float32),
            pltpu.VMEM((2 * capacity, group // 2), bf16),
            pltpu.VMEM((block_rows * 8, group // 2), jnp.float32),
            pltpu.VMEM((2, width_x, width_y, width_z, group), jnp.float32),
            pltpu.SemaphoreType.DMA((parts,)),
            pltpu.SemaphoreType.DMA((parts,)),
        ],
        compiler_params=params(44),
        name="finish",
    )(weights, table, spread, terms, *lasts, *lates, *reads)


def per_device(distribution, refine_level, gain_one, gain_two, loss_kernel):
    if fast_fits(distribution, gain_one.shape[0]):
        return fast_device(distribution, refine_level, gain_one, gain_two, loss_kernel)
    return plain_device(distribution, refine_level, gain_one, gain_two, loss_kernel)


def solution(mesh):
    placed = (P("cx", "cy", None, "vel"), P("cx", "cy", None), P(), P(), P())
    return jax.shard_map(
        per_device,
        mesh=mesh,
        in_specs=placed,
        out_specs=P("cx", "cy", None, "vel"),
        check_vma=False,
    )
```

```python
import functools
import math

import jax
import jax.numpy as jnp
import ml_dtypes
import numpy as np
from jax import lax
from jax.experimental import pallas as pl
from jax.experimental.pallas import tpu as pltpu
from jax.sharding import PartitionSpec as P


def extended(array, sides, width):
    for axis, dim in sides:
        count, length = (lax.axis_size(axis), array.shape[dim])
        up = [(i, (i + 1) % count) for i in range(count)]
        down = [(j, i) for i, j in up]
        last = lax.slice_in_dim(array, length - width, length, axis=dim)
        leading = lax.slice_in_dim(array, 0, width, axis=dim)
        before = lax.ppermute(last, axis, up)
        after = lax.ppermute(leading, axis, down)
        array = jnp.concatenate([before, array, after], axis=dim)
    return array


def dft_tables(points):
    indices = jnp.arange(points, dtype=jnp.int32)
    products = indices[:, None] * indices[None, :] % points
    angles = products.astype(jnp.float32) * (2.0 * math.pi / points)
    cosine = jnp.cos(angles)
    sine_table = jnp.sin(angles)
    forward = jnp.stack([jnp.stack([cosine, sine_table]), jnp.stack([-sine_table, cosine])])
    inverse = jnp.stack([jnp.stack([cosine, -sine_table]), jnp.stack([sine_table, cosine])])
    return (forward.astype(jnp.bfloat16), inverse.astype(jnp.bfloat16))


def contract(pattern, left_side, right_side):
    return jnp.einsum(pattern, left_side, right_side, preferred_element_type=jnp.float32)


def collide(cells, forward, inverse, gain_one, gain_two, loss_kernel):
    points = forward.shape[-1]
    cell_count = cells.shape[0]
    field = cells.reshape(cell_count, points, points, points)
    section_z = contract("nabz,qzw->qnabw", field, forward[:, 0]).astype(jnp.bfloat16)
    section_y = contract("pnayc,qpyw->qnawc", section_z, forward).astype(jnp.bfloat16)
    spectrum = contract("pnxbc,qpxw->qnwbc", section_y, forward)
    scale_factor = 1.0 / float(points**3)

    def filtered(kernel):
        weighted = (spectrum * (kernel * scale_factor)[None, None]).astype(jnp.bfloat16)
        back_x = contract("pnxbc,qpxw->qnwbc", weighted, inverse).astype(jnp.bfloat16)
        back_y = contract("pnayc,qpyw->qnawc", back_x, inverse).astype(jnp.bfloat16)
        return contract("pnabz,pzw->nabw", back_y, inverse[0])

    gain_term = filtered(gain_one) * filtered(gain_two)
    result = gain_term - field.astype(jnp.float32) * filtered(loss_kernel)
    return result.reshape(cell_count, points**3)


def courants(points, first_vel, local_count):
    vel_index = first_vel + jnp.arange(local_count, dtype=jnp.int32)
    index_x = vel_index // (points * points)
    index_y = vel_index // points % points
    index_z = vel_index % points

    def speed(index_part):
        return 0.3 * (2.0 * index_part.astype(jnp.float32) - (points - 1)) / (points - 1)

    return (speed(index_x), speed(index_y), speed(index_z))


def upwind_flux(courant, center, lower_side, upper_side):
    return jnp.maximum(courant, 0.0) * (center - lower_side) + jnp.minimum(courant, 0.0) * (
        upper_side - center
    )


def plain_device(distribution, refine_level, gain_one, gain_two, loss_kernel):
    points = gain_one.shape[0]
    width_x, width_y, width_z, local_vel = distribution.shape
    first_vel = lax.axis_index("vel") * local_vel
    courant_x, courant_y, courant_z = courants(points, first_vel, local_vel)
    padded = extended(distribution, (("cx", 0), ("cy", 1)), 1)
    fluxes = upwind_flux(courant_x, distribution, padded[:-2, 1:-1], padded[2:, 1:-1])
    fluxes = fluxes + upwind_flux(courant_y, distribution, padded[1:-1, :-2], padded[1:-1, 2:])
    fluxes = fluxes + upwind_flux(
        courant_z, distribution, jnp.roll(distribution, 1, 2), jnp.roll(distribution, -1, 2)
    )
    read = distribution - fluxes
    block_cells = width_x * width_y * width_z
    groups = lax.axis_size("vel")
    flattened = read.reshape(block_cells, local_vel).astype(jnp.bfloat16)
    forward, inverse = dft_tables(points)
    active = refine_level.reshape(block_cells) > 0
    slot_index = jnp.cumsum(active.astype(jnp.int32)) - 1
    capacity = block_cells // 2
    picker = (
        (slot_index[None, :] == jnp.arange(capacity, dtype=jnp.int32)[:, None]) & active[None, :]
    ).astype(jnp.bfloat16)
    chosen = jnp.dot(picker, flattened, preferred_element_type=jnp.float32).astype(jnp.bfloat16)
    terms = collide(
        lax.all_to_all(
            chosen.reshape(groups, capacity // groups, local_vel),
            "vel",
            split_axis=0,
            concat_axis=2,
            tiled=True,
        )[0],
        forward,
        inverse,
        gain_one,
        gain_two,
        loss_kernel,
    )[None]
    packed = lax.all_to_all(
        terms.astype(jnp.bfloat16), "vel", split_axis=2, concat_axis=0, tiled=True
    ).astype(terms.dtype)
    packed_rows = packed.reshape(capacity, local_vel)
    safe_slot = jnp.clip(slot_index, 0, capacity - 1)
    rates = jnp.where(active[:, None], packed_rows[safe_slot], 0.0)
    weight = 0.25 * refine_level.astype(jnp.float32)
    return read + weight[..., None] * rates.reshape(width_x, width_y, width_z, local_vel)

LANES = 128
PLANES = 4


def half_set(points):
    middle = points // 2
    pairs = [(b, c) for c in range(1, middle) for b in range(points)]
    pairs += [(b, c) for c in (0, middle) for b in range(middle + 1)]
    weights = [1.0 if b % middle == 0 and c % middle == 0 else 2.0 for b, c in pairs]
    return np.array(pairs), np.array(weights)


def plane_table(points, padded, margin):
    pairs, _ = half_set(points)
    first, second = np.divmod(np.arange(points * points), points)
    products = (first[:, None] * pairs[None, :, 0] + second[:, None] * pairs[None, :, 1]) % points
    angles = 2.0 * np.pi * products / points
    table = np.zeros((points * points + 2 * margin, 2 * padded), np.float32)
    rows = slice(margin, margin + points * points)
    table[rows, : len(pairs)] = np.cos(angles)
    table[rows, padded : padded + len(pairs)] = -np.sin(angles)
    return table.astype(ml_dtypes.bfloat16)


def frequency_select(points, padded):
    pairs, weights = half_set(points)
    select = np.zeros((points * points, 2 * padded), np.float32)
    column = np.arange(len(pairs))
    select[pairs[:, 0] * points + pairs[:, 1], column] = 1.0
    mirror = (-pairs[:, 0]) % points * points + (-pairs[:, 1]) % points
    select[mirror, padded + column] = 1.0
    scale = np.zeros((1, padded), np.float32)
    scale[0, : len(pairs)] = 0.5 * weights / points**3
    return select.astype(ml_dtypes.bfloat16), scale


def weights_kernel(stacked_ref, select_ref, scale_ref, out_ref):
    kernels, points, padded = out_ref.shape
    rest = stacked_ref[...]
    picked = None
    for _ in range(3):
        piece = rest.astype(jnp.bfloat16)
        rest = rest - piece.astype(jnp.float32)
        part = jnp.dot(piece, select_ref[...], preferred_element_type=jnp.float32)
        picked = part if picked is None else picked + part
    for which in range(kernels):
        for a in range(points):
            row, mirror = which * points + a, which * points + (-a) % points
            both = picked[row : row + 1, :padded] + picked[mirror : mirror + 1, padded:]
            out_ref[which, a : a + 1, :] = both * scale_ref[...]


def transform_3(x, sign, wanted=(0, 1, 2)):
    (ar, ai), (br, bi), (cr, ci) = x
    sr, si = br + cr, bi + ci
    out = {}
    if 0 in wanted:
        out[0] = (ar + sr, ai + si)
    if 1 in wanted or 2 in wanted:
        height = sign * math.sqrt(0.75)
        mr, mi = ar - 0.5 * sr, ai - 0.5 * si
        er, ei = height * (br - cr), height * (bi - ci)
        if 1 in wanted:
            out[1] = (mr - ei, mi + er)
        if 2 in wanted:
            out[2] = (mr + ei, mi - er)
    return out


def transform_4(x, sign):
    (ar, ai), (br, bi), (cr, ci), (dr, di) = x
    pr, pi, qr, qi = ar + cr, ai + ci, ar - cr, ai - ci
    sr, si, tr, ti = br + dr, bi + di, br - dr, bi - di
    if sign < 0:
        tr, ti = -tr, -ti
    return [(pr + sr, pi + si), (qr - ti, qi + tr), (pr - sr, pi - si), (qr + ti, qi - tr)]


def transform_8(x, sign):
    even = transform_4(x[0::2], sign)
    odd = transform_4(x[1::2], sign)
    root = math.sqrt(0.5)
    (r0, i0), (r1, i1), (r2, i2), (r3, i3) = odd
    if sign > 0:
        turned = [(r0, i0), (root * (r1 - i1), root * (i1 + r1)), (-i2, r2)]
        turned.append((-root * (r3 + i3), root * (r3 - i3)))
    else:
        turned = [(r0, i0), (root * (r1 + i1), root * (i1 - r1)), (i2, -r2)]
        turned.append((root * (i3 - r3), -root * (i3 + r3)))
    low = [(e[0] + t[0], e[1] + t[1]) for e, t in zip(even, turned)]
    high = [(e[0] - t[0], e[1] - t[1]) for e, t in zip(even, turned)]
    return low + high


def spectrum_of(load):
    stage = {}
    for n2 in range(8):
        part = transform_3([load((8 * n1 + 3 * n2) % 24) for n1 in range(3)], -1)
        for k1 in range(3):
            stage[k1, n2] = part[k1]
    result = {}
    for k1 in range(3):
        part = transform_8([stage[k1, n2] for n2 in range(8)], -1)
        for k2 in range(8):
            result[(16 * k1 + 9 * k2) % 24] = part[k2]
    return result


def first_half_of(spectrum):
    stage = {}
    for k1 in range(3):
        part = transform_8([spectrum[(16 * k1 + 9 * k2) % 24] for k2 in range(8)], 1)
        for n2 in range(8):
            stage[k1, n2] = part[n2]
    result = {}
    for n2 in range(8):
        wanted = {n1: (8 * n1 + 3 * n2) % 24 for n1 in range(3) if (8 * n1 + 3 * n2) % 24 < 12}
        part = transform_3([stage[k1, n2] for k1 in range(3)], 1, tuple(wanted))
        for n1, index in wanted.items():
            result[index] = part[n1]
    return result


def tile_pair(ref, step, rows):
    parts = []
    for parity in range(2):
        at = (2 * step + parity) * LANES
        part = ref[:, :, :, at : at + LANES]
        parts.append(part.reshape(rows, part.shape[2], LANES))
    return jnp.concatenate(parts, axis=1)


def edges_kernel(first, edge_ref, falls_ref, field_ref, *refs):
    down_ref, up_ref, across_ref, low_ref, high_ref, plane_ref, sems = refs
    steps = falls_ref.shape[0] // 8
    width = low_ref.shape[0]
    groups = across_ref.shape[0] // steps
    half_steps = down_ref.shape[0] // groups
    here = pl.ds(first, low_ref.shape[3])
    last_y = field_ref.shape[1] - 1
    sources = [
        field_ref.at[:, pl.ds(0, 1), :, here],
        field_ref.at[:, pl.ds(last_y, 1), :, here],
        field_ref.at[pl.ds(edge_ref[0], 1), :, :, here],
    ]
    loads = [
        pltpu.make_async_copy(source, ref, sems.at[at])
        for at, (source, ref) in enumerate(zip(sources, (low_ref, high_ref, plane_ref)))
    ]
    for load in loads:
        load.start()
    below = [falls_ref[8 * s : 8 * s + 8, :][None] > 0.0 for s in range(steps)]

    def put(ref, at, value):
        ref[at] = value.reshape(-1, LANES).astype(jnp.bfloat16)

    loads[0].wait()
    for g in range(groups):
        row = [tile_pair(low_ref, g * steps + s, width) for s in range(steps)]
        put(down_ref, g * half_steps, row[0])
        for m in range(1, steps // 2 + 1):
            put(down_ref, g * half_steps + m, jnp.where(below[2 * m - 1], row[2 * m - 1], row[2 * m]))
    loads[1].wait()
    for g in range(groups):
        row = [tile_pair(high_ref, g * steps + s, width) for s in range(steps)]
        for m in range(steps // 2):
            put(up_ref, g * half_steps + m, jnp.where(below[2 * m], row[2 * m + 1], row[2 * m]))
        put(up_ref, g * half_steps + steps // 2, row[steps - 1])
    loads[2].wait()
    for s in range(groups * steps):
        put(across_ref, s, tile_pair(plane_ref, s, plane_ref.shape[1]))


def upwind_kernel(
    base,
    place_at,
    into_late,
    side_ref,
    speed_ref,
    picker_ref,
    field_ref,
    down_ref,
    up_ref,
    across_ref,
    *refs,
):
    carried_refs, (read_ref, early_ref, late_ref), scratch = refs[:-8], refs[-8:-5], refs[-5:]
    blocks, wide, border, cells, sems = scratch
    chunks, width_x, width_y, width_z, lanes = blocks.shape
    steps = lanes // (2 * LANES)
    loads = []
    for t in range(chunks):
        source = field_ref.at[:, :, :, pl.ds(base + t * lanes, lanes)]
        loads.append(pltpu.make_async_copy(source, blocks.at[t], sems.at[t]))
        loads[-1].start()
    beside = jnp.where(side_ref[0] == 0, 2, 0)
    place = lax.broadcasted_iota(jnp.int32, (1, 8, LANES), 1) % width_z
    capacity = picker_ref.shape[0] // 2
    late = carried_refs[0].shape[0] if carried_refs else late_ref.shape[0]
    early = capacity - late
    late_at = late_ref.shape[0] - late
    for ref in carried_refs:
        if into_late:
            late_ref[:late, :] = ref[...]
        else:
            early_ref[early:, :] = ref[...]
    half_steps = chunks * steps // 2 + 1
    for t in range(chunks):
        sizes, falls, sinks = [], [], []
        for u in range(steps):
            step = t * steps + u
            speed = [speed_ref[d, 8 * step : 8 * step + 8, :][None] for d in range(3)]
            sizes.append([jnp.abs(c) for c in speed])
            falls.append(speed[1] < 0.0)
            sinks.append(speed[2] < 0.0)
            outer = across_ref[place_at * chunks * steps + step].astype(jnp.float32).reshape(width_y, 8, LANES)
            wide[u, 0] = outer
            wide[u, width_x + 1] = outer
            above = down_ref[place_at * half_steps + (step + 1) // 2].astype(jnp.float32)
            under = up_ref[place_at * half_steps + step // 2].astype(jnp.float32)
            shape = (width_x, 8, LANES)
            border[u] = jnp.where(falls[u], above.reshape(shape), under.reshape(shape))
        loads[t].wait()

        def spread_out(x, carry):
            for u in range(steps):
                at = 2 * u * LANES
                parts = [
                    blocks[t, x, :, :, at + p * LANES : at + (p + 1) * LANES] for p in range(2)
                ]
                wide[u, x + 1] = jnp.concatenate(parts, axis=1)
            return carry

        lax.fori_loop(0, width_x, spread_out, 0, unroll=4)

        def advance(x, carry):
            for u in range(steps):
                field = wide[u, x + 1]
                edge = border[u, pl.ds(x, 1)]
                fluxes = sizes[u][0] * (field - wide[u, x + beside])
                beside_y = jnp.where(
                    falls[u],
                    jnp.concatenate([field[1:], edge], axis=0),
                    jnp.concatenate([edge, field[:-1]], axis=0),
                )
                fluxes = fluxes + sizes[u][1] * (field - beside_y)
                upper = jnp.where(
                    place == width_z - 1, pltpu.roll(field, 3, 1), pltpu.roll(field, 7, 1)
                )
                lower = jnp.where(place == 0, pltpu.roll(field, 5, 1), pltpu.roll(field, 1, 1))
                fluxes = fluxes + sizes[u][2] * (field - jnp.where(sinks[u], upper, lower))
                read = field - fluxes
                row = 8 * (t * steps + u)
                read_ref[pl.ds(x * width_y, width_y), row : row + 8, :] = read
                rows = width_y * 8
                at = pl.multiple_of(x * rows, rows)
                cells[pl.ds(at, rows), u * LANES : (u + 1) * LANES] = read.reshape(
                    rows, LANES
                ).astype(jnp.bfloat16)
            return carry

        lax.fori_loop(0, width_x, advance, 0, unroll=2)
        picked = jnp.dot(
            picker_ref[...], cells[...], preferred_element_type=jnp.float32
        ).astype(jnp.bfloat16)
        for parity in range(2):
            first = parity * capacity
            for u in range(steps):
                tile = 2 * (t * steps + u) + parity
                here = slice(tile * LANES, (tile + 1) * LANES)
                values = picked[first : first + capacity, u * LANES : (u + 1) * LANES]
                early_ref[:early, here] = values[:early]
                late_ref[late_at:, here] = values[early:]


def window_loads(firsts, refs, cells, sems):
    loads = []
    for at, (ref, first) in enumerate(zip(refs, firsts)):
        source = ref.at[pl.ds(first, cells.shape[1])]
        loads.append(pltpu.make_async_copy(source, cells.at[at], sems.at[at]))
        loads[-1].start()
    return loads


def filter_parts(weight_ref, table_ref, cells, loads, section, back):
    count, slots, lanes = cells.shape
    padded = weight_ref.shape[2]
    height = table_ref.shape[0]
    window = height - 64
    pair_lanes = 2 * (height - 128)
    pairs = lanes // pair_lanes
    half = pairs * count
    for side in range(2):
        here = range(side * count // 2, (side + 1) * count // 2)
        for at in here:
            loads[at].wait()
        for parity in range(2):
            rows = []
            for at in here:
                for p in range(pairs):
                    lane = p * pair_lanes + parity * (pair_lanes - window)
                    rows.append(cells[at, :, lane : lane + window])
            start = 64 * (1 - parity)
            out = jnp.dot(
                jnp.concatenate(rows, axis=0),
                table_ref[start : start + window, :],
                preferred_element_type=jnp.float32,
            )
            for at in range(half // 2):
                section[side * half + 2 * at + parity] = out[at * slots : (at + 1) * slots]

    lane_tiles = padded // LANES

    def transform(index, carry):
        row = pl.multiple_of(index // lane_tiles * 16, 16)
        lane = pl.multiple_of(index % lane_tiles * LANES, LANES)
        results = []
        for octet in range(2):
            here = pl.ds(row + 8 * octet, 8)

            def load(i):
                real = section[i, here, pl.ds(lane, LANES)]
                return real, section[i, here, pl.ds(padded + lane, LANES)]

            spectrum = spectrum_of(load)
            per_kernel = []
            for which in range(3):
                weighted = {}
                for a, (real, imag) in spectrum.items():
                    weight = weight_ref[which, pl.ds(a, 1), pl.ds(lane, LANES)]
                    weighted[a] = (real * weight, imag * weight)
                per_kernel.append(first_half_of(weighted))
            results.append(per_kernel)
        for which in range(3):
            for i in range(half):
                for q in range(2):
                    value = jnp.concatenate([results[o][which][i][q] for o in range(2)], axis=0)
                    back[i % 2, which, i // 2, pl.ds(row, 16), pl.ds(q * padded + lane, LANES)] = (
                        value.astype(jnp.bfloat16)
                    )
        return carry

    lax.fori_loop(0, slots // 16 * lane_tiles, transform, 0)


def terms_of(part, table_ref, cells_ref, back, put):
    _, slots, lanes = cells_ref.shape
    height = table_ref.shape[0]
    window = height - 64
    pair_lanes = 2 * (height - 128)
    pairs = lanes // pair_lanes
    outs = []
    for parity in range(2):
        start = 64 * (1 - parity)
        outs.append(
            lax.dot_general(
                back[parity, :, part * pairs : (part + 1) * pairs].reshape(
                    3 * pairs * slots, back.shape[-1]
                ),
                table_ref[start : start + window, :],
                (((1,), (1,)), ((), ())),
                preferred_element_type=jnp.float32,
            ).reshape(3, pairs, slots, window)
        )
    tiles = pair_lanes // LANES
    near = lax.broadcasted_iota(jnp.int32, (slots, LANES), 1) < 64
    for at in range(pairs):
        for tile in range(tiles):
            lane = tile * LANES
            odd_lane = lane - (pair_lanes - window)
            values = []
            for which in range(3):
                if tile < tiles // 2:
                    value = outs[0][which, at, :, lane : lane + LANES]
                elif tile > tiles // 2:
                    value = outs[1][which, at, :, odd_lane : odd_lane + LANES]
                else:
                    value = jnp.where(
                        near,
                        outs[0][which, at, :, lane : lane + LANES],
                        outs[1][which, at, :, odd_lane : odd_lane + LANES],
                    )
                values.append(value)
            lane = at * pair_lanes + lane
            cells = cells_ref[part, :, lane : lane + LANES].astype(jnp.float32)
            put(at * tiles + tile, (values[0] * values[1] - cells * values[2]).astype(jnp.bfloat16))


def collide_kernel(firsts, weight_ref, table_ref, *refs):
    parts = len(firsts) // 2
    terms_ref, cells, section, back, sems = refs[2 * parts :]
    lanes = cells.shape[2]
    loads = window_loads(firsts, refs[: 2 * parts], cells, sems)
    filter_parts(weight_ref, table_ref, cells, loads, section, back)
    for part in range(parts):

        def put(tile, value):
            first = part * lanes + tile * LANES
            terms_ref[:, first : first + LANES] = value

        terms_of(part, table_ref, cells, back, put)


def finish_kernel(firsts, weight_ref, table_ref, spread_ref, early_ref, *refs):
    parts = len(firsts) // 2
    read_refs = refs[2 * parts : 3 * parts]
    out_ref, cells, section, back, reads, spots, added, staged = refs[3 * parts : -3]
    cell_sems, read_sems, out_sems = refs[-3:]
    width_x, width_y, width_z, lanes = staged.shape[1:]
    tiles = lanes // LANES
    loads = window_loads(firsts, refs[: 2 * parts], cells, cell_sems)
    read_loads = [
        pltpu.make_async_copy(read_refs[part], reads.at[part], read_sems.at[part])
        for part in range(parts)
    ]
    for load in read_loads:
        load.start()
    filter_parts(weight_ref, table_ref, cells, loads, section, back)
    early = early_ref.shape[0]
    capacity = early + section.shape[1]
    pieces = out_sems.shape[1]
    piece_x = width_x // pieces
    stores = []
    for part in range(parts):

        def put(tile, value):
            first = tile % 2 * capacity
            columns = slice(tile // 2 * LANES, (tile // 2 + 1) * LANES)
            lane = part * lanes + tile * LANES
            spots[first : first + early, columns] = early_ref[:, lane : lane + LANES]
            spots[first + early : first + capacity, columns] = value

        terms_of(part, table_ref, cells, back, put)
        added[...] = jnp.dot(spread_ref[...], spots[...], preferred_element_type=jnp.float32)
        read_loads[part].wait()
        slot = part % 2
        if part >= 2:
            for store in stores[part - 2]:
                store.wait()

        def add(x, carry):
            for y in range(width_y):
                row = x * width_y + y
                at = pl.multiple_of(row * 8, 8)
                for u in range(tiles // 2):
                    value = (
                        reads[part, row, 8 * u : 8 * u + 8, :]
                        + added[pl.ds(at, 8), u * LANES : (u + 1) * LANES]
                    )
                    for parity in range(2):
                        lane = (2 * u + parity) * LANES
                        half = value[parity * width_z : (parity + 1) * width_z]
                        staged[slot, x, y, :, lane : lane + LANES] = half
            return carry

        stores.append([])
        for piece in range(pieces):
            lax.fori_loop(piece * piece_x, (piece + 1) * piece_x, add, 0)
            rows = pl.ds(piece * piece_x, piece_x)
            store = pltpu.make_async_copy(
                staged.at[slot, rows],
                out_ref.at[rows, :, :, pl.ds(part * lanes, lanes)],
                out_sems.at[part, piece],
            )
            store.start()
            stores[part].append(store)
    for part in range(max(parts - 2, 0), parts):
        for store in stores[part]:
            store.wait()


def params(mib):
    return pltpu.CompilerParams(vmem_limit_bytes=mib * 2**20)


def cost(flops, size):
    return pl.CostEstimate(flops=flops, bytes_accessed=size, transcendentals=0)


def fast_fits(distribution, points):
    width_x, width_y, width_z, local_vel = distribution.shape
    group = PLANES * points * points
    return (
        points == 24
        and lax.axis_size("vel") == 2
        and width_z == 4
        and local_vel * 2 == points**3
        and local_vel == 3 * group
        and width_x * width_y * width_z % 128 == 0
    )


def fast_device(distribution, refine_level, gain_one, gain_two, loss_kernel):
    points = gain_one.shape[0]
    width_x, width_y, width_z, local_vel = distribution.shape
    block_rows = width_x * width_y
    block_cells = block_rows * width_z
    group = PLANES * points * points
    parts = local_vel // group
    group_rows = group // LANES * width_z
    steps = group_rows // 8
    capacity = block_cells // 2
    late = capacity * 3 // 8 // 16 * 16
    counts = (capacity - late, late)
    vel_at = lax.axis_index("vel")
    count_x, count_y = lax.axis_size("cx"), lax.axis_size("cy")

    tiles = local_vel // LANES
    speeds = jnp.stack(courants(points, vel_at * local_vel, local_vel))
    speeds = jnp.broadcast_to(
        speeds.reshape(3, tiles, 1, LANES), (3, tiles, width_z, LANES)
    ).reshape(3, parts, tiles * width_z // parts, LANES)
    speeds = [speeds[:, g] for g in range(parts)]
    falls = np.arange(group) // points % points < points // 2
    falls = np.repeat(falls.reshape(-1, 1, LANES), width_z, axis=1).reshape(-1, LANES)
    falls = jnp.asarray(falls.astype(np.float32))
    side = vel_at.reshape(1).astype(jnp.int32)
    edge = jnp.where(vel_at == 0, 0, width_x - 1).reshape(1).astype(jnp.int32)

    level = refine_level.reshape(block_cells)
    active = level > 0
    cell_at = jnp.arange(block_cells, dtype=jnp.int32)
    before = (cell_at[:, None] < cell_at[None, :]) & active[:, None]
    slot_index = jnp.where(active, jnp.sum(before.astype(jnp.int32), axis=0), -1)
    spot = slot_index.reshape(block_rows, 1, width_z)
    parity = jnp.arange(2, dtype=jnp.int32)[None, :, None]
    shape = (block_rows, 2, width_z)
    wanted = jnp.where(spot >= 0, spot + capacity * parity, -1)
    wanted = jnp.broadcast_to(wanted, shape).reshape(-1)
    numbers = jnp.arange(2 * capacity, dtype=jnp.int32)
    picker = (numbers[:, None] == wanted[None, :]).astype(jnp.bfloat16)
    strength = jnp.broadcast_to(
        (0.25 * level.astype(jnp.float32)).reshape(block_rows, 1, width_z), shape
    ).reshape(-1)
    spread = jnp.where(wanted[:, None] == numbers[None, :], strength[:, None], 0.0)
    spread = spread.astype(jnp.bfloat16)

    padded = -(-len(half_set(points)[1]) // LANES) * LANES
    select, scale = frequency_select(points, padded)
    table = jnp.asarray(plane_table(points, padded, 64))

    towards_lower = [(j, (j - 1) % count_y) for j in range(count_y)]
    towards_upper = [(j, (j + 1) % count_y) for j in range(count_y)]
    across_pairs = [(i, (i - 1) % count_x) for i in range(count_x)]
    across_pairs += [(count_x + i, count_x + (i + 1) % count_x) for i in range(count_x)]
    swap = [(0, 1), (1, 0)]
    bf16 = jnp.bfloat16

    half_steps = steps // 2 + 1
    local = pl.BlockSpec(memory_space=pltpu.VMEM)
    scalar = pl.BlockSpec(memory_space=pltpu.SMEM)
    remote = pl.BlockSpec(memory_space=pltpu.HBM)

    def edges_of(first, groups):
        return pl.pallas_call(
            functools.partial(edges_kernel, first * group),
            in_specs=[scalar, local, remote],
            out_specs=[local] * 3,
            out_shape=[
                jax.ShapeDtypeStruct((groups * half_steps, width_x * 8, LANES), bf16),
                jax.ShapeDtypeStruct((groups * half_steps, width_x * 8, LANES), bf16),
                jax.ShapeDtypeStruct((groups * steps, width_y * 8, LANES), bf16),
            ],
            scratch_shapes=[
                pltpu.VMEM((width_x, 1, width_z, groups * group), jnp.float32),
                pltpu.VMEM((width_x, 1, width_z, groups * group), jnp.float32),
                pltpu.VMEM((1, width_y, width_z, groups * group), jnp.float32),
                pltpu.SemaphoreType.DMA((3,)),
            ],
            compiler_params=params(16),
            cost_estimate=cost(1, 1),
            name="edges",
        )(edge, falls, distribution)

    edges = [edges_of(0, 1), edges_of(1, parts - 1)]
    wide = 3
    chunks = steps // wide

    def upwind(g, halo, carried):
        into_late = g > 1
        heights = (
            capacity if carried and not into_late else counts[0],
            2 * counts[1] if carried and into_late else counts[1],
        )
        return pl.pallas_call(
            functools.partial(upwind_kernel, g * group, max(g - 1, 0), into_late),
            in_specs=[scalar, local, local, remote] + [local] * (len(halo) + len(carried)),
            out_specs=[local] * 3,
            out_shape=[jax.ShapeDtypeStruct((block_rows, group_rows, LANES), jnp.float32)]
            + [jax.ShapeDtypeStruct((height, group), bf16) for height in heights],
            scratch_shapes=[
                pltpu.VMEM((chunks, width_x, width_y, width_z, group // chunks), jnp.float32),
                pltpu.VMEM((wide, width_x + 2, width_y, 8, LANES), jnp.float32),
                pltpu.VMEM((wide, width_x, 8, LANES), jnp.float32),
                pltpu.VMEM((block_rows * 8, wide * LANES), bf16),
                pltpu.SemaphoreType.DMA((chunks,)),
            ],
            compiler_params=params(20),
            cost_estimate=cost(1, 1),
            name="upwind",
        )(side, speeds[g], picker, distribution, *halo, *carried)

    def turn(value, *earlier):
        return lax.optimization_barrier((value, *earlier))[0]

    def swapped(value):
        return lax.ppermute(value, "vel", swap)

    halos = []
    for at in range(2):
        operands = edges[at] if at == 0 else turn(edges[at], halos[0])
        down, up, across = operands
        halos.append(
            (
                lax.ppermute(down, "cy", towards_lower),
                lax.ppermute(up, "cy", towards_upper),
                lax.ppermute(across, ("vel", "cx"), across_pairs),
            )
        )
    reads, firsts, lasts, early = [], [], [], []
    for g in range(parts):
        halo = halos[0] if g == 0 else turn(halos[1], firsts[-1], *early[: g - 1])
        read, first, last = upwind(g, halo, lasts[-1:])
        reads.append(read)
        firsts.append(first)
        lasts.append(last)
        early.append(swapped(first))
    kernels = turn((gain_one, gain_two, loss_kernel), firsts[-1])
    weights = pl.pallas_call(
        weights_kernel,
        out_shape=jax.ShapeDtypeStruct((3, points, padded), jnp.float32),
        compiler_params=params(12),
        cost_estimate=cost(1, 1),
        name="weights",
    )(
        jnp.concatenate([k.reshape(points, points * points) for k in kernels], axis=0),
        jnp.asarray(select),
        jnp.asarray(scale),
    )

    last, weights, spread = turn((lasts[-1], weights, spread), *early)
    late = swapped(last)

    def scratch(count):
        return [
            pltpu.VMEM((2 * parts, count, group), bf16),
            pltpu.VMEM((points, count, 2 * padded), jnp.float32),
            pltpu.VMEM((2, 3, points // 4, count, 2 * padded), bf16),
        ]

    anywhere = pl.BlockSpec(memory_space=pl.ANY)
    sems = pltpu.SemaphoreType.DMA((2 * parts,))
    terms = pl.pallas_call(
        functools.partial(collide_kernel, (0,) * (2 * parts)),
        in_specs=[local] * 2 + [anywhere] * (2 * parts),
        out_specs=local,
        out_shape=jax.ShapeDtypeStruct((counts[0], local_vel), bf16),
        scratch_shapes=scratch(counts[0]) + [sems],
        compiler_params=params(28),
        cost_estimate=cost(1, 1),
        name="collide",
    )(weights, table, *firsts, *early)

    pieces = 4
    own_late = (0, 0, counts[1])
    other_late = (counts[0], 0, counts[1])
    return pl.pallas_call(
        functools.partial(finish_kernel, own_late + other_late),
        in_specs=[local] * 4 + [anywhere] * (3 * parts),
        out_specs=anywhere,
        out_shape=jax.ShapeDtypeStruct(distribution.shape, jnp.float32),
        scratch_shapes=scratch(counts[1])
        + [
            pltpu.VMEM((parts, block_rows, group_rows, LANES), jnp.float32),
            pltpu.VMEM((2 * capacity, group // 2), bf16),
            pltpu.VMEM((block_rows * 8, group // 2), jnp.float32),
            pltpu.VMEM((2, width_x, width_y, width_z, group), jnp.float32),
            sems,
            pltpu.SemaphoreType.DMA((parts,)),
            pltpu.SemaphoreType.DMA((parts, pieces)),
        ],
        compiler_params=params(36),
        name="finish",
    )(weights, table, spread, terms, lasts[0], last, last, early[1], late, late, *reads)


def per_device(distribution, refine_level, gain_one, gain_two, loss_kernel):
    if fast_fits(distribution, gain_one.shape[0]):
        return fast_device(distribution, refine_level, gain_one, gain_two, loss_kernel)
    return plain_device(distribution, refine_level, gain_one, gain_two, loss_kernel)


def solution(mesh):
    placed = (P("cx", "cy", None, "vel"), P("cx", "cy", None), P(), P(), P())
    return jax.shard_map(
        per_device,
        mesh=mesh,
        in_specs=placed,
        out_specs=P("cx", "cy", None, "vel"),
        check_vma=False,
    )
```

```python
import functools
import math

import jax
import jax.numpy as jnp
import ml_dtypes
import numpy as np
from jax import lax
from jax.experimental import pallas as pl
from jax.experimental.pallas import tpu as pltpu
from jax.sharding import PartitionSpec as P


def extended(array, sides, width):
    for axis, dim in sides:
        count, length = (lax.axis_size(axis), array.shape[dim])
        up = [(i, (i + 1) % count) for i in range(count)]
        down = [(j, i) for i, j in up]
        last = lax.slice_in_dim(array, length - width, length, axis=dim)
        leading = lax.slice_in_dim(array, 0, width, axis=dim)
        before = lax.ppermute(last, axis, up)
        after = lax.ppermute(leading, axis, down)
        array = jnp.concatenate([before, array, after], axis=dim)
    return array


def dft_tables(points):
    indices = jnp.arange(points, dtype=jnp.int32)
    products = indices[:, None] * indices[None, :] % points
    angles = products.astype(jnp.float32) * (2.0 * math.pi / points)
    cosine = jnp.cos(angles)
    sine_table = jnp.sin(angles)
    forward = jnp.stack([jnp.stack([cosine, sine_table]), jnp.stack([-sine_table, cosine])])
    inverse = jnp.stack([jnp.stack([cosine, -sine_table]), jnp.stack([sine_table, cosine])])
    return (forward.astype(jnp.bfloat16), inverse.astype(jnp.bfloat16))


def contract(pattern, left_side, right_side):
    return jnp.einsum(pattern, left_side, right_side, preferred_element_type=jnp.float32)


def collide(cells, forward, inverse, gain_one, gain_two, loss_kernel):
    points = forward.shape[-1]
    cell_count = cells.shape[0]
    field = cells.reshape(cell_count, points, points, points)
    section_z = contract("nabz,qzw->qnabw", field, forward[:, 0]).astype(jnp.bfloat16)
    section_y = contract("pnayc,qpyw->qnawc", section_z, forward).astype(jnp.bfloat16)
    spectrum = contract("pnxbc,qpxw->qnwbc", section_y, forward)
    scale_factor = 1.0 / float(points**3)

    def filtered(kernel):
        weighted = (spectrum * (kernel * scale_factor)[None, None]).astype(jnp.bfloat16)
        back_x = contract("pnxbc,qpxw->qnwbc", weighted, inverse).astype(jnp.bfloat16)
        back_y = contract("pnayc,qpyw->qnawc", back_x, inverse).astype(jnp.bfloat16)
        return contract("pnabz,pzw->nabw", back_y, inverse[0])

    gain_term = filtered(gain_one) * filtered(gain_two)
    result = gain_term - field.astype(jnp.float32) * filtered(loss_kernel)
    return result.reshape(cell_count, points**3)


def courants(points, first_vel, local_count):
    vel_index = first_vel + jnp.arange(local_count, dtype=jnp.int32)
    index_x = vel_index // (points * points)
    index_y = vel_index // points % points
    index_z = vel_index % points

    def speed(index_part):
        return 0.3 * (2.0 * index_part.astype(jnp.float32) - (points - 1)) / (points - 1)

    return (speed(index_x), speed(index_y), speed(index_z))


def upwind_flux(courant, center, lower_side, upper_side):
    return jnp.maximum(courant, 0.0) * (center - lower_side) + jnp.minimum(courant, 0.0) * (
        upper_side - center
    )


def plain_device(distribution, refine_level, gain_one, gain_two, loss_kernel):
    points = gain_one.shape[0]
    width_x, width_y, width_z, local_vel = distribution.shape
    first_vel = lax.axis_index("vel") * local_vel
    courant_x, courant_y, courant_z = courants(points, first_vel, local_vel)
    padded = extended(distribution, (("cx", 0), ("cy", 1)), 1)
    fluxes = upwind_flux(courant_x, distribution, padded[:-2, 1:-1], padded[2:, 1:-1])
    fluxes = fluxes + upwind_flux(courant_y, distribution, padded[1:-1, :-2], padded[1:-1, 2:])
    fluxes = fluxes + upwind_flux(
        courant_z, distribution, jnp.roll(distribution, 1, 2), jnp.roll(distribution, -1, 2)
    )
    read = distribution - fluxes
    block_cells = width_x * width_y * width_z
    groups = lax.axis_size("vel")
    flattened = read.reshape(block_cells, local_vel).astype(jnp.bfloat16)
    forward, inverse = dft_tables(points)
    active = refine_level.reshape(block_cells) > 0
    slot_index = jnp.cumsum(active.astype(jnp.int32)) - 1
    capacity = block_cells // 2
    picker = (
        (slot_index[None, :] == jnp.arange(capacity, dtype=jnp.int32)[:, None]) & active[None, :]
    ).astype(jnp.bfloat16)
    chosen = jnp.dot(picker, flattened, preferred_element_type=jnp.float32).astype(jnp.bfloat16)
    terms = collide(
        lax.all_to_all(
            chosen.reshape(groups, capacity // groups, local_vel),
            "vel",
            split_axis=0,
            concat_axis=2,
            tiled=True,
        )[0],
        forward,
        inverse,
        gain_one,
        gain_two,
        loss_kernel,
    )[None]
    packed = lax.all_to_all(
        terms.astype(jnp.bfloat16), "vel", split_axis=2, concat_axis=0, tiled=True
    ).astype(terms.dtype)
    packed_rows = packed.reshape(capacity, local_vel)
    safe_slot = jnp.clip(slot_index, 0, capacity - 1)
    rates = jnp.where(active[:, None], packed_rows[safe_slot], 0.0)
    weight = 0.25 * refine_level.astype(jnp.float32)
    return read + weight[..., None] * rates.reshape(width_x, width_y, width_z, local_vel)

LANES = 128
PLANES = 4
LIMIT = 57


def half_set(points):
    middle = points // 2
    pairs = [(b, c) for c in range(1, middle) for b in range(points)]
    pairs += [(b, c) for c in (0, middle) for b in range(middle + 1)]
    weights = [1.0 if b % middle == 0 and c % middle == 0 else 2.0 for b, c in pairs]
    return np.array(pairs), np.array(weights)


def plane_table(points, padded, margin):
    pairs, _ = half_set(points)
    first, second = np.divmod(np.arange(points * points), points)
    products = (first[:, None] * pairs[None, :, 0] + second[:, None] * pairs[None, :, 1]) % points
    angles = 2.0 * np.pi * products / points
    table = np.zeros((points * points + 2 * margin, 2 * padded), np.float32)
    rows = slice(margin, margin + points * points)
    table[rows, : len(pairs)] = np.cos(angles)
    table[rows, padded : padded + len(pairs)] = -np.sin(angles)
    return table.astype(ml_dtypes.bfloat16)


def frequency_select(points, padded):
    pairs, weights = half_set(points)
    select = np.zeros((points * points, 2 * padded), np.float32)
    column = np.arange(len(pairs))
    select[pairs[:, 0] * points + pairs[:, 1], column] = 1.0
    mirror = (-pairs[:, 0]) % points * points + (-pairs[:, 1]) % points
    select[mirror, padded + column] = 1.0
    scale = np.zeros((1, padded), np.float32)
    scale[0, : len(pairs)] = 0.5 * weights / points**3
    return select.astype(ml_dtypes.bfloat16), scale


def weights_kernel(stacked_ref, select_ref, scale_ref, out_ref):
    kernels, points, padded = out_ref.shape
    rest = stacked_ref[...]
    picked = None
    for _ in range(3):
        piece = rest.astype(jnp.bfloat16)
        rest = rest - piece.astype(jnp.float32)
        part = jnp.dot(piece, select_ref[...], preferred_element_type=jnp.float32)
        picked = part if picked is None else picked + part
    for which in range(kernels):
        for a in range(points):
            row, mirror = which * points + a, which * points + (-a) % points
            both = picked[row : row + 1, :padded] + picked[mirror : mirror + 1, padded:]
            out_ref[which, a : a + 1, :] = both * scale_ref[...]


def transform_3(x, sign, wanted=(0, 1, 2)):
    (ar, ai), (br, bi), (cr, ci) = x
    sr, si = br + cr, bi + ci
    out = {}
    if 0 in wanted:
        out[0] = (ar + sr, ai + si)
    if 1 in wanted or 2 in wanted:
        height = sign * math.sqrt(0.75)
        mr, mi = ar - 0.5 * sr, ai - 0.5 * si
        er, ei = height * (br - cr), height * (bi - ci)
        if 1 in wanted:
            out[1] = (mr - ei, mi + er)
        if 2 in wanted:
            out[2] = (mr + ei, mi - er)
    return out


def transform_4(x, sign):
    (ar, ai), (br, bi), (cr, ci), (dr, di) = x
    pr, pi, qr, qi = ar + cr, ai + ci, ar - cr, ai - ci
    sr, si, tr, ti = br + dr, bi + di, br - dr, bi - di
    if sign < 0:
        tr, ti = -tr, -ti
    return [(pr + sr, pi + si), (qr - ti, qi + tr), (pr - sr, pi - si), (qr + ti, qi - tr)]


def transform_8(x, sign):
    even = transform_4(x[0::2], sign)
    odd = transform_4(x[1::2], sign)
    root = math.sqrt(0.5)
    (r0, i0), (r1, i1), (r2, i2), (r3, i3) = odd
    if sign > 0:
        turned = [(r0, i0), (root * (r1 - i1), root * (i1 + r1)), (-i2, r2)]
        turned.append((-root * (r3 + i3), root * (r3 - i3)))
    else:
        turned = [(r0, i0), (root * (r1 + i1), root * (i1 - r1)), (i2, -r2)]
        turned.append((root * (i3 - r3), -root * (i3 + r3)))
    low = [(e[0] + t[0], e[1] + t[1]) for e, t in zip(even, turned)]
    high = [(e[0] - t[0], e[1] - t[1]) for e, t in zip(even, turned)]
    return low + high


def spectrum_of(load):
    stage = {}
    for n2 in range(8):
        part = transform_3([load((8 * n1 + 3 * n2) % 24) for n1 in range(3)], -1)
        for k1 in range(3):
            stage[k1, n2] = part[k1]
    result = {}
    for k1 in range(3):
        part = transform_8([stage[k1, n2] for n2 in range(8)], -1)
        for k2 in range(8):
            result[(16 * k1 + 9 * k2) % 24] = part[k2]
    return result


def first_half_of(spectrum):
    stage = {}
    for k1 in range(3):
        part = transform_8([spectrum[(16 * k1 + 9 * k2) % 24] for k2 in range(8)], 1)
        for n2 in range(8):
            stage[k1, n2] = part[n2]
    result = {}
    for n2 in range(8):
        wanted = {n1: (8 * n1 + 3 * n2) % 24 for n1 in range(3) if (8 * n1 + 3 * n2) % 24 < 12}
        part = transform_3([stage[k1, n2] for k1 in range(3)], 1, tuple(wanted))
        for n1, index in wanted.items():
            result[index] = part[n1]
    return result


def tile_pair(ref, step, rows):
    parts = []
    for parity in range(2):
        at = (2 * step + parity) * LANES
        part = ref[:, :, :, at : at + LANES]
        parts.append(part.reshape(rows, part.shape[2], LANES))
    return jnp.concatenate(parts, axis=1)


def edges_kernel(first, edge_ref, falls_ref, field_ref, *refs):
    down_ref, up_ref, across_ref, low_ref, high_ref, plane_ref, sems = refs
    steps = falls_ref.shape[0] // 8
    width = low_ref.shape[0]
    groups = across_ref.shape[0] // steps
    half_steps = down_ref.shape[0] // groups
    here = pl.ds(first, low_ref.shape[3])
    last_y = field_ref.shape[1] - 1
    sources = [
        field_ref.at[:, pl.ds(0, 1), :, here],
        field_ref.at[:, pl.ds(last_y, 1), :, here],
        field_ref.at[pl.ds(edge_ref[0], 1), :, :, here],
    ]
    loads = [
        pltpu.make_async_copy(source, ref, sems.at[at])
        for at, (source, ref) in enumerate(zip(sources, (low_ref, high_ref, plane_ref)))
    ]
    for load in loads:
        load.start()
    below = [falls_ref[8 * s : 8 * s + 8, :][None] > 0.0 for s in range(steps)]

    def put(ref, at, value):
        ref[at] = value.reshape(-1, LANES).astype(jnp.bfloat16)

    loads[0].wait()
    for g in range(groups):
        row = [tile_pair(low_ref, g * steps + s, width) for s in range(steps)]
        put(down_ref, g * half_steps, row[0])
        for m in range(1, steps // 2 + 1):
            put(down_ref, g * half_steps + m, jnp.where(below[2 * m - 1], row[2 * m - 1], row[2 * m]))
    loads[1].wait()
    for g in range(groups):
        row = [tile_pair(high_ref, g * steps + s, width) for s in range(steps)]
        for m in range(steps // 2):
            put(up_ref, g * half_steps + m, jnp.where(below[2 * m], row[2 * m + 1], row[2 * m]))
        put(up_ref, g * half_steps + steps // 2, row[steps - 1])
    loads[2].wait()
    for s in range(groups * steps):
        put(across_ref, s, tile_pair(plane_ref, s, plane_ref.shape[1]))


def upwind_kernel(
    base,
    counts,
    side_ref,
    speed_ref,
    picker_ref,
    field_ref,
    down_ref,
    up_ref,
    across_ref,
    out_ref,
    *refs,
):
    chosen_refs, scratch = refs[:-7], refs[-7:]
    blocks, reads, wide, border, cells, load_sems, store_sems = scratch
    chunks, width_x, width_y, width_z, lanes = blocks.shape
    steps = lanes // (2 * LANES)
    group_lanes = chosen_refs[0].shape[1]
    per_group = group_lanes // lanes
    half_steps = per_group * steps // 2 + 1
    loads = []
    for t in range(chunks):
        source = field_ref.at[:, :, :, pl.ds(base + t * lanes, lanes)]
        loads.append(pltpu.make_async_copy(source, blocks.at[t], load_sems.at[t]))
        loads[-1].start()
    beside = jnp.where(side_ref[0] == 0, 2, 0)
    place = lax.broadcasted_iota(jnp.int32, (1, 8, LANES), 1) % width_z
    capacity = picker_ref.shape[0] // 2
    stores = []
    for t in range(chunks):
        group, chunk = t // per_group, t % per_group
        sizes, falls, sinks = [], [], []
        for u in range(steps):
            step = chunk * steps + u
            row = 8 * (t * steps + u)
            speed = [speed_ref[d, row : row + 8, :][None] for d in range(3)]
            sizes.append([jnp.abs(c) for c in speed])
            falls.append(speed[1] < 0.0)
            sinks.append(speed[2] < 0.0)
            outer = across_ref[t * steps + u].astype(jnp.float32).reshape(width_y, 8, LANES)
            wide[u, 0] = outer
            wide[u, width_x + 1] = outer
            above = down_ref[group * half_steps + (step + 1) // 2].astype(jnp.float32)
            under = up_ref[group * half_steps + step // 2].astype(jnp.float32)
            shape = (width_x, 8, LANES)
            border[u] = jnp.where(falls[u], above.reshape(shape), under.reshape(shape))
        loads[t].wait()

        def spread_out(x, carry):
            for u in range(steps):
                at = 2 * u * LANES
                parts = [
                    blocks[t, x, :, :, at + p * LANES : at + (p + 1) * LANES] for p in range(2)
                ]
                wide[u, x + 1] = jnp.concatenate(parts, axis=1)
            return carry

        lax.fori_loop(0, width_x, spread_out, 0, unroll=4)

        def advance(x, carry):
            for u in range(steps):
                field = wide[u, x + 1]
                edge = border[u, pl.ds(x, 1)]
                fluxes = sizes[u][0] * (field - wide[u, x + beside])
                beside_y = jnp.where(
                    falls[u],
                    jnp.concatenate([field[1:], edge], axis=0),
                    jnp.concatenate([edge, field[:-1]], axis=0),
                )
                fluxes = fluxes + sizes[u][1] * (field - beside_y)
                upper = jnp.where(
                    place == width_z - 1, pltpu.roll(field, 3, 1), pltpu.roll(field, 7, 1)
                )
                lower = jnp.where(place == 0, pltpu.roll(field, 5, 1), pltpu.roll(field, 1, 1))
                fluxes = fluxes + sizes[u][2] * (field - jnp.where(sinks[u], upper, lower))
                read = field - fluxes
                reads[t, pl.ds(x * width_y, width_y), 8 * u : 8 * u + 8, :] = read
                rows = width_y * 8
                at = pl.multiple_of(x * rows, rows)
                cells[pl.ds(at, rows), u * LANES : (u + 1) * LANES] = read.reshape(
                    rows, LANES
                ).astype(jnp.bfloat16)
            return carry

        lax.fori_loop(0, width_x, advance, 0, unroll=2)
        target = out_ref.at[:, pl.ds(8 * steps * t, 8 * steps), :]
        stores.append(pltpu.make_async_copy(reads.at[t], target, store_sems.at[t]))
        stores[-1].start()
        picked = jnp.dot(
            picker_ref[...], cells[...], preferred_element_type=jnp.float32
        ).astype(jnp.bfloat16)
        for parity in range(2):
            first = parity * capacity
            for ref, count in zip(chosen_refs, counts):
                rows = slice(group * count, (group + 1) * count)
                for u in range(steps):
                    tile = 2 * (chunk * steps + u) + parity
                    here = slice(tile * LANES, (tile + 1) * LANES)
                    ref[rows, here] = picked[first : first + count, u * LANES : (u + 1) * LANES]
                first += count
    for store in stores:
        store.wait()


def window_loads(firsts, refs, cells, sems):
    loads = []
    for at, (ref, first) in enumerate(zip(refs, firsts)):
        source = ref.at[pl.ds(first, cells.shape[1])]
        loads.append(pltpu.make_async_copy(source, cells.at[at], sems.at[at]))
        loads[-1].start()
    return loads


def filter_parts(weight_ref, table_ref, cells, loads, section, back):
    count, slots, lanes = cells.shape
    padded = weight_ref.shape[2]
    height = table_ref.shape[0]
    window = height - 64
    pair_lanes = 2 * (height - 128)
    pairs = lanes // pair_lanes
    half = pairs * count
    for side in range(2):
        here = range(side * count // 2, (side + 1) * count // 2)
        for at in here:
            loads[at].wait()
        for parity in range(2):
            rows = []
            for at in here:
                for p in range(pairs):
                    lane = p * pair_lanes + parity * (pair_lanes - window)
                    rows.append(cells[at, :, lane : lane + window])
            start = 64 * (1 - parity)
            out = jnp.dot(
                jnp.concatenate(rows, axis=0),
                table_ref[start : start + window, :],
                preferred_element_type=jnp.float32,
            )
            for at in range(half // 2):
                section[side * half + 2 * at + parity] = out[at * slots : (at + 1) * slots]

    lane_tiles = padded // LANES

    def transform(index, carry):
        row = pl.multiple_of(index // lane_tiles * 16, 16)
        lane = pl.multiple_of(index % lane_tiles * LANES, LANES)
        results = []
        for octet in range(2):
            here = pl.ds(row + 8 * octet, 8)

            def load(i):
                real = section[i, here, pl.ds(lane, LANES)]
                return real, section[i, here, pl.ds(padded + lane, LANES)]

            spectrum = spectrum_of(load)
            per_kernel = []
            for which in range(3):
                weighted = {}
                for a, (real, imag) in spectrum.items():
                    weight = weight_ref[which, pl.ds(a, 1), pl.ds(lane, LANES)]
                    weighted[a] = (real * weight, imag * weight)
                per_kernel.append(first_half_of(weighted))
            results.append(per_kernel)
        for which in range(3):
            for i in range(half):
                for q in range(2):
                    value = jnp.concatenate([results[o][which][i][q] for o in range(2)], axis=0)
                    back[i % 2, which, i // 2, pl.ds(row, 16), pl.ds(q * padded + lane, LANES)] = (
                        value.astype(jnp.bfloat16)
                    )
        return carry

    lax.fori_loop(0, slots // 16 * lane_tiles, transform, 0)


def terms_of(part, table_ref, cells_ref, back, put):
    _, slots, lanes = cells_ref.shape
    height = table_ref.shape[0]
    window = height - 64
    pair_lanes = 2 * (height - 128)
    pairs = lanes // pair_lanes
    outs = []
    for parity in range(2):
        start = 64 * (1 - parity)
        outs.append(
            lax.dot_general(
                back[parity, :, part * pairs : (part + 1) * pairs].reshape(
                    3 * pairs * slots, back.shape[-1]
                ),
                table_ref[start : start + window, :],
                (((1,), (1,)), ((), ())),
                preferred_element_type=jnp.float32,
            ).reshape(3, pairs, slots, window)
        )
    tiles = pair_lanes // LANES
    near = lax.broadcasted_iota(jnp.int32, (slots, LANES), 1) < 64
    for at in range(pairs):
        for tile in range(tiles):
            lane = tile * LANES
            odd_lane = lane - (pair_lanes - window)
            values = []
            for which in range(3):
                if tile < tiles // 2:
                    value = outs[0][which, at, :, lane : lane + LANES]
                elif tile > tiles // 2:
                    value = outs[1][which, at, :, odd_lane : odd_lane + LANES]
                else:
                    value = jnp.where(
                        near,
                        outs[0][which, at, :, lane : lane + LANES],
                        outs[1][which, at, :, odd_lane : odd_lane + LANES],
                    )
                values.append(value)
            lane = at * pair_lanes + lane
            cells = cells_ref[part, :, lane : lane + LANES].astype(jnp.float32)
            put(at * tiles + tile, (values[0] * values[1] - cells * values[2]).astype(jnp.bfloat16))


def collide_kernel(firsts, weight_ref, table_ref, *refs):
    parts = len(firsts) // 2
    terms_ref, cells, section, back, sems = refs[2 * parts :]
    lanes = cells.shape[2]
    loads = window_loads(firsts, refs[: 2 * parts], cells, sems)
    filter_parts(weight_ref, table_ref, cells, loads, section, back)
    for part in range(parts):

        def put(tile, value):
            first = part * lanes + tile * LANES
            terms_ref[:, first : first + LANES] = value

        terms_of(part, table_ref, cells, back, put)


def finish_kernel(firsts, sizes, weight_ref, table_ref, spread_any, *refs):
    parts = len(firsts) // 2
    term_refs, refs = refs[: len(sizes) - 1], refs[len(sizes) - 1 :]
    first_read, rest_read = refs[2 * parts : 2 * parts + 2]
    out_ref, cells, section, back, reads, spots, added, staged = refs[2 * parts + 2 : -6]
    spread_ref, early_ref, cell_sems, read_sems, out_sems, extra_sems = refs[-6:]
    width_x, width_y, width_z, lanes = staged.shape[1:]
    tiles = lanes // LANES
    loads = window_loads(firsts, refs[: 2 * parts], cells, cell_sems)
    extra = [pltpu.make_async_copy(spread_any, spread_ref, extra_sems.at[0])]
    at = 0
    for ref, size in zip(term_refs, sizes):
        target = early_ref.at[pl.ds(at, size)]
        extra.append(pltpu.make_async_copy(ref, target, extra_sems.at[len(extra)]))
        at += size
    group_rows = reads.shape[2]
    read_loads = []
    for part in range(parts):
        rows = pl.ds(max(part - 1, 0) * group_rows, group_rows)
        source = (rest_read if part else first_read).at[:, rows, :]
        read_loads.append(pltpu.make_async_copy(source, reads.at[part], read_sems.at[part]))
    for load in extra + read_loads:
        load.start()
    filter_parts(weight_ref, table_ref, cells, loads, section, back)
    for load in extra:
        load.wait()
    early = early_ref.shape[0]
    capacity = early + section.shape[1]
    pieces = out_sems.shape[1]
    piece_x = width_x // pieces
    stores = []
    for part in range(parts):

        def put(tile, value):
            first = tile % 2 * capacity
            columns = slice(tile // 2 * LANES, (tile // 2 + 1) * LANES)
            lane = part * lanes + tile * LANES
            spots[first : first + early, columns] = early_ref[:, lane : lane + LANES]
            spots[first + early : first + capacity, columns] = value

        terms_of(part, table_ref, cells, back, put)
        added[...] = jnp.dot(spread_ref[...], spots[...], preferred_element_type=jnp.float32)
        read_loads[part].wait()
        slot = part % 2
        if part >= 2:
            for store in stores[part - 2]:
                store.wait()

        def add(x, carry):
            for y in range(width_y):
                row = x * width_y + y
                at = pl.multiple_of(row * 8, 8)
                for u in range(tiles // 2):
                    value = (
                        reads[part, row, 8 * u : 8 * u + 8, :]
                        + added[pl.ds(at, 8), u * LANES : (u + 1) * LANES]
                    )
                    for parity in range(2):
                        lane = (2 * u + parity) * LANES
                        half = value[parity * width_z : (parity + 1) * width_z]
                        staged[slot, x, y, :, lane : lane + LANES] = half
            return carry

        stores.append([])
        for piece in range(pieces):
            lax.fori_loop(piece * piece_x, (piece + 1) * piece_x, add, 0)
            rows = pl.ds(piece * piece_x, piece_x)
            store = pltpu.make_async_copy(
                staged.at[slot, rows],
                out_ref.at[rows, :, :, pl.ds(part * lanes, lanes)],
                out_sems.at[part, piece],
            )
            store.start()
            stores[part].append(store)
    for part in range(max(parts - 2, 0), parts):
        for store in stores[part]:
            store.wait()


def params(mib):
    return pltpu.CompilerParams(vmem_limit_bytes=mib * 2**20)


def cost(flops, size):
    return pl.CostEstimate(flops=flops, bytes_accessed=size, transcendentals=0)


def fast_fits(distribution, points):
    width_x, width_y, width_z, local_vel = distribution.shape
    group = PLANES * points * points
    return (
        points == 24
        and lax.axis_size("vel") == 2
        and width_z == 4
        and local_vel * 2 == points**3
        and local_vel == 3 * group
        and width_x * width_y * width_z % 128 == 0
    )


def fast_device(distribution, refine_level, gain_one, gain_two, loss_kernel):
    points = gain_one.shape[0]
    width_x, width_y, width_z, local_vel = distribution.shape
    block_rows = width_x * width_y
    block_cells = block_rows * width_z
    group = PLANES * points * points
    parts = local_vel // group
    group_rows = group // LANES * width_z
    steps = group_rows // 8
    capacity = block_cells // 2
    third = capacity * 3 // 8 // 16 * 16
    counts = (third, third, capacity - 2 * third)
    batches = len(counts)
    vel_at = lax.axis_index("vel")
    count_x, count_y = lax.axis_size("cx"), lax.axis_size("cy")

    tiles = local_vel // LANES
    speeds = jnp.stack(courants(points, vel_at * local_vel, local_vel))
    speeds = jnp.broadcast_to(
        speeds.reshape(3, tiles, 1, LANES), (3, tiles, width_z, LANES)
    ).reshape(3, parts, tiles * width_z // parts, LANES)
    speeds = [speeds[:, 0], speeds[:, 1:].reshape(3, -1, LANES)]
    falls = np.arange(group) // points % points < points // 2
    falls = np.repeat(falls.reshape(-1, 1, LANES), width_z, axis=1).reshape(-1, LANES)
    falls = jnp.asarray(falls.astype(np.float32))
    side = vel_at.reshape(1).astype(jnp.int32)
    edge = jnp.where(vel_at == 0, 0, width_x - 1).reshape(1).astype(jnp.int32)

    level = refine_level.reshape(block_cells)
    active = level > 0
    cell_at = jnp.arange(block_cells, dtype=jnp.int32)
    before = (cell_at[:, None] < cell_at[None, :]) & active[:, None]
    slot_index = jnp.where(active, jnp.sum(before.astype(jnp.int32), axis=0), -1)
    spot = slot_index.reshape(block_rows, 1, width_z)
    parity = jnp.arange(2, dtype=jnp.int32)[None, :, None]
    shape = (block_rows, 2, width_z)
    wanted = jnp.where(spot >= 0, spot + capacity * parity, -1)
    wanted = jnp.broadcast_to(wanted, shape).reshape(-1)
    numbers = jnp.arange(2 * capacity, dtype=jnp.int32)
    picker = (numbers[:, None] == wanted[None, :]).astype(jnp.bfloat16)
    strength = jnp.broadcast_to(
        (0.25 * level.astype(jnp.float32)).reshape(block_rows, 1, width_z), shape
    ).reshape(-1)
    spread = jnp.where(wanted[:, None] == numbers[None, :], strength[:, None], 0.0)
    spread = spread.astype(jnp.bfloat16)

    padded = -(-len(half_set(points)[1]) // LANES) * LANES
    select, scale = frequency_select(points, padded)
    table = jnp.asarray(plane_table(points, padded, 64))

    towards_lower = [(j, (j - 1) % count_y) for j in range(count_y)]
    towards_upper = [(j, (j + 1) % count_y) for j in range(count_y)]
    across_pairs = [(i, (i - 1) % count_x) for i in range(count_x)]
    across_pairs += [(count_x + i, count_x + (i + 1) % count_x) for i in range(count_x)]
    swap = [(0, 1), (1, 0)]
    bf16 = jnp.bfloat16

    half_steps = steps // 2 + 1
    local = pl.BlockSpec(memory_space=pltpu.VMEM)
    scalar = pl.BlockSpec(memory_space=pltpu.SMEM)
    remote = pl.BlockSpec(memory_space=pltpu.HBM)
    anywhere = pl.BlockSpec(memory_space=pl.ANY)

    def edges_of(first, groups):
        return pl.pallas_call(
            functools.partial(edges_kernel, first * group),
            in_specs=[scalar, local, remote],
            out_specs=[local] * 3,
            out_shape=[
                jax.ShapeDtypeStruct((groups * half_steps, width_x * 8, LANES), bf16),
                jax.ShapeDtypeStruct((groups * half_steps, width_x * 8, LANES), bf16),
                jax.ShapeDtypeStruct((groups * steps, width_y * 8, LANES), bf16),
            ],
            scratch_shapes=[
                pltpu.VMEM((width_x, 1, width_z, groups * group), jnp.float32),
                pltpu.VMEM((width_x, 1, width_z, groups * group), jnp.float32),
                pltpu.VMEM((1, width_y, width_z, groups * group), jnp.float32),
                pltpu.SemaphoreType.DMA((3,)),
            ],
            compiler_params=params(LIMIT),
            cost_estimate=cost(1, 1),
            name="edges",
        )(edge, falls, distribution)

    edges = [edges_of(0, 1), edges_of(1, parts - 1)]
    wide = 3
    chunks = steps // wide

    def upwind(at, halo, sizes):
        groups = parts - 1 if at else 1
        return pl.pallas_call(
            functools.partial(upwind_kernel, at * group, sizes),
            in_specs=[scalar, local, local, remote] + [local] * len(halo),
            out_specs=[anywhere] + [local] * len(sizes),
            out_shape=[
                jax.ShapeDtypeStruct((block_rows, groups * group_rows, LANES), jnp.float32)
            ]
            + [jax.ShapeDtypeStruct((groups * size, group), bf16) for size in sizes],
            scratch_shapes=[
                pltpu.VMEM(
                    (groups * chunks, width_x, width_y, width_z, group // chunks), jnp.float32
                ),
                pltpu.VMEM((groups * chunks, block_rows, 8 * wide, LANES), jnp.float32),
                pltpu.VMEM((wide, width_x + 2, width_y, 8, LANES), jnp.float32),
                pltpu.VMEM((wide, width_x, 8, LANES), jnp.float32),
                pltpu.VMEM((block_rows * 8, wide * LANES), bf16),
                pltpu.SemaphoreType.DMA((groups * chunks,)),
                pltpu.SemaphoreType.DMA((groups * chunks,)),
            ],
            compiler_params=params(LIMIT),
            cost_estimate=cost(1, 1),
            name="upwind",
        )(side, speeds[at], picker, distribution, *halo)

    def turn(value, *earlier):
        return lax.optimization_barrier((value, *earlier))[0]

    def swapped(value):
        return lax.ppermute(value, "vel", swap)

    halos = []
    for at in range(2):
        down, up, across = edges[at]
        halos.append(
            (
                lax.ppermute(down, "cy", towards_lower),
                lax.ppermute(up, "cy", towards_upper),
                lax.ppermute(across, ("vel", "cx"), across_pairs),
            )
        )
    first_read, *first = upwind(0, turn(halos[0], edges[1]), counts)
    first_other = [swapped(x) for x in first]
    rest_read, *rest = upwind(1, turn(halos[1], first), counts)
    kernels = turn((gain_one, gain_two, loss_kernel), halos[0])
    weights = pl.pallas_call(
        weights_kernel,
        out_shape=jax.ShapeDtypeStruct((3, points, padded), jnp.float32),
        compiler_params=params(LIMIT),
        cost_estimate=cost(1, 1),
        name="weights",
    )(
        jnp.concatenate([k.reshape(points, points * points) for k in kernels], axis=0),
        jnp.asarray(select),
        jnp.asarray(scale),
    )

    operand, weights, spread = turn((rest[0], weights, spread), first_other)
    others = [swapped(operand)]

    def scratch(count):
        return [
            pltpu.VMEM((2 * parts, count, group), bf16),
            pltpu.VMEM((points, count, 2 * padded), jnp.float32),
            pltpu.VMEM((2, 3, points // 4, count, 2 * padded), bf16),
        ]

    sems = pltpu.SemaphoreType.DMA((2 * parts,))
    terms = []
    for batch in range(batches - 1):
        count = counts[batch]
        starts = (0,) + tuple(g * count for g in range(parts - 1))
        following = turn(rest[batch + 1], others[-1], *terms)
        others.append(swapped(following))
        terms.append(
            pl.pallas_call(
                functools.partial(collide_kernel, starts + starts),
                in_specs=[local] * 2 + [anywhere] * (2 * parts),
                out_specs=local,
                out_shape=jax.ShapeDtypeStruct((count, local_vel), bf16),
                scratch_shapes=scratch(count) + [sems],
                compiler_params=params(LIMIT),
                cost_estimate=cost(1, 1),
                name="collide",
            )(
                weights,
                table,
                first[batch],
                *[rest[batch]] * (parts - 1),
                first_other[batch],
                *[others[batch]] * (parts - 1),
            )
        )

    pieces = 4
    count = counts[-1]
    starts = (0,) + tuple(g * count for g in range(parts - 1))
    return pl.pallas_call(
        functools.partial(finish_kernel, starts + starts, counts),
        in_specs=[local] * 2 + [anywhere] * (batches + 2 * parts + 2),
        out_specs=anywhere,
        out_shape=jax.ShapeDtypeStruct(distribution.shape, jnp.float32),
        scratch_shapes=scratch(count)
        + [
            pltpu.VMEM((parts, block_rows, group_rows, LANES), jnp.float32),
            pltpu.VMEM((2 * capacity, group // 2), bf16),
            pltpu.VMEM((block_rows * 8, group // 2), jnp.float32),
            pltpu.VMEM((2, width_x, width_y, width_z, group), jnp.float32),
            pltpu.VMEM(spread.shape, bf16),
            pltpu.VMEM((capacity - count, local_vel), bf16),
            sems,
            pltpu.SemaphoreType.DMA((parts,)),
            pltpu.SemaphoreType.DMA((parts, pieces)),
            pltpu.SemaphoreType.DMA((batches,)),
        ],
        compiler_params=params(LIMIT),
        name="finish",
    )(
        weights,
        table,
        spread,
        *terms,
        first[-1],
        *[rest[-1]] * (parts - 1),
        first_other[-1],
        *[others[-1]] * (parts - 1),
        first_read,
        rest_read,
    )


def per_device(distribution, refine_level, gain_one, gain_two, loss_kernel):
    if fast_fits(distribution, gain_one.shape[0]):
        return fast_device(distribution, refine_level, gain_one, gain_two, loss_kernel)
    return plain_device(distribution, refine_level, gain_one, gain_two, loss_kernel)


def solution(mesh):
    placed = (P("cx", "cy", None, "vel"), P("cx", "cy", None), P(), P(), P())
    return jax.shard_map(
        per_device,
        mesh=mesh,
        in_specs=placed,
        out_specs=P("cx", "cy", None, "vel"),
        check_vma=False,
    )
```

```python
import functools
import math

import jax
import jax.numpy as jnp
import ml_dtypes
import numpy as np
from jax import lax
from jax.experimental import pallas as pl
from jax.experimental.pallas import tpu as pltpu
from jax.sharding import PartitionSpec as P


def extended(array, sides, width):
    for axis, dim in sides:
        count, length = (lax.axis_size(axis), array.shape[dim])
        up = [(i, (i + 1) % count) for i in range(count)]
        down = [(j, i) for i, j in up]
        last = lax.slice_in_dim(array, length - width, length, axis=dim)
        leading = lax.slice_in_dim(array, 0, width, axis=dim)
        before = lax.ppermute(last, axis, up)
        after = lax.ppermute(leading, axis, down)
        array = jnp.concatenate([before, array, after], axis=dim)
    return array


def dft_tables(points):
    indices = jnp.arange(points, dtype=jnp.int32)
    products = indices[:, None] * indices[None, :] % points
    angles = products.astype(jnp.float32) * (2.0 * math.pi / points)
    cosine = jnp.cos(angles)
    sine_table = jnp.sin(angles)
    forward = jnp.stack([jnp.stack([cosine, sine_table]), jnp.stack([-sine_table, cosine])])
    inverse = jnp.stack([jnp.stack([cosine, -sine_table]), jnp.stack([sine_table, cosine])])
    return (forward.astype(jnp.bfloat16), inverse.astype(jnp.bfloat16))


def contract(pattern, left_side, right_side):
    return jnp.einsum(pattern, left_side, right_side, preferred_element_type=jnp.float32)


def collide(cells, forward, inverse, gain_one, gain_two, loss_kernel):
    points = forward.shape[-1]
    cell_count = cells.shape[0]
    field = cells.reshape(cell_count, points, points, points)
    section_z = contract("nabz,qzw->qnabw", field, forward[:, 0]).astype(jnp.bfloat16)
    section_y = contract("pnayc,qpyw->qnawc", section_z, forward).astype(jnp.bfloat16)
    spectrum = contract("pnxbc,qpxw->qnwbc", section_y, forward)
    scale_factor = 1.0 / float(points**3)

    def filtered(kernel):
        weighted = (spectrum * (kernel * scale_factor)[None, None]).astype(jnp.bfloat16)
        back_x = contract("pnxbc,qpxw->qnwbc", weighted, inverse).astype(jnp.bfloat16)
        back_y = contract("pnayc,qpyw->qnawc", back_x, inverse).astype(jnp.bfloat16)
        return contract("pnabz,pzw->nabw", back_y, inverse[0])

    gain_term = filtered(gain_one) * filtered(gain_two)
    result = gain_term - field.astype(jnp.float32) * filtered(loss_kernel)
    return result.reshape(cell_count, points**3)


def courants(points, first_vel, local_count):
    vel_index = first_vel + jnp.arange(local_count, dtype=jnp.int32)
    index_x = vel_index // (points * points)
    index_y = vel_index // points % points
    index_z = vel_index % points

    def speed(index_part):
        return 0.3 * (2.0 * index_part.astype(jnp.float32) - (points - 1)) / (points - 1)

    return (speed(index_x), speed(index_y), speed(index_z))


def upwind_flux(courant, center, lower_side, upper_side):
    return jnp.maximum(courant, 0.0) * (center - lower_side) + jnp.minimum(courant, 0.0) * (
        upper_side - center
    )


def plain_device(distribution, refine_level, gain_one, gain_two, loss_kernel):
    points = gain_one.shape[0]
    width_x, width_y, width_z, local_vel = distribution.shape
    first_vel = lax.axis_index("vel") * local_vel
    courant_x, courant_y, courant_z = courants(points, first_vel, local_vel)
    padded = extended(distribution, (("cx", 0), ("cy", 1)), 1)
    fluxes = upwind_flux(courant_x, distribution, padded[:-2, 1:-1], padded[2:, 1:-1])
    fluxes = fluxes + upwind_flux(courant_y, distribution, padded[1:-1, :-2], padded[1:-1, 2:])
    fluxes = fluxes + upwind_flux(
        courant_z, distribution, jnp.roll(distribution, 1, 2), jnp.roll(distribution, -1, 2)
    )
    read = distribution - fluxes
    block_cells = width_x * width_y * width_z
    groups = lax.axis_size("vel")
    flattened = read.reshape(block_cells, local_vel).astype(jnp.bfloat16)
    forward, inverse = dft_tables(points)
    active = refine_level.reshape(block_cells) > 0
    slot_index = jnp.cumsum(active.astype(jnp.int32)) - 1
    capacity = block_cells // 2
    picker = (
        (slot_index[None, :] == jnp.arange(capacity, dtype=jnp.int32)[:, None]) & active[None, :]
    ).astype(jnp.bfloat16)
    chosen = jnp.dot(picker, flattened, preferred_element_type=jnp.float32).astype(jnp.bfloat16)
    terms = collide(
        lax.all_to_all(
            chosen.reshape(groups, capacity // groups, local_vel),
            "vel",
            split_axis=0,
            concat_axis=2,
            tiled=True,
        )[0],
        forward,
        inverse,
        gain_one,
        gain_two,
        loss_kernel,
    )[None]
    packed = lax.all_to_all(
        terms.astype(jnp.bfloat16), "vel", split_axis=2, concat_axis=0, tiled=True
    ).astype(terms.dtype)
    packed_rows = packed.reshape(capacity, local_vel)
    safe_slot = jnp.clip(slot_index, 0, capacity - 1)
    rates = jnp.where(active[:, None], packed_rows[safe_slot], 0.0)
    weight = 0.25 * refine_level.astype(jnp.float32)
    return read + weight[..., None] * rates.reshape(width_x, width_y, width_z, local_vel)

LANES = 128
PLANES = 4
LIMIT = 57


def half_set(points):
    middle = points // 2
    pairs = [(b, c) for c in range(1, middle) for b in range(points)]
    pairs += [(b, c) for c in (0, middle) for b in range(middle + 1)]
    weights = [1.0 if b % middle == 0 and c % middle == 0 else 2.0 for b, c in pairs]
    return np.array(pairs), np.array(weights)


def plane_table(points, padded, margin):
    pairs, _ = half_set(points)
    first, second = np.divmod(np.arange(points * points), points)
    products = (first[:, None] * pairs[None, :, 0] + second[:, None] * pairs[None, :, 1]) % points
    angles = 2.0 * np.pi * products / points
    table = np.zeros((points * points + 2 * margin, 2 * padded), np.float32)
    rows = slice(margin, margin + points * points)
    table[rows, : len(pairs)] = np.cos(angles)
    table[rows, padded : padded + len(pairs)] = -np.sin(angles)
    window = points * points + margin
    back = np.stack([table[margin : margin + window].T, table[:window].T])
    return table.astype(ml_dtypes.bfloat16), back.astype(ml_dtypes.bfloat16)


def frequency_select(points, padded):
    pairs, weights = half_set(points)
    select = np.zeros((points * points, 2 * padded), np.float32)
    column = np.arange(len(pairs))
    select[pairs[:, 0] * points + pairs[:, 1], column] = 1.0
    mirror = (-pairs[:, 0]) % points * points + (-pairs[:, 1]) % points
    select[mirror, padded + column] = 1.0
    scale = np.zeros((1, padded), np.float32)
    scale[0, : len(pairs)] = 0.5 * weights / points**3
    return select.astype(ml_dtypes.bfloat16), scale


def weights_kernel(stacked_ref, select_ref, scale_ref, out_ref):
    kernels, points, padded = out_ref.shape
    rest = stacked_ref[...]
    picked = None
    for _ in range(3):
        piece = rest.astype(jnp.bfloat16)
        rest = rest - piece.astype(jnp.float32)
        part = jnp.dot(piece, select_ref[...], preferred_element_type=jnp.float32)
        picked = part if picked is None else picked + part
    for which in range(kernels):
        for a in range(points):
            row, mirror = which * points + a, which * points + (-a) % points
            both = picked[row : row + 1, :padded] + picked[mirror : mirror + 1, padded:]
            out_ref[which, a : a + 1, :] = both * scale_ref[...]


def transform_3(x, sign, wanted=(0, 1, 2)):
    (ar, ai), (br, bi), (cr, ci) = x
    sr, si = br + cr, bi + ci
    out = {}
    if 0 in wanted:
        out[0] = (ar + sr, ai + si)
    if 1 in wanted or 2 in wanted:
        height = sign * math.sqrt(0.75)
        mr, mi = ar - 0.5 * sr, ai - 0.5 * si
        er, ei = height * (br - cr), height * (bi - ci)
        if 1 in wanted:
            out[1] = (mr - ei, mi + er)
        if 2 in wanted:
            out[2] = (mr + ei, mi - er)
    return out


def transform_4(x, sign):
    (ar, ai), (br, bi), (cr, ci), (dr, di) = x
    pr, pi, qr, qi = ar + cr, ai + ci, ar - cr, ai - ci
    sr, si, tr, ti = br + dr, bi + di, br - dr, bi - di
    if sign < 0:
        tr, ti = -tr, -ti
    return [(pr + sr, pi + si), (qr - ti, qi + tr), (pr - sr, pi - si), (qr + ti, qi - tr)]


def transform_8(x, sign):
    even = transform_4(x[0::2], sign)
    odd = transform_4(x[1::2], sign)
    root = math.sqrt(0.5)
    (r0, i0), (r1, i1), (r2, i2), (r3, i3) = odd
    if sign > 0:
        turned = [(r0, i0), (root * (r1 - i1), root * (i1 + r1)), (-i2, r2)]
        turned.append((-root * (r3 + i3), root * (r3 - i3)))
    else:
        turned = [(r0, i0), (root * (r1 + i1), root * (i1 - r1)), (i2, -r2)]
        turned.append((root * (i3 - r3), -root * (i3 + r3)))
    low = [(e[0] + t[0], e[1] + t[1]) for e, t in zip(even, turned)]
    high = [(e[0] - t[0], e[1] - t[1]) for e, t in zip(even, turned)]
    return low + high


def spectrum_of(load):
    stage = {}
    for n2 in range(8):
        part = transform_3([load((8 * n1 + 3 * n2) % 24) for n1 in range(3)], -1)
        for k1 in range(3):
            stage[k1, n2] = part[k1]
    result = {}
    for k1 in range(3):
        part = transform_8([stage[k1, n2] for n2 in range(8)], -1)
        for k2 in range(8):
            result[(16 * k1 + 9 * k2) % 24] = part[k2]
    return result


def first_half_of(spectrum):
    stage = {}
    for k1 in range(3):
        part = transform_8([spectrum[(16 * k1 + 9 * k2) % 24] for k2 in range(8)], 1)
        for n2 in range(8):
            stage[k1, n2] = part[n2]
    result = {}
    for n2 in range(8):
        wanted = {n1: (8 * n1 + 3 * n2) % 24 for n1 in range(3) if (8 * n1 + 3 * n2) % 24 < 12}
        part = transform_3([stage[k1, n2] for k1 in range(3)], 1, tuple(wanted))
        for n1, index in wanted.items():
            result[index] = part[n1]
    return result


def tile_pair(ref, step, rows):
    parts = []
    for parity in range(2):
        at = (2 * step + parity) * LANES
        part = ref[:, :, :, at : at + LANES]
        parts.append(part.reshape(rows, part.shape[2], LANES))
    return jnp.concatenate(parts, axis=1)


def edges_kernel(first, edge_ref, falls_ref, field_ref, *refs):
    down_ref, up_ref, across_ref, low_ref, high_ref, plane_ref, sems = refs
    steps = falls_ref.shape[0] // 8
    width = low_ref.shape[0]
    groups = across_ref.shape[0] // steps
    half_steps = down_ref.shape[0] // groups
    here = pl.ds(first, low_ref.shape[3])
    last_y = field_ref.shape[1] - 1
    sources = [
        field_ref.at[:, pl.ds(0, 1), :, here],
        field_ref.at[:, pl.ds(last_y, 1), :, here],
        field_ref.at[pl.ds(edge_ref[0], 1), :, :, here],
    ]
    loads = [
        pltpu.make_async_copy(source, ref, sems.at[at])
        for at, (source, ref) in enumerate(zip(sources, (low_ref, high_ref, plane_ref)))
    ]
    for load in loads:
        load.start()
    below = [falls_ref[8 * s : 8 * s + 8, :][None] > 0.0 for s in range(steps)]

    def put(ref, at, value):
        ref[at] = value.reshape(-1, LANES).astype(jnp.bfloat16)

    loads[0].wait()
    for g in range(groups):
        row = [tile_pair(low_ref, g * steps + s, width) for s in range(steps)]
        put(down_ref, g * half_steps, row[0])
        for m in range(1, steps // 2 + 1):
            put(down_ref, g * half_steps + m, jnp.where(below[2 * m - 1], row[2 * m - 1], row[2 * m]))
    loads[1].wait()
    for g in range(groups):
        row = [tile_pair(high_ref, g * steps + s, width) for s in range(steps)]
        for m in range(steps // 2):
            put(up_ref, g * half_steps + m, jnp.where(below[2 * m], row[2 * m + 1], row[2 * m]))
        put(up_ref, g * half_steps + steps // 2, row[steps - 1])
    loads[2].wait()
    for s in range(groups * steps):
        put(across_ref, s, tile_pair(plane_ref, s, plane_ref.shape[1]))


def upwind_kernel(base, counts, side_ref, *refs):
    batches = len(counts)
    outer_refs, field_ref = refs[:5], refs[5]
    out_ref, target_refs, scratch = refs[6], refs[7 : 7 + batches], refs[7 + batches :]
    inner_refs, chosen_refs, scratch = scratch[:5], scratch[5 : 5 + batches], scratch[5 + batches :]
    speed_ref, picker_ref, down_ref, up_ref, across_ref = inner_refs
    blocks, reads, wide, border, cells, load_sems, store_sems, side_sems = scratch
    chunks, width_x, width_y, width_z, lanes = blocks.shape
    steps = lanes // (2 * LANES)
    group_lanes = chosen_refs[0].shape[1]
    per_group = group_lanes // lanes
    half_steps = per_group * steps // 2 + 1
    inputs = [
        pltpu.make_async_copy(source, target, side_sems.at[at])
        for at, (source, target) in enumerate(zip(outer_refs, inner_refs))
    ]
    for copy in inputs:
        copy.start()
    loads = []
    for t in range(chunks):
        source = field_ref.at[:, :, :, pl.ds(base + t * lanes, lanes)]
        loads.append(pltpu.make_async_copy(source, blocks.at[t], load_sems.at[t]))
        loads[-1].start()
    beside = jnp.where(side_ref[0] == 0, 2, 0)
    place = lax.broadcasted_iota(jnp.int32, (1, 8, LANES), 1) % width_z
    capacity = picker_ref.shape[0] // 2
    stores = []
    for copy in inputs:
        copy.wait()
    for t in range(chunks):
        group, chunk = t // per_group, t % per_group
        sizes, falls, sinks = [], [], []
        for u in range(steps):
            step = chunk * steps + u
            row = 8 * (t * steps + u)
            speed = [speed_ref[d, row : row + 8, :][None] for d in range(3)]
            sizes.append([jnp.abs(c) for c in speed])
            falls.append(speed[1] < 0.0)
            sinks.append(speed[2] < 0.0)
            outer = across_ref[t * steps + u].astype(jnp.float32).reshape(width_y, 8, LANES)
            wide[u, 0] = outer
            wide[u, width_x + 1] = outer
            above = down_ref[group * half_steps + (step + 1) // 2].astype(jnp.float32)
            under = up_ref[group * half_steps + step // 2].astype(jnp.float32)
            shape = (width_x, 8, LANES)
            border[u] = jnp.where(falls[u], above.reshape(shape), under.reshape(shape))
        loads[t].wait()

        def spread_out(x, carry):
            for u in range(steps):
                at = 2 * u * LANES
                parts = [
                    blocks[t, x, :, :, at + p * LANES : at + (p + 1) * LANES] for p in range(2)
                ]
                wide[u, x + 1] = jnp.concatenate(parts, axis=1)
            return carry

        lax.fori_loop(0, width_x, spread_out, 0, unroll=4)

        def advance(x, carry):
            for u in range(steps):
                field = wide[u, x + 1]
                edge = border[u, pl.ds(x, 1)]
                fluxes = sizes[u][0] * (field - wide[u, x + beside])
                beside_y = jnp.where(
                    falls[u],
                    jnp.concatenate([field[1:], edge], axis=0),
                    jnp.concatenate([edge, field[:-1]], axis=0),
                )
                fluxes = fluxes + sizes[u][1] * (field - beside_y)
                upper = jnp.where(
                    place == width_z - 1, pltpu.roll(field, 3, 1), pltpu.roll(field, 7, 1)
                )
                lower = jnp.where(place == 0, pltpu.roll(field, 5, 1), pltpu.roll(field, 1, 1))
                fluxes = fluxes + sizes[u][2] * (field - jnp.where(sinks[u], upper, lower))
                read = field - fluxes
                reads[t, pl.ds(x * width_y, width_y), 8 * u : 8 * u + 8, :] = read
                rows = width_y * 8
                at = pl.multiple_of(x * rows, rows)
                cells[pl.ds(at, rows), u * LANES : (u + 1) * LANES] = read.reshape(
                    rows, LANES
                ).astype(jnp.bfloat16)
            return carry

        lax.fori_loop(0, width_x, advance, 0, unroll=2)
        target = out_ref.at[:, pl.ds(8 * steps * t, 8 * steps), :]
        stores.append(pltpu.make_async_copy(reads.at[t], target, store_sems.at[t]))
        stores[-1].start()
        picked = jnp.dot(
            picker_ref[...], cells[...], preferred_element_type=jnp.float32
        ).astype(jnp.bfloat16)
        for parity in range(2):
            first = parity * capacity
            for ref, count in zip(chosen_refs, counts):
                rows = slice(group * count, (group + 1) * count)
                for u in range(steps):
                    tile = 2 * (chunk * steps + u) + parity
                    here = slice(tile * LANES, (tile + 1) * LANES)
                    ref[rows, here] = picked[first : first + count, u * LANES : (u + 1) * LANES]
                first += count
    for at, (source, target) in enumerate(zip(chosen_refs, target_refs)):
        stores.append(pltpu.make_async_copy(source, target, store_sems.at[chunks + at]))
        stores[-1].start()
    for store in stores:
        store.wait()


def window_loads(firsts, refs, cells, sems):
    loads = []
    for at, (ref, first) in enumerate(zip(refs, firsts)):
        source = ref.at[pl.ds(first, cells.shape[1])]
        loads.append(pltpu.make_async_copy(source, cells.at[at], sems.at[at]))
        loads[-1].start()
    return loads


def filter_parts(weight_ref, table_ref, cells, loads, section, back):
    count, slots, lanes = cells.shape
    padded = weight_ref.shape[2]
    height = table_ref.shape[0]
    window = height - 64
    pair_lanes = 2 * (height - 128)
    pairs = lanes // pair_lanes
    half = pairs * count
    for side in range(2):
        here = range(side * count // 2, (side + 1) * count // 2)
        for at in here:
            loads[at].wait()
        for parity in range(2):
            rows = []
            for at in here:
                for p in range(pairs):
                    lane = p * pair_lanes + parity * (pair_lanes - window)
                    rows.append(cells[at, :, lane : lane + window])
            start = 64 * (1 - parity)
            out = jnp.dot(
                jnp.concatenate(rows, axis=0),
                table_ref[start : start + window, :],
                preferred_element_type=jnp.float32,
            )
            for at in range(half // 2):
                section[side * half + 2 * at + parity] = out[at * slots : (at + 1) * slots]

    lane_tiles = padded // LANES

    def transform(index, carry):
        row = pl.multiple_of(index // lane_tiles * 16, 16)
        lane = pl.multiple_of(index % lane_tiles * LANES, LANES)
        results = []
        for octet in range(2):
            here = pl.ds(row + 8 * octet, 8)

            def load(i):
                real = section[i, here, pl.ds(lane, LANES)]
                return real, section[i, here, pl.ds(padded + lane, LANES)]

            spectrum = spectrum_of(load)
            per_kernel = []
            for which in range(3):
                weighted = {}
                for a, (real, imag) in spectrum.items():
                    weight = weight_ref[which, pl.ds(a, 1), pl.ds(lane, LANES)]
                    weighted[a] = (real * weight, imag * weight)
                per_kernel.append(first_half_of(weighted))
            results.append(per_kernel)
        for which in range(3):
            for i in range(half):
                for q in range(2):
                    value = jnp.concatenate([results[o][which][i][q] for o in range(2)], axis=0)
                    back[i % 2, which, i // 2, pl.ds(row, 16), pl.ds(q * padded + lane, LANES)] = (
                        value.astype(jnp.bfloat16)
                    )
        return carry

    lax.fori_loop(0, slots // 16 * lane_tiles, transform, 0)


def inverse_parts(back_table, back):
    _, kernels, pairs, slots, depth = back.shape
    window = back_table.shape[2]
    return [
        jnp.dot(
            back[parity].reshape(kernels * pairs * slots, depth),
            back_table[parity],
            preferred_element_type=jnp.float32,
        ).reshape(kernels, pairs, slots, window)
        for parity in range(2)
    ]


def terms_of(part, outs, cells_ref, put):
    _, slots, lanes = cells_ref.shape
    window = outs[0].shape[3]
    pair_lanes = 2 * (window - 64)
    pairs = lanes // pair_lanes
    tiles = pair_lanes // LANES
    near = lax.broadcasted_iota(jnp.int32, (slots, LANES), 1) < 64
    for pair in range(pairs):
        at = part * pairs + pair
        for tile in range(tiles):
            lane = tile * LANES
            odd_lane = lane - (pair_lanes - window)
            values = []
            for which in range(3):
                if tile < tiles // 2:
                    value = outs[0][which, at, :, lane : lane + LANES]
                elif tile > tiles // 2:
                    value = outs[1][which, at, :, odd_lane : odd_lane + LANES]
                else:
                    value = jnp.where(
                        near,
                        outs[0][which, at, :, lane : lane + LANES],
                        outs[1][which, at, :, odd_lane : odd_lane + LANES],
                    )
                values.append(value)
            lane = pair * pair_lanes + lane
            cells = cells_ref[part, :, lane : lane + LANES].astype(jnp.float32)
            put(pair * tiles + tile, (values[0] * values[1] - cells * values[2]).astype(jnp.bfloat16))


def collide_kernel(firsts, weight_ref, table_ref, back_any, *refs):
    parts = len(firsts) // 2
    terms_ref, cells, section, back, back_table, sems = refs[2 * parts :]
    lanes = cells.shape[2]
    loads = window_loads(firsts, refs[: 2 * parts], cells, sems)
    table_load = pltpu.make_async_copy(back_any, back_table, sems.at[2 * parts])
    table_load.start()
    filter_parts(weight_ref, table_ref, cells, loads, section, back)
    table_load.wait()
    outs = inverse_parts(back_table, back)
    for part in range(parts):

        def put(tile, value):
            first = part * lanes + tile * LANES
            terms_ref[:, first : first + LANES] = value

        terms_of(part, outs, cells, put)


def finish_kernel(firsts, sizes, weight_ref, table_ref, back_any, spread_any, *refs):
    parts = len(firsts) // 2
    term_refs, refs = refs[: len(sizes) - 1], refs[len(sizes) - 1 :]
    first_read, rest_read = refs[2 * parts : 2 * parts + 2]
    out_ref, cells, section, back, back_table, reads, spots, added, staged = refs[2 * parts + 2 : -6]
    spread_ref, early_ref, cell_sems, read_sems, out_sems, extra_sems = refs[-6:]
    width_x, width_y, width_z, lanes = staged.shape[1:]
    tiles = lanes // LANES
    loads = window_loads(firsts, refs[: 2 * parts], cells, cell_sems)
    extra = [pltpu.make_async_copy(spread_any, spread_ref, extra_sems.at[0])]
    at = 0
    for ref, size in zip(term_refs, sizes):
        target = early_ref.at[pl.ds(at, size)]
        extra.append(pltpu.make_async_copy(ref, target, extra_sems.at[len(extra)]))
        at += size
    extra.append(pltpu.make_async_copy(back_any, back_table, cell_sems.at[2 * parts]))
    group_rows = reads.shape[2]
    read_loads = []
    for part in range(parts):
        rows = pl.ds(max(part - 1, 0) * group_rows, group_rows)
        source = (rest_read if part else first_read).at[:, rows, :]
        read_loads.append(pltpu.make_async_copy(source, reads.at[part], read_sems.at[part]))
    for load in extra + read_loads:
        load.start()
    filter_parts(weight_ref, table_ref, cells, loads, section, back)
    for load in extra:
        load.wait()
    early = early_ref.shape[0]
    capacity = early + section.shape[1]
    outs = inverse_parts(back_table, back)
    pieces = out_sems.shape[1]
    piece_x = width_x // pieces
    stores = []
    for part in range(parts):

        def put(tile, value):
            first = tile % 2 * capacity
            columns = slice(tile // 2 * LANES, (tile // 2 + 1) * LANES)
            lane = part * lanes + tile * LANES
            spots[first : first + early, columns] = early_ref[:, lane : lane + LANES]
            spots[first + early : first + capacity, columns] = value

        terms_of(part, outs, cells, put)
        added[...] = jnp.dot(spread_ref[...], spots[...], preferred_element_type=jnp.float32)
        read_loads[part].wait()
        slot = part % 2
        if part >= 2:
            for store in stores[part - 2]:
                store.wait()

        def add(x, carry):
            for y in range(width_y):
                row = x * width_y + y
                at = pl.multiple_of(row * 8, 8)
                for u in range(tiles // 2):
                    value = (
                        reads[part, row, 8 * u : 8 * u + 8, :]
                        + added[pl.ds(at, 8), u * LANES : (u + 1) * LANES]
                    )
                    for parity in range(2):
                        lane = (2 * u + parity) * LANES
                        half = value[parity * width_z : (parity + 1) * width_z]
                        staged[slot, x, y, :, lane : lane + LANES] = half
            return carry

        stores.append([])
        for piece in range(pieces):
            lax.fori_loop(piece * piece_x, (piece + 1) * piece_x, add, 0)
            rows = pl.ds(piece * piece_x, piece_x)
            store = pltpu.make_async_copy(
                staged.at[slot, rows],
                out_ref.at[rows, :, :, pl.ds(part * lanes, lanes)],
                out_sems.at[part, piece],
            )
            store.start()
            stores[part].append(store)
    for part in range(max(parts - 2, 0), parts):
        for store in stores[part]:
            store.wait()


def params(mib):
    return pltpu.CompilerParams(vmem_limit_bytes=mib * 2**20)


def cost(flops, size):
    return pl.CostEstimate(flops=flops, bytes_accessed=size, transcendentals=0)


def fast_fits(distribution, points):
    width_x, width_y, width_z, local_vel = distribution.shape
    group = PLANES * points * points
    return (
        points == 24
        and lax.axis_size("vel") == 2
        and width_z == 4
        and local_vel * 2 == points**3
        and local_vel == 3 * group
        and width_x * width_y * width_z % 128 == 0
    )


def fast_device(distribution, refine_level, gain_one, gain_two, loss_kernel):
    points = gain_one.shape[0]
    width_x, width_y, width_z, local_vel = distribution.shape
    block_rows = width_x * width_y
    block_cells = block_rows * width_z
    group = PLANES * points * points
    parts = local_vel // group
    group_rows = group // LANES * width_z
    steps = group_rows // 8
    capacity = block_cells // 2
    third = capacity * 3 // 8 // 16 * 16
    counts = (third, third, capacity - 2 * third)
    batches = len(counts)
    vel_at = lax.axis_index("vel")
    count_x, count_y = lax.axis_size("cx"), lax.axis_size("cy")

    tiles = local_vel // LANES
    speeds = jnp.stack(courants(points, vel_at * local_vel, local_vel))
    speeds = jnp.broadcast_to(
        speeds.reshape(3, tiles, 1, LANES), (3, tiles, width_z, LANES)
    ).reshape(3, parts, tiles * width_z // parts, LANES)
    speeds = [speeds[:, 0], speeds[:, 1:].reshape(3, -1, LANES)]
    falls = np.arange(group) // points % points < points // 2
    falls = np.repeat(falls.reshape(-1, 1, LANES), width_z, axis=1).reshape(-1, LANES)
    falls = jnp.asarray(falls.astype(np.float32))
    side = vel_at.reshape(1).astype(jnp.int32)
    edge = jnp.where(vel_at == 0, 0, width_x - 1).reshape(1).astype(jnp.int32)

    level = refine_level.reshape(block_cells)
    active = level > 0
    cell_at = jnp.arange(block_cells, dtype=jnp.int32)
    before = (cell_at[:, None] < cell_at[None, :]) & active[:, None]
    slot_index = jnp.where(active, jnp.sum(before.astype(jnp.int32), axis=0), -1)
    spot = slot_index.reshape(block_rows, 1, width_z)
    parity = jnp.arange(2, dtype=jnp.int32)[None, :, None]
    shape = (block_rows, 2, width_z)
    wanted = jnp.where(spot >= 0, spot + capacity * parity, -1)
    wanted = jnp.broadcast_to(wanted, shape).reshape(-1)
    numbers = jnp.arange(2 * capacity, dtype=jnp.int32)
    picker = (numbers[:, None] == wanted[None, :]).astype(jnp.bfloat16)
    strength = jnp.broadcast_to(
        (0.25 * level.astype(jnp.float32)).reshape(block_rows, 1, width_z), shape
    ).reshape(-1)
    spread = jnp.where(wanted[:, None] == numbers[None, :], strength[:, None], 0.0)
    spread = spread.astype(jnp.bfloat16)

    padded = -(-len(half_set(points)[1]) // LANES) * LANES
    select, scale = frequency_select(points, padded)
    table, back_table = [jnp.asarray(t) for t in plane_table(points, padded, 64)]

    towards_lower = [(j, (j - 1) % count_y) for j in range(count_y)]
    towards_upper = [(j, (j + 1) % count_y) for j in range(count_y)]
    across_pairs = [(i, (i - 1) % count_x) for i in range(count_x)]
    across_pairs += [(count_x + i, count_x + (i + 1) % count_x) for i in range(count_x)]
    swap = [(0, 1), (1, 0)]
    bf16 = jnp.bfloat16

    half_steps = steps // 2 + 1
    local = pl.BlockSpec(memory_space=pltpu.VMEM)
    scalar = pl.BlockSpec(memory_space=pltpu.SMEM)
    remote = pl.BlockSpec(memory_space=pltpu.HBM)
    anywhere = pl.BlockSpec(memory_space=pl.ANY)

    def edges_of(first, groups):
        return pl.pallas_call(
            functools.partial(edges_kernel, first * group),
            in_specs=[scalar, local, remote],
            out_specs=[local] * 3,
            out_shape=[
                jax.ShapeDtypeStruct((groups * half_steps, width_x * 8, LANES), bf16),
                jax.ShapeDtypeStruct((groups * half_steps, width_x * 8, LANES), bf16),
                jax.ShapeDtypeStruct((groups * steps, width_y * 8, LANES), bf16),
            ],
            scratch_shapes=[
                pltpu.VMEM((width_x, 1, width_z, groups * group), jnp.float32),
                pltpu.VMEM((width_x, 1, width_z, groups * group), jnp.float32),
                pltpu.VMEM((1, width_y, width_z, groups * group), jnp.float32),
                pltpu.SemaphoreType.DMA((3,)),
            ],
            compiler_params=params(LIMIT),
            cost_estimate=cost(1, 1),
            name="edges",
        )(edge, falls, distribution)

    edges = [edges_of(0, 1), edges_of(1, parts - 1)]
    wide = 3
    chunks = steps // wide

    def upwind(at, halo, sizes):
        groups = parts - 1 if at else 1
        operands = (speeds[at], picker, *halo)
        chosen = [(groups * size, group) for size in sizes]
        return pl.pallas_call(
            functools.partial(upwind_kernel, at * group, sizes),
            in_specs=[scalar] + [anywhere] * (len(operands) + 1),
            out_specs=[anywhere] * (1 + len(sizes)),
            out_shape=[
                jax.ShapeDtypeStruct((block_rows, groups * group_rows, LANES), jnp.float32)
            ]
            + [jax.ShapeDtypeStruct(shape, bf16) for shape in chosen],
            scratch_shapes=[pltpu.VMEM(x.shape, x.dtype) for x in operands]
            + [pltpu.VMEM(shape, bf16) for shape in chosen]
            + [
                pltpu.VMEM(
                    (groups * chunks, width_x, width_y, width_z, group // chunks), jnp.float32
                ),
                pltpu.VMEM((groups * chunks, block_rows, 8 * wide, LANES), jnp.float32),
                pltpu.VMEM((wide, width_x + 2, width_y, 8, LANES), jnp.float32),
                pltpu.VMEM((wide, width_x, 8, LANES), jnp.float32),
                pltpu.VMEM((block_rows * 8, wide * LANES), bf16),
                pltpu.SemaphoreType.DMA((groups * chunks,)),
                pltpu.SemaphoreType.DMA((groups * chunks + len(sizes),)),
                pltpu.SemaphoreType.DMA((len(operands),)),
            ],
            compiler_params=params(LIMIT),
            cost_estimate=cost(1, 1),
            name="upwind",
        )(side, *operands, distribution)

    def turn(value, *earlier):
        return lax.optimization_barrier((value, *earlier))[0]

    def swapped(value):
        return lax.ppermute(value, "vel", swap)

    halos = []
    for at in range(2):
        down, up, across = edges[at]
        halos.append(
            (
                lax.ppermute(down, "cy", towards_lower),
                lax.ppermute(up, "cy", towards_upper),
                lax.ppermute(across, ("vel", "cx"), across_pairs),
            )
        )
    first_read, *first = upwind(0, turn(halos[0], edges[1]), counts)
    first_other = [swapped(x) for x in first]
    rest_read, *rest = upwind(1, turn(halos[1], first), counts)
    kernels = turn((gain_one, gain_two, loss_kernel), halos[0])
    weights = pl.pallas_call(
        weights_kernel,
        out_shape=jax.ShapeDtypeStruct((3, points, padded), jnp.float32),
        compiler_params=params(LIMIT),
        cost_estimate=cost(1, 1),
        name="weights",
    )(
        jnp.concatenate([k.reshape(points, points * points) for k in kernels], axis=0),
        jnp.asarray(select),
        jnp.asarray(scale),
    )

    operand, weights, spread = turn((rest[0], weights, spread), first_other)
    others = [swapped(operand)]

    def scratch(count):
        return [
            pltpu.VMEM((2 * parts, count, group), bf16),
            pltpu.VMEM((points, count, 2 * padded), jnp.float32),
            pltpu.VMEM((2, 3, points // 4, count, 2 * padded), bf16),
            pltpu.VMEM(back_table.shape, bf16),
        ]

    sems = pltpu.SemaphoreType.DMA((2 * parts + 1,))
    terms = []
    for batch in range(batches - 1):
        count = counts[batch]
        starts = (0,) + tuple(g * count for g in range(parts - 1))
        following = turn(rest[batch + 1], others[-1], *terms)
        others.append(swapped(following))
        terms.append(
            pl.pallas_call(
                functools.partial(collide_kernel, starts + starts),
                in_specs=[local] * 2 + [anywhere] * (1 + 2 * parts),
                out_specs=local,
                out_shape=jax.ShapeDtypeStruct((count, local_vel), bf16),
                scratch_shapes=scratch(count) + [sems],
                compiler_params=params(LIMIT),
                cost_estimate=cost(1, 1),
                name="collide",
            )(
                weights,
                table,
                back_table,
                first[batch],
                *[rest[batch]] * (parts - 1),
                first_other[batch],
                *[others[batch]] * (parts - 1),
            )
        )

    pieces = 4
    count = counts[-1]
    starts = (0,) + tuple(g * count for g in range(parts - 1))
    return pl.pallas_call(
        functools.partial(finish_kernel, starts + starts, counts),
        in_specs=[local] * 2 + [anywhere] * (1 + batches + 2 * parts + 2),
        out_specs=anywhere,
        out_shape=jax.ShapeDtypeStruct(distribution.shape, jnp.float32),
        scratch_shapes=scratch(count)
        + [
            pltpu.VMEM((parts, block_rows, group_rows, LANES), jnp.float32),
            pltpu.VMEM((2 * capacity, group // 2), bf16),
            pltpu.VMEM((block_rows * 8, group // 2), jnp.float32),
            pltpu.VMEM((2, width_x, width_y, width_z, group), jnp.float32),
            pltpu.VMEM(spread.shape, bf16),
            pltpu.VMEM((capacity - count, local_vel), bf16),
            sems,
            pltpu.SemaphoreType.DMA((parts,)),
            pltpu.SemaphoreType.DMA((parts, pieces)),
            pltpu.SemaphoreType.DMA((batches,)),
        ],
        compiler_params=params(LIMIT),
        name="finish",
    )(
        weights,
        table,
        back_table,
        spread,
        *terms,
        first[-1],
        *[rest[-1]] * (parts - 1),
        first_other[-1],
        *[others[-1]] * (parts - 1),
        first_read,
        rest_read,
    )


def per_device(distribution, refine_level, gain_one, gain_two, loss_kernel):
    if fast_fits(distribution, gain_one.shape[0]):
        return fast_device(distribution, refine_level, gain_one, gain_two, loss_kernel)
    return plain_device(distribution, refine_level, gain_one, gain_two, loss_kernel)


def solution(mesh):
    placed = (P("cx", "cy", None, "vel"), P("cx", "cy", None), P(), P(), P())
    return jax.shard_map(
        per_device,
        mesh=mesh,
        in_specs=placed,
        out_specs=P("cx", "cy", None, "vel"),
        check_vma=False,
    )
```

```python
import functools
import math

import jax
import jax.numpy as jnp
import ml_dtypes
import numpy as np
from jax import lax
from jax.experimental import pallas as pl
from jax.experimental.pallas import tpu as pltpu
from jax.sharding import PartitionSpec as P


def extended(array, sides, width):
    for axis, dim in sides:
        count, length = (lax.axis_size(axis), array.shape[dim])
        up = [(i, (i + 1) % count) for i in range(count)]
        down = [(j, i) for i, j in up]
        last = lax.slice_in_dim(array, length - width, length, axis=dim)
        leading = lax.slice_in_dim(array, 0, width, axis=dim)
        before = lax.ppermute(last, axis, up)
        after = lax.ppermute(leading, axis, down)
        array = jnp.concatenate([before, array, after], axis=dim)
    return array


def dft_tables(points):
    indices = jnp.arange(points, dtype=jnp.int32)
    products = indices[:, None] * indices[None, :] % points
    angles = products.astype(jnp.float32) * (2.0 * math.pi / points)
    cosine = jnp.cos(angles)
    sine_table = jnp.sin(angles)
    forward = jnp.stack([jnp.stack([cosine, sine_table]), jnp.stack([-sine_table, cosine])])
    inverse = jnp.stack([jnp.stack([cosine, -sine_table]), jnp.stack([sine_table, cosine])])
    return (forward.astype(jnp.bfloat16), inverse.astype(jnp.bfloat16))


def contract(pattern, left_side, right_side):
    return jnp.einsum(pattern, left_side, right_side, preferred_element_type=jnp.float32)


def collide(cells, forward, inverse, gain_one, gain_two, loss_kernel):
    points = forward.shape[-1]
    cell_count = cells.shape[0]
    field = cells.reshape(cell_count, points, points, points)
    section_z = contract("nabz,qzw->qnabw", field, forward[:, 0]).astype(jnp.bfloat16)
    section_y = contract("pnayc,qpyw->qnawc", section_z, forward).astype(jnp.bfloat16)
    spectrum = contract("pnxbc,qpxw->qnwbc", section_y, forward)
    scale_factor = 1.0 / float(points**3)

    def filtered(kernel):
        weighted = (spectrum * (kernel * scale_factor)[None, None]).astype(jnp.bfloat16)
        back_x = contract("pnxbc,qpxw->qnwbc", weighted, inverse).astype(jnp.bfloat16)
        back_y = contract("pnayc,qpyw->qnawc", back_x, inverse).astype(jnp.bfloat16)
        return contract("pnabz,pzw->nabw", back_y, inverse[0])

    gain_term = filtered(gain_one) * filtered(gain_two)
    result = gain_term - field.astype(jnp.float32) * filtered(loss_kernel)
    return result.reshape(cell_count, points**3)


def courants(points, first_vel, local_count):
    vel_index = first_vel + jnp.arange(local_count, dtype=jnp.int32)
    index_x = vel_index // (points * points)
    index_y = vel_index // points % points
    index_z = vel_index % points

    def speed(index_part):
        return 0.3 * (2.0 * index_part.astype(jnp.float32) - (points - 1)) / (points - 1)

    return (speed(index_x), speed(index_y), speed(index_z))


def upwind_flux(courant, center, lower_side, upper_side):
    return jnp.maximum(courant, 0.0) * (center - lower_side) + jnp.minimum(courant, 0.0) * (
        upper_side - center
    )


def plain_device(distribution, refine_level, gain_one, gain_two, loss_kernel):
    points = gain_one.shape[0]
    width_x, width_y, width_z, local_vel = distribution.shape
    first_vel = lax.axis_index("vel") * local_vel
    courant_x, courant_y, courant_z = courants(points, first_vel, local_vel)
    padded = extended(distribution, (("cx", 0), ("cy", 1)), 1)
    fluxes = upwind_flux(courant_x, distribution, padded[:-2, 1:-1], padded[2:, 1:-1])
    fluxes = fluxes + upwind_flux(courant_y, distribution, padded[1:-1, :-2], padded[1:-1, 2:])
    fluxes = fluxes + upwind_flux(
        courant_z, distribution, jnp.roll(distribution, 1, 2), jnp.roll(distribution, -1, 2)
    )
    read = distribution - fluxes
    block_cells = width_x * width_y * width_z
    groups = lax.axis_size("vel")
    flattened = read.reshape(block_cells, local_vel).astype(jnp.bfloat16)
    forward, inverse = dft_tables(points)
    active = refine_level.reshape(block_cells) > 0
    slot_index = jnp.cumsum(active.astype(jnp.int32)) - 1
    capacity = block_cells // 2
    picker = (
        (slot_index[None, :] == jnp.arange(capacity, dtype=jnp.int32)[:, None]) & active[None, :]
    ).astype(jnp.bfloat16)
    chosen = jnp.dot(picker, flattened, preferred_element_type=jnp.float32).astype(jnp.bfloat16)
    terms = collide(
        lax.all_to_all(
            chosen.reshape(groups, capacity // groups, local_vel),
            "vel",
            split_axis=0,
            concat_axis=2,
            tiled=True,
        )[0],
        forward,
        inverse,
        gain_one,
        gain_two,
        loss_kernel,
    )[None]
    packed = lax.all_to_all(
        terms.astype(jnp.bfloat16), "vel", split_axis=2, concat_axis=0, tiled=True
    ).astype(terms.dtype)
    packed_rows = packed.reshape(capacity, local_vel)
    safe_slot = jnp.clip(slot_index, 0, capacity - 1)
    rates = jnp.where(active[:, None], packed_rows[safe_slot], 0.0)
    weight = 0.25 * refine_level.astype(jnp.float32)
    return read + weight[..., None] * rates.reshape(width_x, width_y, width_z, local_vel)

LANES = 128
PLANES = 4
LIMIT = 57


def half_set(points):
    middle = points // 2
    pairs = [(b, c) for c in range(1, middle) for b in range(points)]
    pairs += [(b, c) for c in (0, middle) for b in range(middle + 1)]
    weights = [1.0 if b % middle == 0 and c % middle == 0 else 2.0 for b, c in pairs]
    return np.array(pairs), np.array(weights)


def plane_table(points, padded, margin):
    pairs, _ = half_set(points)
    first, second = np.divmod(np.arange(points * points), points)
    index = np.arange(points)
    angles = (index[:, None] * index[None, :] % points).astype(np.float32)
    angles = angles * np.float32(2.0 * np.pi / points)
    cosine, sine = [
        t.astype(ml_dtypes.bfloat16).astype(np.float32) for t in (np.cos(angles), np.sin(angles))
    ]
    cos_y, sin_y = cosine[first][:, pairs[:, 0]], sine[first][:, pairs[:, 0]]
    cos_z, sin_z = cosine[second][:, pairs[:, 1]], sine[second][:, pairs[:, 1]]
    table = np.zeros((points * points + 2 * margin, 2 * padded), np.float32)
    rows = slice(margin, margin + points * points)
    table[rows, : len(pairs)] = cos_y * cos_z - sin_y * sin_z
    table[rows, padded : padded + len(pairs)] = -(cos_y * sin_z + sin_y * cos_z)
    window = points * points + margin
    level = np.flatnonzero(pairs[:, 1] == 0)
    rest = table.copy()
    rest[:, np.concatenate([level, padded + level])] = 0.0
    for start in (points * points + margin, 0):
        rest[start : start + points, level] = cosine[:, pairs[level, 0]]
        rest[start : start + points, padded + level] = -sine[:, pairs[level, 0]]
    back = np.stack([rest[margin : margin + window].T, rest[:window].T])
    copies = np.zeros((2, LANES, window), np.float32)
    place = np.arange(points * points)
    copies[0, (points * points + first) % LANES, place] = 1.0
    copies[1, first, margin + place] = 1.0
    back = np.concatenate([back, copies], axis=1)
    spare = len(pairs)
    lift = np.zeros((LANES, 2 * padded), np.float32)
    for half in (0, padded):
        columns = slice(spare % LANES, spare % LANES + points)
        lift[columns, half + level] = table[margin : margin + points**2 : points, half + level]
        table[:, half + level] = 0.0
    table[margin + place, spare + first] = 1.0
    table = np.concatenate([table, lift])
    return table.astype(ml_dtypes.bfloat16), back.astype(ml_dtypes.bfloat16)


def frequency_select(points, padded):
    pairs, weights = half_set(points)
    select = np.zeros((points * points, 2 * padded), np.float32)
    column = np.arange(len(pairs))
    select[pairs[:, 0] * points + pairs[:, 1], column] = 1.0
    mirror = (-pairs[:, 0]) % points * points + (-pairs[:, 1]) % points
    select[mirror, padded + column] = 1.0
    scale = np.zeros((1, padded), np.float32)
    scale[0, : len(pairs)] = 0.5 * weights / points**3
    return select.astype(ml_dtypes.bfloat16), scale


def weights_kernel(stacked_ref, select_ref, scale_ref, out_ref):
    kernels, points, padded = out_ref.shape
    rest = stacked_ref[...]
    picked = None
    for _ in range(3):
        piece = rest.astype(jnp.bfloat16)
        rest = rest - piece.astype(jnp.float32)
        part = jnp.dot(piece, select_ref[...], preferred_element_type=jnp.float32)
        picked = part if picked is None else picked + part
    for which in range(kernels):
        for a in range(points):
            row, mirror = which * points + a, which * points + (-a) % points
            both = picked[row : row + 1, :padded] + picked[mirror : mirror + 1, padded:]
            out_ref[which, a : a + 1, :] = both * scale_ref[...]


def transform_3(x, sign, wanted=(0, 1, 2)):
    (ar, ai), (br, bi), (cr, ci) = x
    sr, si = br + cr, bi + ci
    out = {}
    if 0 in wanted:
        out[0] = (ar + sr, ai + si)
    if 1 in wanted or 2 in wanted:
        height = sign * math.sqrt(0.75)
        mr, mi = ar - 0.5 * sr, ai - 0.5 * si
        er, ei = height * (br - cr), height * (bi - ci)
        if 1 in wanted:
            out[1] = (mr - ei, mi + er)
        if 2 in wanted:
            out[2] = (mr + ei, mi - er)
    return out


def transform_4(x, sign):
    (ar, ai), (br, bi), (cr, ci), (dr, di) = x
    pr, pi, qr, qi = ar + cr, ai + ci, ar - cr, ai - ci
    sr, si, tr, ti = br + dr, bi + di, br - dr, bi - di
    if sign < 0:
        tr, ti = -tr, -ti
    return [(pr + sr, pi + si), (qr - ti, qi + tr), (pr - sr, pi - si), (qr + ti, qi - tr)]


def transform_8(x, sign):
    even = transform_4(x[0::2], sign)
    odd = transform_4(x[1::2], sign)
    root = math.sqrt(0.5)
    (r0, i0), (r1, i1), (r2, i2), (r3, i3) = odd
    if sign > 0:
        turned = [(r0, i0), (root * (r1 - i1), root * (i1 + r1)), (-i2, r2)]
        turned.append((-root * (r3 + i3), root * (r3 - i3)))
    else:
        turned = [(r0, i0), (root * (r1 + i1), root * (i1 - r1)), (i2, -r2)]
        turned.append((root * (i3 - r3), -root * (i3 + r3)))
    low = [(e[0] + t[0], e[1] + t[1]) for e, t in zip(even, turned)]
    high = [(e[0] - t[0], e[1] - t[1]) for e, t in zip(even, turned)]
    return low + high


def spectrum_of(load):
    stage = {}
    for n2 in range(8):
        part = transform_3([load((8 * n1 + 3 * n2) % 24) for n1 in range(3)], -1)
        for k1 in range(3):
            stage[k1, n2] = part[k1]
    result = {}
    for k1 in range(3):
        part = transform_8([stage[k1, n2] for n2 in range(8)], -1)
        for k2 in range(8):
            result[(16 * k1 + 9 * k2) % 24] = part[k2]
    return result


def first_half_of(spectrum):
    stage = {}
    for k1 in range(3):
        part = transform_8([spectrum[(16 * k1 + 9 * k2) % 24] for k2 in range(8)], 1)
        for n2 in range(8):
            stage[k1, n2] = part[n2]
    result = {}
    for n2 in range(8):
        wanted = {n1: (8 * n1 + 3 * n2) % 24 for n1 in range(3) if (8 * n1 + 3 * n2) % 24 < 12}
        part = transform_3([stage[k1, n2] for k1 in range(3)], 1, tuple(wanted))
        for n1, index in wanted.items():
            result[index] = part[n1]
    return result


def tile_pair(ref, step, rows):
    parts = []
    for parity in range(2):
        at = (2 * step + parity) * LANES
        part = ref[:, :, :, at : at + LANES]
        parts.append(part.reshape(rows, part.shape[2], LANES))
    return jnp.concatenate(parts, axis=1)


def plane_speeds(points, local_vel, width_z):
    index = np.arange(points**3)
    parts = (index // (points * points), index // points % points, index % points)
    speeds = [
        np.float32(0.3) * (np.float32(2.0) * part.astype(np.float32) - np.float32(points - 1))
        / np.float32(points - 1)
        for part in parts
    ]
    tiled = np.stack(speeds).reshape(3, -1, local_vel // LANES, 1, LANES).transpose(1, 0, 2, 3, 4)
    repeated = np.repeat(tiled, width_z, axis=3)
    return repeated.reshape(repeated.shape[0], 3, -1, LANES)


def edges_kernel(first, edge_ref, falls_ref, field_ref, *refs):
    down_ref, up_ref, across_ref, low_ref, high_ref, plane_ref, sems = refs
    steps = falls_ref.shape[0] // 8
    width = low_ref.shape[0]
    groups = across_ref.shape[0] // steps
    half_steps = down_ref.shape[0] // groups
    here = pl.ds(first, low_ref.shape[3])
    last_y = field_ref.shape[1] - 1
    sources = [
        field_ref.at[:, pl.ds(0, 1), :, here],
        field_ref.at[:, pl.ds(last_y, 1), :, here],
        field_ref.at[pl.ds(edge_ref[0], 1), :, :, here],
    ]
    loads = [
        pltpu.make_async_copy(source, ref, sems.at[at])
        for at, (source, ref) in enumerate(zip(sources, (low_ref, high_ref, plane_ref)))
    ]
    for load in loads:
        load.start()
    below = [falls_ref[8 * s : 8 * s + 8, :][None] > 0.0 for s in range(steps)]

    def put(ref, at, value):
        ref[at] = value.reshape(-1, LANES).astype(jnp.bfloat16)

    loads[0].wait()
    for g in range(groups):
        row = [tile_pair(low_ref, g * steps + s, width) for s in range(steps)]
        put(down_ref, g * half_steps, row[0])
        for m in range(1, steps // 2 + 1):
            put(down_ref, g * half_steps + m, jnp.where(below[2 * m - 1], row[2 * m - 1], row[2 * m]))
    loads[1].wait()
    for g in range(groups):
        row = [tile_pair(high_ref, g * steps + s, width) for s in range(steps)]
        for m in range(steps // 2):
            put(up_ref, g * half_steps + m, jnp.where(below[2 * m], row[2 * m + 1], row[2 * m]))
        put(up_ref, g * half_steps + steps // 2, row[steps - 1])
    loads[2].wait()
    for s in range(groups * steps):
        put(across_ref, s, tile_pair(plane_ref, s, plane_ref.shape[1]))


def upwind_kernel(base, counts, side_ref, *refs):
    batches = len(counts)
    outer_refs, field_ref = refs[:5], refs[5]
    out_ref, target_refs, scratch = refs[6], refs[7 : 7 + batches], refs[7 + batches :]
    inner_refs, chosen_refs, scratch = scratch[:5], scratch[5 : 5 + batches], scratch[5 + batches :]
    speed_ref, wanted_ref, down_ref, up_ref, across_ref = inner_refs
    picker_ref, blocks, reads, wide, border, cells, load_sems, store_sems, side_sems = scratch
    chunks, width_x, width_y, width_z, lanes = blocks.shape
    steps = lanes // (2 * LANES)
    group_lanes = chosen_refs[0].shape[1]
    per_group = group_lanes // lanes
    half_steps = per_group * steps // 2 + 1
    first_row = base // LANES * width_z
    rows = pl.ds(first_row, speed_ref.shape[1])
    sources = (outer_refs[0].at[side_ref[0], :, rows, :],) + outer_refs[1:]
    inputs = [
        pltpu.make_async_copy(source, target, side_sems.at[at])
        for at, (source, target) in enumerate(zip(sources, inner_refs))
    ]
    for copy in inputs:
        copy.start()
    loads = []
    for t in range(chunks):
        source = field_ref.at[:, :, :, pl.ds(base + t * lanes, lanes)]
        loads.append(pltpu.make_async_copy(source, blocks.at[t], load_sems.at[t]))
        loads[-1].start()
    beside = jnp.where(side_ref[0] == 0, 2, 0)
    place = lax.broadcasted_iota(jnp.int32, (1, 8, LANES), 1) % width_z
    capacity = picker_ref.shape[0] // 2
    stores = []
    for copy in inputs:
        copy.wait()
    number = lax.broadcasted_iota(jnp.int32, picker_ref.shape, 0)
    matches = number == wanted_ref[0:1, :]
    picker_ref[...] = jnp.where(matches, 1.0, 0.0).astype(jnp.bfloat16)
    for t in range(chunks):
        group, chunk = t // per_group, t % per_group
        sizes, falls, sinks = [], [], []
        for u in range(steps):
            step = chunk * steps + u
            row = 8 * (t * steps + u)
            speed = [speed_ref[d, row : row + 8, :][None] for d in range(3)]
            sizes.append([jnp.abs(c) for c in speed])
            falls.append(speed[1] < 0.0)
            sinks.append(speed[2] < 0.0)
            outer = across_ref[t * steps + u].astype(jnp.float32).reshape(width_y, 8, LANES)
            wide[u, 0] = outer
            wide[u, width_x + 1] = outer
            above = down_ref[group * half_steps + (step + 1) // 2].astype(jnp.float32)
            under = up_ref[group * half_steps + step // 2].astype(jnp.float32)
            shape = (width_x, 8, LANES)
            border[u] = jnp.where(falls[u], above.reshape(shape), under.reshape(shape))
        loads[t].wait()

        def spread_out(x, carry):
            for u in range(steps):
                at = 2 * u * LANES
                parts = [
                    blocks[t, x, :, :, at + p * LANES : at + (p + 1) * LANES] for p in range(2)
                ]
                wide[u, x + 1] = jnp.concatenate(parts, axis=1)
            return carry

        lax.fori_loop(0, width_x, spread_out, 0, unroll=4)

        def advance(x, carry):
            for u in range(steps):
                field = wide[u, x + 1]
                edge = border[u, pl.ds(x, 1)]
                fluxes = sizes[u][0] * (field - wide[u, x + beside])
                beside_y = jnp.where(
                    falls[u],
                    jnp.concatenate([field[1:], edge], axis=0),
                    jnp.concatenate([edge, field[:-1]], axis=0),
                )
                fluxes = fluxes + sizes[u][1] * (field - beside_y)
                turned = pltpu.roll(field, 4, 1)
                upper = pltpu.roll(jnp.where(place == 0, turned, field), 7, 1)
                lower = pltpu.roll(jnp.where(place == width_z - 1, turned, field), 1, 1)
                fluxes = fluxes + sizes[u][2] * (field - jnp.where(sinks[u], upper, lower))
                read = field - fluxes
                reads[t, pl.ds(x * width_y, width_y), 8 * u : 8 * u + 8, :] = read
                rows = width_y * 8
                at = pl.multiple_of(x * rows, rows)
                cells[pl.ds(at, rows), u * LANES : (u + 1) * LANES] = read.reshape(
                    rows, LANES
                ).astype(jnp.bfloat16)
            return carry

        lax.fori_loop(0, width_x, advance, 0, unroll=4)
        target = out_ref.at[:, pl.ds(8 * steps * t, 8 * steps), :]
        stores.append(pltpu.make_async_copy(reads.at[t], target, store_sems.at[t]))
        stores[-1].start()
        picked = jnp.dot(
            picker_ref[...], cells[...], preferred_element_type=jnp.float32
        ).astype(jnp.bfloat16)
        for parity in range(2):
            first = parity * capacity
            for ref, count in zip(chosen_refs, counts):
                rows = slice(group * count, (group + 1) * count)
                for u in range(steps):
                    tile = 2 * (chunk * steps + u) + parity
                    here = slice(tile * LANES, (tile + 1) * LANES)
                    ref[rows, here] = picked[first : first + count, u * LANES : (u + 1) * LANES]
                first += count
    for at, (source, target) in enumerate(zip(chosen_refs, target_refs)):
        stores.append(pltpu.make_async_copy(source, target, store_sems.at[chunks + at]))
        stores[-1].start()
    for store in stores:
        store.wait()


def window_loads(firsts, refs, cells, sems):
    loads = []
    for at, (ref, first) in enumerate(zip(refs, firsts)):
        source = ref.at[pl.ds(first, cells.shape[1])]
        loads.append(pltpu.make_async_copy(source, cells.at[at], sems.at[at]))
        loads[-1].start()
    return loads


def filter_parts(weight_ref, table_ref, cells, loads, section, back):
    count, slots, lanes = cells.shape
    padded = weight_ref.shape[2]
    height = table_ref.shape[0] - LANES
    window = height - 64
    pair_lanes = 2 * (height - 128)
    pairs = lanes // pair_lanes
    half = pairs * count
    sums_at = padded - LANES
    for load in loads:
        load.wait()
    for parity in range(2):
        rows = []
        for at in range(count):
            for p in range(pairs):
                lane = p * pair_lanes + parity * (pair_lanes - window)
                rows.append(cells[at, :, lane : lane + window])
        start = 64 * (1 - parity)
        out = jnp.dot(
            jnp.concatenate(rows, axis=0),
            table_ref[start : start + window, :],
            preferred_element_type=jnp.float32,
        )
        sums = out[:, sums_at : sums_at + LANES].astype(jnp.bfloat16)
        out = out + jnp.dot(sums, table_ref[height:, :], preferred_element_type=jnp.float32)
        out = out.astype(jnp.bfloat16).astype(jnp.float32)
        for at in range(half):
            section[2 * at + parity] = out[at * slots : (at + 1) * slots]

    lane_tiles = padded // LANES
    points = weight_ref.shape[1]
    pairs_of, _ = half_set(points)
    mean_at = int(np.flatnonzero((pairs_of == 0).all(axis=1))[0])

    def transform(index, carry):
        row = pl.multiple_of(index // lane_tiles * 16, 16)
        lane = pl.multiple_of(index % lane_tiles * LANES, LANES)
        mean = lane + lax.broadcasted_iota(jnp.int32, (8, LANES), 1) == mean_at
        results = []
        for octet in range(2):
            here = pl.ds(row + 8 * octet, 8)

            def load(i):
                real = section[i, here, pl.ds(lane, LANES)]
                return real, section[i, here, pl.ds(padded + lane, LANES)]

            spectrum = spectrum_of(load)
            per_kernel = []
            for which in range(3):
                weighted = {}
                for a, (real, imag) in spectrum.items():
                    weight = weight_ref[which, pl.ds(a, 1), pl.ds(lane, LANES)]
                    weighted[a] = (real * weight, imag * weight)
                real = weighted[0][0]
                rounded = real.astype(jnp.bfloat16).astype(jnp.float32)
                weighted[0] = (jnp.where(mean, rounded, real), weighted[0][1])
                per_kernel.append(first_half_of(weighted))
            results.append(per_kernel)
        for which in range(3):
            for i in range(half):
                for q in range(2):
                    value = jnp.concatenate([results[o][which][i][q] for o in range(2)], axis=0)
                    back[i % 2, which, i // 2, pl.ds(row, 16), pl.ds(q * padded + lane, LANES)] = (
                        value.astype(jnp.bfloat16)
                    )
        return carry

    lax.fori_loop(0, slots // 16 * lane_tiles, transform, 0)


def inverse_parts(back_table, back):
    _, kernels, pairs, slots, depth = back.shape
    window = back_table.shape[2]
    outs = []
    for parity in range(2):
        out = jnp.dot(
            back[parity].reshape(kernels * pairs * slots, depth),
            back_table[parity, :depth],
            preferred_element_type=jnp.float32,
        )
        first = 0 if parity else window - LANES
        level = out[:, first : first + LANES].astype(jnp.bfloat16)
        out = out + jnp.dot(level, back_table[parity, depth:], preferred_element_type=jnp.float32)
        outs.append(out.reshape(kernels, pairs, slots, window))
    return outs


def terms_of(part, outs, cells_ref, put):
    _, slots, lanes = cells_ref.shape
    window = outs[0].shape[3]
    pair_lanes = 2 * (window - 64)
    pairs = lanes // pair_lanes
    tiles = pair_lanes // LANES
    near = lax.broadcasted_iota(jnp.int32, (slots, LANES), 1) < 64
    for pair in range(pairs):
        at = part * pairs + pair
        for tile in range(tiles):
            lane = tile * LANES
            odd_lane = lane - (pair_lanes - window)
            values = []
            for which in range(3):
                if tile < tiles // 2:
                    value = outs[0][which, at, :, lane : lane + LANES]
                elif tile > tiles // 2:
                    value = outs[1][which, at, :, odd_lane : odd_lane + LANES]
                else:
                    value = jnp.where(
                        near,
                        outs[0][which, at, :, lane : lane + LANES],
                        outs[1][which, at, :, odd_lane : odd_lane + LANES],
                    )
                values.append(value)
            lane = pair * pair_lanes + lane
            cells = cells_ref[part, :, lane : lane + LANES].astype(jnp.float32)
            put(pair * tiles + tile, (values[0] * values[1] - cells * values[2]).astype(jnp.bfloat16))


def collide_kernel(firsts, weight_ref, table_ref, back_any, *refs):
    parts = len(firsts) // 2
    terms_ref, cells, section, back, back_table, sems = refs[2 * parts :]
    lanes = cells.shape[2]
    loads = window_loads(firsts, refs[: 2 * parts], cells, sems)
    table_load = pltpu.make_async_copy(back_any, back_table, sems.at[2 * parts])
    table_load.start()
    filter_parts(weight_ref, table_ref, cells, loads, section, back)
    table_load.wait()
    outs = inverse_parts(back_table, back)
    for part in range(parts):

        def put(tile, value):
            first = part * lanes + tile * LANES
            terms_ref[:, first : first + LANES] = value

        terms_of(part, outs, cells, put)


def finish_kernel(firsts, sizes, weight_ref, table_ref, back_any, spread_any, *refs):
    parts = len(firsts) // 2
    term_refs, refs = refs[: len(sizes) - 1], refs[len(sizes) - 1 :]
    first_read, rest_read = refs[2 * parts : 2 * parts + 2]
    out_ref, cells, section, back, back_table, reads, spots, added, staged = refs[2 * parts + 2 : -6]
    spread_ref, early_ref, cell_sems, read_sems, out_sems, extra_sems = refs[-6:]
    width_x, width_y, width_z, lanes = staged.shape[1:]
    tiles = lanes // LANES
    loads = window_loads(firsts, refs[: 2 * parts], cells, cell_sems)
    extra = [pltpu.make_async_copy(spread_any, spread_ref, extra_sems.at[0])]
    at = 0
    for ref, size in zip(term_refs, sizes):
        target = early_ref.at[pl.ds(at, size)]
        extra.append(pltpu.make_async_copy(ref, target, extra_sems.at[len(extra)]))
        at += size
    extra.append(pltpu.make_async_copy(back_any, back_table, cell_sems.at[2 * parts]))
    group_rows = reads.shape[2]
    read_loads = []
    for part in range(parts):
        rows = pl.ds(max(part - 1, 0) * group_rows, group_rows)
        source = (rest_read if part else first_read).at[:, rows, :]
        read_loads.append(pltpu.make_async_copy(source, reads.at[part], read_sems.at[part]))
    for load in extra + read_loads:
        load.start()
    filter_parts(weight_ref, table_ref, cells, loads, section, back)
    for load in extra:
        load.wait()
    early = early_ref.shape[0]
    capacity = early + section.shape[1]
    outs = inverse_parts(back_table, back)
    pieces = out_sems.shape[1]
    piece_x = width_x // pieces
    stores = []
    for part in range(parts):

        def put(tile, value):
            first = tile % 2 * capacity
            columns = slice(tile // 2 * LANES, (tile // 2 + 1) * LANES)
            lane = part * lanes + tile * LANES
            spots[first : first + early, columns] = early_ref[:, lane : lane + LANES]
            spots[first + early : first + capacity, columns] = value

        terms_of(part, outs, cells, put)
        added[...] = jnp.dot(spread_ref[...], spots[...], preferred_element_type=jnp.float32)
        read_loads[part].wait()
        slot = part % 2
        if part >= 2:
            for store in stores[part - 2]:
                store.wait()

        def add(x, carry):
            for y in range(width_y):
                row = x * width_y + y
                at = pl.multiple_of(row * 8, 8)
                for u in range(tiles // 2):
                    value = (
                        reads[part, row, 8 * u : 8 * u + 8, :]
                        + added[pl.ds(at, 8), u * LANES : (u + 1) * LANES]
                    )
                    for parity in range(2):
                        lane = (2 * u + parity) * LANES
                        half = value[parity * width_z : (parity + 1) * width_z]
                        staged[slot, x, y, :, lane : lane + LANES] = half
            return carry

        stores.append([])
        for piece in range(pieces):
            lax.fori_loop(piece * piece_x, (piece + 1) * piece_x, add, 0)
            rows = pl.ds(piece * piece_x, piece_x)
            store = pltpu.make_async_copy(
                staged.at[slot, rows],
                out_ref.at[rows, :, :, pl.ds(part * lanes, lanes)],
                out_sems.at[part, piece],
            )
            store.start()
            stores[part].append(store)
    for part in range(max(parts - 2, 0), parts):
        for store in stores[part]:
            store.wait()


def params(mib):
    return pltpu.CompilerParams(vmem_limit_bytes=mib * 2**20)


def cost(flops, size):
    return pl.CostEstimate(flops=flops, bytes_accessed=size, transcendentals=0)


def fast_fits(distribution, points):
    width_x, width_y, width_z, local_vel = distribution.shape
    group = PLANES * points * points
    return (
        points == 24
        and lax.axis_size("vel") == 2
        and width_z == 4
        and local_vel * 2 == points**3
        and local_vel == 3 * group
        and width_x * width_y * width_z % 128 == 0
    )


def fast_device(distribution, refine_level, gain_one, gain_two, loss_kernel):
    points = gain_one.shape[0]
    width_x, width_y, width_z, local_vel = distribution.shape
    block_rows = width_x * width_y
    block_cells = block_rows * width_z
    group = PLANES * points * points
    parts = local_vel // group
    group_rows = group // LANES * width_z
    steps = group_rows // 8
    capacity = block_cells // 2
    third = capacity * 3 // 8 // 16 * 16
    counts = (third, third, capacity - 2 * third)
    batches = len(counts)
    vel_at = lax.axis_index("vel")
    count_x, count_y = lax.axis_size("cx"), lax.axis_size("cy")

    tiles = local_vel // LANES
    speeds = jnp.asarray(plane_speeds(points, local_vel, width_z))
    falls = np.arange(group) // points % points < points // 2
    falls = np.repeat(falls.reshape(-1, 1, LANES), width_z, axis=1).reshape(-1, LANES)
    falls = jnp.asarray(falls.astype(np.float32))
    side = vel_at.reshape(1).astype(jnp.int32)
    edge = jnp.where(vel_at == 0, 0, width_x - 1).reshape(1).astype(jnp.int32)

    level = refine_level.reshape(block_cells)
    active = level > 0
    cell_at = jnp.arange(block_cells, dtype=jnp.int32)
    before = (cell_at[:, None] < cell_at[None, :]) & active[:, None]
    slot_index = jnp.where(active, jnp.sum(before.astype(jnp.int32), axis=0), -1)
    spot = slot_index.reshape(block_rows, 1, width_z)
    parity = jnp.arange(2, dtype=jnp.int32)[None, :, None]
    shape = (block_rows, 2, width_z)
    wanted = jnp.where(spot >= 0, spot + capacity * parity, -1)
    wanted = jnp.broadcast_to(wanted, shape).reshape(-1)
    numbers = jnp.arange(2 * capacity, dtype=jnp.int32)
    wanted_rows = jnp.broadcast_to(wanted[None, :], (8, wanted.shape[0]))
    strength = jnp.broadcast_to(
        (0.25 * level.astype(jnp.float32)).reshape(block_rows, 1, width_z), shape
    ).reshape(-1)
    spread = jnp.where(wanted[:, None] == numbers[None, :], strength[:, None], 0.0)
    spread = spread.astype(jnp.bfloat16)

    padded = -(-len(half_set(points)[1]) // LANES) * LANES
    select, scale = frequency_select(points, padded)
    table, back_table = [jnp.asarray(t) for t in plane_table(points, padded, 64)]

    towards_lower = [(j, (j - 1) % count_y) for j in range(count_y)]
    towards_upper = [(j, (j + 1) % count_y) for j in range(count_y)]
    across_pairs = [(i, (i - 1) % count_x) for i in range(count_x)]
    across_pairs += [(count_x + i, count_x + (i + 1) % count_x) for i in range(count_x)]
    swap = [(0, 1), (1, 0)]
    bf16 = jnp.bfloat16

    half_steps = steps // 2 + 1
    local = pl.BlockSpec(memory_space=pltpu.VMEM)
    scalar = pl.BlockSpec(memory_space=pltpu.SMEM)
    remote = pl.BlockSpec(memory_space=pltpu.HBM)
    anywhere = pl.BlockSpec(memory_space=pl.ANY)

    def edges_of(first, groups):
        return pl.pallas_call(
            functools.partial(edges_kernel, first * group),
            in_specs=[scalar, local, remote],
            out_specs=[local] * 3,
            out_shape=[
                jax.ShapeDtypeStruct((groups * half_steps, width_x * 8, LANES), bf16),
                jax.ShapeDtypeStruct((groups * half_steps, width_x * 8, LANES), bf16),
                jax.ShapeDtypeStruct((groups * steps, width_y * 8, LANES), bf16),
            ],
            scratch_shapes=[
                pltpu.VMEM((width_x, 1, width_z, groups * group), jnp.float32),
                pltpu.VMEM((width_x, 1, width_z, groups * group), jnp.float32),
                pltpu.VMEM((1, width_y, width_z, groups * group), jnp.float32),
                pltpu.SemaphoreType.DMA((3,)),
            ],
            compiler_params=params(LIMIT),
            cost_estimate=cost(1, 1),
            name="edges",
        )(edge, falls, distribution)

    edges = [edges_of(0, 1), edges_of(1, parts - 1)]
    wide = 3
    chunks = steps // wide

    def upwind(at, halo, sizes):
        groups = parts - 1 if at else 1
        operands = (speeds, wanted_rows, *halo)
        local_speeds = jax.ShapeDtypeStruct((3, groups * group_rows, LANES), jnp.float32)
        chosen = [(groups * size, group) for size in sizes]
        return pl.pallas_call(
            functools.partial(upwind_kernel, at * group, sizes),
            in_specs=[scalar] + [anywhere] * (len(operands) + 1),
            out_specs=[anywhere] * (1 + len(sizes)),
            out_shape=[
                jax.ShapeDtypeStruct((block_rows, groups * group_rows, LANES), jnp.float32)
            ]
            + [jax.ShapeDtypeStruct(shape, bf16) for shape in chosen],
            scratch_shapes=[pltpu.VMEM(x.shape, x.dtype) for x in (local_speeds, *operands[1:])]
            + [pltpu.VMEM(shape, bf16) for shape in chosen]
            + [
                pltpu.VMEM((2 * capacity, block_rows * 8), bf16),
                pltpu.VMEM(
                    (groups * chunks, width_x, width_y, width_z, group // chunks), jnp.float32
                ),
                pltpu.VMEM((groups * chunks, block_rows, 8 * wide, LANES), jnp.float32),
                pltpu.VMEM((wide, width_x + 2, width_y, 8, LANES), jnp.float32),
                pltpu.VMEM((wide, width_x, 8, LANES), jnp.float32),
                pltpu.VMEM((block_rows * 8, wide * LANES), bf16),
                pltpu.SemaphoreType.DMA((groups * chunks,)),
                pltpu.SemaphoreType.DMA((groups * chunks + len(sizes),)),
                pltpu.SemaphoreType.DMA((len(operands),)),
            ],
            compiler_params=params(LIMIT),
            cost_estimate=cost(1, 1),
            name="upwind",
        )(side, *operands, distribution)

    def turn(value, *earlier):
        return lax.optimization_barrier((value, *earlier))[0]

    def swapped(value):
        return lax.ppermute(value, "vel", swap)

    halos = []
    for at in range(2):
        down, up, across = edges[at]
        halos.append(
            (
                lax.ppermute(down, "cy", towards_lower),
                lax.ppermute(up, "cy", towards_upper),
                lax.ppermute(across, ("vel", "cx"), across_pairs),
            )
        )
    first_read, *first = upwind(0, turn(halos[0], edges[1]), counts)
    first_other = [swapped(x) for x in first]
    rest_read, *rest = upwind(1, turn(halos[1], first), counts)
    kernels = turn((gain_one, gain_two, loss_kernel), halos[0])
    weights = pl.pallas_call(
        weights_kernel,
        out_shape=jax.ShapeDtypeStruct((3, points, padded), jnp.float32),
        compiler_params=params(LIMIT),
        cost_estimate=cost(1, 1),
        name="weights",
    )(
        jnp.concatenate([k.reshape(points, points * points) for k in kernels], axis=0),
        jnp.asarray(select),
        jnp.asarray(scale),
    )

    operand, weights, spread = turn((rest[0], weights, spread), first_other)
    others = [swapped(operand)]

    def scratch(count):
        return [
            pltpu.VMEM((2 * parts, count, group), bf16),
            pltpu.VMEM((points, count, 2 * padded), jnp.float32),
            pltpu.VMEM((2, 3, points // 4, count, 2 * padded), bf16),
            pltpu.VMEM(back_table.shape, bf16),
        ]

    sems = pltpu.SemaphoreType.DMA((2 * parts + 1,))
    terms = []
    for batch in range(batches - 1):
        count = counts[batch]
        starts = (0,) + tuple(g * count for g in range(parts - 1))
        following = turn(rest[batch + 1], others[-1], *terms)
        others.append(swapped(following))
        terms.append(
            pl.pallas_call(
                functools.partial(collide_kernel, starts + starts),
                in_specs=[local] * 2 + [anywhere] * (1 + 2 * parts),
                out_specs=local,
                out_shape=jax.ShapeDtypeStruct((count, local_vel), bf16),
                scratch_shapes=scratch(count) + [sems],
                compiler_params=params(24),
                cost_estimate=cost(1, 1),
                name="collide",
            )(
                weights,
                table,
                back_table,
                first[batch],
                *[rest[batch]] * (parts - 1),
                first_other[batch],
                *[others[batch]] * (parts - 1),
            )
        )

    pieces = 4
    count = counts[-1]
    starts = (0,) + tuple(g * count for g in range(parts - 1))
    return pl.pallas_call(
        functools.partial(finish_kernel, starts + starts, counts),
        in_specs=[local] * 2 + [anywhere] * (1 + batches + 2 * parts + 2),
        out_specs=anywhere,
        out_shape=jax.ShapeDtypeStruct(distribution.shape, jnp.float32),
        scratch_shapes=scratch(count)
        + [
            pltpu.VMEM((parts, block_rows, group_rows, LANES), jnp.float32),
            pltpu.VMEM((2 * capacity, group // 2), bf16),
            pltpu.VMEM((block_rows * 8, group // 2), jnp.float32),
            pltpu.VMEM((2, width_x, width_y, width_z, group), jnp.float32),
            pltpu.VMEM(spread.shape, bf16),
            pltpu.VMEM((capacity - count, local_vel), bf16),
            sems,
            pltpu.SemaphoreType.DMA((parts,)),
            pltpu.SemaphoreType.DMA((parts, pieces)),
            pltpu.SemaphoreType.DMA((batches,)),
        ],
        compiler_params=params(LIMIT),
        name="finish",
    )(
        weights,
        table,
        back_table,
        spread,
        *terms,
        first[-1],
        *[rest[-1]] * (parts - 1),
        first_other[-1],
        *[others[-1]] * (parts - 1),
        first_read,
        rest_read,
    )


def per_device(distribution, refine_level, gain_one, gain_two, loss_kernel):
    if fast_fits(distribution, gain_one.shape[0]):
        return fast_device(distribution, refine_level, gain_one, gain_two, loss_kernel)
    return plain_device(distribution, refine_level, gain_one, gain_two, loss_kernel)


def solution(mesh):
    placed = (P("cx", "cy", None, "vel"), P("cx", "cy", None), P(), P(), P())
    return jax.shard_map(
        per_device,
        mesh=mesh,
        in_specs=placed,
        out_specs=P("cx", "cy", None, "vel"),
        check_vma=False,
    )
```

```python
import functools
import math

import jax
import jax.numpy as jnp
import ml_dtypes
import numpy as np
from jax import lax
from jax.experimental import pallas as pl
from jax.experimental.pallas import tpu as pltpu
from jax.sharding import PartitionSpec as P


def extended(array, sides, width):
    for axis, dim in sides:
        count, length = (lax.axis_size(axis), array.shape[dim])
        up = [(i, (i + 1) % count) for i in range(count)]
        down = [(j, i) for i, j in up]
        last = lax.slice_in_dim(array, length - width, length, axis=dim)
        leading = lax.slice_in_dim(array, 0, width, axis=dim)
        before = lax.ppermute(last, axis, up)
        after = lax.ppermute(leading, axis, down)
        array = jnp.concatenate([before, array, after], axis=dim)
    return array


def dft_tables(points):
    indices = jnp.arange(points, dtype=jnp.int32)
    products = indices[:, None] * indices[None, :] % points
    angles = products.astype(jnp.float32) * (2.0 * math.pi / points)
    cosine = jnp.cos(angles)
    sine_table = jnp.sin(angles)
    forward = jnp.stack([jnp.stack([cosine, sine_table]), jnp.stack([-sine_table, cosine])])
    inverse = jnp.stack([jnp.stack([cosine, -sine_table]), jnp.stack([sine_table, cosine])])
    return (forward.astype(jnp.bfloat16), inverse.astype(jnp.bfloat16))


def contract(pattern, left_side, right_side):
    return jnp.einsum(pattern, left_side, right_side, preferred_element_type=jnp.float32)


def collide(cells, forward, inverse, gain_one, gain_two, loss_kernel):
    points = forward.shape[-1]
    cell_count = cells.shape[0]
    field = cells.reshape(cell_count, points, points, points)
    section_z = contract("nabz,qzw->qnabw", field, forward[:, 0]).astype(jnp.bfloat16)
    section_y = contract("pnayc,qpyw->qnawc", section_z, forward).astype(jnp.bfloat16)
    spectrum = contract("pnxbc,qpxw->qnwbc", section_y, forward)
    scale_factor = 1.0 / float(points**3)

    def filtered(kernel):
        weighted = (spectrum * (kernel * scale_factor)[None, None]).astype(jnp.bfloat16)
        back_x = contract("pnxbc,qpxw->qnwbc", weighted, inverse).astype(jnp.bfloat16)
        back_y = contract("pnayc,qpyw->qnawc", back_x, inverse).astype(jnp.bfloat16)
        return contract("pnabz,pzw->nabw", back_y, inverse[0])

    gain_term = filtered(gain_one) * filtered(gain_two)
    result = gain_term - field.astype(jnp.float32) * filtered(loss_kernel)
    return result.reshape(cell_count, points**3)


def courants(points, first_vel, local_count):
    vel_index = first_vel + jnp.arange(local_count, dtype=jnp.int32)
    index_x = vel_index // (points * points)
    index_y = vel_index // points % points
    index_z = vel_index % points

    def speed(index_part):
        return 0.3 * (2.0 * index_part.astype(jnp.float32) - (points - 1)) / (points - 1)

    return (speed(index_x), speed(index_y), speed(index_z))


def upwind_flux(courant, center, lower_side, upper_side):
    return jnp.maximum(courant, 0.0) * (center - lower_side) + jnp.minimum(courant, 0.0) * (
        upper_side - center
    )


def plain_device(distribution, refine_level, gain_one, gain_two, loss_kernel):
    points = gain_one.shape[0]
    width_x, width_y, width_z, local_vel = distribution.shape
    first_vel = lax.axis_index("vel") * local_vel
    courant_x, courant_y, courant_z = courants(points, first_vel, local_vel)
    padded = extended(distribution, (("cx", 0), ("cy", 1)), 1)
    fluxes = upwind_flux(courant_x, distribution, padded[:-2, 1:-1], padded[2:, 1:-1])
    fluxes = fluxes + upwind_flux(courant_y, distribution, padded[1:-1, :-2], padded[1:-1, 2:])
    fluxes = fluxes + upwind_flux(
        courant_z, distribution, jnp.roll(distribution, 1, 2), jnp.roll(distribution, -1, 2)
    )
    read = distribution - fluxes
    block_cells = width_x * width_y * width_z
    groups = lax.axis_size("vel")
    flattened = read.reshape(block_cells, local_vel).astype(jnp.bfloat16)
    forward, inverse = dft_tables(points)
    active = refine_level.reshape(block_cells) > 0
    slot_index = jnp.cumsum(active.astype(jnp.int32)) - 1
    capacity = block_cells // 2
    picker = (
        (slot_index[None, :] == jnp.arange(capacity, dtype=jnp.int32)[:, None]) & active[None, :]
    ).astype(jnp.bfloat16)
    chosen = jnp.dot(picker, flattened, preferred_element_type=jnp.float32).astype(jnp.bfloat16)
    terms = collide(
        lax.all_to_all(
            chosen.reshape(groups, capacity // groups, local_vel),
            "vel",
            split_axis=0,
            concat_axis=2,
            tiled=True,
        )[0],
        forward,
        inverse,
        gain_one,
        gain_two,
        loss_kernel,
    )[None]
    packed = lax.all_to_all(
        terms.astype(jnp.bfloat16), "vel", split_axis=2, concat_axis=0, tiled=True
    ).astype(terms.dtype)
    packed_rows = packed.reshape(capacity, local_vel)
    safe_slot = jnp.clip(slot_index, 0, capacity - 1)
    rates = jnp.where(active[:, None], packed_rows[safe_slot], 0.0)
    weight = 0.25 * refine_level.astype(jnp.float32)
    return read + weight[..., None] * rates.reshape(width_x, width_y, width_z, local_vel)

LANES = 128
PLANES = 4
LIMIT = 57


def half_set(points):
    middle = points // 2
    pairs = [(b, c) for c in range(1, middle) for b in range(points)]
    pairs += [(b, c) for c in (0, middle) for b in range(middle + 1)]
    weights = [1.0 if b % middle == 0 and c % middle == 0 else 2.0 for b, c in pairs]
    return np.array(pairs), np.array(weights)


def plane_table(points, padded, margin):
    pairs, _ = half_set(points)
    first, second = np.divmod(np.arange(points * points), points)
    index = np.arange(points)
    angles = (index[:, None] * index[None, :] % points).astype(np.float32)
    angles = angles * np.float32(2.0 * np.pi / points)
    cosine, sine = [
        t.astype(ml_dtypes.bfloat16).astype(np.float32) for t in (np.cos(angles), np.sin(angles))
    ]
    cos_y, sin_y = cosine[first][:, pairs[:, 0]], sine[first][:, pairs[:, 0]]
    cos_z, sin_z = cosine[second][:, pairs[:, 1]], sine[second][:, pairs[:, 1]]
    table = np.zeros((points * points + 2 * margin, 2 * padded), np.float32)
    rows = slice(margin, margin + points * points)
    table[rows, : len(pairs)] = cos_y * cos_z - sin_y * sin_z
    table[rows, padded : padded + len(pairs)] = -(cos_y * sin_z + sin_y * cos_z)
    window = points * points + margin
    level = np.flatnonzero(pairs[:, 1] == 0)
    rest = table.copy()
    rest[:, np.concatenate([level, padded + level])] = 0.0
    for start in (points * points + margin, 0):
        rest[start : start + points, level] = cosine[:, pairs[level, 0]]
        rest[start : start + points, padded + level] = -sine[:, pairs[level, 0]]
    back = np.stack([rest[margin : margin + window].T, rest[:window].T])
    copies = np.zeros((2, LANES, window), np.float32)
    place = np.arange(points * points)
    copies[0, (points * points + first) % LANES, place] = 1.0
    copies[1, first, margin + place] = 1.0
    back = np.concatenate([back, copies], axis=1)
    spare = len(pairs)
    lift = np.zeros((LANES, 2 * padded), np.float32)
    for half in (0, padded):
        columns = slice(spare % LANES, spare % LANES + points)
        lift[columns, half + level] = table[margin : margin + points**2 : points, half + level]
        table[:, half + level] = 0.0
    table[margin + place, spare + first] = 1.0
    table = np.concatenate([table, lift])
    return table.astype(ml_dtypes.bfloat16), back.astype(ml_dtypes.bfloat16)


def frequency_select(points, padded):
    pairs, weights = half_set(points)
    select = np.zeros((points * points, 2 * padded), np.float32)
    column = np.arange(len(pairs))
    select[pairs[:, 0] * points + pairs[:, 1], column] = 1.0
    mirror = (-pairs[:, 0]) % points * points + (-pairs[:, 1]) % points
    select[mirror, padded + column] = 1.0
    scale = np.zeros((1, padded), np.float32)
    scale[0, : len(pairs)] = 0.5 * weights / points**3
    return select.astype(ml_dtypes.bfloat16), scale


def weights_kernel(stacked_ref, select_ref, scale_ref, out_ref):
    kernels, points, padded = out_ref.shape
    rest = stacked_ref[...]
    picked = None
    for _ in range(3):
        piece = rest.astype(jnp.bfloat16)
        rest = rest - piece.astype(jnp.float32)
        part = jnp.dot(piece, select_ref[...], preferred_element_type=jnp.float32)
        picked = part if picked is None else picked + part
    for which in range(kernels):
        for a in range(points):
            row, mirror = which * points + a, which * points + (-a) % points
            both = picked[row : row + 1, :padded] + picked[mirror : mirror + 1, padded:]
            out_ref[which, a : a + 1, :] = both * scale_ref[...]


def transform_3(x, sign, wanted=(0, 1, 2)):
    (ar, ai), (br, bi), (cr, ci) = x
    sr, si = br + cr, bi + ci
    out = {}
    if 0 in wanted:
        out[0] = (ar + sr, ai + si)
    if 1 in wanted or 2 in wanted:
        height = sign * math.sqrt(0.75)
        mr, mi = ar - 0.5 * sr, ai - 0.5 * si
        er, ei = height * (br - cr), height * (bi - ci)
        if 1 in wanted:
            out[1] = (mr - ei, mi + er)
        if 2 in wanted:
            out[2] = (mr + ei, mi - er)
    return out


def transform_4(x, sign):
    (ar, ai), (br, bi), (cr, ci), (dr, di) = x
    pr, pi, qr, qi = ar + cr, ai + ci, ar - cr, ai - ci
    sr, si, tr, ti = br + dr, bi + di, br - dr, bi - di
    if sign < 0:
        tr, ti = -tr, -ti
    return [(pr + sr, pi + si), (qr - ti, qi + tr), (pr - sr, pi - si), (qr + ti, qi - tr)]


def transform_8(x, sign):
    even = transform_4(x[0::2], sign)
    odd = transform_4(x[1::2], sign)
    root = math.sqrt(0.5)
    (r0, i0), (r1, i1), (r2, i2), (r3, i3) = odd
    if sign > 0:
        turned = [(r0, i0), (root * (r1 - i1), root * (i1 + r1)), (-i2, r2)]
        turned.append((-root * (r3 + i3), root * (r3 - i3)))
    else:
        turned = [(r0, i0), (root * (r1 + i1), root * (i1 - r1)), (i2, -r2)]
        turned.append((root * (i3 - r3), -root * (i3 + r3)))
    low = [(e[0] + t[0], e[1] + t[1]) for e, t in zip(even, turned)]
    high = [(e[0] - t[0], e[1] - t[1]) for e, t in zip(even, turned)]
    return low + high


def spectrum_of(load):
    stage = {}
    for n2 in range(8):
        part = transform_3([load((8 * n1 + 3 * n2) % 24) for n1 in range(3)], -1)
        for k1 in range(3):
            stage[k1, n2] = part[k1]
    result = {}
    for k1 in range(3):
        part = transform_8([stage[k1, n2] for n2 in range(8)], -1)
        for k2 in range(8):
            result[(16 * k1 + 9 * k2) % 24] = part[k2]
    return result


def first_half_of(spectrum):
    stage = {}
    for k1 in range(3):
        part = transform_8([spectrum[(16 * k1 + 9 * k2) % 24] for k2 in range(8)], 1)
        for n2 in range(8):
            stage[k1, n2] = part[n2]
    result = {}
    for n2 in range(8):
        wanted = {n1: (8 * n1 + 3 * n2) % 24 for n1 in range(3) if (8 * n1 + 3 * n2) % 24 < 12}
        part = transform_3([stage[k1, n2] for k1 in range(3)], 1, tuple(wanted))
        for n1, index in wanted.items():
            result[index] = part[n1]
    return result


def tile_pair(ref, step, rows):
    parts = []
    for parity in range(2):
        at = (2 * step + parity) * LANES
        part = ref[:, :, :, at : at + LANES]
        parts.append(part.reshape(rows, part.shape[2], LANES))
    return jnp.concatenate(parts, axis=1)


def plane_speeds(points, local_vel, width_z):
    index = np.arange(points**3)
    parts = (index // (points * points), index // points % points, index % points)
    speeds = [
        np.float32(0.3) * (np.float32(2.0) * part.astype(np.float32) - np.float32(points - 1))
        / np.float32(points - 1)
        for part in parts
    ]
    tiled = np.stack(speeds).reshape(3, -1, local_vel // LANES, 1, LANES).transpose(1, 0, 2, 3, 4)
    repeated = np.repeat(tiled, width_z, axis=3)
    return repeated.reshape(repeated.shape[0], 3, -1, LANES)


def edges_kernel(first, edge_ref, falls_ref, field_ref, *refs):
    down_ref, up_ref, across_ref, low_ref, high_ref, plane_ref, sems = refs
    steps = falls_ref.shape[0] // 8
    width = low_ref.shape[0]
    groups = across_ref.shape[0] // steps
    half_steps = down_ref.shape[0] // groups
    here = pl.ds(first, low_ref.shape[3])
    last_y = field_ref.shape[1] - 1
    sources = [
        field_ref.at[:, pl.ds(0, 1), :, here],
        field_ref.at[:, pl.ds(last_y, 1), :, here],
        field_ref.at[pl.ds(edge_ref[0], 1), :, :, here],
    ]
    loads = [
        pltpu.make_async_copy(source, ref, sems.at[at])
        for at, (source, ref) in enumerate(zip(sources, (low_ref, high_ref, plane_ref)))
    ]
    for load in loads:
        load.start()
    below = [falls_ref[8 * s : 8 * s + 8, :][None] > 0.0 for s in range(steps)]

    def put(ref, at, value):
        ref[at] = value.reshape(-1, LANES).astype(jnp.bfloat16)

    loads[0].wait()
    for g in range(groups):
        row = [tile_pair(low_ref, g * steps + s, width) for s in range(steps)]
        put(down_ref, g * half_steps, row[0])
        for m in range(1, steps // 2 + 1):
            put(down_ref, g * half_steps + m, jnp.where(below[2 * m - 1], row[2 * m - 1], row[2 * m]))
    loads[1].wait()
    for g in range(groups):
        row = [tile_pair(high_ref, g * steps + s, width) for s in range(steps)]
        for m in range(steps // 2):
            put(up_ref, g * half_steps + m, jnp.where(below[2 * m], row[2 * m + 1], row[2 * m]))
        put(up_ref, g * half_steps + steps // 2, row[steps - 1])
    loads[2].wait()
    for s in range(groups * steps):
        put(across_ref, s, tile_pair(plane_ref, s, plane_ref.shape[1]))


def upwind_kernel(base, counts, side_ref, *refs):
    batches = len(counts)
    outer_refs, field_ref = refs[:5], refs[5]
    out_ref, target_refs, scratch = refs[6], refs[7 : 7 + batches], refs[7 + batches :]
    inner_refs, chosen_refs, scratch = scratch[:5], scratch[5 : 5 + batches], scratch[5 + batches :]
    speed_ref, wanted_ref, down_ref, up_ref, across_ref = inner_refs
    picker_ref, blocks, reads, wide, border, cells, load_sems, store_sems, side_sems = scratch
    chunks, width_x, width_y, width_z, lanes = blocks.shape
    steps = lanes // (2 * LANES)
    group_lanes = chosen_refs[0].shape[1]
    per_group = group_lanes // lanes
    half_steps = per_group * steps // 2 + 1
    first_row = base // LANES * width_z
    rows = pl.ds(first_row, speed_ref.shape[1])
    sources = (outer_refs[0].at[side_ref[0], :, rows, :],) + outer_refs[1:]
    inputs = [
        pltpu.make_async_copy(source, target, side_sems.at[at])
        for at, (source, target) in enumerate(zip(sources, inner_refs))
    ]
    for copy in inputs:
        copy.start()
    loads = []
    for t in range(chunks):
        source = field_ref.at[:, :, :, pl.ds(base + t * lanes, lanes)]
        loads.append(pltpu.make_async_copy(source, blocks.at[t], load_sems.at[t]))
        loads[-1].start()
    beside = jnp.where(side_ref[0] == 0, 2, 0)
    place = lax.broadcasted_iota(jnp.int32, (1, 8, LANES), 1) % width_z
    capacity = picker_ref.shape[0] // 2
    stores = []
    for copy in inputs:
        copy.wait()
    number = lax.broadcasted_iota(jnp.int32, picker_ref.shape, 0)
    matches = number == wanted_ref[0:1, :]
    picker_ref[...] = jnp.where(matches, 1.0, 0.0).astype(jnp.bfloat16)
    for t in range(chunks):
        group, chunk = t // per_group, t % per_group
        sizes, falls, sinks = [], [], []
        for u in range(steps):
            step = chunk * steps + u
            row = 8 * (t * steps + u)
            speed = [speed_ref[d, row : row + 8, :][None] for d in range(3)]
            sizes.append([jnp.abs(c) for c in speed])
            falls.append(speed[1] < 0.0)
            sinks.append(speed[2] < 0.0)
            outer = across_ref[t * steps + u].astype(jnp.float32).reshape(width_y, 8, LANES)
            wide[u, 0] = outer
            wide[u, width_x + 1] = outer
            above = down_ref[group * half_steps + (step + 1) // 2].astype(jnp.float32)
            under = up_ref[group * half_steps + step // 2].astype(jnp.float32)
            shape = (width_x, 8, LANES)
            border[u] = jnp.where(falls[u], above.reshape(shape), under.reshape(shape))
        loads[t].wait()

        def spread_out(x, carry):
            for u in range(steps):
                at = 2 * u * LANES
                parts = [
                    blocks[t, x, :, :, at + p * LANES : at + (p + 1) * LANES] for p in range(2)
                ]
                wide[u, x + 1] = jnp.concatenate(parts, axis=1)
            return carry

        lax.fori_loop(0, width_x, spread_out, 0, unroll=4)

        def advance(x, carry):
            for u in range(steps):
                field = wide[u, x + 1]
                edge = border[u, pl.ds(x, 1)]
                fluxes = sizes[u][0] * (field - wide[u, x + beside])
                beside_y = jnp.where(
                    falls[u],
                    jnp.concatenate([field[1:], edge], axis=0),
                    jnp.concatenate([edge, field[:-1]], axis=0),
                )
                fluxes = fluxes + sizes[u][1] * (field - beside_y)
                turned = pltpu.roll(field, 4, 1)
                upper = pltpu.roll(jnp.where(place == 0, turned, field), 7, 1)
                lower = pltpu.roll(jnp.where(place == width_z - 1, turned, field), 1, 1)
                fluxes = fluxes + sizes[u][2] * (field - jnp.where(sinks[u], upper, lower))
                read = field - fluxes
                reads[t, pl.ds(x * width_y, width_y), 8 * u : 8 * u + 8, :] = read
                rows = width_y * 8
                at = pl.multiple_of(x * rows, rows)
                cells[pl.ds(at, rows), u * LANES : (u + 1) * LANES] = read.reshape(
                    rows, LANES
                ).astype(jnp.bfloat16)
            return carry

        lax.fori_loop(0, width_x, advance, 0, unroll=4)
        target = out_ref.at[:, pl.ds(8 * steps * t, 8 * steps), :]
        stores.append(pltpu.make_async_copy(reads.at[t], target, store_sems.at[t]))
        stores[-1].start()
        picked = jnp.dot(
            picker_ref[...], cells[...], preferred_element_type=jnp.float32
        ).astype(jnp.bfloat16)
        for parity in range(2):
            first = parity * capacity
            for ref, count in zip(chosen_refs, counts):
                rows = slice(group * count, (group + 1) * count)
                for u in range(steps):
                    tile = 2 * (chunk * steps + u) + parity
                    here = slice(tile * LANES, (tile + 1) * LANES)
                    ref[rows, here] = picked[first : first + count, u * LANES : (u + 1) * LANES]
                first += count
    for at, (source, target) in enumerate(zip(chosen_refs, target_refs)):
        stores.append(pltpu.make_async_copy(source, target, store_sems.at[chunks + at]))
        stores[-1].start()
    for store in stores:
        store.wait()


def window_loads(firsts, refs, cells, sems):
    loads = []
    for at, (ref, first) in enumerate(zip(refs, firsts)):
        source = ref.at[pl.ds(first, cells.shape[1])]
        loads.append(pltpu.make_async_copy(source, cells.at[at], sems.at[at]))
        loads[-1].start()
    return loads


def filter_parts(weight_ref, table_ref, cells, loads, section, back):
    count, slots, lanes = cells.shape
    padded = weight_ref.shape[2]
    height = table_ref.shape[0] - LANES
    window = height - 64
    pair_lanes = 2 * (height - 128)
    pairs = lanes // pair_lanes
    half = pairs * count
    sums_at = padded - LANES
    for load in loads:
        load.wait()
    for parity in range(2):
        rows = []
        for at in range(count):
            for p in range(pairs):
                lane = p * pair_lanes + parity * (pair_lanes - window)
                rows.append(cells[at, :, lane : lane + window])
        start = 64 * (1 - parity)
        out = jnp.dot(
            jnp.concatenate(rows, axis=0),
            table_ref[start : start + window, :],
            preferred_element_type=jnp.float32,
        )
        sums = out[:, sums_at : sums_at + LANES].astype(jnp.bfloat16)
        out = out + jnp.dot(sums, table_ref[height:, :], preferred_element_type=jnp.float32)
        out = out.astype(jnp.bfloat16).astype(jnp.float32)
        for at in range(half):
            section[2 * at + parity] = out[at * slots : (at + 1) * slots]

    lane_tiles = padded // LANES
    points = weight_ref.shape[1]
    pairs_of, _ = half_set(points)
    mean_at = int(np.flatnonzero((pairs_of == 0).all(axis=1))[0])

    def transform(index, carry):
        row = pl.multiple_of(index // lane_tiles * 16, 16)
        lane = pl.multiple_of(index % lane_tiles * LANES, LANES)
        mean = lane + lax.broadcasted_iota(jnp.int32, (8, LANES), 1) == mean_at
        results = []
        for octet in range(2):
            here = pl.ds(row + 8 * octet, 8)

            def load(i):
                real = section[i, here, pl.ds(lane, LANES)]
                return real, section[i, here, pl.ds(padded + lane, LANES)]

            spectrum = spectrum_of(load)
            per_kernel = []
            for which in range(3):
                weighted = {}
                for a, (real, imag) in spectrum.items():
                    weight = weight_ref[which, pl.ds(a, 1), pl.ds(lane, LANES)]
                    weighted[a] = (real * weight, imag * weight)
                real = weighted[0][0]
                rounded = real.astype(jnp.bfloat16).astype(jnp.float32)
                weighted[0] = (jnp.where(mean, rounded, real), weighted[0][1])
                per_kernel.append(first_half_of(weighted))
            results.append(per_kernel)
        for which in range(3):
            for i in range(half):
                for q in range(2):
                    value = jnp.concatenate([results[o][which][i][q] for o in range(2)], axis=0)
                    back[i % 2, which, i // 2, pl.ds(row, 16), pl.ds(q * padded + lane, LANES)] = (
                        value.astype(jnp.bfloat16)
                    )
        return carry

    lax.fori_loop(0, slots // 16 * lane_tiles, transform, 0)


def inverse_parts(back_table, back):
    _, kernels, pairs, slots, depth = back.shape
    window = back_table.shape[2]
    outs = []
    for parity in range(2):
        out = jnp.dot(
            back[parity].reshape(kernels * pairs * slots, depth),
            back_table[parity, :depth],
            preferred_element_type=jnp.float32,
        )
        first = 0 if parity else window - LANES
        level = out[:, first : first + LANES].astype(jnp.bfloat16)
        out = out + jnp.dot(level, back_table[parity, depth:], preferred_element_type=jnp.float32)
        outs.append(out.reshape(kernels, pairs, slots, window))
    return outs


def terms_of(part, outs, cells_ref, put):
    _, slots, lanes = cells_ref.shape
    window = outs[0].shape[3]
    pair_lanes = 2 * (window - 64)
    pairs = lanes // pair_lanes
    tiles = pair_lanes // LANES
    near = lax.broadcasted_iota(jnp.int32, (slots, LANES), 1) < 64
    for pair in range(pairs):
        at = part * pairs + pair
        for tile in range(tiles):
            lane = tile * LANES
            odd_lane = lane - (pair_lanes - window)
            values = []
            for which in range(3):
                if tile < tiles // 2:
                    value = outs[0][which, at, :, lane : lane + LANES]
                elif tile > tiles // 2:
                    value = outs[1][which, at, :, odd_lane : odd_lane + LANES]
                else:
                    value = jnp.where(
                        near,
                        outs[0][which, at, :, lane : lane + LANES],
                        outs[1][which, at, :, odd_lane : odd_lane + LANES],
                    )
                values.append(value)
            lane = pair * pair_lanes + lane
            cells = cells_ref[part, :, lane : lane + LANES].astype(jnp.float32)
            put(pair * tiles + tile, (values[0] * values[1] - cells * values[2]).astype(jnp.bfloat16))


def collide_kernel(firsts, weight_ref, table_ref, back_any, *refs):
    parts = len(firsts) // 2
    terms_ref, cells, section, back, back_table, sems = refs[2 * parts :]
    lanes = cells.shape[2]
    loads = window_loads(firsts, refs[: 2 * parts], cells, sems)
    table_load = pltpu.make_async_copy(back_any, back_table, sems.at[2 * parts])
    table_load.start()
    filter_parts(weight_ref, table_ref, cells, loads, section, back)
    table_load.wait()
    outs = inverse_parts(back_table, back)
    for part in range(parts):

        def put(tile, value):
            first = part * lanes + tile * LANES
            terms_ref[:, first : first + LANES] = value

        terms_of(part, outs, cells, put)


def finish_kernel(firsts, sizes, weight_ref, table_ref, back_any, spread_any, *refs):
    parts = len(firsts) // 2
    term_refs, refs = refs[: len(sizes) - 1], refs[len(sizes) - 1 :]
    first_read, rest_read = refs[2 * parts : 2 * parts + 2]
    out_ref, cells, section, back, back_table, reads, spots, added, staged = refs[2 * parts + 2 : -6]
    spread_ref, early_ref, cell_sems, read_sems, out_sems, extra_sems = refs[-6:]
    width_x, width_y, width_z, lanes = staged.shape[1:]
    tiles = lanes // LANES
    loads = window_loads(firsts, refs[: 2 * parts], cells, cell_sems)
    extra = [pltpu.make_async_copy(spread_any, spread_ref, extra_sems.at[0])]
    at = 0
    for ref, size in zip(term_refs, sizes):
        target = early_ref.at[pl.ds(at, size)]
        extra.append(pltpu.make_async_copy(ref, target, extra_sems.at[len(extra)]))
        at += size
    extra.append(pltpu.make_async_copy(back_any, back_table, cell_sems.at[2 * parts]))
    group_rows = reads.shape[2]
    read_loads = []
    for part in range(parts):
        rows = pl.ds(max(part - 1, 0) * group_rows, group_rows)
        source = (rest_read if part else first_read).at[:, rows, :]
        read_loads.append(pltpu.make_async_copy(source, reads.at[part], read_sems.at[part]))
    for load in extra + read_loads:
        load.start()
    filter_parts(weight_ref, table_ref, cells, loads, section, back)
    for load in extra:
        load.wait()
    early = early_ref.shape[0]
    capacity = early + section.shape[1]
    outs = inverse_parts(back_table, back)
    pieces = out_sems.shape[1]
    piece_x = width_x // pieces
    stores = []
    for part in range(parts):

        def put(tile, value):
            first = tile % 2 * capacity
            columns = slice(tile // 2 * LANES, (tile // 2 + 1) * LANES)
            lane = part * lanes + tile * LANES
            spots[first : first + early, columns] = early_ref[:, lane : lane + LANES]
            spots[first + early : first + capacity, columns] = value

        terms_of(part, outs, cells, put)
        added[...] = jnp.dot(spread_ref[...], spots[...], preferred_element_type=jnp.float32)
        read_loads[part].wait()
        slot = part % 2
        if part >= 2:
            for store in stores[part - 2]:
                store.wait()

        def add(x, carry):
            for y in range(width_y):
                row = x * width_y + y
                at = pl.multiple_of(row * 8, 8)
                for u in range(tiles // 2):
                    value = (
                        reads[part, row, 8 * u : 8 * u + 8, :]
                        + added[pl.ds(at, 8), u * LANES : (u + 1) * LANES]
                    )
                    for parity in range(2):
                        lane = (2 * u + parity) * LANES
                        half = value[parity * width_z : (parity + 1) * width_z]
                        staged[slot, x, y, :, lane : lane + LANES] = half
            return carry

        stores.append([])
        for piece in range(pieces):
            lax.fori_loop(piece * piece_x, (piece + 1) * piece_x, add, 0)
            rows = pl.ds(piece * piece_x, piece_x)
            store = pltpu.make_async_copy(
                staged.at[slot, rows],
                out_ref.at[rows, :, :, pl.ds(part * lanes, lanes)],
                out_sems.at[part, piece],
            )
            store.start()
            stores[part].append(store)
    for part in range(max(parts - 2, 0), parts):
        for store in stores[part]:
            store.wait()


def params(mib):
    return pltpu.CompilerParams(vmem_limit_bytes=mib * 2**20)


def cost(flops, size):
    return pl.CostEstimate(flops=flops, bytes_accessed=size, transcendentals=0)


def fast_fits(distribution, points):
    width_x, width_y, width_z, local_vel = distribution.shape
    group = PLANES * points * points
    return (
        points == 24
        and lax.axis_size("vel") == 2
        and width_z == 4
        and local_vel * 2 == points**3
        and local_vel == 3 * group
        and width_x * width_y * width_z % 128 == 0
    )


def fast_device(distribution, refine_level, gain_one, gain_two, loss_kernel):
    points = gain_one.shape[0]
    width_x, width_y, width_z, local_vel = distribution.shape
    block_rows = width_x * width_y
    block_cells = block_rows * width_z
    group = PLANES * points * points
    parts = local_vel // group
    group_rows = group // LANES * width_z
    steps = group_rows // 8
    capacity = block_cells // 2
    early_count = capacity // 2 // 16 * 16
    counts = (early_count, capacity - early_count)
    batches = len(counts)
    vel_at = lax.axis_index("vel")
    count_x, count_y = lax.axis_size("cx"), lax.axis_size("cy")

    tiles = local_vel // LANES
    speeds = jnp.asarray(plane_speeds(points, local_vel, width_z))
    falls = np.arange(group) // points % points < points // 2
    falls = np.repeat(falls.reshape(-1, 1, LANES), width_z, axis=1).reshape(-1, LANES)
    falls = jnp.asarray(falls.astype(np.float32))
    side = vel_at.reshape(1).astype(jnp.int32)
    edge = jnp.where(vel_at == 0, 0, width_x - 1).reshape(1).astype(jnp.int32)

    level = refine_level.reshape(block_cells)
    active = level > 0
    cell_at = jnp.arange(block_cells, dtype=jnp.int32)
    before = (cell_at[:, None] < cell_at[None, :]) & active[:, None]
    slot_index = jnp.where(active, jnp.sum(before.astype(jnp.int32), axis=0), -1)
    spot = slot_index.reshape(block_rows, 1, width_z)
    parity = jnp.arange(2, dtype=jnp.int32)[None, :, None]
    shape = (block_rows, 2, width_z)
    wanted = jnp.where(spot >= 0, spot + capacity * parity, -1)
    wanted = jnp.broadcast_to(wanted, shape).reshape(-1)
    numbers = jnp.arange(2 * capacity, dtype=jnp.int32)
    wanted_rows = jnp.broadcast_to(wanted[None, :], (8, wanted.shape[0]))
    strength = jnp.broadcast_to(
        (0.25 * level.astype(jnp.float32)).reshape(block_rows, 1, width_z), shape
    ).reshape(-1)
    spread = jnp.where(wanted[:, None] == numbers[None, :], strength[:, None], 0.0)
    spread = spread.astype(jnp.bfloat16)

    padded = -(-len(half_set(points)[1]) // LANES) * LANES
    select, scale = frequency_select(points, padded)
    table, back_table = [jnp.asarray(t) for t in plane_table(points, padded, 64)]

    towards_lower = [(j, (j - 1) % count_y) for j in range(count_y)]
    towards_upper = [(j, (j + 1) % count_y) for j in range(count_y)]
    across_pairs = [(i, (i - 1) % count_x) for i in range(count_x)]
    across_pairs += [(count_x + i, count_x + (i + 1) % count_x) for i in range(count_x)]
    swap = [(0, 1), (1, 0)]
    bf16 = jnp.bfloat16

    half_steps = steps // 2 + 1
    local = pl.BlockSpec(memory_space=pltpu.VMEM)
    scalar = pl.BlockSpec(memory_space=pltpu.SMEM)
    remote = pl.BlockSpec(memory_space=pltpu.HBM)
    anywhere = pl.BlockSpec(memory_space=pl.ANY)

    def edges_of(first, groups):
        return pl.pallas_call(
            functools.partial(edges_kernel, first * group),
            in_specs=[scalar, local, remote],
            out_specs=[local] * 3,
            out_shape=[
                jax.ShapeDtypeStruct((groups * half_steps, width_x * 8, LANES), bf16),
                jax.ShapeDtypeStruct((groups * half_steps, width_x * 8, LANES), bf16),
                jax.ShapeDtypeStruct((groups * steps, width_y * 8, LANES), bf16),
            ],
            scratch_shapes=[
                pltpu.VMEM((width_x, 1, width_z, groups * group), jnp.float32),
                pltpu.VMEM((width_x, 1, width_z, groups * group), jnp.float32),
                pltpu.VMEM((1, width_y, width_z, groups * group), jnp.float32),
                pltpu.SemaphoreType.DMA((3,)),
            ],
            compiler_params=params(LIMIT),
            cost_estimate=cost(1, 1),
            name="edges",
        )(edge, falls, distribution)

    edges = [edges_of(0, 1), edges_of(1, parts - 1)]
    wide = 3
    chunks = steps // wide

    def upwind(at, halo, sizes):
        groups = parts - 1 if at else 1
        operands = (speeds, wanted_rows, *halo)
        local_speeds = jax.ShapeDtypeStruct((3, groups * group_rows, LANES), jnp.float32)
        chosen = [(groups * size, group) for size in sizes]
        return pl.pallas_call(
            functools.partial(upwind_kernel, at * group, sizes),
            in_specs=[scalar] + [anywhere] * (len(operands) + 1),
            out_specs=[anywhere] * (1 + len(sizes)),
            out_shape=[
                jax.ShapeDtypeStruct((block_rows, groups * group_rows, LANES), jnp.float32)
            ]
            + [jax.ShapeDtypeStruct(shape, bf16) for shape in chosen],
            scratch_shapes=[pltpu.VMEM(x.shape, x.dtype) for x in (local_speeds, *operands[1:])]
            + [pltpu.VMEM(shape, bf16) for shape in chosen]
            + [
                pltpu.VMEM((2 * capacity, block_rows * 8), bf16),
                pltpu.VMEM(
                    (groups * chunks, width_x, width_y, width_z, group // chunks), jnp.float32
                ),
                pltpu.VMEM((groups * chunks, block_rows, 8 * wide, LANES), jnp.float32),
                pltpu.VMEM((wide, width_x + 2, width_y, 8, LANES), jnp.float32),
                pltpu.VMEM((wide, width_x, 8, LANES), jnp.float32),
                pltpu.VMEM((block_rows * 8, wide * LANES), bf16),
                pltpu.SemaphoreType.DMA((groups * chunks,)),
                pltpu.SemaphoreType.DMA((groups * chunks + len(sizes),)),
                pltpu.SemaphoreType.DMA((len(operands),)),
            ],
            compiler_params=params(LIMIT),
            cost_estimate=cost(1, 1),
            name="upwind",
        )(side, *operands, distribution)

    def turn(value, *earlier):
        return lax.optimization_barrier((value, *earlier))[0]

    def swapped(value):
        return lax.ppermute(value, "vel", swap)

    halos = []
    for at in range(2):
        down, up, across = edges[at]
        halos.append(
            (
                lax.ppermute(down, "cy", towards_lower),
                lax.ppermute(up, "cy", towards_upper),
                lax.ppermute(across, ("vel", "cx"), across_pairs),
            )
        )
    first_read, *first = upwind(0, turn(halos[0], edges[1]), counts)
    first_other = [swapped(x) for x in first]
    rest_read, *rest = upwind(1, turn(halos[1], first), counts)
    kernels = turn((gain_one, gain_two, loss_kernel), halos[0])
    weights = pl.pallas_call(
        weights_kernel,
        out_shape=jax.ShapeDtypeStruct((3, points, padded), jnp.float32),
        compiler_params=params(LIMIT),
        cost_estimate=cost(1, 1),
        name="weights",
    )(
        jnp.concatenate([k.reshape(points, points * points) for k in kernels], axis=0),
        jnp.asarray(select),
        jnp.asarray(scale),
    )

    operand, weights, spread = turn((rest[0], weights, spread), first_other)
    others = [swapped(operand)]

    def scratch(count):
        return [
            pltpu.VMEM((2 * parts, count, group), bf16),
            pltpu.VMEM((points, count, 2 * padded), jnp.float32),
            pltpu.VMEM((2, 3, points // 4, count, 2 * padded), bf16),
            pltpu.VMEM(back_table.shape, bf16),
        ]

    sems = pltpu.SemaphoreType.DMA((2 * parts + 1,))
    terms = []
    for batch in range(batches - 1):
        count = counts[batch]
        starts = (0,) + tuple(g * count for g in range(parts - 1))
        following = turn(rest[batch + 1], others[-1], *terms)
        others.append(swapped(following))
        terms.append(
            pl.pallas_call(
                functools.partial(collide_kernel, starts + starts),
                in_specs=[local] * 2 + [anywhere] * (1 + 2 * parts),
                out_specs=local,
                out_shape=jax.ShapeDtypeStruct((count, local_vel), bf16),
                scratch_shapes=scratch(count) + [sems],
                compiler_params=params(34),
                cost_estimate=cost(1, 1),
                name="collide",
            )(
                weights,
                table,
                back_table,
                first[batch],
                *[rest[batch]] * (parts - 1),
                first_other[batch],
                *[others[batch]] * (parts - 1),
            )
        )

    pieces = 4
    count = counts[-1]
    starts = (0,) + tuple(g * count for g in range(parts - 1))
    return pl.pallas_call(
        functools.partial(finish_kernel, starts + starts, counts),
        in_specs=[local] * 2 + [anywhere] * (1 + batches + 2 * parts + 2),
        out_specs=anywhere,
        out_shape=jax.ShapeDtypeStruct(distribution.shape, jnp.float32),
        scratch_shapes=scratch(count)
        + [
            pltpu.VMEM((parts, block_rows, group_rows, LANES), jnp.float32),
            pltpu.VMEM((2 * capacity, group // 2), bf16),
            pltpu.VMEM((block_rows * 8, group // 2), jnp.float32),
            pltpu.VMEM((2, width_x, width_y, width_z, group), jnp.float32),
            pltpu.VMEM(spread.shape, bf16),
            pltpu.VMEM((capacity - count, local_vel), bf16),
            sems,
            pltpu.SemaphoreType.DMA((parts,)),
            pltpu.SemaphoreType.DMA((parts, pieces)),
            pltpu.SemaphoreType.DMA((batches,)),
        ],
        compiler_params=params(LIMIT),
        name="finish",
    )(
        weights,
        table,
        back_table,
        spread,
        *terms,
        first[-1],
        *[rest[-1]] * (parts - 1),
        first_other[-1],
        *[others[-1]] * (parts - 1),
        first_read,
        rest_read,
    )


def per_device(distribution, refine_level, gain_one, gain_two, loss_kernel):
    if fast_fits(distribution, gain_one.shape[0]):
        return fast_device(distribution, refine_level, gain_one, gain_two, loss_kernel)
    return plain_device(distribution, refine_level, gain_one, gain_two, loss_kernel)


def solution(mesh):
    placed = (P("cx", "cy", None, "vel"), P("cx", "cy", None), P(), P(), P())
    return jax.shard_map(
        per_device,
        mesh=mesh,
        in_specs=placed,
        out_specs=P("cx", "cy", None, "vel"),
        check_vma=False,
    )
```

```python
import functools
import math

import jax
import jax.numpy as jnp
import ml_dtypes
import numpy as np
from jax import lax
from jax.experimental import pallas as pl
from jax.experimental.pallas import tpu as pltpu
from jax.sharding import PartitionSpec as P


def extended(array, sides, width):
    for axis, dim in sides:
        count, length = (lax.axis_size(axis), array.shape[dim])
        up = [(i, (i + 1) % count) for i in range(count)]
        down = [(j, i) for i, j in up]
        last = lax.slice_in_dim(array, length - width, length, axis=dim)
        leading = lax.slice_in_dim(array, 0, width, axis=dim)
        before = lax.ppermute(last, axis, up)
        after = lax.ppermute(leading, axis, down)
        array = jnp.concatenate([before, array, after], axis=dim)
    return array


def dft_tables(points):
    indices = jnp.arange(points, dtype=jnp.int32)
    products = indices[:, None] * indices[None, :] % points
    angles = products.astype(jnp.float32) * (2.0 * math.pi / points)
    cosine = jnp.cos(angles)
    sine_table = jnp.sin(angles)
    forward = jnp.stack([jnp.stack([cosine, sine_table]), jnp.stack([-sine_table, cosine])])
    inverse = jnp.stack([jnp.stack([cosine, -sine_table]), jnp.stack([sine_table, cosine])])
    return (forward.astype(jnp.bfloat16), inverse.astype(jnp.bfloat16))


def contract(pattern, left_side, right_side):
    return jnp.einsum(pattern, left_side, right_side, preferred_element_type=jnp.float32)


def collide(cells, forward, inverse, gain_one, gain_two, loss_kernel):
    points = forward.shape[-1]
    cell_count = cells.shape[0]
    field = cells.reshape(cell_count, points, points, points)
    section_z = contract("nabz,qzw->qnabw", field, forward[:, 0]).astype(jnp.bfloat16)
    section_y = contract("pnayc,qpyw->qnawc", section_z, forward).astype(jnp.bfloat16)
    spectrum = contract("pnxbc,qpxw->qnwbc", section_y, forward)
    scale_factor = 1.0 / float(points**3)

    def filtered(kernel):
        weighted = (spectrum * (kernel * scale_factor)[None, None]).astype(jnp.bfloat16)
        back_x = contract("pnxbc,qpxw->qnwbc", weighted, inverse).astype(jnp.bfloat16)
        back_y = contract("pnayc,qpyw->qnawc", back_x, inverse).astype(jnp.bfloat16)
        return contract("pnabz,pzw->nabw", back_y, inverse[0])

    gain_term = filtered(gain_one) * filtered(gain_two)
    result = gain_term - field.astype(jnp.float32) * filtered(loss_kernel)
    return result.reshape(cell_count, points**3)


def courants(points, first_vel, local_count):
    vel_index = first_vel + jnp.arange(local_count, dtype=jnp.int32)
    index_x = vel_index // (points * points)
    index_y = vel_index // points % points
    index_z = vel_index % points

    def speed(index_part):
        return 0.3 * (2.0 * index_part.astype(jnp.float32) - (points - 1)) / (points - 1)

    return (speed(index_x), speed(index_y), speed(index_z))


def upwind_flux(courant, center, lower_side, upper_side):
    return jnp.maximum(courant, 0.0) * (center - lower_side) + jnp.minimum(courant, 0.0) * (
        upper_side - center
    )


def plain_device(distribution, refine_level, gain_one, gain_two, loss_kernel):
    points = gain_one.shape[0]
    width_x, width_y, width_z, local_vel = distribution.shape
    first_vel = lax.axis_index("vel") * local_vel
    courant_x, courant_y, courant_z = courants(points, first_vel, local_vel)
    padded = extended(distribution, (("cx", 0), ("cy", 1)), 1)
    fluxes = upwind_flux(courant_x, distribution, padded[:-2, 1:-1], padded[2:, 1:-1])
    fluxes = fluxes + upwind_flux(courant_y, distribution, padded[1:-1, :-2], padded[1:-1, 2:])
    fluxes = fluxes + upwind_flux(
        courant_z, distribution, jnp.roll(distribution, 1, 2), jnp.roll(distribution, -1, 2)
    )
    read = distribution - fluxes
    block_cells = width_x * width_y * width_z
    groups = lax.axis_size("vel")
    flattened = read.reshape(block_cells, local_vel).astype(jnp.bfloat16)
    forward, inverse = dft_tables(points)
    active = refine_level.reshape(block_cells) > 0
    slot_index = jnp.cumsum(active.astype(jnp.int32)) - 1
    capacity = block_cells // 2
    picker = (
        (slot_index[None, :] == jnp.arange(capacity, dtype=jnp.int32)[:, None]) & active[None, :]
    ).astype(jnp.bfloat16)
    chosen = jnp.dot(picker, flattened, preferred_element_type=jnp.float32).astype(jnp.bfloat16)
    terms = collide(
        lax.all_to_all(
            chosen.reshape(groups, capacity // groups, local_vel),
            "vel",
            split_axis=0,
            concat_axis=2,
            tiled=True,
        )[0],
        forward,
        inverse,
        gain_one,
        gain_two,
        loss_kernel,
    )[None]
    packed = lax.all_to_all(
        terms.astype(jnp.bfloat16), "vel", split_axis=2, concat_axis=0, tiled=True
    ).astype(terms.dtype)
    packed_rows = packed.reshape(capacity, local_vel)
    safe_slot = jnp.clip(slot_index, 0, capacity - 1)
    rates = jnp.where(active[:, None], packed_rows[safe_slot], 0.0)
    weight = 0.25 * refine_level.astype(jnp.float32)
    return read + weight[..., None] * rates.reshape(width_x, width_y, width_z, local_vel)

LANES = 128
PLANES = 4
LIMIT = 57


def half_set(points):
    middle = points // 2
    pairs = [(b, c) for c in range(1, middle) for b in range(points)]
    pairs += [(b, c) for c in (0, middle) for b in range(middle + 1)]
    weights = [1.0 if b % middle == 0 and c % middle == 0 else 2.0 for b, c in pairs]
    return np.array(pairs), np.array(weights)


def plane_table(points, padded, margin):
    pairs, _ = half_set(points)
    first, second = np.divmod(np.arange(points * points), points)
    index = np.arange(points)
    angles = (index[:, None] * index[None, :] % points).astype(np.float32)
    angles = angles * np.float32(2.0 * np.pi / points)
    cosine, sine = [
        t.astype(ml_dtypes.bfloat16).astype(np.float32) for t in (np.cos(angles), np.sin(angles))
    ]
    cos_y, sin_y = cosine[first][:, pairs[:, 0]], sine[first][:, pairs[:, 0]]
    cos_z, sin_z = cosine[second][:, pairs[:, 1]], sine[second][:, pairs[:, 1]]
    table = np.zeros((points * points + 2 * margin, 2 * padded), np.float32)
    rows = slice(margin, margin + points * points)
    table[rows, : len(pairs)] = cos_y * cos_z - sin_y * sin_z
    table[rows, padded : padded + len(pairs)] = -(cos_y * sin_z + sin_y * cos_z)
    window = points * points + margin
    level = np.flatnonzero(pairs[:, 1] == 0)
    rest = table.copy()
    rest[:, np.concatenate([level, padded + level])] = 0.0
    for start in (points * points + margin, 0):
        rest[start : start + points, level] = cosine[:, pairs[level, 0]]
        rest[start : start + points, padded + level] = -sine[:, pairs[level, 0]]
    back = np.stack([rest[margin : margin + window].T, rest[:window].T])
    copies = np.zeros((2, LANES, window), np.float32)
    place = np.arange(points * points)
    copies[0, (points * points + first) % LANES, place] = 1.0
    copies[1, first, margin + place] = 1.0
    back = np.concatenate([back, copies], axis=1)
    spare = len(pairs)
    lift = np.zeros((LANES, 2 * padded), np.float32)
    for half in (0, padded):
        columns = slice(spare % LANES, spare % LANES + points)
        lift[columns, half + level] = table[margin : margin + points**2 : points, half + level]
        table[:, half + level] = 0.0
    table[margin + place, spare + first] = 1.0
    table = np.concatenate([table, lift])
    return table.astype(ml_dtypes.bfloat16), back.astype(ml_dtypes.bfloat16)


def frequency_select(points, padded):
    pairs, weights = half_set(points)
    select = np.zeros((points * points, 2 * padded), np.float32)
    column = np.arange(len(pairs))
    select[pairs[:, 0] * points + pairs[:, 1], column] = 1.0
    mirror = (-pairs[:, 0]) % points * points + (-pairs[:, 1]) % points
    select[mirror, padded + column] = 1.0
    scale = np.zeros((1, padded), np.float32)
    scale[0, : len(pairs)] = 0.5 * weights / points**3
    return select.astype(ml_dtypes.bfloat16), scale


def weights_kernel(stacked_ref, select_ref, scale_ref, out_ref):
    kernels, points, padded = out_ref.shape
    rest = stacked_ref[...]
    picked = None
    for _ in range(3):
        piece = rest.astype(jnp.bfloat16)
        rest = rest - piece.astype(jnp.float32)
        part = jnp.dot(piece, select_ref[...], preferred_element_type=jnp.float32)
        picked = part if picked is None else picked + part
    for which in range(kernels):
        for a in range(points):
            row, mirror = which * points + a, which * points + (-a) % points
            both = picked[row : row + 1, :padded] + picked[mirror : mirror + 1, padded:]
            out_ref[which, a : a + 1, :] = both * scale_ref[...]


def transform_3(x, sign, wanted=(0, 1, 2)):
    (ar, ai), (br, bi), (cr, ci) = x
    sr, si = br + cr, bi + ci
    out = {}
    if 0 in wanted:
        out[0] = (ar + sr, ai + si)
    if 1 in wanted or 2 in wanted:
        height = sign * math.sqrt(0.75)
        mr, mi = ar - 0.5 * sr, ai - 0.5 * si
        er, ei = height * (br - cr), height * (bi - ci)
        if 1 in wanted:
            out[1] = (mr - ei, mi + er)
        if 2 in wanted:
            out[2] = (mr + ei, mi - er)
    return out


def transform_4(x, sign):
    (ar, ai), (br, bi), (cr, ci), (dr, di) = x
    pr, pi, qr, qi = ar + cr, ai + ci, ar - cr, ai - ci
    sr, si, tr, ti = br + dr, bi + di, br - dr, bi - di
    if sign < 0:
        tr, ti = -tr, -ti
    return [(pr + sr, pi + si), (qr - ti, qi + tr), (pr - sr, pi - si), (qr + ti, qi - tr)]


def transform_8(x, sign):
    even = transform_4(x[0::2], sign)
    odd = transform_4(x[1::2], sign)
    root = math.sqrt(0.5)
    (r0, i0), (r1, i1), (r2, i2), (r3, i3) = odd
    if sign > 0:
        turned = [(r0, i0), (root * (r1 - i1), root * (i1 + r1)), (-i2, r2)]
        turned.append((-root * (r3 + i3), root * (r3 - i3)))
    else:
        turned = [(r0, i0), (root * (r1 + i1), root * (i1 - r1)), (i2, -r2)]
        turned.append((root * (i3 - r3), -root * (i3 + r3)))
    low = [(e[0] + t[0], e[1] + t[1]) for e, t in zip(even, turned)]
    high = [(e[0] - t[0], e[1] - t[1]) for e, t in zip(even, turned)]
    return low + high


def spectrum_of(load):
    stage = {}
    for n2 in range(8):
        part = transform_3([load((8 * n1 + 3 * n2) % 24) for n1 in range(3)], -1)
        for k1 in range(3):
            stage[k1, n2] = part[k1]
    result = {}
    for k1 in range(3):
        part = transform_8([stage[k1, n2] for n2 in range(8)], -1)
        for k2 in range(8):
            result[(16 * k1 + 9 * k2) % 24] = part[k2]
    return result


def first_half_of(spectrum):
    stage = {}
    for k1 in range(3):
        part = transform_8([spectrum[(16 * k1 + 9 * k2) % 24] for k2 in range(8)], 1)
        for n2 in range(8):
            stage[k1, n2] = part[n2]
    result = {}
    for n2 in range(8):
        wanted = {n1: (8 * n1 + 3 * n2) % 24 for n1 in range(3) if (8 * n1 + 3 * n2) % 24 < 12}
        part = transform_3([stage[k1, n2] for k1 in range(3)], 1, tuple(wanted))
        for n1, index in wanted.items():
            result[index] = part[n1]
    return result


def tile_pair(ref, step, rows):
    parts = []
    for parity in range(2):
        at = (2 * step + parity) * LANES
        part = ref[:, :, :, at : at + LANES]
        parts.append(part.reshape(rows, part.shape[2], LANES))
    return jnp.concatenate(parts, axis=1)


def plane_speeds(points, local_vel, width_z):
    index = np.arange(points**3)
    parts = (index // (points * points), index // points % points, index % points)
    speeds = [
        np.float32(0.3) * (np.float32(2.0) * part.astype(np.float32) - np.float32(points - 1))
        / np.float32(points - 1)
        for part in parts
    ]
    tiled = np.stack(speeds).reshape(3, -1, local_vel // LANES, 1, LANES).transpose(1, 0, 2, 3, 4)
    repeated = np.repeat(tiled, width_z, axis=3)
    return repeated.reshape(repeated.shape[0], 3, -1, LANES)


def edges_kernel(first, edge_ref, falls_ref, field_ref, *refs):
    down_ref, up_ref, across_ref, low_ref, high_ref, plane_ref, sems = refs
    steps = falls_ref.shape[0] // 8
    width = low_ref.shape[0]
    groups = across_ref.shape[0] // steps
    half_steps = down_ref.shape[0] // groups
    here = pl.ds(first, low_ref.shape[3])
    last_y = field_ref.shape[1] - 1
    sources = [
        field_ref.at[:, pl.ds(0, 1), :, here],
        field_ref.at[:, pl.ds(last_y, 1), :, here],
        field_ref.at[pl.ds(edge_ref[0], 1), :, :, here],
    ]
    loads = [
        pltpu.make_async_copy(source, ref, sems.at[at])
        for at, (source, ref) in enumerate(zip(sources, (low_ref, high_ref, plane_ref)))
    ]
    for load in loads:
        load.start()
    below = [falls_ref[8 * s : 8 * s + 8, :][None] > 0.0 for s in range(steps)]

    def put(ref, at, value):
        ref[at] = value.reshape(-1, LANES).astype(jnp.bfloat16)

    loads[0].wait()
    for g in range(groups):
        row = [tile_pair(low_ref, g * steps + s, width) for s in range(steps)]
        put(down_ref, g * half_steps, row[0])
        for m in range(1, steps // 2 + 1):
            put(down_ref, g * half_steps + m, jnp.where(below[2 * m - 1], row[2 * m - 1], row[2 * m]))
    loads[1].wait()
    for g in range(groups):
        row = [tile_pair(high_ref, g * steps + s, width) for s in range(steps)]
        for m in range(steps // 2):
            put(up_ref, g * half_steps + m, jnp.where(below[2 * m], row[2 * m + 1], row[2 * m]))
        put(up_ref, g * half_steps + steps // 2, row[steps - 1])
    loads[2].wait()
    for s in range(groups * steps):
        put(across_ref, s, tile_pair(plane_ref, s, plane_ref.shape[1]))


def upwind_kernel(base, counts, side_ref, *refs):
    batches = len(counts)
    outer_refs, field_ref = refs[:5], refs[5]
    out_ref, target_refs, scratch = refs[6], refs[7 : 7 + batches], refs[7 + batches :]
    inner_refs, chosen_refs, scratch = scratch[:5], scratch[5 : 5 + batches], scratch[5 + batches :]
    speed_ref, wanted_ref, down_ref, up_ref, across_ref = inner_refs
    picker_ref, blocks, reads, wide, border, cells, load_sems, store_sems, side_sems = scratch
    chunks, width_x, width_y, width_z, lanes = blocks.shape
    steps = lanes // (2 * LANES)
    group_lanes = chosen_refs[0].shape[1]
    per_group = group_lanes // lanes
    half_steps = per_group * steps // 2 + 1
    first_row = base // LANES * width_z
    rows = pl.ds(first_row, speed_ref.shape[1])
    sources = (outer_refs[0].at[side_ref[0], :, rows, :],) + outer_refs[1:]
    inputs = [
        pltpu.make_async_copy(source, target, side_sems.at[at])
        for at, (source, target) in enumerate(zip(sources, inner_refs))
    ]
    for copy in inputs:
        copy.start()
    loads = []
    for t in range(chunks):
        source = field_ref.at[:, :, :, pl.ds(base + t * lanes, lanes)]
        loads.append(pltpu.make_async_copy(source, blocks.at[t], load_sems.at[t]))
    for load in loads[:2]:
        load.start()
    beside = jnp.where(side_ref[0] == 0, 2, 0)
    place = lax.broadcasted_iota(jnp.int32, (1, 8, LANES), 1) % width_z
    capacity = picker_ref.shape[0] // 2
    stores = []
    for copy in inputs:
        copy.wait()
    number = lax.broadcasted_iota(jnp.int32, picker_ref.shape, 0)
    matches = number == wanted_ref[0:1, :]
    picker_ref[...] = jnp.where(matches, 1.0, 0.0).astype(jnp.bfloat16)
    for t in range(chunks):
        group, chunk = t // per_group, t % per_group
        sizes, falls, sinks = [], [], []
        for u in range(steps):
            step = chunk * steps + u
            row = 8 * (t * steps + u)
            speed = [speed_ref[d, row : row + 8, :][None] for d in range(3)]
            sizes.append([jnp.abs(c) for c in speed])
            falls.append(speed[1] < 0.0)
            sinks.append(speed[2] < 0.0)
            outer = across_ref[t * steps + u].astype(jnp.float32).reshape(width_y, 8, LANES)
            wide[u, 0] = outer
            wide[u, width_x + 1] = outer
            above = down_ref[group * half_steps + (step + 1) // 2].astype(jnp.float32)
            under = up_ref[group * half_steps + step // 2].astype(jnp.float32)
            shape = (width_x, 8, LANES)
            border[u] = jnp.where(falls[u], above.reshape(shape), under.reshape(shape))
        loads[t].wait()
        if t + 2 < chunks:
            loads[t + 2].start()

        def spread_out(x, carry):
            for u in range(steps):
                at = 2 * u * LANES
                parts = [
                    blocks[t, x, :, :, at + p * LANES : at + (p + 1) * LANES] for p in range(2)
                ]
                wide[u, x + 1] = jnp.concatenate(parts, axis=1)
            return carry

        lax.fori_loop(0, width_x, spread_out, 0, unroll=4)

        def advance(x, carry):
            for u in range(steps):
                field = wide[u, x + 1]
                edge = border[u, pl.ds(x, 1)]
                fluxes = sizes[u][0] * (field - wide[u, x + beside])
                beside_y = jnp.where(
                    falls[u],
                    jnp.concatenate([field[1:], edge], axis=0),
                    jnp.concatenate([edge, field[:-1]], axis=0),
                )
                fluxes = fluxes + sizes[u][1] * (field - beside_y)
                turned = pltpu.roll(field, 4, 1)
                upper = pltpu.roll(jnp.where(place == 0, turned, field), 7, 1)
                lower = pltpu.roll(jnp.where(place == width_z - 1, turned, field), 1, 1)
                fluxes = fluxes + sizes[u][2] * (field - jnp.where(sinks[u], upper, lower))
                read = field - fluxes
                reads[t, pl.ds(x * width_y, width_y), 8 * u : 8 * u + 8, :] = read
                rows = width_y * 8
                at = pl.multiple_of(x * rows, rows)
                cells[pl.ds(at, rows), u * LANES : (u + 1) * LANES] = read.reshape(
                    rows, LANES
                ).astype(jnp.bfloat16)
            return carry

        lax.fori_loop(0, width_x, advance, 0, unroll=4)
        target = out_ref.at[:, pl.ds(8 * steps * t, 8 * steps), :]
        stores.append(pltpu.make_async_copy(reads.at[t], target, store_sems.at[t]))
        stores[-1].start()
        picked = jnp.dot(
            picker_ref[...], cells[...], preferred_element_type=jnp.float32
        ).astype(jnp.bfloat16)
        for parity in range(2):
            first = parity * capacity
            for ref, count in zip(chosen_refs, counts):
                rows = slice(group * count, (group + 1) * count)
                for u in range(steps):
                    tile = 2 * (chunk * steps + u) + parity
                    here = slice(tile * LANES, (tile + 1) * LANES)
                    ref[rows, here] = picked[first : first + count, u * LANES : (u + 1) * LANES]
                first += count
    for at, (source, target) in enumerate(zip(chosen_refs, target_refs)):
        stores.append(pltpu.make_async_copy(source, target, store_sems.at[chunks + at]))
        stores[-1].start()
    for store in stores:
        store.wait()


def window_loads(firsts, refs, cells, sems):
    loads = []
    for at, (ref, first) in enumerate(zip(refs, firsts)):
        source = ref.at[pl.ds(first, cells.shape[1])]
        loads.append(pltpu.make_async_copy(source, cells.at[at], sems.at[at]))
        loads[-1].start()
    return loads


def filter_parts(weight_ref, table_ref, cells, loads, later, section, back):
    count, slots, lanes = cells.shape
    padded = weight_ref.shape[2]
    height = table_ref.shape[0] - LANES
    window = height - 64
    pair_lanes = 2 * (height - 128)
    pairs = lanes // pair_lanes
    half = pairs * count
    sums_at = padded - LANES
    for load in loads:
        load.wait()
    for load in later:
        load.start()
    for parity in range(2):
        rows = []
        for at in range(count):
            for p in range(pairs):
                lane = p * pair_lanes + parity * (pair_lanes - window)
                rows.append(cells[at, :, lane : lane + window])
        start = 64 * (1 - parity)
        out = jnp.dot(
            jnp.concatenate(rows, axis=0),
            table_ref[start : start + window, :],
            preferred_element_type=jnp.float32,
        )
        sums = out[:, sums_at : sums_at + LANES].astype(jnp.bfloat16)
        pieces = []
        for first in (0, padded):
            lift = table_ref[height:, first + sums_at : first + padded]
            lifted = jnp.dot(sums, lift, preferred_element_type=jnp.float32)
            pieces.append(out[:, first : first + sums_at])
            pieces.append(out[:, first + sums_at : first + padded] + lifted)
        lane = 0
        for piece in pieces:
            piece = piece.astype(jnp.bfloat16).astype(jnp.float32)
            here = slice(lane, lane + piece.shape[1])
            for at in range(half):
                section[2 * at + parity, :, here] = piece[at * slots : (at + 1) * slots]
            lane += piece.shape[1]

    lane_tiles = padded // LANES
    points = weight_ref.shape[1]
    pairs_of, _ = half_set(points)
    mean_at = int(np.flatnonzero((pairs_of == 0).all(axis=1))[0])

    def transform(index, carry):
        row = pl.multiple_of(index // lane_tiles * 16, 16)
        lane = pl.multiple_of(index % lane_tiles * LANES, LANES)
        mean = lane + lax.broadcasted_iota(jnp.int32, (8, LANES), 1) == mean_at
        results = []
        for octet in range(2):
            here = pl.ds(row + 8 * octet, 8)

            def load(i):
                real = section[i, here, pl.ds(lane, LANES)]
                return real, section[i, here, pl.ds(padded + lane, LANES)]

            spectrum = spectrum_of(load)
            per_kernel = []
            for which in range(3):
                weighted = {}
                for a, (real, imag) in spectrum.items():
                    weight = weight_ref[which, pl.ds(a, 1), pl.ds(lane, LANES)]
                    weighted[a] = (real * weight, imag * weight)
                real = weighted[0][0]
                rounded = real.astype(jnp.bfloat16).astype(jnp.float32)
                weighted[0] = (jnp.where(mean, rounded, real), weighted[0][1])
                per_kernel.append(first_half_of(weighted))
            results.append(per_kernel)
        for which in range(3):
            for i in range(half):
                for q in range(2):
                    value = jnp.concatenate([results[o][which][i][q] for o in range(2)], axis=0)
                    back[i % 2, which, i // 2, pl.ds(row, 16), pl.ds(q * padded + lane, LANES)] = (
                        value.astype(jnp.bfloat16)
                    )
        return carry

    lax.fori_loop(0, slots // 16 * lane_tiles, transform, 0)


def inverse_parts(back_table, back):
    _, kernels, pairs, slots, depth = back.shape
    window = back_table.shape[2]
    outs = []
    for parity in range(2):
        out = jnp.dot(
            back[parity].reshape(kernels * pairs * slots, depth),
            back_table[parity, :depth],
            preferred_element_type=jnp.float32,
        )
        first = 0 if parity else window - LANES
        level = out[:, first : first + LANES].astype(jnp.bfloat16)
        out = out + jnp.dot(level, back_table[parity, depth:], preferred_element_type=jnp.float32)
        outs.append(out.reshape(kernels, pairs, slots, window))
    return outs


def terms_of(part, outs, cells_ref, put):
    _, slots, lanes = cells_ref.shape
    window = outs[0].shape[3]
    pair_lanes = 2 * (window - 64)
    pairs = lanes // pair_lanes
    tiles = pair_lanes // LANES
    near = lax.broadcasted_iota(jnp.int32, (slots, LANES), 1) < 64
    for pair in range(pairs):
        at = part * pairs + pair
        for tile in range(tiles):
            lane = tile * LANES
            odd_lane = lane - (pair_lanes - window)
            values = []
            for which in range(3):
                if tile < tiles // 2:
                    value = outs[0][which, at, :, lane : lane + LANES]
                elif tile > tiles // 2:
                    value = outs[1][which, at, :, odd_lane : odd_lane + LANES]
                else:
                    value = jnp.where(
                        near,
                        outs[0][which, at, :, lane : lane + LANES],
                        outs[1][which, at, :, odd_lane : odd_lane + LANES],
                    )
                values.append(value)
            lane = pair * pair_lanes + lane
            cells = cells_ref[part, :, lane : lane + LANES].astype(jnp.float32)
            put(pair * tiles + tile, (values[0] * values[1] - cells * values[2]).astype(jnp.bfloat16))


def collide_kernel(firsts, weight_ref, table_ref, back_any, *refs):
    parts = len(firsts) // 2
    terms_ref, cells, section, back, back_table, sems = refs[2 * parts :]
    lanes = cells.shape[2]
    loads = window_loads(firsts, refs[: 2 * parts], cells, sems)
    table_load = pltpu.make_async_copy(back_any, back_table, sems.at[2 * parts])
    filter_parts(weight_ref, table_ref, cells, loads, [table_load], section, back)
    table_load.wait()
    outs = inverse_parts(back_table, back)
    for part in range(parts):

        def put(tile, value):
            first = part * lanes + tile * LANES
            terms_ref[:, first : first + LANES] = value

        terms_of(part, outs, cells, put)


def finish_kernel(firsts, sizes, weight_ref, table_ref, back_any, spread_any, *refs):
    parts = len(firsts) // 2
    term_refs, refs = refs[: len(sizes) - 1], refs[len(sizes) - 1 :]
    first_read, rest_read = refs[2 * parts : 2 * parts + 2]
    out_ref, cells, section, back, back_table, reads, spots, added, staged = refs[2 * parts + 2 : -6]
    spread_ref, early_ref, cell_sems, read_sems, out_sems, extra_sems = refs[-6:]
    width_x, width_y, width_z, lanes = staged.shape[1:]
    tiles = lanes // LANES
    loads = window_loads(firsts, refs[: 2 * parts], cells, cell_sems)
    extra = [pltpu.make_async_copy(spread_any, spread_ref, extra_sems.at[0])]
    at = 0
    for ref, size in zip(term_refs, sizes):
        target = early_ref.at[pl.ds(at, size)]
        extra.append(pltpu.make_async_copy(ref, target, extra_sems.at[len(extra)]))
        at += size
    extra.append(pltpu.make_async_copy(back_any, back_table, cell_sems.at[2 * parts]))
    group_rows = reads.shape[2]
    read_loads = []
    for part in range(parts):
        rows = pl.ds(max(part - 1, 0) * group_rows, group_rows)
        source = (rest_read if part else first_read).at[:, rows, :]
        read_loads.append(pltpu.make_async_copy(source, reads.at[part], read_sems.at[part]))
    filter_parts(weight_ref, table_ref, cells, loads, extra + read_loads, section, back)
    for load in extra:
        load.wait()
    early = early_ref.shape[0]
    capacity = early + section.shape[1]
    outs = inverse_parts(back_table, back)
    pieces = out_sems.shape[1]
    piece_x = width_x // pieces
    stores = []
    for part in range(parts):

        def put(tile, value):
            first = tile % 2 * capacity
            columns = slice(tile // 2 * LANES, (tile // 2 + 1) * LANES)
            lane = part * lanes + tile * LANES
            spots[first : first + early, columns] = early_ref[:, lane : lane + LANES]
            spots[first + early : first + capacity, columns] = value

        terms_of(part, outs, cells, put)
        added[...] = jnp.dot(spread_ref[...], spots[...], preferred_element_type=jnp.float32)
        read_loads[part].wait()
        slot = part % 2
        if part >= 2:
            for store in stores[part - 2]:
                store.wait()

        def add(x, carry):
            for y in range(width_y):
                row = x * width_y + y
                at = pl.multiple_of(row * 8, 8)
                for u in range(tiles // 2):
                    value = (
                        reads[part, row, 8 * u : 8 * u + 8, :]
                        + added[pl.ds(at, 8), u * LANES : (u + 1) * LANES]
                    )
                    for parity in range(2):
                        lane = (2 * u + parity) * LANES
                        half = value[parity * width_z : (parity + 1) * width_z]
                        staged[slot, x, y, :, lane : lane + LANES] = half
            return carry

        stores.append([])
        for piece in range(pieces):
            lax.fori_loop(piece * piece_x, (piece + 1) * piece_x, add, 0)
            rows = pl.ds(piece * piece_x, piece_x)
            store = pltpu.make_async_copy(
                staged.at[slot, rows],
                out_ref.at[rows, :, :, pl.ds(part * lanes, lanes)],
                out_sems.at[part, piece],
            )
            store.start()
            stores[part].append(store)
    for part in range(max(parts - 2, 0), parts):
        for store in stores[part]:
            store.wait()


def params(mib):
    return pltpu.CompilerParams(vmem_limit_bytes=mib * 2**20)


def cost(flops, size):
    return pl.CostEstimate(flops=flops, bytes_accessed=size, transcendentals=0)


def fast_fits(distribution, points):
    width_x, width_y, width_z, local_vel = distribution.shape
    group = PLANES * points * points
    return (
        points == 24
        and lax.axis_size("vel") == 2
        and width_z == 4
        and local_vel * 2 == points**3
        and local_vel == 3 * group
        and width_x * width_y * width_z % 128 == 0
    )


def fast_device(distribution, refine_level, gain_one, gain_two, loss_kernel):
    points = gain_one.shape[0]
    width_x, width_y, width_z, local_vel = distribution.shape
    block_rows = width_x * width_y
    block_cells = block_rows * width_z
    group = PLANES * points * points
    parts = local_vel // group
    group_rows = group // LANES * width_z
    steps = group_rows // 8
    capacity = block_cells // 2
    early_count = capacity // 2 // 16 * 16
    counts = (early_count, capacity - early_count)
    batches = len(counts)
    vel_at = lax.axis_index("vel")
    count_x, count_y = lax.axis_size("cx"), lax.axis_size("cy")

    tiles = local_vel // LANES
    speeds = jnp.asarray(plane_speeds(points, local_vel, width_z))
    falls = np.arange(group) // points % points < points // 2
    falls = np.repeat(falls.reshape(-1, 1, LANES), width_z, axis=1).reshape(-1, LANES)
    falls = jnp.asarray(falls.astype(np.float32))
    side = vel_at.reshape(1).astype(jnp.int32)
    edge = jnp.where(vel_at == 0, 0, width_x - 1).reshape(1).astype(jnp.int32)

    level = refine_level.reshape(block_cells)
    active = level > 0
    cell_at = jnp.arange(block_cells, dtype=jnp.int32)
    before = (cell_at[:, None] < cell_at[None, :]) & active[:, None]
    slot_index = jnp.where(active, jnp.sum(before.astype(jnp.int32), axis=0), -1)
    spot = slot_index.reshape(block_rows, 1, width_z)
    parity = jnp.arange(2, dtype=jnp.int32)[None, :, None]
    shape = (block_rows, 2, width_z)
    wanted = jnp.where(spot >= 0, spot + capacity * parity, -1)
    wanted = jnp.broadcast_to(wanted, shape).reshape(-1)
    numbers = jnp.arange(2 * capacity, dtype=jnp.int32)
    wanted_rows = jnp.broadcast_to(wanted[None, :], (8, wanted.shape[0]))
    strength = jnp.broadcast_to(
        (0.25 * level.astype(jnp.float32)).reshape(block_rows, 1, width_z), shape
    ).reshape(-1)
    spread = jnp.where(wanted[:, None] == numbers[None, :], strength[:, None], 0.0)
    spread = spread.astype(jnp.bfloat16)

    padded = -(-len(half_set(points)[1]) // LANES) * LANES
    select, scale = frequency_select(points, padded)
    table, back_table = [jnp.asarray(t) for t in plane_table(points, padded, 64)]

    towards_lower = [(j, (j - 1) % count_y) for j in range(count_y)]
    towards_upper = [(j, (j + 1) % count_y) for j in range(count_y)]
    across_pairs = [(i, (i - 1) % count_x) for i in range(count_x)]
    across_pairs += [(count_x + i, count_x + (i + 1) % count_x) for i in range(count_x)]
    swap = [(0, 1), (1, 0)]
    bf16 = jnp.bfloat16

    half_steps = steps // 2 + 1
    local = pl.BlockSpec(memory_space=pltpu.VMEM)
    scalar = pl.BlockSpec(memory_space=pltpu.SMEM)
    remote = pl.BlockSpec(memory_space=pltpu.HBM)
    anywhere = pl.BlockSpec(memory_space=pl.ANY)

    def edges_of(first, groups):
        return pl.pallas_call(
            functools.partial(edges_kernel, first * group),
            in_specs=[scalar, local, remote],
            out_specs=[local] * 3,
            out_shape=[
                jax.ShapeDtypeStruct((groups * half_steps, width_x * 8, LANES), bf16),
                jax.ShapeDtypeStruct((groups * half_steps, width_x * 8, LANES), bf16),
                jax.ShapeDtypeStruct((groups * steps, width_y * 8, LANES), bf16),
            ],
            scratch_shapes=[
                pltpu.VMEM((width_x, 1, width_z, groups * group), jnp.float32),
                pltpu.VMEM((width_x, 1, width_z, groups * group), jnp.float32),
                pltpu.VMEM((1, width_y, width_z, groups * group), jnp.float32),
                pltpu.SemaphoreType.DMA((3,)),
            ],
            compiler_params=params(LIMIT),
            cost_estimate=cost(1, 1),
            name="edges",
        )(edge, falls, distribution)

    edges = [edges_of(0, 1), edges_of(1, parts - 1)]
    wide = 3
    chunks = steps // wide

    def upwind(at, halo, sizes):
        groups = parts - 1 if at else 1
        operands = (speeds, wanted_rows, *halo)
        local_speeds = jax.ShapeDtypeStruct((3, groups * group_rows, LANES), jnp.float32)
        chosen = [(groups * size, group) for size in sizes]
        return pl.pallas_call(
            functools.partial(upwind_kernel, at * group, sizes),
            in_specs=[scalar] + [anywhere] * (len(operands) + 1),
            out_specs=[anywhere] * (1 + len(sizes)),
            out_shape=[
                jax.ShapeDtypeStruct((block_rows, groups * group_rows, LANES), jnp.float32)
            ]
            + [jax.ShapeDtypeStruct(shape, bf16) for shape in chosen],
            scratch_shapes=[pltpu.VMEM(x.shape, x.dtype) for x in (local_speeds, *operands[1:])]
            + [pltpu.VMEM(shape, bf16) for shape in chosen]
            + [
                pltpu.VMEM((2 * capacity, block_rows * 8), bf16),
                pltpu.VMEM(
                    (groups * chunks, width_x, width_y, width_z, group // chunks), jnp.float32
                ),
                pltpu.VMEM((groups * chunks, block_rows, 8 * wide, LANES), jnp.float32),
                pltpu.VMEM((wide, width_x + 2, width_y, 8, LANES), jnp.float32),
                pltpu.VMEM((wide, width_x, 8, LANES), jnp.float32),
                pltpu.VMEM((block_rows * 8, wide * LANES), bf16),
                pltpu.SemaphoreType.DMA((groups * chunks,)),
                pltpu.SemaphoreType.DMA((groups * chunks + len(sizes),)),
                pltpu.SemaphoreType.DMA((len(operands),)),
            ],
            compiler_params=params(LIMIT),
            cost_estimate=cost(1, 1),
            name="upwind",
        )(side, *operands, distribution)

    def turn(value, *earlier):
        return lax.optimization_barrier((value, *earlier))[0]

    def swapped(value):
        return lax.ppermute(value, "vel", swap)

    halos = []
    for at in range(2):
        down, up, across = edges[at]
        halos.append(
            (
                lax.ppermute(down, "cy", towards_lower),
                lax.ppermute(up, "cy", towards_upper),
                lax.ppermute(across, ("vel", "cx"), across_pairs),
            )
        )
    first_read, *first = upwind(0, turn(halos[0], edges[1]), counts)
    first_other = [swapped(x) for x in first]
    rest_read, *rest = upwind(1, turn(halos[1], first), counts)
    kernels = turn((gain_one, gain_two, loss_kernel), halos[0])
    weights = pl.pallas_call(
        weights_kernel,
        out_shape=jax.ShapeDtypeStruct((3, points, padded), jnp.float32),
        compiler_params=params(LIMIT),
        cost_estimate=cost(1, 1),
        name="weights",
    )(
        jnp.concatenate([k.reshape(points, points * points) for k in kernels], axis=0),
        jnp.asarray(select),
        jnp.asarray(scale),
    )

    operand, weights, spread = turn((rest[0], weights, spread), first_other)
    others = [swapped(operand)]

    def scratch(count):
        return [
            pltpu.VMEM((2 * parts, count, group), bf16),
            pltpu.VMEM((points, count, 2 * padded), jnp.float32),
            pltpu.VMEM((2, 3, points // 4, count, 2 * padded), bf16),
            pltpu.VMEM(back_table.shape, bf16),
        ]

    sems = pltpu.SemaphoreType.DMA((2 * parts + 1,))
    terms = []
    for batch in range(batches - 1):
        count = counts[batch]
        starts = (0,) + tuple(g * count for g in range(parts - 1))
        following = turn(rest[batch + 1], others[-1], *terms)
        others.append(swapped(following))
        terms.append(
            pl.pallas_call(
                functools.partial(collide_kernel, starts + starts),
                in_specs=[local] * 2 + [anywhere] * (1 + 2 * parts),
                out_specs=local,
                out_shape=jax.ShapeDtypeStruct((count, local_vel), bf16),
                scratch_shapes=scratch(count) + [sems],
                compiler_params=params(34),
                cost_estimate=cost(1, 1),
                name="collide",
            )(
                weights,
                table,
                back_table,
                first[batch],
                *[rest[batch]] * (parts - 1),
                first_other[batch],
                *[others[batch]] * (parts - 1),
            )
        )

    pieces = 4
    count = counts[-1]
    starts = (0,) + tuple(g * count for g in range(parts - 1))
    return pl.pallas_call(
        functools.partial(finish_kernel, starts + starts, counts),
        in_specs=[local] * 2 + [anywhere] * (1 + batches + 2 * parts + 2),
        out_specs=anywhere,
        out_shape=jax.ShapeDtypeStruct(distribution.shape, jnp.float32),
        scratch_shapes=scratch(count)
        + [
            pltpu.VMEM((parts, block_rows, group_rows, LANES), jnp.float32),
            pltpu.VMEM((2 * capacity, group // 2), bf16),
            pltpu.VMEM((block_rows * 8, group // 2), jnp.float32),
            pltpu.VMEM((2, width_x, width_y, width_z, group), jnp.float32),
            pltpu.VMEM(spread.shape, bf16),
            pltpu.VMEM((capacity - count, local_vel), bf16),
            sems,
            pltpu.SemaphoreType.DMA((parts,)),
            pltpu.SemaphoreType.DMA((parts, pieces)),
            pltpu.SemaphoreType.DMA((batches,)),
        ],
        compiler_params=params(LIMIT),
        name="finish",
    )(
        weights,
        table,
        back_table,
        spread,
        *terms,
        first[-1],
        *[rest[-1]] * (parts - 1),
        first_other[-1],
        *[others[-1]] * (parts - 1),
        first_read,
        rest_read,
    )


def per_device(distribution, refine_level, gain_one, gain_two, loss_kernel):
    if fast_fits(distribution, gain_one.shape[0]):
        return fast_device(distribution, refine_level, gain_one, gain_two, loss_kernel)
    return plain_device(distribution, refine_level, gain_one, gain_two, loss_kernel)


def solution(mesh):
    placed = (P("cx", "cy", None, "vel"), P("cx", "cy", None), P(), P(), P())
    return jax.shard_map(
        per_device,
        mesh=mesh,
        in_specs=placed,
        out_specs=P("cx", "cy", None, "vel"),
        check_vma=False,
    )
```

```python
import functools
import math

import jax
import jax.numpy as jnp
import ml_dtypes
import numpy as np
from jax import lax
from jax.experimental import pallas as pl
from jax.experimental.pallas import tpu as pltpu
from jax.sharding import PartitionSpec as P


def extended(array, sides, width):
    for axis, dim in sides:
        count, length = (lax.axis_size(axis), array.shape[dim])
        up = [(i, (i + 1) % count) for i in range(count)]
        down = [(j, i) for i, j in up]
        last = lax.slice_in_dim(array, length - width, length, axis=dim)
        leading = lax.slice_in_dim(array, 0, width, axis=dim)
        before = lax.ppermute(last, axis, up)
        after = lax.ppermute(leading, axis, down)
        array = jnp.concatenate([before, array, after], axis=dim)
    return array


def dft_tables(points):
    indices = jnp.arange(points, dtype=jnp.int32)
    products = indices[:, None] * indices[None, :] % points
    angles = products.astype(jnp.float32) * (2.0 * math.pi / points)
    cosine = jnp.cos(angles)
    sine_table = jnp.sin(angles)
    forward = jnp.stack([jnp.stack([cosine, sine_table]), jnp.stack([-sine_table, cosine])])
    inverse = jnp.stack([jnp.stack([cosine, -sine_table]), jnp.stack([sine_table, cosine])])
    return (forward.astype(jnp.bfloat16), inverse.astype(jnp.bfloat16))


def contract(pattern, left_side, right_side):
    return jnp.einsum(pattern, left_side, right_side, preferred_element_type=jnp.float32)


def collide(cells, forward, inverse, gain_one, gain_two, loss_kernel):
    points = forward.shape[-1]
    cell_count = cells.shape[0]
    field = cells.reshape(cell_count, points, points, points)
    section_z = contract("nabz,qzw->qnabw", field, forward[:, 0]).astype(jnp.bfloat16)
    section_y = contract("pnayc,qpyw->qnawc", section_z, forward).astype(jnp.bfloat16)
    spectrum = contract("pnxbc,qpxw->qnwbc", section_y, forward)
    scale_factor = 1.0 / float(points**3)

    def filtered(kernel):
        weighted = (spectrum * (kernel * scale_factor)[None, None]).astype(jnp.bfloat16)
        back_x = contract("pnxbc,qpxw->qnwbc", weighted, inverse).astype(jnp.bfloat16)
        back_y = contract("pnayc,qpyw->qnawc", back_x, inverse).astype(jnp.bfloat16)
        return contract("pnabz,pzw->nabw", back_y, inverse[0])

    gain_term = filtered(gain_one) * filtered(gain_two)
    result = gain_term - field.astype(jnp.float32) * filtered(loss_kernel)
    return result.reshape(cell_count, points**3)


def courants(points, first_vel, local_count):
    vel_index = first_vel + jnp.arange(local_count, dtype=jnp.int32)
    index_x = vel_index // (points * points)
    index_y = vel_index // points % points
    index_z = vel_index % points

    def speed(index_part):
        return 0.3 * (2.0 * index_part.astype(jnp.float32) - (points - 1)) / (points - 1)

    return (speed(index_x), speed(index_y), speed(index_z))


def upwind_flux(courant, center, lower_side, upper_side):
    return jnp.maximum(courant, 0.0) * (center - lower_side) + jnp.minimum(courant, 0.0) * (
        upper_side - center
    )


def plain_device(distribution, refine_level, gain_one, gain_two, loss_kernel):
    points = gain_one.shape[0]
    width_x, width_y, width_z, local_vel = distribution.shape
    first_vel = lax.axis_index("vel") * local_vel
    courant_x, courant_y, courant_z = courants(points, first_vel, local_vel)
    padded = extended(distribution, (("cx", 0), ("cy", 1)), 1)
    fluxes = upwind_flux(courant_x, distribution, padded[:-2, 1:-1], padded[2:, 1:-1])
    fluxes = fluxes + upwind_flux(courant_y, distribution, padded[1:-1, :-2], padded[1:-1, 2:])
    fluxes = fluxes + upwind_flux(
        courant_z, distribution, jnp.roll(distribution, 1, 2), jnp.roll(distribution, -1, 2)
    )
    read = distribution - fluxes
    block_cells = width_x * width_y * width_z
    groups = lax.axis_size("vel")
    flattened = read.reshape(block_cells, local_vel).astype(jnp.bfloat16)
    forward, inverse = dft_tables(points)
    active = refine_level.reshape(block_cells) > 0
    slot_index = jnp.cumsum(active.astype(jnp.int32)) - 1
    capacity = block_cells // 2
    picker = (
        (slot_index[None, :] == jnp.arange(capacity, dtype=jnp.int32)[:, None]) & active[None, :]
    ).astype(jnp.bfloat16)
    chosen = jnp.dot(picker, flattened, preferred_element_type=jnp.float32).astype(jnp.bfloat16)
    terms = collide(
        lax.all_to_all(
            chosen.reshape(groups, capacity // groups, local_vel),
            "vel",
            split_axis=0,
            concat_axis=2,
            tiled=True,
        )[0],
        forward,
        inverse,
        gain_one,
        gain_two,
        loss_kernel,
    )[None]
    packed = lax.all_to_all(
        terms.astype(jnp.bfloat16), "vel", split_axis=2, concat_axis=0, tiled=True
    ).astype(terms.dtype)
    packed_rows = packed.reshape(capacity, local_vel)
    safe_slot = jnp.clip(slot_index, 0, capacity - 1)
    rates = jnp.where(active[:, None], packed_rows[safe_slot], 0.0)
    weight = 0.25 * refine_level.astype(jnp.float32)
    return read + weight[..., None] * rates.reshape(width_x, width_y, width_z, local_vel)

LANES = 128
PLANES = 4
LIMIT = 57


def half_set(points):
    middle = points // 2
    pairs = [(b, c) for c in range(1, middle) for b in range(points)]
    pairs += [(b, c) for c in (0, middle) for b in range(middle + 1)]
    weights = [1.0 if b % middle == 0 and c % middle == 0 else 2.0 for b, c in pairs]
    return np.array(pairs), np.array(weights)


def plane_table(points, padded, margin):
    pairs, _ = half_set(points)
    first, second = np.divmod(np.arange(points * points), points)
    index = np.arange(points)
    angles = (index[:, None] * index[None, :] % points).astype(np.float32)
    angles = angles * np.float32(2.0 * np.pi / points)
    cosine, sine = [
        t.astype(ml_dtypes.bfloat16).astype(np.float32) for t in (np.cos(angles), np.sin(angles))
    ]
    cos_y, sin_y = cosine[first][:, pairs[:, 0]], sine[first][:, pairs[:, 0]]
    cos_z, sin_z = cosine[second][:, pairs[:, 1]], sine[second][:, pairs[:, 1]]
    table = np.zeros((points * points + 2 * margin, 2 * padded), np.float32)
    rows = slice(margin, margin + points * points)
    table[rows, : len(pairs)] = cos_y * cos_z - sin_y * sin_z
    table[rows, padded : padded + len(pairs)] = -(cos_y * sin_z + sin_y * cos_z)
    window = points * points + margin
    level = np.flatnonzero(pairs[:, 1] == 0)
    rest = table.copy()
    rest[:, np.concatenate([level, padded + level])] = 0.0
    for start in (points * points + margin, 0):
        rest[start : start + points, level] = cosine[:, pairs[level, 0]]
        rest[start : start + points, padded + level] = -sine[:, pairs[level, 0]]
    back = np.stack([rest[margin : margin + window].T, rest[:window].T])
    copies = np.zeros((2, LANES, window), np.float32)
    place = np.arange(points * points)
    copies[0, (points * points + first) % LANES, place] = 1.0
    copies[1, first, margin + place] = 1.0
    back = np.concatenate([back, copies], axis=1)
    spare = len(pairs)
    lift = np.zeros((LANES, 2 * padded), np.float32)
    for half in (0, padded):
        columns = slice(spare % LANES, spare % LANES + points)
        lift[columns, half + level] = table[margin : margin + points**2 : points, half + level]
        table[:, half + level] = 0.0
    table[margin + place, spare + first] = 1.0
    table = np.concatenate([table, lift])
    return table.astype(ml_dtypes.bfloat16), back.astype(ml_dtypes.bfloat16)


def frequency_select(points, padded):
    pairs, weights = half_set(points)
    select = np.zeros((points * points, 2 * padded), np.float32)
    column = np.arange(len(pairs))
    select[pairs[:, 0] * points + pairs[:, 1], column] = 1.0
    mirror = (-pairs[:, 0]) % points * points + (-pairs[:, 1]) % points
    select[mirror, padded + column] = 1.0
    scale = np.zeros((1, padded), np.float32)
    scale[0, : len(pairs)] = 0.5 * weights / points**3
    return select.astype(ml_dtypes.bfloat16), scale


def weights_kernel(stacked_ref, select_ref, scale_ref, out_ref):
    kernels, points, padded = out_ref.shape
    rest = stacked_ref[...]
    picked = None
    for _ in range(3):
        piece = rest.astype(jnp.bfloat16)
        rest = rest - piece.astype(jnp.float32)
        part = jnp.dot(piece, select_ref[...], preferred_element_type=jnp.float32)
        picked = part if picked is None else picked + part
    for which in range(kernels):
        for a in range(points):
            row, mirror = which * points + a, which * points + (-a) % points
            both = picked[row : row + 1, :padded] + picked[mirror : mirror + 1, padded:]
            out_ref[which, a : a + 1, :] = both * scale_ref[...]


def transform_3(x, sign, wanted=(0, 1, 2)):
    (ar, ai), (br, bi), (cr, ci) = x
    sr, si = br + cr, bi + ci
    out = {}
    if 0 in wanted:
        out[0] = (ar + sr, ai + si)
    if 1 in wanted or 2 in wanted:
        height = sign * math.sqrt(0.75)
        mr, mi = ar - 0.5 * sr, ai - 0.5 * si
        er, ei = height * (br - cr), height * (bi - ci)
        if 1 in wanted:
            out[1] = (mr - ei, mi + er)
        if 2 in wanted:
            out[2] = (mr + ei, mi - er)
    return out


def transform_4(x, sign):
    (ar, ai), (br, bi), (cr, ci), (dr, di) = x
    pr, pi, qr, qi = ar + cr, ai + ci, ar - cr, ai - ci
    sr, si, tr, ti = br + dr, bi + di, br - dr, bi - di
    if sign < 0:
        tr, ti = -tr, -ti
    return [(pr + sr, pi + si), (qr - ti, qi + tr), (pr - sr, pi - si), (qr + ti, qi - tr)]


def transform_8(x, sign):
    even = transform_4(x[0::2], sign)
    odd = transform_4(x[1::2], sign)
    root = math.sqrt(0.5)
    (r0, i0), (r1, i1), (r2, i2), (r3, i3) = odd
    if sign > 0:
        turned = [(r0, i0), (root * (r1 - i1), root * (i1 + r1)), (-i2, r2)]
        turned.append((-root * (r3 + i3), root * (r3 - i3)))
    else:
        turned = [(r0, i0), (root * (r1 + i1), root * (i1 - r1)), (i2, -r2)]
        turned.append((root * (i3 - r3), -root * (i3 + r3)))
    low = [(e[0] + t[0], e[1] + t[1]) for e, t in zip(even, turned)]
    high = [(e[0] - t[0], e[1] - t[1]) for e, t in zip(even, turned)]
    return low + high


def spectrum_of(load):
    stage = {}
    for n2 in range(8):
        part = transform_3([load((8 * n1 + 3 * n2) % 24) for n1 in range(3)], -1)
        for k1 in range(3):
            stage[k1, n2] = part[k1]
    result = {}
    for k1 in range(3):
        part = transform_8([stage[k1, n2] for n2 in range(8)], -1)
        for k2 in range(8):
            result[(16 * k1 + 9 * k2) % 24] = part[k2]
    return result


def first_half_of(spectrum):
    stage = {}
    for k1 in range(3):
        part = transform_8([spectrum[(16 * k1 + 9 * k2) % 24] for k2 in range(8)], 1)
        for n2 in range(8):
            stage[k1, n2] = part[n2]
    result = {}
    for n2 in range(8):
        wanted = {n1: (8 * n1 + 3 * n2) % 24 for n1 in range(3) if (8 * n1 + 3 * n2) % 24 < 12}
        part = transform_3([stage[k1, n2] for k1 in range(3)], 1, tuple(wanted))
        for n1, index in wanted.items():
            result[index] = part[n1]
    return result


def tile_pair(ref, step, rows):
    parts = []
    for parity in range(2):
        at = (2 * step + parity) * LANES
        part = ref[:, :, :, at : at + LANES]
        parts.append(part.reshape(rows, part.shape[2], LANES))
    return jnp.concatenate(parts, axis=1)


def plane_speeds(points, local_vel, width_z):
    index = np.arange(points**3)
    parts = (index // (points * points), index // points % points, index % points)
    speeds = [
        np.float32(0.3) * (np.float32(2.0) * part.astype(np.float32) - np.float32(points - 1))
        / np.float32(points - 1)
        for part in parts
    ]
    tiled = np.stack(speeds).reshape(3, -1, local_vel // LANES, 1, LANES).transpose(1, 0, 2, 3, 4)
    repeated = np.repeat(tiled, width_z, axis=3)
    return repeated.reshape(repeated.shape[0], 3, -1, LANES)


def edges_kernel(first, edge_ref, falls_ref, field_ref, *refs):
    down_ref, up_ref, across_ref, low_ref, high_ref, plane_ref, sems = refs
    steps = falls_ref.shape[0] // 8
    width = low_ref.shape[0]
    groups = across_ref.shape[0] // steps
    half_steps = down_ref.shape[0] // groups
    here = pl.ds(first, low_ref.shape[3])
    last_y = field_ref.shape[1] - 1
    sources = [
        field_ref.at[:, pl.ds(0, 1), :, here],
        field_ref.at[:, pl.ds(last_y, 1), :, here],
        field_ref.at[pl.ds(edge_ref[0], 1), :, :, here],
    ]
    loads = [
        pltpu.make_async_copy(source, ref, sems.at[at])
        for at, (source, ref) in enumerate(zip(sources, (low_ref, high_ref, plane_ref)))
    ]
    for load in loads:
        load.start()
    below = [falls_ref[8 * s : 8 * s + 8, :][None] > 0.0 for s in range(steps)]

    def put(ref, at, value):
        ref[at] = value.reshape(-1, LANES).astype(jnp.bfloat16)

    loads[0].wait()
    for g in range(groups):
        row = [tile_pair(low_ref, g * steps + s, width) for s in range(steps)]
        put(down_ref, g * half_steps, row[0])
        for m in range(1, steps // 2 + 1):
            put(down_ref, g * half_steps + m, jnp.where(below[2 * m - 1], row[2 * m - 1], row[2 * m]))
    loads[1].wait()
    for g in range(groups):
        row = [tile_pair(high_ref, g * steps + s, width) for s in range(steps)]
        for m in range(steps // 2):
            put(up_ref, g * half_steps + m, jnp.where(below[2 * m], row[2 * m + 1], row[2 * m]))
        put(up_ref, g * half_steps + steps // 2, row[steps - 1])
    loads[2].wait()
    for s in range(groups * steps):
        put(across_ref, s, tile_pair(plane_ref, s, plane_ref.shape[1]))


def upwind_kernel(base, counts, side_ref, *refs):
    batches = len(counts)
    outer_refs, field_ref = refs[:5], refs[5]
    out_ref, target_refs, scratch = refs[6], refs[7 : 7 + batches], refs[7 + batches :]
    inner_refs, chosen_refs, scratch = scratch[:5], scratch[5 : 5 + batches], scratch[5 + batches :]
    speed_ref, wanted_ref, down_ref, up_ref, across_ref = inner_refs
    picker_ref, blocks, reads, wide, border, cells, load_sems, store_sems, side_sems = scratch
    chunks, width_x, width_y, width_z, lanes = blocks.shape
    steps = lanes // (2 * LANES)
    group_lanes = chosen_refs[0].shape[1]
    per_group = group_lanes // lanes
    half_steps = per_group * steps // 2 + 1
    first_row = base // LANES * width_z
    rows = pl.ds(first_row, speed_ref.shape[1])
    sources = (outer_refs[0].at[side_ref[0], :, rows, :],) + outer_refs[1:]
    inputs = [
        pltpu.make_async_copy(source, target, side_sems.at[at])
        for at, (source, target) in enumerate(zip(sources, inner_refs))
    ]
    for copy in inputs:
        copy.start()
    loads = []
    for t in range(chunks):
        source = field_ref.at[:, :, :, pl.ds(base + t * lanes, lanes)]
        loads.append(pltpu.make_async_copy(source, blocks.at[t], load_sems.at[t]))
    for load in loads[:2]:
        load.start()
    beside = jnp.where(side_ref[0] == 0, 2, 0)
    place = lax.broadcasted_iota(jnp.int32, (1, 8, LANES), 1) % width_z
    capacity = picker_ref.shape[0] // 2
    stores = []
    for copy in inputs:
        copy.wait()
    number = lax.broadcasted_iota(jnp.int32, picker_ref.shape, 0)
    matches = number == wanted_ref[0:1, :]
    picker_ref[...] = jnp.where(matches, 1.0, 0.0).astype(jnp.bfloat16)
    for t in range(chunks):
        group, chunk = t // per_group, t % per_group
        sizes, falls, sinks = [], [], []
        for u in range(steps):
            step = chunk * steps + u
            row = 8 * (t * steps + u)
            speed = [speed_ref[d, row : row + 8, :][None] for d in range(3)]
            sizes.append([jnp.abs(c) for c in speed])
            falls.append(speed[1] < 0.0)
            sinks.append(speed[2] < 0.0)
            outer = across_ref[t * steps + u].astype(jnp.float32).reshape(width_y, 8, LANES)
            wide[u, 0] = outer
            wide[u, width_x + 1] = outer
            above = down_ref[group * half_steps + (step + 1) // 2].astype(jnp.float32)
            under = up_ref[group * half_steps + step // 2].astype(jnp.float32)
            shape = (width_x, 8, LANES)
            border[u] = jnp.where(falls[u], above.reshape(shape), under.reshape(shape))
        loads[t].wait()
        if t + 2 < chunks:
            loads[t + 2].start()

        def spread_out(x, carry):
            for u in range(steps):
                at = 2 * u * LANES
                parts = [
                    blocks[t, x, :, :, at + p * LANES : at + (p + 1) * LANES] for p in range(2)
                ]
                wide[u, x + 1] = jnp.concatenate(parts, axis=1)
            return carry

        lax.fori_loop(0, width_x, spread_out, 0, unroll=4)

        def advance(x, carry):
            for u in range(steps):
                field = wide[u, x + 1]
                edge = border[u, pl.ds(x, 1)]
                fluxes = sizes[u][0] * (field - wide[u, x + beside])
                beside_y = jnp.where(
                    falls[u],
                    jnp.concatenate([field[1:], edge], axis=0),
                    jnp.concatenate([edge, field[:-1]], axis=0),
                )
                fluxes = fluxes + sizes[u][1] * (field - beside_y)
                turned = pltpu.roll(field, 4, 1)
                upper = pltpu.roll(jnp.where(place == 0, turned, field), 7, 1)
                lower = pltpu.roll(jnp.where(place == width_z - 1, turned, field), 1, 1)
                fluxes = fluxes + sizes[u][2] * (field - jnp.where(sinks[u], upper, lower))
                read = field - fluxes
                reads[t, pl.ds(x * width_y, width_y), 8 * u : 8 * u + 8, :] = read
                rows = width_y * 8
                at = pl.multiple_of(x * rows, rows)
                cells[pl.ds(at, rows), u * LANES : (u + 1) * LANES] = read.reshape(
                    rows, LANES
                ).astype(jnp.bfloat16)
            return carry

        lax.fori_loop(0, width_x, advance, 0, unroll=4)
        target = out_ref.at[:, pl.ds(8 * steps * t, 8 * steps), :]
        stores.append(pltpu.make_async_copy(reads.at[t], target, store_sems.at[t]))
        stores[-1].start()
        picked = jnp.dot(
            picker_ref[...], cells[...], preferred_element_type=jnp.float32
        ).astype(jnp.bfloat16)
        for parity in range(2):
            first = parity * capacity
            for ref, count in zip(chosen_refs, counts):
                rows = slice(group * count, (group + 1) * count)
                for u in range(steps):
                    tile = 2 * (chunk * steps + u) + parity
                    here = slice(tile * LANES, (tile + 1) * LANES)
                    ref[rows, here] = picked[first : first + count, u * LANES : (u + 1) * LANES]
                first += count
    for at, (source, target) in enumerate(zip(chosen_refs, target_refs)):
        stores.append(pltpu.make_async_copy(source, target, store_sems.at[chunks + at]))
        stores[-1].start()
    for store in stores:
        store.wait()


def window_loads(firsts, refs, cells, sems):
    loads = []
    for at, (ref, first) in enumerate(zip(refs, firsts)):
        source = ref.at[pl.ds(first, cells.shape[1])]
        loads.append(pltpu.make_async_copy(source, cells.at[at], sems.at[at]))
        loads[-1].start()
    return loads


def filter_parts(weight_ref, table_ref, cells, loads, later, section, back):
    count, slots, lanes = cells.shape
    padded = weight_ref.shape[2]
    height = table_ref.shape[0] - LANES
    window = height - 64
    pair_lanes = 2 * (height - 128)
    pairs = lanes // pair_lanes
    half = pairs * count
    sums_at = padded - LANES
    for load in loads:
        load.wait()
    for load in later:
        load.start()
    for parity in range(2):
        rows = []
        for at in range(count):
            for p in range(pairs):
                lane = p * pair_lanes + parity * (pair_lanes - window)
                rows.append(cells[at, :, lane : lane + window])
        start = 64 * (1 - parity)
        out = jnp.dot(
            jnp.concatenate(rows, axis=0),
            table_ref[start : start + window, :],
            preferred_element_type=jnp.float32,
        )
        sums = out[:, sums_at : sums_at + LANES].astype(jnp.bfloat16)
        pieces = []
        for first in (0, padded):
            lift = table_ref[height:, first + sums_at : first + padded]
            lifted = jnp.dot(sums, lift, preferred_element_type=jnp.float32)
            pieces.append(out[:, first : first + sums_at])
            pieces.append(out[:, first + sums_at : first + padded] + lifted)
        lane = 0
        for piece in pieces:
            piece = piece.astype(jnp.bfloat16).astype(jnp.float32)
            here = slice(lane, lane + piece.shape[1])
            for at in range(half):
                section[2 * at + parity, :, here] = piece[at * slots : (at + 1) * slots]
            lane += piece.shape[1]

    lane_tiles = padded // LANES
    points = weight_ref.shape[1]
    pairs_of, _ = half_set(points)
    mean_at = int(np.flatnonzero((pairs_of == 0).all(axis=1))[0])

    def transform(index, carry):
        row = pl.multiple_of(index // lane_tiles * 16, 16)
        lane = pl.multiple_of(index % lane_tiles * LANES, LANES)
        mean = lane + lax.broadcasted_iota(jnp.int32, (8, LANES), 1) == mean_at
        results = []
        for octet in range(2):
            here = pl.ds(row + 8 * octet, 8)

            def load(i):
                real = section[i, here, pl.ds(lane, LANES)]
                return real, section[i, here, pl.ds(padded + lane, LANES)]

            spectrum = spectrum_of(load)
            per_kernel = []
            for which in range(3):
                weighted = {}
                for a, (real, imag) in spectrum.items():
                    weight = weight_ref[which, pl.ds(a, 1), pl.ds(lane, LANES)]
                    weighted[a] = (real * weight, imag * weight)
                real = weighted[0][0]
                rounded = real.astype(jnp.bfloat16).astype(jnp.float32)
                weighted[0] = (jnp.where(mean, rounded, real), weighted[0][1])
                per_kernel.append(first_half_of(weighted))
            results.append(per_kernel)
        for which in range(3):
            for i in range(half):
                for q in range(2):
                    value = jnp.concatenate([results[o][which][i][q] for o in range(2)], axis=0)
                    back[i % 2, which, i // 2, pl.ds(row, 16), pl.ds(q * padded + lane, LANES)] = (
                        value.astype(jnp.bfloat16)
                    )
        return carry

    lax.fori_loop(0, slots // 16 * lane_tiles, transform, 0)


def inverse_parts(back_table, back):
    _, kernels, pairs, slots, depth = back.shape
    window = back_table.shape[2]
    outs = []
    for parity in range(2):
        out = jnp.dot(
            back[parity].reshape(kernels * pairs * slots, depth),
            back_table[parity, :depth],
            preferred_element_type=jnp.float32,
        )
        first = 0 if parity else window - LANES
        level = out[:, first : first + LANES].astype(jnp.bfloat16)
        out = out + jnp.dot(level, back_table[parity, depth:], preferred_element_type=jnp.float32)
        outs.append(out.reshape(kernels, pairs, slots, window))
    return outs


def terms_of(part, outs, cells_ref, put):
    _, slots, lanes = cells_ref.shape
    window = outs[0].shape[3]
    pair_lanes = 2 * (window - 64)
    pairs = lanes // pair_lanes
    tiles = pair_lanes // LANES
    near = lax.broadcasted_iota(jnp.int32, (slots, LANES), 1) < 64
    for pair in range(pairs):
        at = part * pairs + pair
        for tile in range(tiles):
            lane = tile * LANES
            odd_lane = lane - (pair_lanes - window)
            values = []
            for which in range(3):
                if tile < tiles // 2:
                    value = outs[0][which, at, :, lane : lane + LANES]
                elif tile > tiles // 2:
                    value = outs[1][which, at, :, odd_lane : odd_lane + LANES]
                else:
                    value = jnp.where(
                        near,
                        outs[0][which, at, :, lane : lane + LANES],
                        outs[1][which, at, :, odd_lane : odd_lane + LANES],
                    )
                values.append(value)
            lane = pair * pair_lanes + lane
            cells = cells_ref[part, :, lane : lane + LANES].astype(jnp.float32)
            put(pair * tiles + tile, (values[0] * values[1] - cells * values[2]).astype(jnp.bfloat16))


def collide_kernel(firsts, weight_ref, table_ref, back_any, *refs):
    parts = len(firsts) // 2
    terms_ref, cells, section, back, back_table, sems = refs[2 * parts :]
    lanes = cells.shape[2]
    loads = window_loads(firsts, refs[: 2 * parts], cells, sems)
    table_load = pltpu.make_async_copy(back_any, back_table, sems.at[2 * parts])
    filter_parts(weight_ref, table_ref, cells, loads, [table_load], section, back)
    table_load.wait()
    outs = inverse_parts(back_table, back)
    for part in range(parts):

        def put(tile, value):
            first = part * lanes + tile * LANES
            terms_ref[:, first : first + LANES] = value

        terms_of(part, outs, cells, put)


def finish_kernel(firsts, sizes, weight_ref, table_ref, back_any, spread_any, *refs):
    parts = len(firsts) // 2
    term_refs, refs = refs[: len(sizes) - 1], refs[len(sizes) - 1 :]
    first_read, rest_read = refs[2 * parts : 2 * parts + 2]
    out_ref, cells, section, back, back_table, reads, spots, added, staged = refs[2 * parts + 2 : -6]
    spread_ref, early_ref, cell_sems, read_sems, out_sems, extra_sems = refs[-6:]
    width_x, width_y, width_z, lanes = staged.shape[1:]
    tiles = lanes // LANES
    loads = window_loads(firsts, refs[: 2 * parts], cells, cell_sems)
    extra = [pltpu.make_async_copy(spread_any, spread_ref, extra_sems.at[0])]
    at = 0
    for ref, size in zip(term_refs, sizes):
        target = early_ref.at[pl.ds(at, size)]
        extra.append(pltpu.make_async_copy(ref, target, extra_sems.at[len(extra)]))
        at += size
    extra.append(pltpu.make_async_copy(back_any, back_table, cell_sems.at[2 * parts]))
    group_rows = reads.shape[2]
    read_loads = []
    for part in range(parts):
        rows = pl.ds(max(part - 1, 0) * group_rows, group_rows)
        source = (rest_read if part else first_read).at[:, rows, :]
        read_loads.append(pltpu.make_async_copy(source, reads.at[part], read_sems.at[part]))
    filter_parts(weight_ref, table_ref, cells, loads, extra + read_loads, section, back)
    for load in extra:
        load.wait()
    early = early_ref.shape[0]
    capacity = early + section.shape[1]
    outs = inverse_parts(back_table, back)
    pieces = out_sems.shape[1]
    piece_x = width_x // pieces
    stores = []
    for part in range(parts):

        def put(tile, value):
            first = tile % 2 * capacity
            columns = slice(tile // 2 * LANES, (tile // 2 + 1) * LANES)
            lane = part * lanes + tile * LANES
            spots[first : first + early, columns] = early_ref[:, lane : lane + LANES]
            spots[first + early : first + capacity, columns] = value

        terms_of(part, outs, cells, put)
        added[...] = jnp.dot(spread_ref[...], spots[...], preferred_element_type=jnp.float32)
        read_loads[part].wait()
        slot = part % 2
        if part >= 2:
            for store in stores[part - 2]:
                store.wait()

        def add(x, carry):
            for y in range(width_y):
                row = x * width_y + y
                at = pl.multiple_of(row * 8, 8)
                for u in range(tiles // 2):
                    value = (
                        reads[part, row, 8 * u : 8 * u + 8, :]
                        + added[pl.ds(at, 8), u * LANES : (u + 1) * LANES]
                    )
                    for parity in range(2):
                        lane = (2 * u + parity) * LANES
                        half = value[parity * width_z : (parity + 1) * width_z]
                        staged[slot, x, y, :, lane : lane + LANES] = half
            return carry

        stores.append([])
        for piece in range(pieces):
            lax.fori_loop(piece * piece_x, (piece + 1) * piece_x, add, 0)
            rows = pl.ds(piece * piece_x, piece_x)
            store = pltpu.make_async_copy(
                staged.at[slot, rows],
                out_ref.at[rows, :, :, pl.ds(part * lanes, lanes)],
                out_sems.at[part, piece],
            )
            store.start()
            stores[part].append(store)
    for part in range(max(parts - 2, 0), parts):
        for store in stores[part]:
            store.wait()


def params(mib):
    return pltpu.CompilerParams(vmem_limit_bytes=mib * 2**20)


def cost(flops, size):
    return pl.CostEstimate(flops=flops, bytes_accessed=size, transcendentals=0)


def fast_fits(distribution, points):
    width_x, width_y, width_z, local_vel = distribution.shape
    group = PLANES * points * points
    return (
        points == 24
        and lax.axis_size("vel") == 2
        and width_z == 4
        and local_vel * 2 == points**3
        and local_vel == 3 * group
        and width_x * width_y * width_z % 128 == 0
    )


def fast_device(distribution, refine_level, gain_one, gain_two, loss_kernel):
    points = gain_one.shape[0]
    width_x, width_y, width_z, local_vel = distribution.shape
    block_rows = width_x * width_y
    block_cells = block_rows * width_z
    group = PLANES * points * points
    parts = local_vel // group
    group_rows = group // LANES * width_z
    steps = group_rows // 8
    capacity = block_cells // 2
    early_count = capacity // 2 // 16 * 16
    counts = (early_count, capacity - early_count)
    batches = len(counts)
    vel_at = lax.axis_index("vel")
    count_x, count_y = lax.axis_size("cx"), lax.axis_size("cy")

    tiles = local_vel // LANES
    speeds = jnp.asarray(plane_speeds(points, local_vel, width_z))
    falls = np.arange(group) // points % points < points // 2
    falls = np.repeat(falls.reshape(-1, 1, LANES), width_z, axis=1).reshape(-1, LANES)
    falls = jnp.asarray(falls.astype(np.float32))
    side = vel_at.reshape(1).astype(jnp.int32)
    edge = jnp.where(vel_at == 0, 0, width_x - 1).reshape(1).astype(jnp.int32)

    level = refine_level.reshape(block_cells)
    active = level > 0
    cell_at = jnp.arange(block_cells, dtype=jnp.int32)
    before = (cell_at[:, None] < cell_at[None, :]) & active[:, None]
    slot_index = jnp.where(active, jnp.sum(before.astype(jnp.int32), axis=0), -1)
    spot = slot_index.reshape(block_rows, 1, width_z)
    parity = jnp.arange(2, dtype=jnp.int32)[None, :, None]
    shape = (block_rows, 2, width_z)
    wanted = jnp.where(spot >= 0, spot + capacity * parity, -1)
    wanted = jnp.broadcast_to(wanted, shape).reshape(-1)
    numbers = jnp.arange(2 * capacity, dtype=jnp.int32)
    wanted_rows = jnp.broadcast_to(wanted[None, :], (8, wanted.shape[0]))
    strength = jnp.broadcast_to(
        (0.25 * level.astype(jnp.float32)).reshape(block_rows, 1, width_z), shape
    ).reshape(-1)
    spread = jnp.where(wanted[:, None] == numbers[None, :], strength[:, None], 0.0)
    spread = spread.astype(jnp.bfloat16)

    padded = -(-len(half_set(points)[1]) // LANES) * LANES
    select, scale = frequency_select(points, padded)
    table, back_table = [jnp.asarray(t) for t in plane_table(points, padded, 64)]

    towards_lower = [(j, (j - 1) % count_y) for j in range(count_y)]
    towards_upper = [(j, (j + 1) % count_y) for j in range(count_y)]
    across_pairs = [(i, (i - 1) % count_x) for i in range(count_x)]
    across_pairs += [(count_x + i, count_x + (i + 1) % count_x) for i in range(count_x)]
    swap = [(0, 1), (1, 0)]
    bf16 = jnp.bfloat16

    half_steps = steps // 2 + 1
    local = pl.BlockSpec(memory_space=pltpu.VMEM)
    scalar = pl.BlockSpec(memory_space=pltpu.SMEM)
    remote = pl.BlockSpec(memory_space=pltpu.HBM)
    anywhere = pl.BlockSpec(memory_space=pl.ANY)

    def edges_of(first, groups):
        return pl.pallas_call(
            functools.partial(edges_kernel, first * group),
            in_specs=[scalar, local, remote],
            out_specs=[local] * 3,
            out_shape=[
                jax.ShapeDtypeStruct((groups * half_steps, width_x * 8, LANES), bf16),
                jax.ShapeDtypeStruct((groups * half_steps, width_x * 8, LANES), bf16),
                jax.ShapeDtypeStruct((groups * steps, width_y * 8, LANES), bf16),
            ],
            scratch_shapes=[
                pltpu.VMEM((width_x, 1, width_z, groups * group), jnp.float32),
                pltpu.VMEM((width_x, 1, width_z, groups * group), jnp.float32),
                pltpu.VMEM((1, width_y, width_z, groups * group), jnp.float32),
                pltpu.SemaphoreType.DMA((3,)),
            ],
            compiler_params=params(LIMIT),
            cost_estimate=cost(1, 1),
            name="edges",
        )(edge, falls, distribution)

    edges = [edges_of(0, 1), edges_of(1, parts - 1)]
    wide = 3
    chunks = steps // wide

    def upwind(at, halo, sizes):
        groups = parts - 1 if at else 1
        operands = (speeds, wanted_rows, *halo)
        local_speeds = jax.ShapeDtypeStruct((3, groups * group_rows, LANES), jnp.float32)
        chosen = [(groups * size, group) for size in sizes]
        return pl.pallas_call(
            functools.partial(upwind_kernel, at * group, sizes),
            in_specs=[scalar] + [anywhere] * (len(operands) + 1),
            out_specs=[anywhere] * (1 + len(sizes)),
            out_shape=[
                jax.ShapeDtypeStruct((block_rows, groups * group_rows, LANES), jnp.float32)
            ]
            + [jax.ShapeDtypeStruct(shape, bf16) for shape in chosen],
            scratch_shapes=[pltpu.VMEM(x.shape, x.dtype) for x in (local_speeds, *operands[1:])]
            + [pltpu.VMEM(shape, bf16) for shape in chosen]
            + [
                pltpu.VMEM((2 * capacity, block_rows * 8), bf16),
                pltpu.VMEM(
                    (groups * chunks, width_x, width_y, width_z, group // chunks), jnp.float32
                ),
                pltpu.VMEM((groups * chunks, block_rows, 8 * wide, LANES), jnp.float32),
                pltpu.VMEM((wide, width_x + 2, width_y, 8, LANES), jnp.float32),
                pltpu.VMEM((wide, width_x, 8, LANES), jnp.float32),
                pltpu.VMEM((block_rows * 8, wide * LANES), bf16),
                pltpu.SemaphoreType.DMA((groups * chunks,)),
                pltpu.SemaphoreType.DMA((groups * chunks + len(sizes),)),
                pltpu.SemaphoreType.DMA((len(operands),)),
            ],
            compiler_params=params(LIMIT),
            cost_estimate=cost(1, 1),
            name="upwind",
        )(side, *operands, distribution)

    def turn(value, *earlier):
        return lax.optimization_barrier((value, *earlier))[0]

    def swapped(value):
        return lax.ppermute(value, "vel", swap)

    halos = []
    for at in range(2):
        down, up, across = edges[at]
        halos.append(
            (
                lax.ppermute(down, "cy", towards_lower),
                lax.ppermute(up, "cy", towards_upper),
                lax.ppermute(across, ("vel", "cx"), across_pairs),
            )
        )
    first_read, *first = upwind(0, turn(halos[0], edges[1]), counts)
    first_other = [swapped(x) for x in first]
    rest_read, *rest = upwind(1, turn(halos[1], first), counts)
    kernels = turn((gain_one, gain_two, loss_kernel), halos[0])
    weights = pl.pallas_call(
        weights_kernel,
        out_shape=jax.ShapeDtypeStruct((3, points, padded), jnp.float32),
        compiler_params=params(LIMIT),
        cost_estimate=cost(1, 1),
        name="weights",
    )(
        jnp.concatenate([k.reshape(points, points * points) for k in kernels], axis=0),
        jnp.asarray(select),
        jnp.asarray(scale),
    )

    operand, weights, spread = turn((rest[0], weights, spread), first_other)
    others = [swapped(operand)]

    def scratch(count):
        return [
            pltpu.VMEM((2 * parts, count, group), bf16),
            pltpu.VMEM((points, count, 2 * padded), jnp.float32),
            pltpu.VMEM((2, 3, points // 4, count, 2 * padded), bf16),
            pltpu.VMEM(back_table.shape, bf16),
        ]

    sems = pltpu.SemaphoreType.DMA((2 * parts + 1,))
    terms = []
    for batch in range(batches - 1):
        count = counts[batch]
        starts = (0,) + tuple(g * count for g in range(parts - 1))
        following = turn(rest[batch + 1], others[-1], *terms)
        others.append(swapped(following))
        terms.append(
            pl.pallas_call(
                functools.partial(collide_kernel, starts + starts),
                in_specs=[local] * 2 + [anywhere] * (1 + 2 * parts),
                out_specs=local,
                out_shape=jax.ShapeDtypeStruct((count, local_vel), bf16),
                scratch_shapes=scratch(count) + [sems],
                compiler_params=params(34),
                cost_estimate=cost(1, 1),
                name="collide",
            )(
                weights,
                table,
                back_table,
                first[batch],
                *[rest[batch]] * (parts - 1),
                first_other[batch],
                *[others[batch]] * (parts - 1),
            )
        )

    pieces = 4
    count = counts[-1]
    starts = (0,) + tuple(g * count for g in range(parts - 1))
    return pl.pallas_call(
        functools.partial(finish_kernel, starts + starts, counts),
        in_specs=[local] * 2 + [anywhere] * (1 + batches + 2 * parts + 2),
        out_specs=anywhere,
        out_shape=jax.ShapeDtypeStruct(distribution.shape, jnp.float32),
        scratch_shapes=scratch(count)
        + [
            pltpu.VMEM((parts, block_rows, group_rows, LANES), jnp.float32),
            pltpu.VMEM((2 * capacity, group // 2), bf16),
            pltpu.VMEM((block_rows * 8, group // 2), jnp.float32),
            pltpu.VMEM((2, width_x, width_y, width_z, group), jnp.float32),
            pltpu.VMEM(spread.shape, bf16),
            pltpu.VMEM((capacity - count, local_vel), bf16),
            sems,
            pltpu.SemaphoreType.DMA((parts,)),
            pltpu.SemaphoreType.DMA((parts, pieces)),
            pltpu.SemaphoreType.DMA((batches,)),
        ],
        compiler_params=params(47),
        name="finish",
    )(
        weights,
        table,
        back_table,
        spread,
        *terms,
        first[-1],
        *[rest[-1]] * (parts - 1),
        first_other[-1],
        *[others[-1]] * (parts - 1),
        first_read,
        rest_read,
    )


def per_device(distribution, refine_level, gain_one, gain_two, loss_kernel):
    if fast_fits(distribution, gain_one.shape[0]):
        return fast_device(distribution, refine_level, gain_one, gain_two, loss_kernel)
    return plain_device(distribution, refine_level, gain_one, gain_two, loss_kernel)


def solution(mesh):
    placed = (P("cx", "cy", None, "vel"), P("cx", "cy", None), P(), P(), P())
    return jax.shard_map(
        per_device,
        mesh=mesh,
        in_specs=placed,
        out_specs=P("cx", "cy", None, "vel"),
        check_vma=False,
    )
```

```python
import functools
import math

import jax
import jax.numpy as jnp
import ml_dtypes
import numpy as np
from jax import lax
from jax.experimental import pallas as pl
from jax.experimental.pallas import tpu as pltpu
from jax.sharding import PartitionSpec as P


def extended(array, sides, width):
    for axis, dim in sides:
        count, length = (lax.axis_size(axis), array.shape[dim])
        up = [(i, (i + 1) % count) for i in range(count)]
        down = [(j, i) for i, j in up]
        last = lax.slice_in_dim(array, length - width, length, axis=dim)
        leading = lax.slice_in_dim(array, 0, width, axis=dim)
        before = lax.ppermute(last, axis, up)
        after = lax.ppermute(leading, axis, down)
        array = jnp.concatenate([before, array, after], axis=dim)
    return array


def dft_tables(points):
    indices = jnp.arange(points, dtype=jnp.int32)
    products = indices[:, None] * indices[None, :] % points
    angles = products.astype(jnp.float32) * (2.0 * math.pi / points)
    cosine = jnp.cos(angles)
    sine_table = jnp.sin(angles)
    forward = jnp.stack([jnp.stack([cosine, sine_table]), jnp.stack([-sine_table, cosine])])
    inverse = jnp.stack([jnp.stack([cosine, -sine_table]), jnp.stack([sine_table, cosine])])
    return (forward.astype(jnp.bfloat16), inverse.astype(jnp.bfloat16))


def contract(pattern, left_side, right_side):
    return jnp.einsum(pattern, left_side, right_side, preferred_element_type=jnp.float32)


def collide(cells, forward, inverse, gain_one, gain_two, loss_kernel):
    points = forward.shape[-1]
    cell_count = cells.shape[0]
    field = cells.reshape(cell_count, points, points, points)
    section_z = contract("nabz,qzw->qnabw", field, forward[:, 0]).astype(jnp.bfloat16)
    section_y = contract("pnayc,qpyw->qnawc", section_z, forward).astype(jnp.bfloat16)
    spectrum = contract("pnxbc,qpxw->qnwbc", section_y, forward)
    scale_factor = 1.0 / float(points**3)

    def filtered(kernel):
        weighted = (spectrum * (kernel * scale_factor)[None, None]).astype(jnp.bfloat16)
        back_x = contract("pnxbc,qpxw->qnwbc", weighted, inverse).astype(jnp.bfloat16)
        back_y = contract("pnayc,qpyw->qnawc", back_x, inverse).astype(jnp.bfloat16)
        return contract("pnabz,pzw->nabw", back_y, inverse[0])

    gain_term = filtered(gain_one) * filtered(gain_two)
    result = gain_term - field.astype(jnp.float32) * filtered(loss_kernel)
    return result.reshape(cell_count, points**3)


def courants(points, first_vel, local_count):
    vel_index = first_vel + jnp.arange(local_count, dtype=jnp.int32)
    index_x = vel_index // (points * points)
    index_y = vel_index // points % points
    index_z = vel_index % points

    def speed(index_part):
        return 0.3 * (2.0 * index_part.astype(jnp.float32) - (points - 1)) / (points - 1)

    return (speed(index_x), speed(index_y), speed(index_z))


def upwind_flux(courant, center, lower_side, upper_side):
    return jnp.maximum(courant, 0.0) * (center - lower_side) + jnp.minimum(courant, 0.0) * (
        upper_side - center
    )


def plain_device(distribution, refine_level, gain_one, gain_two, loss_kernel):
    points = gain_one.shape[0]
    width_x, width_y, width_z, local_vel = distribution.shape
    first_vel = lax.axis_index("vel") * local_vel
    courant_x, courant_y, courant_z = courants(points, first_vel, local_vel)
    padded = extended(distribution, (("cx", 0), ("cy", 1)), 1)
    fluxes = upwind_flux(courant_x, distribution, padded[:-2, 1:-1], padded[2:, 1:-1])
    fluxes = fluxes + upwind_flux(courant_y, distribution, padded[1:-1, :-2], padded[1:-1, 2:])
    fluxes = fluxes + upwind_flux(
        courant_z, distribution, jnp.roll(distribution, 1, 2), jnp.roll(distribution, -1, 2)
    )
    read = distribution - fluxes
    block_cells = width_x * width_y * width_z
    groups = lax.axis_size("vel")
    flattened = read.reshape(block_cells, local_vel).astype(jnp.bfloat16)
    forward, inverse = dft_tables(points)
    active = refine_level.reshape(block_cells) > 0
    slot_index = jnp.cumsum(active.astype(jnp.int32)) - 1
    capacity = block_cells // 2
    picker = (
        (slot_index[None, :] == jnp.arange(capacity, dtype=jnp.int32)[:, None]) & active[None, :]
    ).astype(jnp.bfloat16)
    chosen = jnp.dot(picker, flattened, preferred_element_type=jnp.float32).astype(jnp.bfloat16)
    terms = collide(
        lax.all_to_all(
            chosen.reshape(groups, capacity // groups, local_vel),
            "vel",
            split_axis=0,
            concat_axis=2,
            tiled=True,
        )[0],
        forward,
        inverse,
        gain_one,
        gain_two,
        loss_kernel,
    )[None]
    packed = lax.all_to_all(
        terms.astype(jnp.bfloat16), "vel", split_axis=2, concat_axis=0, tiled=True
    ).astype(terms.dtype)
    packed_rows = packed.reshape(capacity, local_vel)
    safe_slot = jnp.clip(slot_index, 0, capacity - 1)
    rates = jnp.where(active[:, None], packed_rows[safe_slot], 0.0)
    weight = 0.25 * refine_level.astype(jnp.float32)
    return read + weight[..., None] * rates.reshape(width_x, width_y, width_z, local_vel)

LANES = 128
PLANES = 4
LIMIT = 57


def half_set(points):
    middle = points // 2
    pairs = [(b, c) for c in range(1, middle) for b in range(points)]
    pairs += [(b, c) for c in (0, middle) for b in range(middle + 1)]
    weights = [1.0 if b % middle == 0 and c % middle == 0 else 2.0 for b, c in pairs]
    return np.array(pairs), np.array(weights)


def plane_table(points, padded, margin):
    pairs, _ = half_set(points)
    first, second = np.divmod(np.arange(points * points), points)
    index = np.arange(points)
    angles = (index[:, None] * index[None, :] % points).astype(np.float32)
    angles = angles * np.float32(2.0 * np.pi / points)
    cosine, sine = [
        t.astype(ml_dtypes.bfloat16).astype(np.float32) for t in (np.cos(angles), np.sin(angles))
    ]
    cos_y, sin_y = cosine[first][:, pairs[:, 0]], sine[first][:, pairs[:, 0]]
    cos_z, sin_z = cosine[second][:, pairs[:, 1]], sine[second][:, pairs[:, 1]]
    table = np.zeros((points * points + 2 * margin, 2 * padded), np.float32)
    rows = slice(margin, margin + points * points)
    table[rows, : len(pairs)] = cos_y * cos_z - sin_y * sin_z
    table[rows, padded : padded + len(pairs)] = -(cos_y * sin_z + sin_y * cos_z)
    window = points * points + margin
    level = np.flatnonzero(pairs[:, 1] == 0)
    rest = table.copy()
    rest[:, np.concatenate([level, padded + level])] = 0.0
    for start in (points * points + margin, 0):
        rest[start : start + points, level] = cosine[:, pairs[level, 0]]
        rest[start : start + points, padded + level] = -sine[:, pairs[level, 0]]
    back = np.stack([rest[margin : margin + window].T, rest[:window].T])
    copies = np.zeros((2, LANES, window), np.float32)
    place = np.arange(points * points)
    copies[0, (points * points + first) % LANES, place] = 1.0
    copies[1, first, margin + place] = 1.0
    back = np.concatenate([back, copies], axis=1)
    spare = len(pairs)
    lift = np.zeros((LANES, 2 * padded), np.float32)
    for half in (0, padded):
        columns = slice(spare % LANES, spare % LANES + points)
        lift[columns, half + level] = table[margin : margin + points**2 : points, half + level]
        table[:, half + level] = 0.0
    table[margin + place, spare + first] = 1.0
    table = np.concatenate([table, lift])
    return table.astype(ml_dtypes.bfloat16), back.astype(ml_dtypes.bfloat16)


def frequency_select(points, padded):
    pairs, weights = half_set(points)
    select = np.zeros((points * points, 2 * padded), np.float32)
    column = np.arange(len(pairs))
    select[pairs[:, 0] * points + pairs[:, 1], column] = 1.0
    mirror = (-pairs[:, 0]) % points * points + (-pairs[:, 1]) % points
    select[mirror, padded + column] = 1.0
    scale = np.zeros((1, padded), np.float32)
    scale[0, : len(pairs)] = 0.5 * weights / points**3
    return select.astype(ml_dtypes.bfloat16), scale


def weights_kernel(stacked_ref, select_ref, scale_ref, out_ref):
    kernels, points, padded = out_ref.shape
    rest = stacked_ref[...]
    picked = None
    for _ in range(3):
        piece = rest.astype(jnp.bfloat16)
        rest = rest - piece.astype(jnp.float32)
        part = jnp.dot(piece, select_ref[...], preferred_element_type=jnp.float32)
        picked = part if picked is None else picked + part
    for which in range(kernels):
        for a in range(points):
            row, mirror = which * points + a, which * points + (-a) % points
            both = picked[row : row + 1, :padded] + picked[mirror : mirror + 1, padded:]
            out_ref[which, a : a + 1, :] = both * scale_ref[...]


def transform_3(x, sign, wanted=(0, 1, 2)):
    (ar, ai), (br, bi), (cr, ci) = x
    sr, si = br + cr, bi + ci
    out = {}
    if 0 in wanted:
        out[0] = (ar + sr, ai + si)
    if 1 in wanted or 2 in wanted:
        height = sign * math.sqrt(0.75)
        mr, mi = ar - 0.5 * sr, ai - 0.5 * si
        er, ei = height * (br - cr), height * (bi - ci)
        if 1 in wanted:
            out[1] = (mr - ei, mi + er)
        if 2 in wanted:
            out[2] = (mr + ei, mi - er)
    return out


def transform_4(x, sign):
    (ar, ai), (br, bi), (cr, ci), (dr, di) = x
    pr, pi, qr, qi = ar + cr, ai + ci, ar - cr, ai - ci
    sr, si, tr, ti = br + dr, bi + di, br - dr, bi - di
    if sign < 0:
        tr, ti = -tr, -ti
    return [(pr + sr, pi + si), (qr - ti, qi + tr), (pr - sr, pi - si), (qr + ti, qi - tr)]


def transform_8(x, sign):
    even = transform_4(x[0::2], sign)
    odd = transform_4(x[1::2], sign)
    root = math.sqrt(0.5)
    (r0, i0), (r1, i1), (r2, i2), (r3, i3) = odd
    if sign > 0:
        turned = [(r0, i0), (root * (r1 - i1), root * (i1 + r1)), (-i2, r2)]
        turned.append((-root * (r3 + i3), root * (r3 - i3)))
    else:
        turned = [(r0, i0), (root * (r1 + i1), root * (i1 - r1)), (i2, -r2)]
        turned.append((root * (i3 - r3), -root * (i3 + r3)))
    low = [(e[0] + t[0], e[1] + t[1]) for e, t in zip(even, turned)]
    high = [(e[0] - t[0], e[1] - t[1]) for e, t in zip(even, turned)]
    return low + high


def spectrum_of(load):
    stage = {}
    for n2 in range(8):
        part = transform_3([load((8 * n1 + 3 * n2) % 24) for n1 in range(3)], -1)
        for k1 in range(3):
            stage[k1, n2] = part[k1]
    result = {}
    for k1 in range(3):
        part = transform_8([stage[k1, n2] for n2 in range(8)], -1)
        for k2 in range(8):
            result[(16 * k1 + 9 * k2) % 24] = part[k2]
    return result


def first_half_of(spectrum):
    stage = {}
    for k1 in range(3):
        part = transform_8([spectrum[(16 * k1 + 9 * k2) % 24] for k2 in range(8)], 1)
        for n2 in range(8):
            stage[k1, n2] = part[n2]
    result = {}
    for n2 in range(8):
        wanted = {n1: (8 * n1 + 3 * n2) % 24 for n1 in range(3) if (8 * n1 + 3 * n2) % 24 < 12}
        part = transform_3([stage[k1, n2] for k1 in range(3)], 1, tuple(wanted))
        for n1, index in wanted.items():
            result[index] = part[n1]
    return result


def tile_pair(ref, step, rows):
    parts = []
    for parity in range(2):
        at = (2 * step + parity) * LANES
        part = ref[:, :, :, at : at + LANES]
        parts.append(part.reshape(rows, part.shape[2], LANES))
    return jnp.concatenate(parts, axis=1)


def plane_speeds(points, local_vel, width_z):
    index = np.arange(points**3)
    parts = (index // (points * points), index // points % points, index % points)
    speeds = [
        np.float32(0.3) * (np.float32(2.0) * part.astype(np.float32) - np.float32(points - 1))
        / np.float32(points - 1)
        for part in parts
    ]
    tiled = np.stack(speeds).reshape(3, -1, local_vel // LANES, 1, LANES).transpose(1, 0, 2, 3, 4)
    repeated = np.repeat(tiled, width_z, axis=3)
    return repeated.reshape(repeated.shape[0], 3, -1, LANES)


def edges_kernel(first, edge_ref, falls_ref, field_ref, *refs):
    down_ref, up_ref, across_ref, low_ref, high_ref, plane_ref, sems = refs
    steps = falls_ref.shape[0] // 8
    width = low_ref.shape[0]
    groups = across_ref.shape[0] // steps
    half_steps = down_ref.shape[0] // groups
    here = pl.ds(first, low_ref.shape[3])
    last_y = field_ref.shape[1] - 1
    sources = [
        field_ref.at[:, pl.ds(0, 1), :, here],
        field_ref.at[:, pl.ds(last_y, 1), :, here],
        field_ref.at[pl.ds(edge_ref[0], 1), :, :, here],
    ]
    loads = [
        pltpu.make_async_copy(source, ref, sems.at[at])
        for at, (source, ref) in enumerate(zip(sources, (low_ref, high_ref, plane_ref)))
    ]
    for load in loads:
        load.start()
    below = [falls_ref[8 * s : 8 * s + 8, :][None] > 0.0 for s in range(steps)]

    def put(ref, at, value):
        ref[at] = value.reshape(-1, LANES).astype(jnp.bfloat16)

    loads[0].wait()
    for g in range(groups):
        row = [tile_pair(low_ref, g * steps + s, width) for s in range(steps)]
        put(down_ref, g * half_steps, row[0])
        for m in range(1, steps // 2 + 1):
            put(down_ref, g * half_steps + m, jnp.where(below[2 * m - 1], row[2 * m - 1], row[2 * m]))
    loads[1].wait()
    for g in range(groups):
        row = [tile_pair(high_ref, g * steps + s, width) for s in range(steps)]
        for m in range(steps // 2):
            put(up_ref, g * half_steps + m, jnp.where(below[2 * m], row[2 * m + 1], row[2 * m]))
        put(up_ref, g * half_steps + steps // 2, row[steps - 1])
    loads[2].wait()
    for s in range(groups * steps):
        put(across_ref, s, tile_pair(plane_ref, s, plane_ref.shape[1]))


def upwind_kernel(base, counts, side_ref, *refs):
    batches = len(counts)
    outer_refs, field_ref = refs[:5], refs[5]
    out_ref, target_refs, scratch = refs[6], refs[7 : 7 + batches], refs[7 + batches :]
    inner_refs, chosen_refs, scratch = scratch[:5], scratch[5 : 5 + batches], scratch[5 + batches :]
    speed_ref, wanted_ref, down_ref, up_ref, across_ref = inner_refs
    picker_ref, blocks, reads, wide, border, cells, load_sems, store_sems, side_sems = scratch
    chunks, width_x, width_y, width_z, lanes = blocks.shape
    steps = lanes // (2 * LANES)
    group_lanes = chosen_refs[0].shape[1]
    per_group = group_lanes // lanes
    half_steps = per_group * steps // 2 + 1
    first_row = base // LANES * width_z
    rows = pl.ds(first_row, speed_ref.shape[1])
    sources = (outer_refs[0].at[side_ref[0], :, rows, :],) + outer_refs[1:]
    inputs = [
        pltpu.make_async_copy(source, target, side_sems.at[at])
        for at, (source, target) in enumerate(zip(sources, inner_refs))
    ]
    for copy in inputs:
        copy.start()
    loads = []
    for t in range(chunks):
        source = field_ref.at[:, :, :, pl.ds(base + t * lanes, lanes)]
        loads.append(pltpu.make_async_copy(source, blocks.at[t], load_sems.at[t]))
    for load in loads[:2]:
        load.start()
    beside = jnp.where(side_ref[0] == 0, 2, 0)
    place = lax.broadcasted_iota(jnp.int32, (1, 8, LANES), 1) % width_z
    capacity = picker_ref.shape[0] // 2
    stores = []
    for copy in inputs:
        copy.wait()
    number = lax.broadcasted_iota(jnp.int32, picker_ref.shape, 0)
    matches = number == wanted_ref[0:1, :]
    picker_ref[...] = jnp.where(matches, 1.0, 0.0).astype(jnp.bfloat16)
    for t in range(chunks):
        group, chunk = t // per_group, t % per_group
        sizes, falls, sinks = [], [], []
        for u in range(steps):
            step = chunk * steps + u
            row = 8 * (t * steps + u)
            speed = [speed_ref[d, row : row + 8, :][None] for d in range(3)]
            sizes.append([jnp.abs(c) for c in speed])
            falls.append(speed[1] < 0.0)
            sinks.append(speed[2] < 0.0)
            outer = across_ref[t * steps + u].astype(jnp.float32).reshape(width_y, 8, LANES)
            wide[u, 0] = outer
            wide[u, width_x + 1] = outer
            above = down_ref[group * half_steps + (step + 1) // 2].astype(jnp.float32)
            under = up_ref[group * half_steps + step // 2].astype(jnp.float32)
            shape = (width_x, 8, LANES)
            border[u] = jnp.where(falls[u], above.reshape(shape), under.reshape(shape))
        loads[t].wait()
        if t + 2 < chunks:
            loads[t + 2].start()

        def spread_out(x, carry):
            for u in range(steps):
                at = 2 * u * LANES
                parts = [
                    blocks[t, x, :, :, at + p * LANES : at + (p + 1) * LANES] for p in range(2)
                ]
                wide[u, x + 1] = jnp.concatenate(parts, axis=1)
            return carry

        lax.fori_loop(0, width_x, spread_out, 0, unroll=4)

        def advance(x, carry):
            for u in range(steps):
                field = wide[u, x + 1]
                edge = border[u, pl.ds(x, 1)]
                fluxes = sizes[u][0] * (field - wide[u, x + beside])
                beside_y = jnp.where(
                    falls[u],
                    jnp.concatenate([field[1:], edge], axis=0),
                    jnp.concatenate([edge, field[:-1]], axis=0),
                )
                fluxes = fluxes + sizes[u][1] * (field - beside_y)
                turned = pltpu.roll(field, 4, 1)
                upper = pltpu.roll(jnp.where(place == 0, turned, field), 7, 1)
                lower = pltpu.roll(jnp.where(place == width_z - 1, turned, field), 1, 1)
                fluxes = fluxes + sizes[u][2] * (field - jnp.where(sinks[u], upper, lower))
                read = field - fluxes
                reads[t, pl.ds(x * width_y, width_y), 8 * u : 8 * u + 8, :] = read
                rows = width_y * 8
                at = pl.multiple_of(x * rows, rows)
                cells[pl.ds(at, rows), u * LANES : (u + 1) * LANES] = read.reshape(
                    rows, LANES
                ).astype(jnp.bfloat16)
            return carry

        lax.fori_loop(0, width_x, advance, 0, unroll=4)
        target = out_ref.at[:, pl.ds(8 * steps * t, 8 * steps), :]
        stores.append(pltpu.make_async_copy(reads.at[t], target, store_sems.at[t]))
        stores[-1].start()
        picked = jnp.dot(
            picker_ref[...], cells[...], preferred_element_type=jnp.float32
        ).astype(jnp.bfloat16)
        for parity in range(2):
            first = parity * capacity
            for ref, count in zip(chosen_refs, counts):
                rows = slice(group * count, (group + 1) * count)
                for u in range(steps):
                    tile = 2 * (chunk * steps + u) + parity
                    here = slice(tile * LANES, (tile + 1) * LANES)
                    ref[rows, here] = picked[first : first + count, u * LANES : (u + 1) * LANES]
                first += count
    for at, (source, target) in enumerate(zip(chosen_refs, target_refs)):
        stores.append(pltpu.make_async_copy(source, target, store_sems.at[chunks + at]))
        stores[-1].start()
    for store in stores:
        store.wait()


def window_loads(firsts, refs, cells, sems):
    loads = []
    for at, (ref, first) in enumerate(zip(refs, firsts)):
        source = ref.at[pl.ds(first, cells.shape[1])]
        loads.append(pltpu.make_async_copy(source, cells.at[at], sems.at[at]))
        loads[-1].start()
    return loads


def filter_parts(weight_ref, table_ref, cells, loads, later, section, back):
    count, slots, lanes = cells.shape
    padded = weight_ref.shape[2]
    height = table_ref.shape[0] - LANES
    window = height - 64
    pair_lanes = 2 * (height - 128)
    pairs = lanes // pair_lanes
    half = pairs * count
    sums_at = padded - LANES
    for load in loads:
        load.wait()
    for load in later:
        load.start()
    for parity in range(2):
        rows = []
        for at in range(count):
            for p in range(pairs):
                lane = p * pair_lanes + parity * (pair_lanes - window)
                rows.append(cells[at, :, lane : lane + window])
        start = 64 * (1 - parity)
        out = jnp.dot(
            jnp.concatenate(rows, axis=0),
            table_ref[start : start + window, :],
            preferred_element_type=jnp.float32,
        )
        sums = out[:, sums_at : sums_at + LANES].astype(jnp.bfloat16)
        pieces = []
        for first in (0, padded):
            lift = table_ref[height:, first + sums_at : first + padded]
            lifted = jnp.dot(sums, lift, preferred_element_type=jnp.float32)
            pieces.append(out[:, first : first + sums_at])
            pieces.append(out[:, first + sums_at : first + padded] + lifted)
        lane = 0
        for piece in pieces:
            piece = piece.astype(jnp.bfloat16).astype(jnp.float32)
            here = slice(lane, lane + piece.shape[1])
            for at in range(half):
                section[2 * at + parity, :, here] = piece[at * slots : (at + 1) * slots]
            lane += piece.shape[1]

    lane_tiles = padded // LANES
    points = weight_ref.shape[1]
    pairs_of, _ = half_set(points)
    mean_at = int(np.flatnonzero((pairs_of == 0).all(axis=1))[0])

    def transform(index, carry):
        row = pl.multiple_of(index // lane_tiles * 16, 16)
        lane = pl.multiple_of(index % lane_tiles * LANES, LANES)
        mean = lane + lax.broadcasted_iota(jnp.int32, (8, LANES), 1) == mean_at
        results = []
        for octet in range(2):
            here = pl.ds(row + 8 * octet, 8)

            def load(i):
                real = section[i, here, pl.ds(lane, LANES)]
                return real, section[i, here, pl.ds(padded + lane, LANES)]

            spectrum = spectrum_of(load)
            per_kernel = []
            for which in range(3):
                weighted = {}
                for a, (real, imag) in spectrum.items():
                    weight = weight_ref[which, pl.ds(a, 1), pl.ds(lane, LANES)]
                    weighted[a] = (real * weight, imag * weight)
                real = weighted[0][0]
                rounded = real.astype(jnp.bfloat16).astype(jnp.float32)
                weighted[0] = (jnp.where(mean, rounded, real), weighted[0][1])
                per_kernel.append(first_half_of(weighted))
            results.append(per_kernel)
        for which in range(3):
            for i in range(half):
                for q in range(2):
                    value = jnp.concatenate([results[o][which][i][q] for o in range(2)], axis=0)
                    back[i % 2, which, i // 2, pl.ds(row, 16), pl.ds(q * padded + lane, LANES)] = (
                        value.astype(jnp.bfloat16)
                    )
        return carry

    lax.fori_loop(0, slots // 16 * lane_tiles, transform, 0)


def inverse_parts(back_table, back):
    _, kernels, pairs, slots, depth = back.shape
    window = back_table.shape[2]
    outs = []
    for parity in range(2):
        out = jnp.dot(
            back[parity].reshape(kernels * pairs * slots, depth),
            back_table[parity, :depth],
            preferred_element_type=jnp.float32,
        )
        first = 0 if parity else window - LANES
        level = out[:, first : first + LANES].astype(jnp.bfloat16)
        out = out + jnp.dot(level, back_table[parity, depth:], preferred_element_type=jnp.float32)
        outs.append(out.reshape(kernels, pairs, slots, window))
    return outs


def terms_of(part, outs, cells_ref, put):
    _, slots, lanes = cells_ref.shape
    window = outs[0].shape[3]
    pair_lanes = 2 * (window - 64)
    pairs = lanes // pair_lanes
    tiles = pair_lanes // LANES
    near = lax.broadcasted_iota(jnp.int32, (slots, LANES), 1) < 64
    for pair in range(pairs):
        at = part * pairs + pair
        for tile in range(tiles):
            lane = tile * LANES
            odd_lane = lane - (pair_lanes - window)
            values = []
            for which in range(3):
                if tile < tiles // 2:
                    value = outs[0][which, at, :, lane : lane + LANES]
                elif tile > tiles // 2:
                    value = outs[1][which, at, :, odd_lane : odd_lane + LANES]
                else:
                    value = jnp.where(
                        near,
                        outs[0][which, at, :, lane : lane + LANES],
                        outs[1][which, at, :, odd_lane : odd_lane + LANES],
                    )
                values.append(value)
            lane = pair * pair_lanes + lane
            cells = cells_ref[part, :, lane : lane + LANES].astype(jnp.float32)
            put(pair * tiles + tile, (values[0] * values[1] - cells * values[2]).astype(jnp.bfloat16))


def collide_kernel(firsts, weight_ref, table_ref, back_any, *refs):
    parts = len(firsts) // 2
    terms_ref, cells, section, back, back_table, sems = refs[2 * parts :]
    lanes = cells.shape[2]
    loads = window_loads(firsts, refs[: 2 * parts], cells, sems)
    table_load = pltpu.make_async_copy(back_any, back_table, sems.at[2 * parts])
    filter_parts(weight_ref, table_ref, cells, loads, [table_load], section, back)
    table_load.wait()
    outs = inverse_parts(back_table, back)
    for part in range(parts):

        def put(tile, value):
            first = part * lanes + tile * LANES
            terms_ref[:, first : first + LANES] = value

        terms_of(part, outs, cells, put)


def finish_kernel(firsts, sizes, weight_ref, table_ref, back_any, spread_any, *refs):
    parts = len(firsts) // 2
    term_refs, refs = refs[: len(sizes) - 1], refs[len(sizes) - 1 :]
    first_read, rest_read = refs[2 * parts : 2 * parts + 2]
    out_ref, cells, section, back, back_table, reads, spots, added, staged = refs[2 * parts + 2 : -6]
    spread_ref, early_ref, cell_sems, read_sems, out_sems, extra_sems = refs[-6:]
    width_x, width_y, width_z, lanes = staged.shape[1:]
    tiles = lanes // LANES
    loads = window_loads(firsts, refs[: 2 * parts], cells, cell_sems)
    extra = [pltpu.make_async_copy(spread_any, spread_ref, extra_sems.at[0])]
    at = 0
    for ref, size in zip(term_refs, sizes):
        target = early_ref.at[pl.ds(at, size)]
        extra.append(pltpu.make_async_copy(ref, target, extra_sems.at[len(extra)]))
        at += size
    extra.append(pltpu.make_async_copy(back_any, back_table, cell_sems.at[2 * parts]))
    group_rows = reads.shape[2]
    read_loads = []
    for part in range(parts):
        rows = pl.ds(max(part - 1, 0) * group_rows, group_rows)
        source = (rest_read if part else first_read).at[:, rows, :]
        read_loads.append(pltpu.make_async_copy(source, reads.at[part], read_sems.at[part]))
    filter_parts(weight_ref, table_ref, cells, loads, extra + read_loads, section, back)
    for load in extra:
        load.wait()
    early = early_ref.shape[0]
    capacity = early + section.shape[1]
    outs = inverse_parts(back_table, back)
    pieces = out_sems.shape[1]
    piece_x = width_x // pieces
    stores = []
    for part in range(parts):

        def put(tile, value):
            first = tile % 2 * capacity
            columns = slice(tile // 2 * LANES, (tile // 2 + 1) * LANES)
            lane = part * lanes + tile * LANES
            spots[first : first + early, columns] = early_ref[:, lane : lane + LANES]
            spots[first + early : first + capacity, columns] = value

        terms_of(part, outs, cells, put)
        added[...] = jnp.dot(spread_ref[...], spots[...], preferred_element_type=jnp.float32)
        read_loads[part].wait()
        slot = part % 2
        if part >= 2:
            for store in stores[part - 2]:
                store.wait()

        def add(x, carry):
            for y in range(width_y):
                row = x * width_y + y
                at = pl.multiple_of(row * 8, 8)
                for u in range(tiles // 2):
                    value = (
                        reads[part, row, 8 * u : 8 * u + 8, :]
                        + added[pl.ds(at, 8), u * LANES : (u + 1) * LANES]
                    )
                    for parity in range(2):
                        lane = (2 * u + parity) * LANES
                        half = value[parity * width_z : (parity + 1) * width_z]
                        staged[slot, x, y, :, lane : lane + LANES] = half
            return carry

        stores.append([])
        for piece in range(pieces):
            lax.fori_loop(piece * piece_x, (piece + 1) * piece_x, add, 0, unroll=2)
            rows = pl.ds(piece * piece_x, piece_x)
            store = pltpu.make_async_copy(
                staged.at[slot, rows],
                out_ref.at[rows, :, :, pl.ds(part * lanes, lanes)],
                out_sems.at[part, piece],
            )
            store.start()
            stores[part].append(store)
    for part in range(max(parts - 2, 0), parts):
        for store in stores[part]:
            store.wait()


def params(mib):
    return pltpu.CompilerParams(vmem_limit_bytes=mib * 2**20)


def cost(flops, size):
    return pl.CostEstimate(flops=flops, bytes_accessed=size, transcendentals=0)


def fast_fits(distribution, points):
    width_x, width_y, width_z, local_vel = distribution.shape
    group = PLANES * points * points
    return (
        points == 24
        and lax.axis_size("vel") == 2
        and width_z == 4
        and local_vel * 2 == points**3
        and local_vel == 3 * group
        and width_x * width_y * width_z % 128 == 0
    )


def fast_device(distribution, refine_level, gain_one, gain_two, loss_kernel):
    points = gain_one.shape[0]
    width_x, width_y, width_z, local_vel = distribution.shape
    block_rows = width_x * width_y
    block_cells = block_rows * width_z
    group = PLANES * points * points
    parts = local_vel // group
    group_rows = group // LANES * width_z
    steps = group_rows // 8
    capacity = block_cells // 2
    early_count = capacity // 2 // 16 * 16
    counts = (early_count, capacity - early_count)
    batches = len(counts)
    vel_at = lax.axis_index("vel")
    count_x, count_y = lax.axis_size("cx"), lax.axis_size("cy")

    tiles = local_vel // LANES
    speeds = jnp.asarray(plane_speeds(points, local_vel, width_z))
    falls = np.arange(group) // points % points < points // 2
    falls = np.repeat(falls.reshape(-1, 1, LANES), width_z, axis=1).reshape(-1, LANES)
    falls = jnp.asarray(falls.astype(np.float32))
    side = vel_at.reshape(1).astype(jnp.int32)
    edge = jnp.where(vel_at == 0, 0, width_x - 1).reshape(1).astype(jnp.int32)

    level = refine_level.reshape(block_cells)
    active = level > 0
    cell_at = jnp.arange(block_cells, dtype=jnp.int32)
    before = (cell_at[:, None] < cell_at[None, :]) & active[:, None]
    slot_index = jnp.where(active, jnp.sum(before.astype(jnp.int32), axis=0), -1)
    spot = slot_index.reshape(block_rows, 1, width_z)
    parity = jnp.arange(2, dtype=jnp.int32)[None, :, None]
    shape = (block_rows, 2, width_z)
    wanted = jnp.where(spot >= 0, spot + capacity * parity, -1)
    wanted = jnp.broadcast_to(wanted, shape).reshape(-1)
    numbers = jnp.arange(2 * capacity, dtype=jnp.int32)
    wanted_rows = jnp.broadcast_to(wanted[None, :], (8, wanted.shape[0]))
    strength = jnp.broadcast_to(
        (0.25 * level.astype(jnp.float32)).reshape(block_rows, 1, width_z), shape
    ).reshape(-1)
    spread = jnp.where(wanted[:, None] == numbers[None, :], strength[:, None], 0.0)
    spread = spread.astype(jnp.bfloat16)

    padded = -(-len(half_set(points)[1]) // LANES) * LANES
    select, scale = frequency_select(points, padded)
    table, back_table = [jnp.asarray(t) for t in plane_table(points, padded, 64)]

    towards_lower = [(j, (j - 1) % count_y) for j in range(count_y)]
    towards_upper = [(j, (j + 1) % count_y) for j in range(count_y)]
    across_pairs = [(i, (i - 1) % count_x) for i in range(count_x)]
    across_pairs += [(count_x + i, count_x + (i + 1) % count_x) for i in range(count_x)]
    swap = [(0, 1), (1, 0)]
    bf16 = jnp.bfloat16

    half_steps = steps // 2 + 1
    local = pl.BlockSpec(memory_space=pltpu.VMEM)
    scalar = pl.BlockSpec(memory_space=pltpu.SMEM)
    remote = pl.BlockSpec(memory_space=pltpu.HBM)
    anywhere = pl.BlockSpec(memory_space=pl.ANY)

    def edges_of(first, groups):
        return pl.pallas_call(
            functools.partial(edges_kernel, first * group),
            in_specs=[scalar, local, remote],
            out_specs=[local] * 3,
            out_shape=[
                jax.ShapeDtypeStruct((groups * half_steps, width_x * 8, LANES), bf16),
                jax.ShapeDtypeStruct((groups * half_steps, width_x * 8, LANES), bf16),
                jax.ShapeDtypeStruct((groups * steps, width_y * 8, LANES), bf16),
            ],
            scratch_shapes=[
                pltpu.VMEM((width_x, 1, width_z, groups * group), jnp.float32),
                pltpu.VMEM((width_x, 1, width_z, groups * group), jnp.float32),
                pltpu.VMEM((1, width_y, width_z, groups * group), jnp.float32),
                pltpu.SemaphoreType.DMA((3,)),
            ],
            compiler_params=params(LIMIT),
            cost_estimate=cost(1, 1),
            name="edges",
        )(edge, falls, distribution)

    edges = [edges_of(0, 1), edges_of(1, parts - 1)]
    wide = 3
    chunks = steps // wide

    def upwind(at, halo, sizes):
        groups = parts - 1 if at else 1
        operands = (speeds, wanted_rows, *halo)
        local_speeds = jax.ShapeDtypeStruct((3, groups * group_rows, LANES), jnp.float32)
        chosen = [(groups * size, group) for size in sizes]
        return pl.pallas_call(
            functools.partial(upwind_kernel, at * group, sizes),
            in_specs=[scalar] + [anywhere] * (len(operands) + 1),
            out_specs=[anywhere] * (1 + len(sizes)),
            out_shape=[
                jax.ShapeDtypeStruct((block_rows, groups * group_rows, LANES), jnp.float32)
            ]
            + [jax.ShapeDtypeStruct(shape, bf16) for shape in chosen],
            scratch_shapes=[pltpu.VMEM(x.shape, x.dtype) for x in (local_speeds, *operands[1:])]
            + [pltpu.VMEM(shape, bf16) for shape in chosen]
            + [
                pltpu.VMEM((2 * capacity, block_rows * 8), bf16),
                pltpu.VMEM(
                    (groups * chunks, width_x, width_y, width_z, group // chunks), jnp.float32
                ),
                pltpu.VMEM((groups * chunks, block_rows, 8 * wide, LANES), jnp.float32),
                pltpu.VMEM((wide, width_x + 2, width_y, 8, LANES), jnp.float32),
                pltpu.VMEM((wide, width_x, 8, LANES), jnp.float32),
                pltpu.VMEM((block_rows * 8, wide * LANES), bf16),
                pltpu.SemaphoreType.DMA((groups * chunks,)),
                pltpu.SemaphoreType.DMA((groups * chunks + len(sizes),)),
                pltpu.SemaphoreType.DMA((len(operands),)),
            ],
            compiler_params=params(LIMIT),
            cost_estimate=cost(1, 1),
            name="upwind",
        )(side, *operands, distribution)

    def turn(value, *earlier):
        return lax.optimization_barrier((value, *earlier))[0]

    def swapped(value):
        return lax.ppermute(value, "vel", swap)

    halos = []
    for at in range(2):
        down, up, across = edges[at]
        halos.append(
            (
                lax.ppermute(down, "cy", towards_lower),
                lax.ppermute(up, "cy", towards_upper),
                lax.ppermute(across, ("vel", "cx"), across_pairs),
            )
        )
    first_read, *first = upwind(0, turn(halos[0], edges[1]), counts)
    first_other = [swapped(x) for x in first]
    rest_read, *rest = upwind(1, turn(halos[1], first), counts)
    kernels = turn((gain_one, gain_two, loss_kernel), halos[0])
    weights = pl.pallas_call(
        weights_kernel,
        out_shape=jax.ShapeDtypeStruct((3, points, padded), jnp.float32),
        compiler_params=params(LIMIT),
        cost_estimate=cost(1, 1),
        name="weights",
    )(
        jnp.concatenate([k.reshape(points, points * points) for k in kernels], axis=0),
        jnp.asarray(select),
        jnp.asarray(scale),
    )

    operand, weights, spread = turn((rest[0], weights, spread), first_other)
    others = [swapped(operand)]

    def scratch(count):
        return [
            pltpu.VMEM((2 * parts, count, group), bf16),
            pltpu.VMEM((points, count, 2 * padded), jnp.float32),
            pltpu.VMEM((2, 3, points // 4, count, 2 * padded), bf16),
            pltpu.VMEM(back_table.shape, bf16),
        ]

    sems = pltpu.SemaphoreType.DMA((2 * parts + 1,))
    terms = []
    for batch in range(batches - 1):
        count = counts[batch]
        starts = (0,) + tuple(g * count for g in range(parts - 1))
        following = turn(rest[batch + 1], others[-1], *terms)
        others.append(swapped(following))
        terms.append(
            pl.pallas_call(
                functools.partial(collide_kernel, starts + starts),
                in_specs=[local] * 2 + [anywhere] * (1 + 2 * parts),
                out_specs=local,
                out_shape=jax.ShapeDtypeStruct((count, local_vel), bf16),
                scratch_shapes=scratch(count) + [sems],
                compiler_params=params(34),
                cost_estimate=cost(1, 1),
                name="collide",
            )(
                weights,
                table,
                back_table,
                first[batch],
                *[rest[batch]] * (parts - 1),
                first_other[batch],
                *[others[batch]] * (parts - 1),
            )
        )

    pieces = 4
    count = counts[-1]
    starts = (0,) + tuple(g * count for g in range(parts - 1))
    return pl.pallas_call(
        functools.partial(finish_kernel, starts + starts, counts),
        in_specs=[local] * 2 + [anywhere] * (1 + batches + 2 * parts + 2),
        out_specs=anywhere,
        out_shape=jax.ShapeDtypeStruct(distribution.shape, jnp.float32),
        scratch_shapes=scratch(count)
        + [
            pltpu.VMEM((parts, block_rows, group_rows, LANES), jnp.float32),
            pltpu.VMEM((2 * capacity, group // 2), bf16),
            pltpu.VMEM((block_rows * 8, group // 2), jnp.float32),
            pltpu.VMEM((2, width_x, width_y, width_z, group), jnp.float32),
            pltpu.VMEM(spread.shape, bf16),
            pltpu.VMEM((capacity - count, local_vel), bf16),
            sems,
            pltpu.SemaphoreType.DMA((parts,)),
            pltpu.SemaphoreType.DMA((parts, pieces)),
            pltpu.SemaphoreType.DMA((batches,)),
        ],
        compiler_params=params(47),
        name="finish",
    )(
        weights,
        table,
        back_table,
        spread,
        *terms,
        first[-1],
        *[rest[-1]] * (parts - 1),
        first_other[-1],
        *[others[-1]] * (parts - 1),
        first_read,
        rest_read,
    )


def per_device(distribution, refine_level, gain_one, gain_two, loss_kernel):
    if fast_fits(distribution, gain_one.shape[0]):
        return fast_device(distribution, refine_level, gain_one, gain_two, loss_kernel)
    return plain_device(distribution, refine_level, gain_one, gain_two, loss_kernel)


def solution(mesh):
    placed = (P("cx", "cy", None, "vel"), P("cx", "cy", None), P(), P(), P())
    return jax.shard_map(
        per_device,
        mesh=mesh,
        in_specs=placed,
        out_specs=P("cx", "cy", None, "vel"),
        check_vma=False,
    )
```
